32 devices in a mesh: wide: 8 (over z, y), narrow: 4 (over x, core).
Axes of the slice: x: 2, y: 2, z: 4, core: 2. Of those that a mesh axis runs over, the one named last changes fastest.
Arguments:
- observed: bfloat16 [96, 121, 256], P(('wide', 'narrow')), may hold values from -4 to 4
- following: bfloat16 [96, 121, 256], P(('wide', 'narrow')), may hold values from -4 to 4
- game_ids: int32 [96], P(('wide', 'narrow')), may hold values from 0 to 3
- actions: int32 [96, 2], P(('wide', 'narrow')), may hold values from 0 to 17, as said below
- legal_mask: int32 [96, 18], P(('wide', 'narrow')), may hold values from 0 to 1
- rewards: float32 [96], P(('wide', 'narrow')), may hold values from -1 to 1
- discounts: float32 [96], P(('wide', 'narrow')), may hold values from 0.5 to 0.99
- done_flags: int32 [96], P(('wide', 'narrow')), may hold values 0 or 1
- params_top: float32 [3700736], P(('wide', 'narrow')), may hold values from -8 to 8
- params_blocks: float32 [2, 4462592], P(None, ('wide', 'narrow')), may hold values from -8 to 8
- first_top: float32 [3700736], P(('wide', 'narrow')), may hold values from -1 to 1
- first_blocks: float32 [2, 4462592], P(None, ('wide', 'narrow')), may hold values from -1 to 1
- second_top: float32 [3700736], P(('wide', 'narrow')), may hold values from 0 to 1, as said below
- second_blocks: float32 [2, 4462592], P(None, ('wide', 'narrow')), may hold values from 0 to 1, as said below
- average_top: float32 [3700736], P(('wide', 'narrow')), may hold values from -8 to 8
- average_blocks: float32 [2, 4462592], P(None, ('wide', 'narrow')), may hold values from -8 to 8
- target_top: bfloat16 [3700736], P(('wide', 'narrow')), may hold values from -8 to 8
- target_blocks: bfloat16 [2, 4462592], P(None, ('wide', 'narrow')), may hold values from -8 to 8
Outputs:
- loss_total: float32 [], replicated
- matrix_norms: float32 [2, 12], replicated
- updated_top: float32 [3700736], P(('wide', 'narrow'))
- half_top: bfloat16 [3700736], P(('wide', 'narrow'))
- momentum_top: float32 [3700736], P(('wide', 'narrow'))
- variance_top: float32 [3700736], P(('wide', 'narrow'))
- averaged_top: float32 [3700736], P(('wide', 'narrow'))
- updated_blocks: float32 [2, 4462592], P(None, ('wide', 'narrow'))
- half_blocks: bfloat16 [2, 4462592], P(None, ('wide', 'narrow'))
- momentum_blocks: float32 [2, 4462592], P(None, ('wide', 'narrow'))
- variance_blocks: float32 [2, 4462592], P(None, ('wide', 'narrow'))
- averaged_blocks: float32 [2, 4462592], P(None, ('wide', 'narrow'))
- gain_grads: float32 [2, 6144], P(None, ('wide', 'narrow'))
The draws below stay inside these ranges and needn't reach their ends.
Inputs may be any that keep to these rules, and one draw needn't show every extreme that they name: `actions`: column 0 is legal in legal_mask; column 1 is any action. `second_top`: positive. `second_blocks`: positive.
All inputs are finite; a program needn't handle non-finite values. No bound on the sum of `done_flags` on one device may be relied on, other than what follows from the above.
Results may differ from the reference program's by a relative error of at most 0.025.
Values may be sent and summed in bfloat16 or wider, within the bound.
No kernel may reach another device: no remote copies, remote signals or barrier semaphores. Data moves between devices by JAX's collectives and lax.ppermute only.
A program may use at most 320 MiB of HBM per device.

```python
import math
import jax
import jax.numpy as jnp
from jax import lax

D = 2048
BOT = 512
GROUPS = 32
PATCH_IN = 256
DPROJ = 512
ACTIONS = 18
ATOMS = 51
GAMES = 4
BLOCKS = 2
SIDE = 11
STEP = 5
PIX = 121
FRAMES = 96
DEVICES = 32


def top_lengths():
    return [PATCH_IN * D, D * PIX, D * DPROJ, DPROJ * GAMES * ACTIONS * ATOMS]


def block_lengths():
    return [D * BOT, 9 * BOT * BOT, BOT * D, 2 * (2 * BOT + D)]


def rising(count, low_end, high_end):
    return low_end + (high_end - low_end) * jnp.arange(count, dtype=jnp.float32) / count


def lay_out(segments):
    return jnp.concatenate([piece.reshape(DEVICES, -1) for piece in segments], axis=1).reshape(-1)


def values(key, count, scale, blend, low_end, high_end):
    normal_part = jax.random.truncated_normal(key, -3.0, 3.0, (count,), jnp.float32)
    flat_part = jax.random.uniform(jax.random.fold_in(key, 1), (count,), jnp.float32, -1.7, 1.7)
    return scale * ((1.0 - blend) * normal_part + blend * flat_part) * rising(count, low_end, high_end)


def gain_values(key, blend, low_end, high_end):
    parts = []
    for index, width in enumerate([BOT, BOT, BOT, BOT, D, D]):
        sub = jax.random.fold_in(key, index)
        if index % 2 == 0:
            parts.append(jax.random.uniform(sub, (width,), jnp.float32, 0.6, 1.4))
        else:
            parts.append(values(sub, width, 0.3, blend, 1.0, 1.0))
    return jnp.concatenate(parts) * rising(2 * (2 * BOT + D), low_end, high_end)


def weight_top(key, blend, low_end, high_end):
    scales = [PATCH_IN ** (-0.5), 1.0 / SIDE, D ** (-0.5), 2.5 * DPROJ ** (-0.5)]
    segments = [values(jax.random.fold_in(key, index), count, scale, blend, low_end, high_end) for index, (count, scale) in enumerate(zip(top_lengths(), scales))]
    return lay_out(segments)


def weight_blocks(key, blend, low_end, high_end):
    lengths = block_lengths()
    scales = [D ** (-0.5), (9 * BOT) ** (-0.5), BOT ** (-0.5)]
    rows = []
    for block in range(BLOCKS):
        sub = jax.random.fold_in(key, block)
        segments = [values(jax.random.fold_in(sub, index), lengths[index], scales[index], blend, low_end, high_end) for index in range(3)]
        segments.append(gain_values(jax.random.fold_in(sub, 3), blend, low_end, high_end))
        rows.append(lay_out(segments))
    return jnp.stack(rows)


def moment_flat(key, lengths, scales, power, blend, low_end, high_end):
    segments = []
    for index, (count, scale) in enumerate(zip(lengths, scales)):
        sub = jax.random.fold_in(key, index)
        if power == 1:
            segments.append(values(sub, count, scale, blend, 1.0, 1.0))
        else:
            factor = jnp.exp(jax.random.uniform(sub, (count,), jnp.float32, 0.0, math.log(4.0)))
            segments.append(scale * scale * factor / jnp.square(rising(count, low_end, high_end)))
    return lay_out(segments)


def top_scales():
    root = FRAMES ** (-0.5)
    return [0.005 * root, 0.004 * root, 0.012 * root, 0.0015 * root]


def block_scales():
    root = FRAMES ** (-0.5)
    return [0.005 * root, 0.005 * root, 0.005 * root, 0.05 * root]


def moment_blocks(key, power, blend, low_end, high_end):
    return jnp.stack([moment_flat(jax.random.fold_in(key, block), block_lengths(), block_scales(), power, blend, low_end, high_end) for block in range(BLOCKS)])


def draw_params_top(key, part):
    key = jax.random.fold_in(key, 11)
    return weight_top(key, 0.0, 0.75, 1.5)


def draw_params_blocks(key, part):
    key = jax.random.fold_in(key, 12)
    return weight_blocks(key, 0.0, 0.75, 1.5)


def draw_average_top(key, part):
    key = jax.random.fold_in(key, 13)
    return weight_top(key, 0.0, 0.75, 1.5)


def draw_average_blocks(key, part):
    key = jax.random.fold_in(key, 14)
    return weight_blocks(key, 0.0, 0.75, 1.5)


def draw_target_top(key, part):
    key = jax.random.fold_in(key, 15)
    return weight_top(key, 0.0, 0.75, 1.5).astype(jnp.bfloat16)


def draw_target_blocks(key, part):
    key = jax.random.fold_in(key, 16)
    return weight_blocks(key, 0.0, 0.75, 1.5).astype(jnp.bfloat16)


def draw_first_top(key, part):
    key = jax.random.fold_in(key, 17)
    return moment_flat(key, top_lengths(), top_scales(), 1, 0.0, 1.0, 1.0)


def draw_first_blocks(key, part):
    key = jax.random.fold_in(key, 18)
    return moment_blocks(key, 1, 0.0, 1.0, 1.0)


def draw_second_top(key, part):
    key = jax.random.fold_in(key, 19)
    return moment_flat(key, top_lengths(), top_scales(), 2, 0.0, 0.75, 1.5)


def draw_second_blocks(key, part):
    key = jax.random.fold_in(key, 20)
    return moment_blocks(key, 2, 0.0, 0.75, 1.5)


def picks_and_mask(key):
    picked = jax.random.randint(key, (FRAMES, 2), 0, ACTIONS)
    bits = (jax.random.randint(jax.random.fold_in(key, 1), (FRAMES, ACTIONS), 0, 10) < 7).astype(jnp.int32)
    forced = (jnp.arange(ACTIONS)[None, :] == picked[:, 0:1]).astype(jnp.int32)
    return (picked, jnp.maximum(bits, forced))


def draw_actions(key, part):
    picked, legal = picks_and_mask(key)
    key = jax.random.fold_in(key, 21)
    return picked


def draw_legal_mask(key, part):
    picked, legal = picks_and_mask(key)
    key = jax.random.fold_in(key, 22)
    return legal


def draw_rewards(key, part):
    key = jax.random.fold_in(key, 23)
    base = jax.random.uniform(key, (FRAMES,), jnp.float32, -1.0, 1.0)
    return base * rising(FRAMES, 0.35, 1.0)


def plant(array, key, low, high):
    longest = array.shape.index(max(array.shape))
    spots = []
    for shift in (0, 1):
        where = [jax.random.randint(jax.random.fold_in(key, axis), (), 0, length) for axis, length in enumerate(array.shape)]
        where[longest] = (where[longest] + shift) % array.shape[longest]
        spots.append(tuple(where))
    return array.at[spots[0]].set(low).at[spots[1]].set(high)


def levels(stream_key, extent, shards, low, high):
    loudness, own = 1.0, jax.random.fold_in(stream_key, 6)
    for dim, blocks in shards:
        steps = jnp.exp(jax.random.uniform(jax.random.fold_in(own, dim), (blocks,), jnp.float32, low / len(shards), high / len(shards)))
        loudness = loudness * jnp.repeat(steps, extent[dim] // blocks).reshape([-1 if axis == dim else 1 for axis in range(len(extent))])
    return loudness


def gaussian(key, dims, scale, bound, shards=(), held_as=jnp.bfloat16):
    loudness = levels(key, dims, shards, -0.22, 0.18) if shards else 1.0
    entries = jax.random.normal(key, dims, jnp.float32) * scale * loudness
    return jnp.minimum(jnp.maximum(entries, -bound), bound).astype(held_as)


def setup_inputs(seed: int = 0) -> dict:
    key_list = jax.random.split(jax.random.key(seed), 19)
    return {
        "observed": gaussian(key_list[0], (FRAMES, PIX, PATCH_IN), 1.0, 4.0, ((0, 32),)),
        "following": gaussian(key_list[1], (FRAMES, PIX, PATCH_IN), 1.0, 4.0, ((0, 32),)),
        "game_ids": plant(jax.random.randint(key_list[2], (FRAMES,), 0, GAMES), jax.random.fold_in(key_list[2], 1), 0, GAMES - 1).astype(jnp.int32),
        "actions": draw_actions(jax.random.fold_in(key_list[18], 71), 0),
        "legal_mask": draw_legal_mask(jax.random.fold_in(key_list[18], 71), 0),
        "rewards": draw_rewards(jax.random.fold_in(key_list[18], 71), 0),
        "discounts": jnp.clip(0.5 + 0.49 * jax.random.uniform(key_list[6], (FRAMES,), jnp.float32) ** levels(key_list[6], (FRAMES,), ((0, 32),), -0.2, 0.2), 0.5, 0.99),
        "done_flags": plant((jax.random.randint(key_list[7], (FRAMES,), 0, 5) < 1).astype(jnp.int32), jax.random.fold_in(key_list[7], 1), 0, 1),
        "params_top": draw_params_top(jax.random.fold_in(key_list[18], 71), 0),
        "params_blocks": draw_params_blocks(jax.random.fold_in(key_list[18], 71), 0),
        "first_top": draw_first_top(jax.random.fold_in(key_list[18], 71), 0),
        "first_blocks": draw_first_blocks(jax.random.fold_in(key_list[18], 71), 0),
        "second_top": draw_second_top(jax.random.fold_in(key_list[18], 71), 0),
        "second_blocks": draw_second_blocks(jax.random.fold_in(key_list[18], 71), 0),
        "average_top": draw_average_top(jax.random.fold_in(key_list[18], 71), 0),
        "average_blocks": draw_average_blocks(jax.random.fold_in(key_list[18], 71), 0),
        "target_top": draw_target_top(jax.random.fold_in(key_list[18], 71), 0),
        "target_blocks": draw_target_blocks(jax.random.fold_in(key_list[18], 71), 0),
    }


FULL_PRECISION = lax.Precision.HIGHEST
CQL_WEIGHT = 0.05
BETA_ONE = 0.5
BETA_TWO = 0.5
LEARNING_RATE = 0.25
WEIGHT_DECAY = 0.01

@jax.custom_vjp
def low(v):
    return lax.optimization_barrier(v.astype(jnp.bfloat16)).astype(jnp.float32)

@jax.custom_vjp
def low_back(v):
    return v

def low_keep(v):
    return (low(v), None)

def low_pass(kept, grad):
    return (grad,)

def back_keep(v):
    return (v, None)

def back_low(kept, grad):
    return (low(grad),)
low.defvjp(low_keep, low_pass)
low_back.defvjp(back_keep, back_low)

def average_decay():
    return min(0.99, (1.0 + STEP) / (10.0 + STEP))

def matmul(left, right):
    return jnp.dot(left, right, precision=FULL_PRECISION)

def segment_lengths():
    top = [PATCH_IN * D, D * PIX, D * DPROJ, DPROJ * GAMES * ACTIONS * ATOMS]
    block = [D * BOT, 9 * BOT * BOT, BOT * D, 2 * (2 * BOT + D)]
    return (top, block)

def cut_points(lengths):
    cuts = []
    offset = 0
    for length in lengths:
        width = length // DEVICES
        cuts.append((offset, width))
        offset += width
    return cuts

def unpack(flat, lengths):
    grid = flat.reshape(DEVICES, -1)
    return [grid[:, start:start + width].reshape(-1) for start, width in cut_points(lengths)]

def split_gains(gains):
    pieces = []
    offset = 0
    for width in [BOT, BOT, BOT, BOT, D, D]:
        pieces.append(gains[offset:offset + width])
        offset += width
    return pieces

def group_norm(hidden, gain, bias):
    chans = hidden.shape[-1]
    split = hidden.reshape(-1, PIX, GROUPS, chans // GROUPS)
    mean = lax.optimization_barrier(jnp.mean(split, axis=(1, 3), keepdims=True))
    centered = split - mean
    var = lax.optimization_barrier(jnp.mean(centered * centered, axis=(1, 3), keepdims=True))
    return (centered * lax.rsqrt(var + 1e-05)).reshape(hidden.shape) * gain + bias

def columns(acts):
    chans = acts.shape[-1]
    grid = jnp.pad(acts.reshape(-1, SIDE, SIDE, chans), ((0, 0), (1, 1), (1, 1), (0, 0)))
    taps = [grid[:, row:row + SIDE, col:col + SIDE, :] for row in range(3) for col in range(3)]
    return jnp.concatenate(taps, axis=-1).reshape(-1, 9 * chans)

def block_apply(stream, flats):
    weight_in, weight_mid, weight_out, gains = flats
    gain_one, bias_one, gain_two, bias_two, gain_three, bias_three = split_gains(low(gains))
    first_pre = low_back(matmul(low(stream), low(weight_in).reshape(D, BOT)))
    first_act = jax.nn.silu(group_norm(first_pre, gain_one, bias_one))
    second_pre = low_back(matmul(columns(low(first_act)), low(weight_mid).reshape(9 * BOT, BOT)))
    second_act = jax.nn.silu(group_norm(second_pre, gain_two, bias_two))
    third_pre = low_back(matmul(low(second_act), low(weight_out).reshape(BOT, D)))
    return jax.nn.silu(stream + group_norm(third_pre, gain_three, bias_three))

def network(top, blocks, frames, game_hot):
    top_lengths, block_lengths = segment_lengths()
    patch_w, pool_w, proj_w, heads_w = unpack(top, top_lengths)
    count = frames.shape[0]
    stream = low_back(matmul(frames.reshape(-1, PATCH_IN), low(patch_w).reshape(PATCH_IN, D)))
    for index in range(BLOCKS):
        stream = block_apply(stream, unpack(blocks[index], block_lengths))
    pooled = low_back(jnp.einsum('npc,cp->nc', low(stream).reshape(count, PIX, D), low(pool_w).reshape(D, PIX), precision=FULL_PRECISION))
    hidden = jax.nn.silu(low_back(matmul(low(pooled), low(proj_w).reshape(D, DPROJ))))
    scores = low_back(matmul(low(hidden), low(heads_w).reshape(DPROJ, GAMES * ACTIONS * ATOMS)))
    return select(scores, game_hot)

def select(scores, game_hot):
    count = scores.shape[0]
    picked = jnp.einsum('ng,ngk->nk', game_hot, scores.reshape(count, GAMES, ACTIONS * ATOMS), precision=FULL_PRECISION)
    return picked.reshape(count, ACTIONS, ATOMS)

def support():
    return -10.0 + 20.0 / (ATOMS - 1) * jnp.arange(ATOMS, dtype=jnp.float32)

def target_dist(logits_next, next_hot, rewards, discounts, done_flags):
    chosen = jnp.einsum('na,naz->nz', next_hot, logits_next, precision=FULL_PRECISION)
    probs = jax.nn.softmax(chosen, axis=-1)
    atoms = support()
    spacing = 20.0 / (ATOMS - 1)
    keep = discounts * (1.0 - done_flags.astype(jnp.float32))
    moved = jnp.clip(rewards[:, None] + keep[:, None] * atoms[None, :], -10.0, 10.0)
    kernel = jnp.clip(1.0 - jnp.abs(moved[:, :, None] - atoms[None, None, :]) / spacing, 0.0, 1.0)
    return jnp.einsum('nj,nji->ni', probs, kernel, precision=FULL_PRECISION)

def frame_losses(logits, target, taken_hot, legal_now):
    logp = jax.nn.log_softmax(logits, axis=-1)
    action_values = lax.optimization_barrier(jnp.sum(jnp.exp(logp) * support(), axis=-1))
    taken_logp = lax.optimization_barrier(jnp.sum(taken_hot[:, :, None] * logp, axis=1))
    cross = -lax.optimization_barrier(jnp.sum(target * taken_logp, axis=-1))
    masked = jnp.where(legal_now > 0, action_values, -1e+30)
    largest = lax.optimization_barrier(jnp.max(masked, axis=-1, keepdims=True))
    spread = jnp.log(lax.optimization_barrier(jnp.sum(jnp.exp(masked - largest), axis=-1))) + largest[:, 0]
    return cross + CQL_WEIGHT * (spread - lax.optimization_barrier(jnp.sum(taken_hot * action_values, axis=-1)))

def lamb_parts(params, grads, first, second):
    momentum = BETA_ONE * first + (1.0 - BETA_ONE) * grads
    variance = BETA_TWO * second + (1.0 - BETA_TWO) * grads * grads
    direction = momentum / (1.0 - BETA_ONE ** STEP) / (jnp.sqrt(variance / (1.0 - BETA_TWO ** STEP)) + 1e-06) + WEIGHT_DECAY * params
    return (momentum, variance, direction)

def squares(grid, cuts):
    return jnp.stack([lax.optimization_barrier(jnp.sum(jnp.square(grid[..., start:start + width]), axis=(-2, -1))) for start, width in cuts], axis=-1)

def spread_ratio(ratio, grid, cuts):
    parts = [jnp.broadcast_to(ratio[..., None, index:index + 1], grid.shape[:-1] + (width,)) for index, (start, width) in enumerate(cuts)]
    return jnp.concatenate(parts, axis=-1)

def reference(observed, following, game_ids, actions, legal_mask, rewards, discounts, done_flags, params_top, params_blocks, first_top, first_blocks, second_top, second_blocks, average_top, average_blocks, target_top, target_blocks):
    frames_all = observed.shape[0]
    groups = DEVICES // 4
    size = frames_all // groups
    top_lengths, block_lengths = segment_lengths()
    target_tops = target_top.astype(jnp.float32)
    target_mids = target_blocks.astype(jnp.float32)
    game_hot = (game_ids[:, None] == jnp.arange(GAMES)[None, :]).astype(jnp.float32)
    taken_hot = (actions[:, 0:1] == jnp.arange(ACTIONS)[None, :]).astype(jnp.float32)
    next_hot = (actions[:, 1:2] == jnp.arange(ACTIONS)[None, :]).astype(jnp.float32)
    batch = (observed.astype(jnp.float32), following.astype(jnp.float32), game_hot, taken_hot, next_hot, legal_mask, rewards, discounts, done_flags)
    batch = jax.tree.map(lambda value: value.reshape((groups, size) + value.shape[1:]), batch)

    def one_group(carry, item):
        frames, nexts, games, taken, chosen, legal_now, reward, discount, done = item
        target = target_dist(network(target_tops, target_mids, nexts, games), chosen, reward, discount, done)

        def objective(top, blocks):
            losses = frame_losses(network(top, blocks, frames, games), target, taken, legal_now)
            return (jnp.sum(losses) / frames_all, jnp.sum(losses))
        value, back, total = jax.vjp(objective, params_top, params_blocks, has_aux=True)
        grad_top, grad_blocks = back(jnp.float32(1.0))
        return ((carry[0] + grad_top, carry[1] + grad_blocks, carry[2] + total), None)
    start = (jnp.zeros_like(params_top), jnp.zeros_like(params_blocks), jnp.float32(0.0))
    (grad_top, grad_blocks, loss_total), ignored = lax.scan(one_group, start, batch)
    momentum_top, variance_top, direction_top = lamb_parts(params_top, grad_top, first_top, second_top)
    momentum_blocks, variance_blocks, direction_blocks = lamb_parts(params_blocks, grad_blocks, first_blocks, second_blocks)
    top_cuts = cut_points(top_lengths)
    block_cuts = cut_points(block_lengths)
    grid_top = params_top.reshape(DEVICES, -1)
    grid_blocks = params_blocks.reshape(BLOCKS, DEVICES, -1)
    weight_sq = jnp.concatenate([squares(grid_top, top_cuts), squares(grid_blocks, block_cuts).reshape(-1)])
    update_sq = jnp.concatenate([squares(direction_top.reshape(DEVICES, -1), top_cuts), squares(direction_blocks.reshape(BLOCKS, DEVICES, -1), block_cuts).reshape(-1)])
    weight_norm = jnp.sqrt(weight_sq)
    update_norm = jnp.sqrt(update_sq)
    ratio = weight_norm / (update_norm + 1e-06)
    scale_top = spread_ratio(ratio[:4], grid_top, top_cuts).reshape(-1)
    scale_blocks = spread_ratio(ratio[4:].reshape(BLOCKS, 4), grid_blocks, block_cuts).reshape(BLOCKS, -1)
    updated_top = params_top - LEARNING_RATE * scale_top * direction_top
    updated_blocks = params_blocks - LEARNING_RATE * scale_blocks * direction_blocks
    decay = average_decay()
    averaged_top = decay * average_top + (1.0 - decay) * updated_top
    averaged_blocks = decay * average_blocks + (1.0 - decay) * updated_blocks
    matrix_norms = jnp.stack([weight_norm, update_norm])
    gain_start, gain_width = block_cuts[3]
    gain_grads = grad_blocks.reshape(BLOCKS, DEVICES, -1)[:, :, gain_start:gain_start + gain_width].reshape(BLOCKS, -1)
    return (loss_total, matrix_norms, updated_top, updated_top.astype(jnp.bfloat16), momentum_top, variance_top, averaged_top, updated_blocks, updated_blocks.astype(jnp.bfloat16), momentum_blocks, variance_blocks, averaged_blocks, gain_grads)
```

```python
import functools

import jax
import jax.numpy as jnp
from jax import lax
from jax.experimental import pallas as pl
from jax.experimental.pallas import tpu as pltpu
from jax.sharding import PartitionSpec as P

D = 2048
BOT = 512
GROUPS = 32
SIDE = 11
PIX = 121
TAPS = 9

ROWS = 128
LANES = 256
VMEM_LIMIT = 60 * 1024 * 1024


def shifts():
    pixel = jnp.arange(ROWS)
    row, col = (pixel // SIDE, pixel % SIDE)
    mats = []
    for tap in range(TAPS):
        at_row, at_col = (row + tap // 3 - 1, col + tap % 3 - 1)
        inside = (at_row >= 0) & (at_row < SIDE) & (at_col >= 0) & (at_col < SIDE) & (pixel < PIX)
        mats.append((inside[:, None] & (pixel[None, :] == (at_row * SIDE + at_col)[:, None])))
    return jnp.concatenate(mats, axis=0).astype(jnp.bfloat16)


def dot(left, right):
    return jnp.dot(left, right, preferred_element_type=jnp.float32)


def dot_rows(left, right):
    return lax.dot_general(
        left, right, (((0,), (0,)), ((), ())), preferred_element_type=jnp.float32
    )


def dot_lanes(left, right):
    return lax.dot_general(
        left, right, (((1,), (1,)), ((), ())), preferred_element_type=jnp.float32
    )


def each_chunk(count, chans, body, unroll=1):
    per = chans // LANES

    def step(index, carry):
        frame = index // per
        rows = pl.ds(pl.multiple_of(frame * ROWS, ROWS), ROWS)
        lanes = pl.ds(pl.multiple_of((index % per) * LANES, LANES), LANES)
        body(pl.ds(frame, 1), rows, lanes)
        return carry

    lax.fori_loop(0, count * per, step, 0, unroll=unroll)


def real_rows():
    return lax.broadcasted_iota(jnp.int32, (ROWS, LANES), 0) < PIX


def group_mean(sums):
    chans = sums.shape[1]
    width = chans // GROUPS
    lane = lax.broadcasted_iota(jnp.int32, sums.shape, 1)
    step = 1
    while step < width:
        ahead = pltpu.roll(sums, chans - step, 1)
        behind = pltpu.roll(sums, step, 1)
        sums = sums + jnp.where((lane & step) == 0, ahead, behind)
        step *= 2
    return sums * (1.0 / (PIX * width))


def silu(value):
    return value / (1.0 + jnp.exp(-value))


def silu_slope(value):
    gate = 1.0 / (1.0 + jnp.exp(-value))
    return gate * (1.0 + value * (1.0 - gate))


def normalise(count, chans, hid, sums, rstd, rstd_at):
    whole = pl.ds(0, chans)
    sums[:, whole] = jnp.zeros((sums.shape[0], chans), jnp.float32)

    def add(frame, rows, lanes):
        sums[frame, lanes] = jnp.sum(hid[rows, lanes], axis=0, keepdims=True)

    each_chunk(count, chans, add, unroll=2)
    sums[:, whole] = group_mean(sums[:, whole])

    def center(frame, rows, lanes):
        value = jnp.where(real_rows(), hid[rows, lanes] - sums[frame, lanes], 0.0)
        hid[rows, lanes] = value
        sums[frame, lanes] = jnp.sum(value * value, axis=0, keepdims=True)

    each_chunk(count, chans, center, unroll=2)
    at = pl.ds(rstd_at, chans)
    rstd[:, at] = lax.rsqrt(group_mean(sums[:, whole]) + 1e-05)


def forward_kernel(count, keep, *refs):
    x, w_in, w_mid, w_out, gains, shift, out = refs[:7]
    hid_one, hid_two, hid_three, rstd, low, act, cols, sums = refs[7:]

    def cast(frame, rows, lanes):
        low[rows, lanes] = x[rows, lanes].astype(jnp.bfloat16)

    def activate(hid, at, offset):
        def body(frame, rows, lanes):
            gain = gains[:, pl.ds(offset + lanes.start, LANES)]
            bias = gains[:, pl.ds(offset + BOT + lanes.start, LANES)]
            value = hid[rows, lanes] * rstd[frame, pl.ds(at + lanes.start, LANES)]
            hid[rows, lanes] = value
            value = jnp.where(real_rows(), silu(value * gain + bias), 0.0)
            act[rows, lanes] = value.astype(jnp.bfloat16)

        return body

    each_chunk(count, D, cast)
    hid_one[...] = dot(low[...], w_in[...])
    normalise(count, BOT, hid_one, sums, rstd, 0)
    each_chunk(count, BOT, activate(hid_one, 0, 0))
    for frame in range(count):
        rows = pl.ds(frame * ROWS, ROWS)
        for tap in range(TAPS):
            picked = dot(shift[pl.ds(tap * ROWS, ROWS), :], act[rows, :])
            cols[rows, pl.ds(tap * BOT, BOT)] = picked.astype(jnp.bfloat16)
    hid_two[...] = dot(cols[...], w_mid[...])
    normalise(count, BOT, hid_two, sums, rstd, BOT)
    each_chunk(count, BOT, activate(hid_two, BOT, 2 * BOT))
    for part in range(D // BOT):
        lanes = pl.ds(part * BOT, BOT)
        hid_three[:, lanes] = dot(act[...], w_out[:, lanes])
    normalise(count, D, hid_three, sums, rstd, 2 * BOT)

    def finish(frame, rows, lanes):
        gain = gains[:, pl.ds(4 * BOT + lanes.start, LANES)]
        bias = gains[:, pl.ds(4 * BOT + D + lanes.start, LANES)]
        value = hid_three[rows, lanes] * rstd[frame, pl.ds(2 * BOT + lanes.start, LANES)]
        if keep:
            hid_three[rows, lanes] = value
        value = silu(x[rows, lanes] + value * gain + bias)
        out[rows, lanes] = jnp.where(real_rows(), value, 0.0)

    each_chunk(count, D, finish)


def in_vmem(number):
    return [pl.BlockSpec(memory_space=pltpu.VMEM)] * number


def f32(*shape):
    return jax.ShapeDtypeStruct(shape, jnp.float32)


def bf16(*shape):
    return jax.ShapeDtypeStruct(shape, jnp.bfloat16)


def stat_rows(count):
    return -(-count // 8) * 8


def block_forward(stream, w_in, w_mid, w_out, gains, shift, keep):
    rows = stream.shape[0]
    count = rows // ROWS
    stats = stat_rows(count)
    kept = [
        ((rows, BOT), jnp.float32),
        ((rows, BOT), jnp.float32),
        ((rows, D), jnp.float32),
        ((stats, 2 * BOT + D), jnp.float32),
    ]
    scratch = [
        ((rows, D), jnp.bfloat16),
        ((rows, BOT), jnp.bfloat16),
        ((rows, TAPS * BOT), jnp.bfloat16),
        ((stats, D), jnp.float32),
    ]
    out_shape = [f32(rows, D)]
    if keep:
        out_shape += [jax.ShapeDtypeStruct(*item) for item in kept]
    else:
        scratch = kept + scratch
    return pl.pallas_call(
        functools.partial(forward_kernel, count, keep),
        out_shape=out_shape,
        in_specs=in_vmem(6),
        out_specs=in_vmem(len(out_shape)),
        scratch_shapes=[pltpu.VMEM(*item) for item in scratch],
        compiler_params=pltpu.CompilerParams(vmem_limit_bytes=VMEM_LIMIT),
        cost_estimate=pl.CostEstimate(
            flops=2 * rows * BOT * (2 * D + 9 * BOT), bytes_accessed=20_000_000, transcendentals=0
        ),
        name="block_forward",
    )(stream, w_in, w_mid, w_out, gains, shift)


def norm_back(count, chans, slope, hid, sums, more, rstd, rstd_at, gain, grad_gain, grad_bias, store):
    whole = pl.ds(0, chans)
    sums[:, whole] = jnp.zeros((sums.shape[0], chans), jnp.float32)
    more[:, whole] = jnp.zeros((sums.shape[0], chans), jnp.float32)

    def add(frame, rows, lanes):
        value = slope(frame, rows, lanes)
        sums[frame, lanes] = jnp.sum(value, axis=0, keepdims=True)
        more[frame, lanes] = jnp.sum(value * hid[rows, lanes], axis=0, keepdims=True)

    each_chunk(count, chans, add)
    grad_bias[...] = jnp.sum(sums[:, whole], axis=0, keepdims=True)
    grad_gain[...] = jnp.sum(more[:, whole], axis=0, keepdims=True)
    sums[:, whole] = group_mean(sums[:, whole] * gain[...])
    more[:, whole] = group_mean(more[:, whole] * gain[...])

    def spread(frame, rows, lanes):
        store(
            rows,
            lanes,
            lambda value: jnp.where(
                real_rows(),
                rstd[frame, pl.ds(rstd_at + lanes.start, LANES)]
                * (value * gain[:, lanes] - sums[frame, lanes] - hid[rows, lanes] * more[frame, lanes]),
                0.0,
            ).astype(jnp.bfloat16),
        )

    each_chunk(count, chans, spread)


def back_out_kernel(count, *refs):
    grad, x, hid_two, hid_three, rstd, w_out, gains = refs[:7]
    dres, dlow, dw_out, dgains = refs[7:11]
    third, act, dact, sums, more = refs[11:]
    gain_three, bias_three = (gains.at[:, pl.ds(4 * BOT, D)], gains.at[:, pl.ds(4 * BOT + D, D)])

    def slope_three(frame, rows, lanes):
        value = x[rows, lanes] + hid_three[rows, lanes] * gain_three[:, lanes] + bias_three[:, lanes]
        value = jnp.where(real_rows(), grad[rows, lanes] * silu_slope(value), 0.0)
        dres[rows, lanes] = value
        return value

    def store_three(rows, lanes, back):
        third[rows, lanes] = back(dres[rows, lanes])

    norm_back(
        count, D, slope_three, hid_three, sums, more, rstd, 2 * BOT, gain_three,
        dgains.at[:, pl.ds(2 * BOT, D)], dgains.at[:, pl.ds(2 * BOT + D, D)], store_three,
    )
    total = None
    for part in range(D // BOT):
        lanes = pl.ds(part * BOT, BOT)
        term = dot_lanes(third[:, lanes], w_out[:, lanes])
        total = term if total is None else total + term
    dact[...] = total
    gain_two, bias_two = (gains.at[:, pl.ds(2 * BOT, BOT)], gains.at[:, pl.ds(3 * BOT, BOT)])

    def slope_two(frame, rows, lanes):
        value = hid_two[rows, lanes] * gain_two[:, lanes] + bias_two[:, lanes]
        gate = 1.0 / (1.0 + jnp.exp(-value))
        act[rows, lanes] = jnp.where(real_rows(), value * gate, 0.0).astype(jnp.bfloat16)
        value = dact[rows, lanes] * (gate * (1.0 + value * (1.0 - gate)))
        value = jnp.where(real_rows(), value, 0.0)
        dact[rows, lanes] = value
        return value

    def store_two(rows, lanes, back):
        dlow[rows, lanes] = back(dact[rows, lanes])

    norm_back(
        count, BOT, slope_two, hid_two, sums, more, rstd, BOT, gain_two,
        dgains.at[:, pl.ds(0, BOT)], dgains.at[:, pl.ds(BOT, BOT)], store_two,
    )
    for part in range(D // BOT):
        lanes = pl.ds(part * BOT, BOT)
        dw_out[:, lanes] = dot_rows(act[...], third[:, lanes]).astype(jnp.bfloat16)


def back_out(grad, stream, hid_two, hid_three, rstd, w_out, gains):
    rows = stream.shape[0]
    count = rows // ROWS
    stats = stat_rows(count)
    return pl.pallas_call(
        functools.partial(back_out_kernel, count),
        out_shape=[f32(rows, D), bf16(rows, BOT), bf16(BOT, D), f32(1, 2 * BOT + 2 * D)],
        in_specs=in_vmem(7),
        out_specs=in_vmem(4),
        scratch_shapes=[
            pltpu.VMEM((rows, D), jnp.bfloat16),
            pltpu.VMEM((rows, BOT), jnp.bfloat16),
            pltpu.VMEM((rows, BOT), jnp.float32),
            pltpu.VMEM((stats, D), jnp.float32),
            pltpu.VMEM((stats, D), jnp.float32),
        ],
        compiler_params=pltpu.CompilerParams(vmem_limit_bytes=VMEM_LIMIT),
        cost_estimate=pl.CostEstimate(
            flops=4 * rows * BOT * D, bytes_accessed=20_000_000, transcendentals=0
        ),
        name="back_out",
    )(grad, stream, hid_two, hid_three, rstd, w_out, gains)


def back_mid_kernel(count, *refs):
    grad, hid_one, rstd, w_mid, gains, shift = refs[:6]
    dlow, dw_mid, dgains = refs[6:9]
    act, cols, dact, sums, more = refs[9:]
    gain_one, bias_one = (gains.at[:, pl.ds(0, BOT)], gains.at[:, pl.ds(BOT, BOT)])
    for frame in range(count):
        rows = pl.ds(frame * ROWS, ROWS)
        for tap in range(TAPS):
            picked = dot(shift[pl.ds((TAPS - 1 - tap) * ROWS, ROWS), :], grad[rows, :])
            cols[rows, pl.ds(tap * BOT, BOT)] = picked.astype(jnp.bfloat16)
    total = None
    for tap in range(TAPS):
        lanes = pl.ds(tap * BOT, BOT)
        term = dot_lanes(cols[:, lanes], w_mid[lanes, :])
        total = term if total is None else total + term
    dact[...] = total

    def slope_one(frame, rows, lanes):
        value = hid_one[rows, lanes] * gain_one[:, lanes] + bias_one[:, lanes]
        gate = 1.0 / (1.0 + jnp.exp(-value))
        act[rows, lanes] = jnp.where(real_rows(), value * gate, 0.0).astype(jnp.bfloat16)
        value = dact[rows, lanes] * (gate * (1.0 + value * (1.0 - gate)))
        value = jnp.where(real_rows(), value, 0.0)
        dact[rows, lanes] = value
        return value

    def store_one(rows, lanes, back):
        dlow[rows, lanes] = back(dact[rows, lanes])

    norm_back(
        count, BOT, slope_one, hid_one, sums, more, rstd, 0, gain_one,
        dgains.at[:, pl.ds(0, BOT)], dgains.at[:, pl.ds(BOT, BOT)], store_one,
    )
    for tap in range(TAPS):
        lanes = pl.ds(tap * BOT, BOT)
        dw_mid[lanes, :] = dot_rows(act[...], cols[:, lanes]).astype(jnp.bfloat16)


def back_mid(grad, hid_one, rstd, w_mid, gains, shift):
    rows = grad.shape[0]
    count = rows // ROWS
    stats = stat_rows(count)
    return pl.pallas_call(
        functools.partial(back_mid_kernel, count),
        out_shape=[bf16(rows, BOT), bf16(TAPS * BOT, BOT), f32(1, 2 * BOT)],
        in_specs=in_vmem(6),
        out_specs=in_vmem(3),
        scratch_shapes=[
            pltpu.VMEM((rows, BOT), jnp.bfloat16),
            pltpu.VMEM((rows, TAPS * BOT), jnp.bfloat16),
            pltpu.VMEM((rows, BOT), jnp.float32),
            pltpu.VMEM((stats, BOT), jnp.float32),
            pltpu.VMEM((stats, BOT), jnp.float32),
        ],
        compiler_params=pltpu.CompilerParams(vmem_limit_bytes=VMEM_LIMIT),
        cost_estimate=pl.CostEstimate(
            flops=4 * rows * BOT * TAPS * BOT, bytes_accessed=12_000_000, transcendentals=0
        ),
        name="back_mid",
    )(grad, hid_one, rstd, w_mid, gains, shift)


def back_in_kernel(count, *refs):
    grad, x, dres, w_in, dw_in, dx, low = refs

    def cast(frame, rows, lanes):
        low[rows, lanes] = x[rows, lanes].astype(jnp.bfloat16)

    each_chunk(count, D, cast)
    for part in range(D // BOT):
        lanes = pl.ds(part * BOT, BOT)
        dw_in[lanes, :] = dot_rows(low[:, lanes], grad[...]).astype(jnp.bfloat16)
        dx[:, lanes] = dres[:, lanes] + dot_lanes(grad[...], w_in[lanes, :])


def back_in(grad, stream, dres, w_in):
    rows = grad.shape[0]
    return pl.pallas_call(
        functools.partial(back_in_kernel, rows // ROWS),
        out_shape=[bf16(D, BOT), f32(rows, D)],
        in_specs=in_vmem(4),
        out_specs=in_vmem(2),
        scratch_shapes=[pltpu.VMEM((rows, D), jnp.bfloat16)],
        compiler_params=pltpu.CompilerParams(vmem_limit_bytes=VMEM_LIMIT),
        cost_estimate=pl.CostEstimate(
            flops=4 * rows * BOT * D, bytes_accessed=15_000_000, transcendentals=0
        ),
        name="back_in",
    )(grad, stream, dres, w_in)


FULL_PRECISION = lax.Precision.HIGHEST
CQL_WEIGHT = 0.05
BETA_ONE = 0.5
BETA_TWO = 0.5
LEARNING_RATE = 0.25
WEIGHT_DECAY = 0.01
PATCH_IN = 256
DPROJ = 512
ACTIONS = 18
ATOMS = 51
GAMES = 4
BLOCKS = 2
STEP = 5
AXES = ("wide", "narrow")
SCORES = GAMES * ACTIONS * ATOMS


def average_decay():
    return min(0.99, (1.0 + STEP) / (10.0 + STEP))


def segment_lengths():
    top = [PATCH_IN * D, D * PIX, D * DPROJ, DPROJ * SCORES]
    block = [D * BOT, 9 * BOT * BOT, BOT * D, 2 * (2 * BOT + D)]
    return (top, block)


def cut_points(lengths, devices):
    cuts = []
    offset = 0
    for length in lengths:
        width = length // devices
        cuts.append((offset, width))
        offset += width
    return cuts


def rows_of(flat, cuts, widths):
    return [
        flat[start : start + size].reshape(-1, width)
        for (start, size), width in zip(cuts, widths)
    ]


def whole(rows):
    return lax.all_gather(rows, AXES, axis=0, tiled=True)


def own_sum(matrix):
    return lax.psum_scatter(matrix, AXES, scatter_dimension=0, tiled=True)


def select(scores, game_hot):
    count = scores.shape[0]
    picked = jnp.einsum(
        "ng,ngk->nk",
        game_hot,
        scores.reshape(count, GAMES, ACTIONS * ATOMS),
        precision=FULL_PRECISION,
    )
    return picked.reshape(count, ACTIONS, ATOMS)


def support():
    return -10.0 + 20.0 / (ATOMS - 1) * jnp.arange(ATOMS, dtype=jnp.float32)


def target_dist(logits_next, next_hot, rewards, discounts, done_flags):
    chosen = jnp.einsum("na,naz->nz", next_hot, logits_next, precision=FULL_PRECISION)
    probs = jax.nn.softmax(chosen, axis=-1)
    atoms = support()
    spacing = 20.0 / (ATOMS - 1)
    keep = discounts * (1.0 - done_flags.astype(jnp.float32))
    moved = jnp.clip(rewards[:, None] + keep[:, None] * atoms[None, :], -10.0, 10.0)
    kernel = jnp.clip(1.0 - jnp.abs(moved[:, :, None] - atoms[None, None, :]) / spacing, 0.0, 1.0)
    return jnp.einsum("nj,nji->ni", probs, kernel, precision=FULL_PRECISION)


def frame_losses(logits, target, taken_hot, legal_now):
    logp = jax.nn.log_softmax(logits, axis=-1)
    action_values = jnp.sum(jnp.exp(logp) * support(), axis=-1)
    taken_logp = jnp.sum(taken_hot[:, :, None] * logp, axis=1)
    cross = -jnp.sum(target * taken_logp, axis=-1)
    masked = jnp.where(legal_now > 0, action_values, -1e30)
    largest = jnp.max(masked, axis=-1, keepdims=True)
    spread = jnp.log(jnp.sum(jnp.exp(masked - largest), axis=-1)) + largest[:, 0]
    return cross + CQL_WEIGHT * (spread - jnp.sum(taken_hot * action_values, axis=-1))


def head_scores(stream, pool_w, proj_w, heads_w):
    low = stream.astype(jnp.bfloat16).reshape(-1, ROWS, D)
    pooled = jnp.einsum("npc,cp->nc", low, pool_w, preferred_element_type=jnp.float32)
    pooled = pooled.astype(jnp.bfloat16)
    before = dot(pooled, proj_w)
    hidden = jax.nn.silu(before).astype(jnp.bfloat16)
    return (dot(hidden, heads_w), (low, pooled, before, hidden))


def lamb_parts(params, grads, first, second):
    momentum = BETA_ONE * first + (1.0 - BETA_ONE) * grads
    variance = BETA_TWO * second + (1.0 - BETA_TWO) * grads * grads
    direction = (
        momentum / (1.0 - BETA_ONE**STEP) / (jnp.sqrt(variance / (1.0 - BETA_TWO**STEP)) + 1e-06)
        + WEIGHT_DECAY * params
    )
    return (momentum, variance, direction)


def squares(flat, cuts):
    return jnp.stack(
        [jnp.sum(jnp.square(flat[..., start : start + width]), axis=-1) for start, width in cuts],
        axis=-1,
    )


def spread_ratio(ratio, flat, cuts):
    parts = [
        jnp.broadcast_to(ratio[..., index : index + 1], flat.shape[:-1] + (width,))
        for index, (start, width) in enumerate(cuts)
    ]
    return jnp.concatenate(parts, axis=-1)


def frame_rows(frames):
    count = frames.shape[0]
    return jnp.pad(frames, ((0, 0), (0, ROWS - PIX), (0, 0))).reshape(count * ROWS, PATCH_IN)


def on_device(
    observed,
    following,
    game_ids,
    actions,
    legal_mask,
    rewards,
    discounts,
    done_flags,
    params_top,
    params_blocks,
    first_top,
    first_blocks,
    second_top,
    second_blocks,
    average_top,
    average_blocks,
    target_top,
    target_blocks,
):
    devices = lax.axis_size(AXES)
    frames_all = observed.shape[0] * devices
    top_lengths, block_lengths = segment_lengths()
    top_cuts = cut_points(top_lengths, devices)
    block_cuts = cut_points(block_lengths, devices)
    top_widths = (D, PIX, DPROJ, SCORES)
    block_widths = (BOT, BOT, D)
    shift = shifts()
    weight_parts = jnp.concatenate(
        [squares(params_top, top_cuts), squares(params_blocks, block_cuts).reshape(-1)]
    )
    weight_sq = lax.psum(weight_parts, AXES)

    game_hot = (game_ids[:, None] == jnp.arange(GAMES)[None, :]).astype(jnp.float32)
    taken_hot = (actions[:, 0:1] == jnp.arange(ACTIONS)[None, :]).astype(jnp.float32)
    next_hot = (actions[:, 1:2] == jnp.arange(ACTIONS)[None, :]).astype(jnp.float32)

    low_top = params_top.astype(jnp.bfloat16)
    low_blocks = params_blocks.astype(jnp.bfloat16)
    gain_start, gain_width = block_cuts[3]
    gain_rows = jnp.concatenate([target_blocks, low_blocks])[:, gain_start:]
    gains = lax.all_gather(gain_rows, AXES, axis=1, tiled=True).astype(jnp.float32)

    def fetch_top(flat):
        patch, pool, proj, heads = rows_of(flat, top_cuts, top_widths)
        pool = jnp.pad(pool, ((0, 0), (0, ROWS - PIX)))
        return (whole(patch), whole(pool), whole(proj), whole(heads))

    def fetch_block(flat):
        return [whole(rows) for rows in rows_of(flat, block_cuts[:3], block_widths)]

    target_patch, target_pool, target_proj, target_heads = fetch_top(target_top)
    stream = dot(frame_rows(following), target_patch)
    for index in range(BLOCKS):
        stream = block_forward(
            stream, *fetch_block(target_blocks[index]), gains[index : index + 1], shift, False
        )[0]
    target_scores, ignored = head_scores(stream, target_pool, target_proj, target_heads)
    target = target_dist(select(target_scores, game_hot), next_hot, rewards, discounts, done_flags)

    patch_w, pool_w, proj_w, heads_w = fetch_top(low_top)
    rows = frame_rows(observed)
    stream = dot(rows, patch_w)
    kept = []
    for index in range(BLOCKS):
        weights = fetch_block(low_blocks[index])
        gain = gains[BLOCKS + index : BLOCKS + index + 1]
        out, hid_one, hid_two, hid_three, rstd = block_forward(stream, *weights, gain, shift, True)
        kept.append((stream, hid_one, hid_two, hid_three, rstd, weights, gain))
        stream = out
    scores, (low, pooled, before, hidden) = head_scores(stream, pool_w, proj_w, heads_w)

    def objective(scores_in):
        return jnp.sum(frame_losses(select(scores_in, game_hot), target, taken_hot, legal_mask))

    loss_part, back_loss = jax.vjp(objective, scores)
    grad_scores = back_loss(jnp.float32(1.0 / frames_all))[0].astype(jnp.bfloat16)
    grad_heads = dot_rows(hidden, grad_scores).astype(jnp.bfloat16)
    grad_hidden = dot_lanes(grad_scores, heads_w)
    grad_before = jax.vjp(jax.nn.silu, before)[1](grad_hidden)[0].astype(jnp.bfloat16)
    grad_proj = dot_rows(pooled, grad_before).astype(jnp.bfloat16)
    grad_pooled = dot_lanes(grad_before, proj_w).astype(jnp.bfloat16)
    grad_pool = jnp.einsum(
        "npc,nc->cp", low, grad_pooled, preferred_element_type=jnp.float32
    ).astype(jnp.bfloat16)
    grad_stream = jnp.einsum(
        "nc,cp->npc", grad_pooled, pool_w, preferred_element_type=jnp.float32
    ).reshape(-1, D)

    grad_blocks = [None] * BLOCKS
    for index in reversed(range(BLOCKS)):
        stream, hid_one, hid_two, hid_three, rstd, weights, gain = kept[index]
        w_in, w_mid, w_out = weights
        dres, dsecond, dw_out, dgains_late = back_out(
            grad_stream, stream, hid_two, hid_three, rstd, w_out, gain
        )
        dfirst, dw_mid, dgains_early = back_mid(dsecond, hid_one, rstd, w_mid, gain, shift)
        dw_in, grad_stream = back_in(dfirst, stream, dres, w_in)
        dgains = jnp.concatenate([dgains_early, dgains_late], axis=1).reshape(devices, -1)
        parts = [own_sum(part).astype(jnp.float32) for part in (dw_in, dw_mid, dw_out, dgains)]
        grad_blocks[index] = jnp.concatenate([part.reshape(-1) for part in parts])
    grad_patch = dot_rows(rows, grad_stream.astype(jnp.bfloat16)).astype(jnp.bfloat16)
    grad_blocks = jnp.stack(grad_blocks)
    parts = [
        own_sum(part).astype(jnp.float32)
        for part in (grad_patch, grad_pool, grad_proj, grad_heads)
    ]
    parts[1] = parts[1][:, :PIX]
    grad_top = jnp.concatenate([part.reshape(-1) for part in parts])

    momentum_top, variance_top, direction_top = lamb_parts(
        params_top, grad_top, first_top, second_top
    )
    momentum_blocks, variance_blocks, direction_blocks = lamb_parts(
        params_blocks, grad_blocks, first_blocks, second_blocks
    )
    update_parts = jnp.concatenate(
        [squares(direction_top, top_cuts), squares(direction_blocks, block_cuts).reshape(-1)]
    )
    update_sq, loss_total = lax.psum((update_parts, loss_part), AXES)
    weight_norm = jnp.sqrt(weight_sq)
    update_norm = jnp.sqrt(update_sq)
    ratio = weight_norm / (update_norm + 1e-06)
    scale_top = spread_ratio(ratio[:4], params_top, top_cuts)
    scale_blocks = spread_ratio(ratio[4:].reshape(BLOCKS, 4), params_blocks, block_cuts)
    updated_top = params_top - LEARNING_RATE * scale_top * direction_top
    updated_blocks = params_blocks - LEARNING_RATE * scale_blocks * direction_blocks
    decay = average_decay()
    averaged_top = decay * average_top + (1.0 - decay) * updated_top
    averaged_blocks = decay * average_blocks + (1.0 - decay) * updated_blocks
    matrix_norms = jnp.stack([weight_norm, update_norm])
    gain_grads = grad_blocks[:, gain_start : gain_start + gain_width]
    return (
        loss_total,
        matrix_norms,
        updated_top,
        updated_top.astype(jnp.bfloat16),
        momentum_top,
        variance_top,
        averaged_top,
        updated_blocks,
        updated_blocks.astype(jnp.bfloat16),
        momentum_blocks,
        variance_blocks,
        averaged_blocks,
        gain_grads,
    )


def solution(mesh):
    one = P(AXES)
    flat = P(None, AXES)
    return jax.shard_map(
        on_device,
        mesh=mesh,
        in_specs=(P(AXES, None, None),) * 2
        + (one, P(AXES, None), P(AXES, None))
        + (one,) * 3
        + (one, flat) * 5,
        out_specs=(P(), P()) + (one,) * 5 + (flat,) * 6,
        check_vma=False,
    )
```

```python
import functools
import itertools

import jax
import jax.numpy as jnp
from jax import lax
from jax.experimental import pallas as pl
from jax.experimental.pallas import tpu as pltpu
from jax.sharding import PartitionSpec as P

D = 2048
BOT = 512
GROUPS = 32
SIDE = 11
PIX = 121
TAPS = 9

ROWS = 128
LANES = 256
VMEM_LIMIT = 60 * 1024 * 1024


def shifts():
    pixel = jnp.arange(ROWS)
    row, col = (pixel // SIDE, pixel % SIDE)
    mats = []
    for tap in range(TAPS):
        at_row, at_col = (row + tap // 3 - 1, col + tap % 3 - 1)
        inside = (at_row >= 0) & (at_row < SIDE) & (at_col >= 0) & (at_col < SIDE) & (pixel < PIX)
        mats.append((inside[:, None] & (pixel[None, :] == (at_row * SIDE + at_col)[:, None])))
    return jnp.concatenate(mats, axis=0).astype(jnp.bfloat16)


def dot(left, right):
    return jnp.dot(left, right, preferred_element_type=jnp.float32)


def dot_rows(left, right):
    return lax.dot_general(
        left, right, (((0,), (0,)), ((), ())), preferred_element_type=jnp.float32
    )


def dot_lanes(left, right):
    return lax.dot_general(
        left, right, (((1,), (1,)), ((), ())), preferred_element_type=jnp.float32
    )


def each_chunk(count, chans, body, unroll=1):
    per = chans // LANES

    def step(index, carry):
        frame = index // per
        rows = pl.ds(pl.multiple_of(frame * ROWS, ROWS), ROWS)
        lanes = pl.ds(pl.multiple_of((index % per) * LANES, LANES), LANES)
        body(pl.ds(frame, 1), rows, lanes)
        return carry

    lax.fori_loop(0, count * per, step, 0, unroll=unroll)


def real_rows():
    return lax.broadcasted_iota(jnp.int32, (ROWS, LANES), 0) < PIX


def group_mean(sums):
    chans = sums.shape[1]
    width = chans // GROUPS
    lane = lax.broadcasted_iota(jnp.int32, sums.shape, 1)
    step = 1
    while step < width:
        ahead = pltpu.roll(sums, chans - step, 1)
        behind = pltpu.roll(sums, step, 1)
        sums = sums + jnp.where((lane & step) == 0, ahead, behind)
        step *= 2
    return sums * (1.0 / (PIX * width))


def silu(value):
    return value / (1.0 + jnp.exp(-value))


def silu_slope(value):
    gate = 1.0 / (1.0 + jnp.exp(-value))
    return gate * (1.0 + value * (1.0 - gate))


def normalise(count, chans, hid, sums, rstd, rstd_at):
    whole = pl.ds(0, chans)
    sums[:, whole] = jnp.zeros((sums.shape[0], chans), jnp.float32)

    def add(frame, rows, lanes):
        sums[frame, lanes] = jnp.sum(hid[rows, lanes], axis=0, keepdims=True)

    each_chunk(count, chans, add, unroll=2)
    sums[:, whole] = group_mean(sums[:, whole])

    def center(frame, rows, lanes):
        value = jnp.where(real_rows(), hid[rows, lanes] - sums[frame, lanes], 0.0)
        hid[rows, lanes] = value
        sums[frame, lanes] = jnp.sum(value * value, axis=0, keepdims=True)

    each_chunk(count, chans, center, unroll=2)
    at = pl.ds(rstd_at, chans)
    rstd[:, at] = lax.rsqrt(group_mean(sums[:, whole]) + 1e-05)


def forward_kernel(count, keep, *refs):
    x, w_in, w_mid, w_out, gains, shift, out = refs[:7]
    hid_one, hid_two, hid_three, rstd, low, act, cols, sums = refs[7:]

    def cast(frame, rows, lanes):
        low[rows, lanes] = x[rows, lanes].astype(jnp.bfloat16)

    def activate(hid, at, offset):
        def body(frame, rows, lanes):
            gain = gains[:, pl.ds(offset + lanes.start, LANES)]
            bias = gains[:, pl.ds(offset + BOT + lanes.start, LANES)]
            value = hid[rows, lanes] * rstd[frame, pl.ds(at + lanes.start, LANES)]
            hid[rows, lanes] = value
            value = jnp.where(real_rows(), silu(value * gain + bias), 0.0)
            act[rows, lanes] = value.astype(jnp.bfloat16)

        return body

    each_chunk(count, D, cast)
    hid_one[...] = dot(low[...], w_in[...])
    normalise(count, BOT, hid_one, sums, rstd, 0)
    each_chunk(count, BOT, activate(hid_one, 0, 0))
    for frame in range(count):
        rows = pl.ds(frame * ROWS, ROWS)
        for tap in range(TAPS):
            picked = dot(shift[pl.ds(tap * ROWS, ROWS), :], act[rows, :])
            cols[rows, pl.ds(tap * BOT, BOT)] = picked.astype(jnp.bfloat16)
    hid_two[...] = dot(cols[...], w_mid[...])
    normalise(count, BOT, hid_two, sums, rstd, BOT)
    each_chunk(count, BOT, activate(hid_two, BOT, 2 * BOT))
    for part in range(D // BOT):
        lanes = pl.ds(part * BOT, BOT)
        hid_three[:, lanes] = dot(act[...], w_out[lanes, :])
    normalise(count, D, hid_three, sums, rstd, 2 * BOT)

    def finish(frame, rows, lanes):
        gain = gains[:, pl.ds(4 * BOT + lanes.start, LANES)]
        bias = gains[:, pl.ds(4 * BOT + D + lanes.start, LANES)]
        value = hid_three[rows, lanes] * rstd[frame, pl.ds(2 * BOT + lanes.start, LANES)]
        if keep:
            hid_three[rows, lanes] = value
        value = silu(x[rows, lanes] + value * gain + bias)
        out[rows, lanes] = jnp.where(real_rows(), value, 0.0)

    each_chunk(count, D, finish)


def f32(*shape):
    return jax.ShapeDtypeStruct(shape, jnp.float32)


def bf16(*shape):
    return jax.ShapeDtypeStruct(shape, jnp.bfloat16)


def stat_rows(count):
    return -(-count // 8) * 8


def block_forward(stream, w_in, w_mid, w_out, gains, shift, keep):
    rows = stream.shape[0]
    count = rows // ROWS
    stats = stat_rows(count)
    kept = [
        ((rows, BOT), jnp.float32),
        ((rows, BOT), jnp.float32),
        ((rows, D), jnp.float32),
        ((stats, 2 * BOT + D), jnp.float32),
    ]
    scratch = [
        ((rows, D), jnp.bfloat16),
        ((rows, BOT), jnp.bfloat16),
        ((rows, TAPS * BOT), jnp.bfloat16),
        ((stats, D), jnp.float32),
    ]
    out_shape = [f32(rows, D)]
    if keep:
        out_shape += [jax.ShapeDtypeStruct(*item) for item in kept]
    else:
        scratch = kept + scratch
    return pl.pallas_call(
        functools.partial(forward_kernel, count, keep),
        out_shape=out_shape,
        in_specs=in_vmem(6),
        out_specs=in_vmem(len(out_shape)),
        scratch_shapes=[pltpu.VMEM(*item) for item in scratch],
        compiler_params=pltpu.CompilerParams(vmem_limit_bytes=VMEM_LIMIT),
        cost_estimate=pl.CostEstimate(
            flops=2 * rows * BOT * (2 * D + 9 * BOT), bytes_accessed=20_000_000, transcendentals=0
        ),
        name="block_forward",
    )(stream, w_in, w_mid, w_out, gains, shift)


def norm_back(count, chans, slope, hid, sums, more, rstd, rstd_at, gain, grad_gain, grad_bias, store):
    whole = pl.ds(0, chans)
    sums[:, whole] = jnp.zeros((sums.shape[0], chans), jnp.float32)
    more[:, whole] = jnp.zeros((sums.shape[0], chans), jnp.float32)

    def add(frame, rows, lanes):
        value = slope(frame, rows, lanes)
        sums[frame, lanes] = jnp.sum(value, axis=0, keepdims=True)
        more[frame, lanes] = jnp.sum(value * hid[rows, lanes], axis=0, keepdims=True)

    each_chunk(count, chans, add)
    grad_bias[...] = jnp.sum(sums[:, whole], axis=0, keepdims=True)
    grad_gain[...] = jnp.sum(more[:, whole], axis=0, keepdims=True)
    sums[:, whole] = group_mean(sums[:, whole] * gain[...])
    more[:, whole] = group_mean(more[:, whole] * gain[...])

    def spread(frame, rows, lanes):
        store(
            rows,
            lanes,
            lambda value: jnp.where(
                real_rows(),
                rstd[frame, pl.ds(rstd_at + lanes.start, LANES)]
                * (value * gain[:, lanes] - sums[frame, lanes] - hid[rows, lanes] * more[frame, lanes]),
                0.0,
            ).astype(jnp.bfloat16),
        )

    each_chunk(count, chans, spread)


def back_out_kernel(count, *refs):
    grad, x, hid_two, hid_three, rstd, w_out, gains = refs[:7]
    dres, dlow, dw_out, dgains = refs[7:11]
    third, act, dact, sums, more = refs[11:]
    gain_three, bias_three = (gains.at[:, pl.ds(4 * BOT, D)], gains.at[:, pl.ds(4 * BOT + D, D)])

    def slope_three(frame, rows, lanes):
        value = x[rows, lanes] + hid_three[rows, lanes] * gain_three[:, lanes] + bias_three[:, lanes]
        value = jnp.where(real_rows(), grad[rows, lanes] * silu_slope(value), 0.0)
        dres[rows, lanes] = value
        return value

    def store_three(rows, lanes, back):
        third[rows, lanes] = back(dres[rows, lanes])

    norm_back(
        count, D, slope_three, hid_three, sums, more, rstd, 2 * BOT, gain_three,
        dgains.at[:, pl.ds(2 * BOT, D)], dgains.at[:, pl.ds(2 * BOT + D, D)], store_three,
    )
    total = None
    for part in range(D // BOT):
        lanes = pl.ds(part * BOT, BOT)
        term = dot_lanes(third[:, lanes], w_out[lanes, :])
        total = term if total is None else total + term
    dact[...] = total
    gain_two, bias_two = (gains.at[:, pl.ds(2 * BOT, BOT)], gains.at[:, pl.ds(3 * BOT, BOT)])

    def slope_two(frame, rows, lanes):
        value = hid_two[rows, lanes] * gain_two[:, lanes] + bias_two[:, lanes]
        gate = 1.0 / (1.0 + jnp.exp(-value))
        act[rows, lanes] = jnp.where(real_rows(), value * gate, 0.0).astype(jnp.bfloat16)
        value = dact[rows, lanes] * (gate * (1.0 + value * (1.0 - gate)))
        value = jnp.where(real_rows(), value, 0.0)
        dact[rows, lanes] = value
        return value

    def store_two(rows, lanes, back):
        dlow[rows, lanes] = back(dact[rows, lanes])

    norm_back(
        count, BOT, slope_two, hid_two, sums, more, rstd, BOT, gain_two,
        dgains.at[:, pl.ds(0, BOT)], dgains.at[:, pl.ds(BOT, BOT)], store_two,
    )
    for part in range(D // BOT):
        lanes = pl.ds(part * BOT, BOT)
        dw_out[lanes, :] = dot_rows(act[...], third[:, lanes]).astype(jnp.bfloat16)


def back_out(grad, stream, hid_two, hid_three, rstd, w_out, gains):
    rows = stream.shape[0]
    count = rows // ROWS
    stats = stat_rows(count)
    return pl.pallas_call(
        functools.partial(back_out_kernel, count),
        out_shape=[f32(rows, D), bf16(rows, BOT), bf16(D, BOT), f32(1, 2 * BOT + 2 * D)],
        in_specs=in_vmem(7),
        out_specs=in_vmem(4),
        scratch_shapes=[
            pltpu.VMEM((rows, D), jnp.bfloat16),
            pltpu.VMEM((rows, BOT), jnp.bfloat16),
            pltpu.VMEM((rows, BOT), jnp.float32),
            pltpu.VMEM((stats, D), jnp.float32),
            pltpu.VMEM((stats, D), jnp.float32),
        ],
        compiler_params=pltpu.CompilerParams(vmem_limit_bytes=VMEM_LIMIT),
        cost_estimate=pl.CostEstimate(
            flops=4 * rows * BOT * D, bytes_accessed=20_000_000, transcendentals=0
        ),
        name="back_out",
    )(grad, stream, hid_two, hid_three, rstd, w_out, gains)


def back_mid_kernel(count, *refs):
    grad, hid_one, rstd, w_mid, gains, shift = refs[:6]
    dlow, dw_mid, dgains = refs[6:9]
    act, cols, dact, sums, more = refs[9:]
    gain_one, bias_one = (gains.at[:, pl.ds(0, BOT)], gains.at[:, pl.ds(BOT, BOT)])
    for frame in range(count):
        rows = pl.ds(frame * ROWS, ROWS)
        for tap in range(TAPS):
            picked = dot(shift[pl.ds((TAPS - 1 - tap) * ROWS, ROWS), :], grad[rows, :])
            cols[rows, pl.ds(tap * BOT, BOT)] = picked.astype(jnp.bfloat16)
    total = None
    for tap in range(TAPS):
        lanes = pl.ds(tap * BOT, BOT)
        term = dot_lanes(cols[:, lanes], w_mid[lanes, :])
        total = term if total is None else total + term
    dact[...] = total

    def slope_one(frame, rows, lanes):
        value = hid_one[rows, lanes] * gain_one[:, lanes] + bias_one[:, lanes]
        gate = 1.0 / (1.0 + jnp.exp(-value))
        act[rows, lanes] = jnp.where(real_rows(), value * gate, 0.0).astype(jnp.bfloat16)
        value = dact[rows, lanes] * (gate * (1.0 + value * (1.0 - gate)))
        value = jnp.where(real_rows(), value, 0.0)
        dact[rows, lanes] = value
        return value

    def store_one(rows, lanes, back):
        dlow[rows, lanes] = back(dact[rows, lanes])

    norm_back(
        count, BOT, slope_one, hid_one, sums, more, rstd, 0, gain_one,
        dgains.at[:, pl.ds(0, BOT)], dgains.at[:, pl.ds(BOT, BOT)], store_one,
    )
    for tap in range(TAPS):
        lanes = pl.ds(tap * BOT, BOT)
        dw_mid[lanes, :] = dot_rows(act[...], cols[:, lanes]).astype(jnp.bfloat16)


def back_mid(grad, hid_one, rstd, w_mid, gains, shift):
    rows = grad.shape[0]
    count = rows // ROWS
    stats = stat_rows(count)
    return pl.pallas_call(
        functools.partial(back_mid_kernel, count),
        out_shape=[bf16(rows, BOT), bf16(TAPS * BOT, BOT), f32(1, 2 * BOT)],
        in_specs=in_vmem(6),
        out_specs=in_vmem(3),
        scratch_shapes=[
            pltpu.VMEM((rows, BOT), jnp.bfloat16),
            pltpu.VMEM((rows, TAPS * BOT), jnp.bfloat16),
            pltpu.VMEM((rows, BOT), jnp.float32),
            pltpu.VMEM((stats, BOT), jnp.float32),
            pltpu.VMEM((stats, BOT), jnp.float32),
        ],
        compiler_params=pltpu.CompilerParams(vmem_limit_bytes=VMEM_LIMIT),
        cost_estimate=pl.CostEstimate(
            flops=4 * rows * BOT * TAPS * BOT, bytes_accessed=12_000_000, transcendentals=0
        ),
        name="back_mid",
    )(grad, hid_one, rstd, w_mid, gains, shift)


def back_in_kernel(count, *refs):
    grad, x, dres, w_in, dw_in, dx, low = refs

    def cast(frame, rows, lanes):
        low[rows, lanes] = x[rows, lanes].astype(jnp.bfloat16)

    each_chunk(count, D, cast)
    for part in range(D // BOT):
        lanes = pl.ds(part * BOT, BOT)
        dw_in[lanes, :] = dot_rows(low[:, lanes], grad[...]).astype(jnp.bfloat16)
        dx[:, lanes] = dres[:, lanes] + dot_lanes(grad[...], w_in[lanes, :])


def back_in(grad, stream, dres, w_in):
    rows = grad.shape[0]
    return pl.pallas_call(
        functools.partial(back_in_kernel, rows // ROWS),
        out_shape=[bf16(D, BOT), f32(rows, D)],
        in_specs=in_vmem(4),
        out_specs=in_vmem(2),
        scratch_shapes=[pltpu.VMEM((rows, D), jnp.bfloat16)],
        compiler_params=pltpu.CompilerParams(vmem_limit_bytes=VMEM_LIMIT),
        cost_estimate=pl.CostEstimate(
            flops=4 * rows * BOT * D, bytes_accessed=15_000_000, transcendentals=0
        ),
        name="back_in",
    )(grad, stream, dres, w_in)


def spread_pixels(devices):
    rows = PATCH_IN // devices
    value = jnp.arange(PATCH_IN)
    at = value // rows * 2 * rows + value % rows
    return jnp.stack(
        [jnp.arange(2 * PATCH_IN)[None, :] == (at + half * rows)[:, None] for half in range(2)]
    ).astype(jnp.bfloat16)


def embed_kernel(pixels, spread, patch, out):
    for half in range(2):
        wide = dot(pixels[...], spread[half]).astype(jnp.bfloat16)
        for block in range(2):
            lanes = pl.ds((2 * half + block) * WIDTH, WIDTH)
            out[:, lanes] = dot(wide, patch[block])


def embed(pixels, spread, patch):
    return pl.pallas_call(
        embed_kernel,
        out_shape=f32(pixels.shape[0], D),
        in_specs=in_vmem(3),
        out_specs=in_vmem(1)[0],
        compiler_params=pltpu.CompilerParams(vmem_limit_bytes=VMEM_LIMIT),
        name="embed",
    )(pixels, spread, patch)


def embed_back_kernel(pixels, spread, grad, out):
    wide = [dot(pixels[...], spread[half]).astype(jnp.bfloat16) for half in range(2)]
    for block in range(2):
        total = None
        for half in range(2):
            lanes = pl.ds((2 * half + block) * WIDTH, WIDTH)
            term = dot_rows(wide[half], grad[:, lanes].astype(jnp.bfloat16))
            total = term if total is None else total + term
        out[block] = total.astype(jnp.bfloat16)


def embed_back(pixels, spread, grad):
    return pl.pallas_call(
        embed_back_kernel,
        out_shape=bf16(2, 2 * PATCH_IN, WIDTH),
        in_specs=in_vmem(3),
        out_specs=in_vmem(1)[0],
        compiler_params=pltpu.CompilerParams(vmem_limit_bytes=VMEM_LIMIT),
        name="embed_back",
    )(pixels, spread, grad)


WIDTH = 512
TILE = 16
AXES = ("wide", "narrow")


def grid_sizes():
    return (lax.axis_size("wide") // 2, 2, lax.axis_size("narrow") // 2, 2)


def spot():
    sizes = grid_sizes()
    wide, narrow = (lax.axis_index("wide"), lax.axis_index("narrow"))
    return jnp.stack(
        [wide // sizes[1], wide % sizes[1], narrow // sizes[3], narrow % sizes[3]]
    ).astype(jnp.int32)


def hop(array, axis_of_core, step=1):
    sizes = grid_sizes()
    pairs = []
    for place in itertools.product(*[range(size) for size in sizes]):
        axis = axis_of_core[place[3]]
        other = list(place)
        other[axis] = (place[axis] + step) % sizes[axis]
        source, target = [
            ((z * sizes[1] + y) * sizes[2] + x) * sizes[3] + core for z, y, x, core in (place, other)
        ]
        pairs.append((source, target))
    return lax.ppermute(array, AXES, pairs)


ALONG_Z = (0, 0)
ACROSS = (3, 3)
NEAR = (2, 1)
FAR = (1, 2)


def hbm(number):
    return [pl.BlockSpec(memory_space=pl.ANY)] * number


def in_vmem(number):
    return [pl.BlockSpec(memory_space=pltpu.VMEM)] * number


def in_smem():
    return [pl.BlockSpec(memory_space=pltpu.SMEM)]


def copies(pairs, sems):
    started = [
        pltpu.make_async_copy(source, target, sems.at[index])
        for index, (source, target) in enumerate(pairs)
    ]
    for copy in started:
        copy.start()
    for copy in started:
        copy.wait()


class Part:
    def __init__(self, blocks, rows, lanes):
        self.blocks, self.rows, self.lanes = (blocks, rows, lanes)
        self.across = WIDTH // lanes
        self.travel = blocks * rows // self.across

    def moves(self):
        if self.across > 1:
            deep = self.rows // self.across
            return [(0, part * self.lanes, deep, 0, part * deep) for part in range(self.across)]
        return [(block * self.rows, 0, self.rows, block, 0) for block in range(self.blocks)]

    def pack(self, piece):
        if self.across > 1:
            piece = piece.reshape(self.across, self.rows // self.across, self.lanes)
            return piece.transpose(1, 0, 2).reshape(self.travel, WIDTH)
        return piece.reshape(self.travel, WIDTH)

    def unpack(self, rows):
        if self.across > 1:
            rows = rows.reshape(self.rows // self.across, self.across, self.lanes)
            return rows.transpose(1, 0, 2).reshape(1, self.rows, self.lanes)
        return rows.reshape(self.blocks, self.rows, self.lanes)

    def full(self, depth):
        return (self.blocks, depth, 2, 2, 2, self.rows, self.lanes)


def half_rows(parts):
    total = sum(part.travel for part in parts)
    return -(-total // (2 * TILE)) * TILE


def half_moves(parts):
    cut = half_rows(parts)
    halves = ([], [])
    offset = 0
    for index, part in enumerate(parts):
        for row, lane, rows, block, inner in part.moves():
            row = row + offset
            before = max(0, min(rows, cut - row))
            if before:
                halves[0].append((index, row, lane, before, block, inner))
            if rows - before:
                halves[1].append((index, row + before - cut, lane, rows - before, block, inner + before))
        offset += part.travel
    return halves


def unit(parts, depth):
    return (depth, 2, half_rows(parts), WIDTH)


def pack(parts, pieces):
    rows = jnp.concatenate([part.pack(piece) for part, piece in zip(parts, pieces)])
    return jnp.pad(rows, ((0, 2 * half_rows(parts) - rows.shape[0]), (0, 0)))


def stack_kernel(size, place, *refs):
    pairs = [
        (refs[step], refs[size].at[lax.rem(place[0] - step + size, size)]) for step in range(size)
    ]
    copies(pairs, refs[size + 1])


def stack_z(arrays, place):
    size = len(arrays)
    return pl.pallas_call(
        functools.partial(stack_kernel, size),
        out_shape=jax.ShapeDtypeStruct((size,) + arrays[0].shape, arrays[0].dtype),
        in_specs=in_smem() + hbm(size),
        out_specs=in_vmem(1)[0],
        scratch_shapes=[pltpu.SemaphoreType.DMA((size,))],
        name="stack_z",
    )(place, *arrays)


def assemble_pairs(parts, core, y, x, ins, outs):
    pairs = []
    for number, (other, far, near) in enumerate(itertools.product((0, 1), repeat=3)):
        half = core ^ other
        step = [0, 0, 0, 0]
        step[NEAR[half]], step[FAR[half]] = (near, far)
        at_y, at_x = (lax.rem(y + step[1], 2), lax.rem(x + step[2], 2))
        for index, row, lane, rows, block, inner in half_moves(parts)[half]:
            pairs.append(
                (
                    ins[number].at[:, :, pl.ds(row, rows), pl.ds(lane, parts[index].lanes)],
                    outs[index].at[block, :, at_y, at_x, :, pl.ds(inner, rows)],
                )
            )
    return pairs


def assemble_copies(parts):
    return 4 * sum(len(moves) for moves in half_moves(parts))


def assemble_kernel(parts, place, *refs):
    for core in (0, 1):

        @pl.when(place[3] == core)
        def _():
            copies(
                assemble_pairs(parts, core, place[1], place[2], refs[:8], refs[8:-1]), refs[-1]
            )


def assemble(parts, buffers, place):
    depth = buffers[0].shape[0]
    full = pl.pallas_call(
        functools.partial(assemble_kernel, parts),
        out_shape=[jax.ShapeDtypeStruct(part.full(depth), jnp.bfloat16) for part in parts],
        in_specs=in_smem() + hbm(8),
        out_specs=in_vmem(len(parts)),
        scratch_shapes=[pltpu.SemaphoreType.DMA((assemble_copies(parts),))],
        compiler_params=pltpu.CompilerParams(vmem_limit_bytes=VMEM_LIMIT),
        name="assemble",
    )(place, *buffers)
    return [item.reshape(item.shape[0], -1, item.shape[-1]) for item in full]


def both_cores(own, other, core):
    first = jnp.where(core == 0, own, other)
    second = jnp.where(core == 0, other, own)
    return jnp.stack([first, second])


def gather_all(groups, pieces, place):
    depth = grid_sizes()[0]
    core = place[3]
    packed = [pack(parts, items) for parts, items in zip(groups, pieces)]
    halves = [half_rows(parts) for parts in groups]
    kept = [lax.dynamic_slice_in_dim(rows, core * half, half) for rows, half in zip(packed, halves)]
    sent = [
        lax.dynamic_slice_in_dim(rows, (1 - core) * half, half) for rows, half in zip(packed, halves)
    ]
    got = hop(jnp.concatenate(sent), ACROSS)
    held = []
    offset = 0
    for keep, half in zip(kept, halves):
        held.append([both_cores(keep, got[offset : offset + half], core)])
        offset += half
    count = len(groups)
    ready = {}
    for tick in range(count + 3):
        live = [index for index in range(tick - 3, tick + 1) if 0 <= index < count]
        flat, tree = jax.tree.flatten([held[index] for index in live])
        for index, items in zip(live, jax.tree.unflatten(tree, lax.optimization_barrier(flat))):
            held[index] = items
        for index in live:
            items = held[index]
            stage = tick - index
            if stage == 0:
                held[index] = items + [hop(items[0], ALONG_Z, step) for step in range(1, depth)]
            elif stage == 1:
                stacked = stack_z(items, place)
                held[index] = [stacked, hop(stacked, NEAR)]
            elif stage == 2:
                held[index] = items + [hop(item, FAR) for item in items]
            else:
                held[index] = items + [hop(item, ACROSS) for item in items]
    return held


def deal_kernel(parts, place, *refs):
    number = len(parts)
    ins, outs, sems = (refs[:number], refs[number:-1], refs[-1])
    to_core, to_far, to_near, own = outs
    y, x = (place[1], place[2])
    for core in (0, 1):

        @pl.when(place[3] == core)
        def _():
            pairs = []
            for other, far, near in itertools.product((0, 1), repeat=3):
                half = core ^ other
                step = [0, 0, 0, 0]
                step[NEAR[half]], step[FAR[half]] = (near, far)
                at_y, at_x = (lax.rem(y + step[1], 2), lax.rem(x + step[2], 2))
                if other:
                    target = to_core.at[far, near]
                elif far:
                    target = to_far.at[near]
                else:
                    target = to_near if near else own
                for index, row, lane, rows, block, inner in half_moves(parts)[half]:
                    pairs.append(
                        (
                            ins[index].at[block, :, at_y, at_x, :, pl.ds(inner, rows)],
                            target.at[:, :, pl.ds(row, rows), pl.ds(lane, parts[index].lanes)],
                        )
                    )
            copies(pairs, sems)


def deal(parts, arrays, place):
    depth = arrays[0].shape[1]
    size = unit(parts, depth)
    return pl.pallas_call(
        functools.partial(deal_kernel, parts),
        out_shape=[
            jax.ShapeDtypeStruct(lead + size, jnp.bfloat16) for lead in ((2, 2), (2,), (), ())
        ],
        in_specs=in_smem() + in_vmem(len(parts)),
        out_specs=hbm(4),
        scratch_shapes=[pltpu.SemaphoreType.DMA((assemble_copies(parts),))],
        compiler_params=pltpu.CompilerParams(vmem_limit_bytes=VMEM_LIMIT),
        name="deal",
    )(place, *arrays)


def add_up(*terms):
    total = terms[0].astype(jnp.float32)
    for term in terms[1:]:
        total = total + term.astype(jnp.float32)
    return total


def low_add(*terms):
    return add_up(*terms).astype(jnp.bfloat16)


def scatter(parts, arrays, place):
    depth = grid_sizes()[0]
    arrays = [array.reshape(part.full(depth)) for part, array in zip(parts, arrays)]
    to_core, to_far, to_near, own = deal(parts, arrays, place)
    z, core = (place[0], place[3])
    from_core = hop(to_core, ACROSS)
    from_far = hop(low_add(to_far, from_core[1]), FAR)
    from_near = hop(low_add(to_near, from_core[0, 1], from_far[1]), NEAR)

    def mine(at):
        pick = [own, from_core[0, 0], from_far[0], from_near]
        return [lax.dynamic_index_in_dim(item, at, 0, False) for item in pick]

    along = [hop(low_add(*mine(lax.rem(z + step, depth))), ALONG_Z, step) for step in range(1, depth)]
    total = add_up(*mine(z), *along)
    keep = lax.dynamic_index_in_dim(total, core, 0, False)
    other = hop(lax.dynamic_index_in_dim(total, 1 - core, 0, False), ACROSS)
    rows = both_cores(keep, other, core).reshape(-1, WIDTH)
    pieces = []
    offset = 0
    for part in parts:
        pieces.append(part.unpack(rows[offset : offset + part.travel]))
        offset += part.travel
    return pieces


FULL_PRECISION = lax.Precision.HIGHEST
CQL_WEIGHT = 0.05
BETA_ONE = 0.5
BETA_TWO = 0.5
LEARNING_RATE = 0.25
WEIGHT_DECAY = 0.01
PATCH_IN = 256
DPROJ = 512
ACTIONS = 18
ATOMS = 51
GAMES = 4
BLOCKS = 2
STEP = 5
PLAYS = ACTIONS * ATOMS


def average_decay():
    return min(0.99, (1.0 + STEP) / (10.0 + STEP))


def segment_lengths():
    top = [PATCH_IN * D, D * PIX, D * DPROJ, DPROJ * GAMES * PLAYS]
    block = [D * BOT, 9 * BOT * BOT, BOT * D, 2 * (2 * BOT + D)]
    return (top, block)


def cut_points(lengths, devices):
    cuts = []
    offset = 0
    for length in lengths:
        width = length // devices
        cuts.append((offset, width))
        offset += width
    return cuts


def pack_top(flat, cuts):
    patch, pool, proj, heads = [flat[start : start + size] for start, size in cuts]
    patch = patch.reshape(-1, 2, 2, WIDTH).transpose(2, 1, 0, 3).reshape(2, -1, WIDTH)
    pool = jnp.pad(pool.reshape(1, -1, PIX), ((0, 0), (0, 0), (0, ROWS - PIX)))
    heads = jnp.pad(heads.reshape(-1, GAMES, PLAYS), ((0, 0), (0, 0), (0, 2 * WIDTH - PLAYS)))
    heads = heads.reshape(-1, 2 * GAMES, WIDTH).transpose(1, 0, 2)
    return [patch, pool, proj.reshape(1, -1, WIDTH), heads]


def flat_top(patch, pool, proj, heads):
    patch = patch.reshape(2, 2, -1, WIDTH).transpose(2, 1, 0, 3)
    heads = heads.transpose(1, 0, 2).reshape(-1, GAMES, 2 * WIDTH)[:, :, :PLAYS]
    return jnp.concatenate(
        [item.reshape(-1) for item in (patch, pool[:, :, :PIX], proj, heads)]
    )


def pack_block(flat, cuts):
    w_in, w_mid, w_out = [flat[start : start + size] for start, size in cuts[:3]]
    w_out = w_out.reshape(-1, D // BOT, BOT).transpose(1, 0, 2)
    return [w_in.reshape(1, -1, BOT), w_mid.reshape(1, -1, BOT), w_out]


def flat_block(w_in, w_mid, w_out, gains):
    return jnp.concatenate(
        [item.reshape(-1) for item in (w_in, w_mid, w_out.transpose(1, 0, 2), gains)]
    )


def parts_for(devices):
    rows = {"patch": 2 * PATCH_IN, "pool": D, "proj": D, "heads": DPROJ}
    rows |= {"w_in": D, "w_mid": TAPS * BOT, "w_out": BOT, "gains": TILE * devices}
    blocks = {"patch": 2, "heads": 2 * GAMES, "w_out": D // BOT}
    return {
        name: Part(blocks.get(name, 1), count // devices, ROWS if name == "pool" else WIDTH)
        for name, count in rows.items()
    }


def is_tuned(devices):
    parts = parts_for(devices).values()
    whole = all(part.rows // part.across % TILE == 0 for part in parts)
    return whole and lax.axis_size("wide") == 8 and lax.axis_size("narrow") == 4


def plain_gather(piece):
    return lax.all_gather(piece, AXES, axis=1, tiled=True)


def plain_scatter(array):
    return lax.psum_scatter(array, AXES, scatter_dimension=1, tiled=True).astype(jnp.float32)


def total(array):
    if lax.axis_size("wide") != 8 or lax.axis_size("narrow") != 4:
        return lax.psum(array, AXES)
    array = array + hop(array, ACROSS)
    array = array + hop(array, (2, 2))
    array = array + hop(array, (1, 1))
    one, two, three = [hop(array, ALONG_Z, step) for step in (1, 2, 3)]
    return (array + two) + (one + three)


def select(scores, game_hot):
    count = scores.shape[0]
    picked = jnp.einsum(
        "ng,ngk->nk",
        game_hot,
        scores,
        precision=FULL_PRECISION,
    )
    return picked.reshape(count, ACTIONS, ATOMS)


def support():
    return -10.0 + 20.0 / (ATOMS - 1) * jnp.arange(ATOMS, dtype=jnp.float32)


def target_dist(logits_next, next_hot, rewards, discounts, done_flags):
    chosen = jnp.einsum("na,naz->nz", next_hot, logits_next, precision=FULL_PRECISION)
    probs = jax.nn.softmax(chosen, axis=-1)
    atoms = support()
    spacing = 20.0 / (ATOMS - 1)
    keep = discounts * (1.0 - done_flags.astype(jnp.float32))
    moved = jnp.clip(rewards[:, None] + keep[:, None] * atoms[None, :], -10.0, 10.0)
    kernel = jnp.clip(1.0 - jnp.abs(moved[:, :, None] - atoms[None, None, :]) / spacing, 0.0, 1.0)
    return jnp.einsum("nj,nji->ni", probs, kernel, precision=FULL_PRECISION)


def frame_losses(logits, target, taken_hot, legal_now):
    logp = jax.nn.log_softmax(logits, axis=-1)
    action_values = jnp.sum(jnp.exp(logp) * support(), axis=-1)
    taken_logp = jnp.sum(taken_hot[:, :, None] * logp, axis=1)
    cross = -jnp.sum(target * taken_logp, axis=-1)
    masked = jnp.where(legal_now > 0, action_values, -1e30)
    largest = jnp.max(masked, axis=-1, keepdims=True)
    spread = jnp.log(jnp.sum(jnp.exp(masked - largest), axis=-1)) + largest[:, 0]
    return cross + CQL_WEIGHT * (spread - jnp.sum(taken_hot * action_values, axis=-1))


def head_scores(stream, pool_w, proj_w, heads_w):
    low = stream.astype(jnp.bfloat16).reshape(-1, ROWS, D)
    pooled = jnp.einsum("npc,cp->nc", low, pool_w, preferred_element_type=jnp.float32)
    pooled = pooled.astype(jnp.bfloat16)
    before = dot(pooled, proj_w)
    hidden = jax.nn.silu(before).astype(jnp.bfloat16)
    scores = jnp.einsum("nk,bkl->nbl", hidden, heads_w, preferred_element_type=jnp.float32)
    scores = scores.reshape(-1, GAMES, 2 * WIDTH)[:, :, :PLAYS]
    return (scores, (low, pooled, before, hidden))


def lamb_parts(params, grads, first, second):
    momentum = BETA_ONE * first + (1.0 - BETA_ONE) * grads
    variance = BETA_TWO * second + (1.0 - BETA_TWO) * grads * grads
    direction = (
        momentum / (1.0 - BETA_ONE**STEP) / (jnp.sqrt(variance / (1.0 - BETA_TWO**STEP)) + 1e-06)
        + WEIGHT_DECAY * params
    )
    return (momentum, variance, direction)


def squares(flat, cuts):
    return jnp.stack(
        [jnp.sum(jnp.square(flat[..., start : start + width]), axis=-1) for start, width in cuts],
        axis=-1,
    )


def spread_ratio(ratio, flat, cuts):
    parts = [
        jnp.broadcast_to(ratio[..., index : index + 1], flat.shape[:-1] + (width,))
        for index, (start, width) in enumerate(cuts)
    ]
    return jnp.concatenate(parts, axis=-1)


def frame_rows(frames):
    count = frames.shape[0]
    return jnp.pad(frames, ((0, 0), (0, ROWS - PIX), (0, 0))).reshape(count * ROWS, PATCH_IN)


def on_device(
    observed,
    following,
    game_ids,
    actions,
    legal_mask,
    rewards,
    discounts,
    done_flags,
    params_top,
    params_blocks,
    first_top,
    first_blocks,
    second_top,
    second_blocks,
    average_top,
    average_blocks,
    target_top,
    target_blocks,
):
    devices = lax.axis_size(AXES)
    frames_all = observed.shape[0] * devices
    top_lengths, block_lengths = segment_lengths()
    top_cuts = cut_points(top_lengths, devices)
    block_cuts = cut_points(block_lengths, devices)
    gain_start, gain_width = block_cuts[3]
    parts = parts_for(devices)
    tuned = is_tuned(devices)
    place = spot()
    shift = shifts()
    spread = spread_pixels(devices)
    weight_parts = jnp.concatenate(
        [squares(params_top, top_cuts), squares(params_blocks, block_cuts).reshape(-1)]
    )

    game_hot = (game_ids[:, None] == jnp.arange(GAMES)[None, :]).astype(jnp.float32)
    taken_hot = (actions[:, 0:1] == jnp.arange(ACTIONS)[None, :]).astype(jnp.float32)
    next_hot = (actions[:, 1:2] == jnp.arange(ACTIONS)[None, :]).astype(jnp.float32)

    low_blocks = params_blocks.astype(jnp.bfloat16)
    own = {}
    for net, top, blocks in (
        ("target", target_top, target_blocks),
        ("online", params_top.astype(jnp.bfloat16), low_blocks),
    ):
        for name, piece in zip(("patch", "pool", "proj", "heads"), pack_top(top, top_cuts)):
            own[net, name] = piece
        for index in range(BLOCKS):
            for name, piece in zip(("w_in", "w_mid", "w_out"), pack_block(blocks[index], block_cuts)):
                own[net, name, index] = piece
    gain_rows = jnp.concatenate([target_blocks, low_blocks])[:, gain_start:]
    own["gains",] = jnp.pad(
        gain_rows, ((0, TILE - 2 * BLOCKS), (0, WIDTH - gain_width))
    ).reshape(1, TILE, WIDTH)
    block_names = ("w_in", "w_mid", "w_out")
    keys = []
    for net in ("target", "online"):
        ends = [(net, name) for name in ("pool", "proj")]
        if net == "target":
            keys.append([("gains",)] + ends)
        keys.append([(net, "patch")] + [(net, name, 0) for name in block_names])
        for index in range(1, BLOCKS):
            keys.append([(net, name, index) for name in block_names])
        keys.append([(net, "heads")] + (ends if net == "online" else []))

    def part_of(key):
        return parts[key[0] if key[0] == "gains" else key[1]]

    full = {}
    if tuned:
        groups = [[part_of(key) for key in group] for group in keys]
        held = gather_all(groups, [[own[key] for key in group] for group in keys], place)
        for group, kinds, buffers in zip(keys, groups, held):
            full |= dict(zip(group, assemble(kinds, buffers, place)))
    else:
        for key, piece in own.items():
            full[key] = plain_gather(piece)
    gains = full["gains",].reshape(devices, TILE, WIDTH)[:, : 2 * BLOCKS, :gain_width]
    gains = gains.transpose(1, 0, 2).reshape(2 * BLOCKS, -1).astype(jnp.float32)

    def block_weights(net, index):
        w_in, w_mid, w_out = [full[net, name, index] for name in block_names]
        return (w_in[0], w_mid[0], w_out.reshape(D, BOT))

    def top_weights(net):
        return (full[net, "pool"][0], full[net, "proj"][0], full[net, "heads"])

    stream = embed(frame_rows(following), spread, full["target", "patch"])
    for index in range(BLOCKS):
        stream = block_forward(
            stream, *block_weights("target", index), gains[index : index + 1], shift, False
        )[0]
    target_scores, ignored = head_scores(stream, *top_weights("target"))
    target = target_dist(select(target_scores, game_hot), next_hot, rewards, discounts, done_flags)

    pixels = frame_rows(observed)
    stream = embed(pixels, spread, full["online", "patch"])
    kept = []
    for index in range(BLOCKS):
        weights = block_weights("online", index)
        gain = gains[BLOCKS + index : BLOCKS + index + 1]
        out, hid_one, hid_two, hid_three, rstd = block_forward(stream, *weights, gain, shift, True)
        kept.append((stream, hid_one, hid_two, hid_three, rstd, weights, gain))
        stream = out
    pool_w, proj_w, heads_w = top_weights("online")
    scores, (low, pooled, before, hidden) = head_scores(stream, pool_w, proj_w, heads_w)

    def objective(scores_in):
        return jnp.sum(frame_losses(select(scores_in, game_hot), target, taken_hot, legal_mask))

    loss_part, back_loss = jax.vjp(objective, scores)
    grad_scores = back_loss(jnp.float32(1.0 / frames_all))[0].astype(jnp.bfloat16)
    grad_scores = jnp.pad(grad_scores, ((0, 0), (0, 0), (0, 2 * WIDTH - PLAYS)))
    grad_scores = grad_scores.reshape(-1, 2 * GAMES, WIDTH)
    grads = {}
    grads["heads",] = jnp.einsum(
        "nk,nbl->bkl", hidden, grad_scores, preferred_element_type=jnp.float32
    ).astype(jnp.bfloat16)
    grad_hidden = jnp.einsum(
        "nbl,bkl->nk", grad_scores, heads_w, preferred_element_type=jnp.float32
    )
    grad_before = jax.vjp(jax.nn.silu, before)[1](grad_hidden)[0].astype(jnp.bfloat16)
    grads["proj",] = dot_rows(pooled, grad_before).astype(jnp.bfloat16)[None]
    grad_pooled = dot_lanes(grad_before, proj_w).astype(jnp.bfloat16)
    grads["pool",] = jnp.einsum(
        "npc,nc->cp", low, grad_pooled, preferred_element_type=jnp.float32
    ).astype(jnp.bfloat16)[None]
    grad_stream = jnp.einsum(
        "nc,cp->npc", grad_pooled, pool_w, preferred_element_type=jnp.float32
    ).reshape(-1, D)

    dgains = [None] * BLOCKS
    for index in reversed(range(BLOCKS)):
        stream, hid_one, hid_two, hid_three, rstd, weights, gain = kept[index]
        w_in, w_mid, w_out = weights
        dres, dsecond, dw_out, late = back_out(
            grad_stream, stream, hid_two, hid_three, rstd, w_out, gain
        )
        dfirst, dw_mid, early = back_mid(dsecond, hid_one, rstd, w_mid, gain, shift)
        dw_in, grad_stream = back_in(dfirst, stream, dres, w_in)
        dgains[index] = jnp.concatenate([early, late], axis=1)
        grads["w_in", index] = dw_in[None]
        grads["w_mid", index] = dw_mid[None]
        grads["w_out", index] = dw_out.reshape(D // BOT, BOT, BOT)
    grads["patch",] = embed_back(pixels, spread, grad_stream)
    dgains = jnp.concatenate(dgains).reshape(BLOCKS, devices, gain_width).transpose(1, 0, 2)
    dgains = jnp.pad(dgains, ((0, 0), (0, TILE - BLOCKS), (0, WIDTH - gain_width)))
    grads["gains",] = dgains.reshape(1, -1, WIDTH).astype(jnp.bfloat16)

    keys = [[("heads",), ("proj",)], [("w_out", BLOCKS - 1), ("pool",)]]
    for index in reversed(range(BLOCKS)):
        keys.append([("w_mid", index)])
        keys.append([("w_in", index)])
        keys[-1] += [("w_out", index - 1)] if index else [("patch",), ("gains",)]
    mine = {}
    for group in keys:
        arrays = [grads[key] for key in group]
        if tuned:
            sums = scatter([parts[key[0]] for key in group], arrays, place)
        else:
            sums = [plain_scatter(array) for array in arrays]
        mine |= dict(zip(group, sums))
    grad_top = flat_top(*[mine[name,] for name in ("patch", "pool", "proj", "heads")])
    grad_blocks = jnp.stack(
        [
            flat_block(*[mine[name, index] for name in block_names], mine["gains",][0, index, :gain_width])
            for index in range(BLOCKS)
        ]
    )

    momentum_top, variance_top, direction_top = lamb_parts(
        params_top, grad_top, first_top, second_top
    )
    momentum_blocks, variance_blocks, direction_blocks = lamb_parts(
        params_blocks, grad_blocks, first_blocks, second_blocks
    )
    update_parts = jnp.concatenate(
        [squares(direction_top, top_cuts), squares(direction_blocks, block_cuts).reshape(-1)]
    )
    sums = total(jnp.concatenate([weight_parts, update_parts, loss_part[None]])[None])[0]
    count = weight_parts.shape[0]
    weight_sq, update_sq, loss_total = (sums[:count], sums[count : 2 * count], sums[2 * count])
    weight_norm = jnp.sqrt(weight_sq)
    update_norm = jnp.sqrt(update_sq)
    ratio = weight_norm / (update_norm + 1e-06)
    scale_top = spread_ratio(ratio[:4], params_top, top_cuts)
    scale_blocks = spread_ratio(ratio[4:].reshape(BLOCKS, 4), params_blocks, block_cuts)
    updated_top = params_top - LEARNING_RATE * scale_top * direction_top
    updated_blocks = params_blocks - LEARNING_RATE * scale_blocks * direction_blocks
    decay = average_decay()
    averaged_top = decay * average_top + (1.0 - decay) * updated_top
    averaged_blocks = decay * average_blocks + (1.0 - decay) * updated_blocks
    matrix_norms = jnp.stack([weight_norm, update_norm])
    gain_grads = grad_blocks[:, gain_start : gain_start + gain_width]
    return (
        loss_total,
        matrix_norms,
        updated_top,
        updated_top.astype(jnp.bfloat16),
        momentum_top,
        variance_top,
        averaged_top,
        updated_blocks,
        updated_blocks.astype(jnp.bfloat16),
        momentum_blocks,
        variance_blocks,
        averaged_blocks,
        gain_grads,
    )


def solution(mesh):
    one = P(AXES)
    flat = P(None, AXES)
    return jax.shard_map(
        on_device,
        mesh=mesh,
        in_specs=(P(AXES, None, None),) * 2
        + (one, P(AXES, None), P(AXES, None))
        + (one,) * 3
        + (one, flat) * 5,
        out_specs=(P(), P()) + (one,) * 5 + (flat,) * 6,
        check_vma=False,
    )
```

```python
import functools
import itertools

import jax
import jax.numpy as jnp
from jax import lax
from jax.experimental import pallas as pl
from jax.experimental.pallas import tpu as pltpu
from jax.sharding import PartitionSpec as P

D = 2048
BOT = 512
GROUPS = 32
SIDE = 11
PIX = 121
TAPS = 9

ROWS = 128
LANES = 256
VMEM_LIMIT = 60 * 1024 * 1024
LIGHT = pl.CostEstimate(flops=1024, bytes_accessed=1024, transcendentals=0)


def shifts():
    pixel = jnp.arange(ROWS)
    row, col = (pixel // SIDE, pixel % SIDE)
    mats = []
    for tap in range(TAPS):
        at_row, at_col = (row + tap // 3 - 1, col + tap % 3 - 1)
        inside = (at_row >= 0) & (at_row < SIDE) & (at_col >= 0) & (at_col < SIDE) & (pixel < PIX)
        mats.append((inside[:, None] & (pixel[None, :] == (at_row * SIDE + at_col)[:, None])))
    return jnp.concatenate(mats, axis=0).astype(jnp.bfloat16)


def dot(left, right):
    return jnp.dot(left, right, preferred_element_type=jnp.float32)


def dot_rows(left, right):
    return lax.dot_general(
        left, right, (((0,), (0,)), ((), ())), preferred_element_type=jnp.float32
    )


def dot_lanes(left, right):
    return lax.dot_general(
        left, right, (((1,), (1,)), ((), ())), preferred_element_type=jnp.float32
    )


def each_chunk(count, chans, body, unroll=1):
    per = chans // LANES

    def step(index, carry):
        frame = index // per
        rows = pl.ds(pl.multiple_of(frame * ROWS, ROWS), ROWS)
        lanes = pl.ds(pl.multiple_of((index % per) * LANES, LANES), LANES)
        body(pl.ds(frame, 1), rows, lanes)
        return carry

    lax.fori_loop(0, count * per, step, 0, unroll=unroll)


def real_rows():
    return lax.broadcasted_iota(jnp.int32, (ROWS, LANES), 0) < PIX


def group_mean(sums):
    chans = sums.shape[1]
    width = chans // GROUPS
    lane = lax.broadcasted_iota(jnp.int32, sums.shape, 1)
    step = 1
    while step < width:
        ahead = pltpu.roll(sums, chans - step, 1)
        behind = pltpu.roll(sums, step, 1)
        sums = sums + jnp.where((lane & step) == 0, ahead, behind)
        step *= 2
    return sums * (1.0 / (PIX * width))


def silu(value):
    return value / (1.0 + jnp.exp(-value))


def silu_slope(value):
    gate = 1.0 / (1.0 + jnp.exp(-value))
    return gate * (1.0 + value * (1.0 - gate))


def normalise(count, chans, hid, sums, rstd, rstd_at):
    whole = pl.ds(0, chans)
    sums[:, whole] = jnp.zeros((sums.shape[0], chans), jnp.float32)

    def add(frame, rows, lanes):
        sums[frame, lanes] = jnp.sum(hid[rows, lanes], axis=0, keepdims=True)

    each_chunk(count, chans, add, unroll=2)
    sums[:, whole] = group_mean(sums[:, whole])

    def center(frame, rows, lanes):
        value = jnp.where(real_rows(), hid[rows, lanes] - sums[frame, lanes], 0.0)
        hid[rows, lanes] = value
        sums[frame, lanes] = jnp.sum(value * value, axis=0, keepdims=True)

    each_chunk(count, chans, center, unroll=2)
    at = pl.ds(rstd_at, chans)
    rstd[:, at] = lax.rsqrt(group_mean(sums[:, whole]) + 1e-05)


def forward_kernel(count, keep, parts, tuned, *refs):
    refs = list(refs)
    first = len(parts) > 3

    def take(number):
        taken = refs[:number]
        del refs[:number]
        return taken

    (place,) = take(1)
    x = take(2 if first else 1)
    gains, shift = take(2)
    sources = take(2 if tuned else len(parts))
    (out,) = take(1)
    if keep:
        if first:
            (start,) = take(1)
        hid_one, hid_two, hid_three, rstd = take(4)
        kept_weights = take(3)
    weights = take(len(parts))
    sems, back_sems, low, act, cols, sums = take(6)
    if not keep:
        hid_one, hid_two, hid_three, rstd = take(4)
        if first:
            (start,) = take(1)
    fetch(parts, tuned, place, sources, weights, sems)

    def arrived(index):
        index += len(parts)
        pltpu.make_async_copy(weights[index], weights[index], sems.at[index]).wait()
        if keep and index >= len(parts) - 3:
            number = index - len(parts) + 3
            pltpu.make_async_copy(weights[index], kept_weights[number], back_sems.at[number]).start()
        return weights[index]

    def whole(value):
        return value.reshape(-1, value.shape[-1])

    if first:
        pixels, spread = x
        x = start
        patch = arrived(-4)
        for half in range(2):
            wide = dot(pixels[...], spread[half]).astype(jnp.bfloat16)
            for block in range(2):
                lanes = pl.ds((2 * half + block) * WIDTH, WIDTH)
                x[:, lanes] = dot(wide, whole(patch[block]))
    else:
        (x,) = x

    def cast(frame, rows, lanes):
        low[rows, lanes] = x[rows, lanes].astype(jnp.bfloat16)

    def activate(hid, at, offset):
        def body(frame, rows, lanes):
            gain = gains[:, pl.ds(offset + lanes.start, LANES)]
            bias = gains[:, pl.ds(offset + BOT + lanes.start, LANES)]
            value = hid[rows, lanes] * rstd[frame, pl.ds(at + lanes.start, LANES)]
            hid[rows, lanes] = value
            value = jnp.where(real_rows(), silu(value * gain + bias), 0.0)
            act[rows, lanes] = value.astype(jnp.bfloat16)

        return body

    each_chunk(count, D, cast)
    hid_one[...] = dot(low[...], whole(arrived(-3)[...]))
    normalise(count, BOT, hid_one, sums, rstd, 0)
    each_chunk(count, BOT, activate(hid_one, 0, 0))
    for frame in range(count):
        rows = pl.ds(frame * ROWS, ROWS)
        for tap in range(TAPS):
            picked = dot(shift[pl.ds(tap * ROWS, ROWS), :], act[rows, :])
            cols[rows, pl.ds(tap * BOT, BOT)] = picked.astype(jnp.bfloat16)
    hid_two[...] = dot(cols[...], whole(arrived(-2)[...]))
    normalise(count, BOT, hid_two, sums, rstd, BOT)
    each_chunk(count, BOT, activate(hid_two, BOT, 2 * BOT))
    w_out = arrived(-1)
    for part in range(D // BOT):
        hid_three[:, pl.ds(part * BOT, BOT)] = dot(act[...], whole(w_out[part]))
    normalise(count, D, hid_three, sums, rstd, 2 * BOT)

    def finish(frame, rows, lanes):
        gain = gains[:, pl.ds(4 * BOT + lanes.start, LANES)]
        bias = gains[:, pl.ds(4 * BOT + D + lanes.start, LANES)]
        value = hid_three[rows, lanes] * rstd[frame, pl.ds(2 * BOT + lanes.start, LANES)]
        if keep:
            hid_three[rows, lanes] = value
        value = silu(x[rows, lanes] + value * gain + bias)
        out[rows, lanes] = jnp.where(real_rows(), value, 0.0)

    each_chunk(count, D, finish)
    if keep:
        for number in range(3):
            weight = weights[len(parts) - 3 + number]
            pltpu.make_async_copy(weight, kept_weights[number], back_sems.at[number]).wait()


def f32(*shape):
    return jax.ShapeDtypeStruct(shape, jnp.float32)


def bf16(*shape):
    return jax.ShapeDtypeStruct(shape, jnp.bfloat16)


def stat_rows(count):
    return -(-count // 8) * 8


def block_forward(stream, gains, shift, parts, buffers, place, keep, tuned):
    first = len(parts) > 3
    rows = stream[0].shape[0]
    count = rows // ROWS
    stats = stat_rows(count)
    kept = [
        ((rows, BOT), jnp.float32),
        ((rows, BOT), jnp.float32),
        ((rows, D), jnp.float32),
        ((stats, 2 * BOT + D), jnp.float32),
    ]
    start = [((rows, D), jnp.float32)] if first else []
    weights = weight_shapes(parts, buffers, tuned)
    out_shape = [f32(rows, D)]
    out_specs = in_vmem(1)
    scratch = [pltpu.VMEM(shape, jnp.bfloat16) for shape in weights]
    scratch += [
        pltpu.SemaphoreType.DMA((len(parts),)),
        pltpu.SemaphoreType.DMA((3,)),
        pltpu.VMEM((rows, D), jnp.bfloat16),
        pltpu.VMEM((rows, BOT), jnp.bfloat16),
        pltpu.VMEM((rows, TAPS * BOT), jnp.bfloat16),
        pltpu.VMEM((stats, D), jnp.float32),
    ]
    if keep:
        out_shape += [jax.ShapeDtypeStruct(*item) for item in start + kept]
        out_shape += [jax.ShapeDtypeStruct(shape, jnp.bfloat16) for shape in weights[-3:]]
        out_specs += in_vmem(len(start + kept)) + hbm(3)
    else:
        scratch += [pltpu.VMEM(*item) for item in kept + start]
    return pl.pallas_call(
        functools.partial(forward_kernel, count, keep, parts, tuned),
        out_shape=out_shape,
        in_specs=in_smem() + in_vmem(len(stream) + 2) + hbm(len(buffers)),
        out_specs=out_specs,
        scratch_shapes=scratch,
        compiler_params=pltpu.CompilerParams(vmem_limit_bytes=VMEM_LIMIT),
        cost_estimate=LIGHT,
        name="block_forward",
    )(place, *stream, gains, shift, *buffers)


def norm_back(count, chans, slope, hid, sums, more, rstd, rstd_at, gain, grad_gain, grad_bias, store):
    whole = pl.ds(0, chans)
    sums[:, whole] = jnp.zeros((sums.shape[0], chans), jnp.float32)
    more[:, whole] = jnp.zeros((sums.shape[0], chans), jnp.float32)

    def add(frame, rows, lanes):
        value = slope(frame, rows, lanes)
        sums[frame, lanes] = jnp.sum(value, axis=0, keepdims=True)
        more[frame, lanes] = jnp.sum(value * hid[rows, lanes], axis=0, keepdims=True)

    each_chunk(count, chans, add)
    grad_bias[...] = jnp.sum(sums[:, whole], axis=0, keepdims=True)
    grad_gain[...] = jnp.sum(more[:, whole], axis=0, keepdims=True)
    sums[:, whole] = group_mean(sums[:, whole] * gain[...])
    more[:, whole] = group_mean(more[:, whole] * gain[...])

    def spread(frame, rows, lanes):
        store(
            rows,
            lanes,
            lambda value: jnp.where(
                real_rows(),
                rstd[frame, pl.ds(rstd_at + lanes.start, LANES)]
                * (value * gain[:, lanes] - sums[frame, lanes] - hid[rows, lanes] * more[frame, lanes]),
                0.0,
            ).astype(jnp.bfloat16),
        )

    each_chunk(count, chans, spread)


def back_out_kernel(count, *refs):
    grad, x, hid_two, hid_three, rstd, w_out, gains = refs[:7]
    dres, dlow, dw_out, dgains = refs[7:11]
    third, act, dact, sums, more = refs[11:]
    gain_three, bias_three = (gains.at[:, pl.ds(4 * BOT, D)], gains.at[:, pl.ds(4 * BOT + D, D)])

    def slope_three(frame, rows, lanes):
        value = x[rows, lanes] + hid_three[rows, lanes] * gain_three[:, lanes] + bias_three[:, lanes]
        value = jnp.where(real_rows(), grad[rows, lanes] * silu_slope(value), 0.0)
        dres[rows, lanes] = value
        return value

    def store_three(rows, lanes, back):
        third[rows, lanes] = back(dres[rows, lanes])

    norm_back(
        count, D, slope_three, hid_three, sums, more, rstd, 2 * BOT, gain_three,
        dgains.at[:, pl.ds(2 * BOT, D)], dgains.at[:, pl.ds(2 * BOT + D, D)], store_three,
    )
    total = None
    for part in range(D // BOT):
        lanes = pl.ds(part * BOT, BOT)
        term = dot_lanes(third[:, lanes], w_out[lanes, :])
        total = term if total is None else total + term
    dact[...] = total
    gain_two, bias_two = (gains.at[:, pl.ds(2 * BOT, BOT)], gains.at[:, pl.ds(3 * BOT, BOT)])

    def slope_two(frame, rows, lanes):
        value = hid_two[rows, lanes] * gain_two[:, lanes] + bias_two[:, lanes]
        gate = 1.0 / (1.0 + jnp.exp(-value))
        act[rows, lanes] = jnp.where(real_rows(), value * gate, 0.0).astype(jnp.bfloat16)
        value = dact[rows, lanes] * (gate * (1.0 + value * (1.0 - gate)))
        value = jnp.where(real_rows(), value, 0.0)
        dact[rows, lanes] = value
        return value

    def store_two(rows, lanes, back):
        dlow[rows, lanes] = back(dact[rows, lanes])

    norm_back(
        count, BOT, slope_two, hid_two, sums, more, rstd, BOT, gain_two,
        dgains.at[:, pl.ds(0, BOT)], dgains.at[:, pl.ds(BOT, BOT)], store_two,
    )
    for part in range(D // BOT):
        lanes = pl.ds(part * BOT, BOT)
        dw_out[lanes, :] = dot_rows(act[...], third[:, lanes]).astype(jnp.bfloat16)


def back_out(grad, stream, hid_two, hid_three, rstd, w_out, gains):
    rows = stream.shape[0]
    count = rows // ROWS
    stats = stat_rows(count)
    return pl.pallas_call(
        functools.partial(back_out_kernel, count),
        out_shape=[f32(rows, D), bf16(rows, BOT), bf16(D, BOT), f32(1, 2 * BOT + 2 * D)],
        in_specs=in_vmem(7),
        out_specs=in_vmem(4),
        scratch_shapes=[
            pltpu.VMEM((rows, D), jnp.bfloat16),
            pltpu.VMEM((rows, BOT), jnp.bfloat16),
            pltpu.VMEM((rows, BOT), jnp.float32),
            pltpu.VMEM((stats, D), jnp.float32),
            pltpu.VMEM((stats, D), jnp.float32),
        ],
        compiler_params=pltpu.CompilerParams(vmem_limit_bytes=VMEM_LIMIT),
        cost_estimate=LIGHT,
        name="back_out",
    )(grad, stream, hid_two, hid_three, rstd, w_out, gains)


def back_mid_kernel(count, *refs):
    grad, hid_one, rstd, w_mid, gains, shift = refs[:6]
    dlow, dw_mid, dgains = refs[6:9]
    act, cols, dact, sums, more = refs[9:]
    gain_one, bias_one = (gains.at[:, pl.ds(0, BOT)], gains.at[:, pl.ds(BOT, BOT)])
    for frame in range(count):
        rows = pl.ds(frame * ROWS, ROWS)
        for tap in range(TAPS):
            picked = dot(shift[pl.ds((TAPS - 1 - tap) * ROWS, ROWS), :], grad[rows, :])
            cols[rows, pl.ds(tap * BOT, BOT)] = picked.astype(jnp.bfloat16)
    total = None
    for tap in range(TAPS):
        lanes = pl.ds(tap * BOT, BOT)
        term = dot_lanes(cols[:, lanes], w_mid[lanes, :])
        total = term if total is None else total + term
    dact[...] = total

    def slope_one(frame, rows, lanes):
        value = hid_one[rows, lanes] * gain_one[:, lanes] + bias_one[:, lanes]
        gate = 1.0 / (1.0 + jnp.exp(-value))
        act[rows, lanes] = jnp.where(real_rows(), value * gate, 0.0).astype(jnp.bfloat16)
        value = dact[rows, lanes] * (gate * (1.0 + value * (1.0 - gate)))
        value = jnp.where(real_rows(), value, 0.0)
        dact[rows, lanes] = value
        return value

    def store_one(rows, lanes, back):
        dlow[rows, lanes] = back(dact[rows, lanes])

    norm_back(
        count, BOT, slope_one, hid_one, sums, more, rstd, 0, gain_one,
        dgains.at[:, pl.ds(0, BOT)], dgains.at[:, pl.ds(BOT, BOT)], store_one,
    )
    for tap in range(TAPS):
        lanes = pl.ds(tap * BOT, BOT)
        dw_mid[lanes, :] = dot_rows(act[...], cols[:, lanes]).astype(jnp.bfloat16)


def back_mid(grad, hid_one, rstd, w_mid, gains, shift):
    rows = grad.shape[0]
    count = rows // ROWS
    stats = stat_rows(count)
    return pl.pallas_call(
        functools.partial(back_mid_kernel, count),
        out_shape=[bf16(rows, BOT), bf16(TAPS * BOT, BOT), f32(1, 2 * BOT)],
        in_specs=in_vmem(6),
        out_specs=in_vmem(3),
        scratch_shapes=[
            pltpu.VMEM((rows, BOT), jnp.bfloat16),
            pltpu.VMEM((rows, TAPS * BOT), jnp.bfloat16),
            pltpu.VMEM((rows, BOT), jnp.float32),
            pltpu.VMEM((stats, BOT), jnp.float32),
            pltpu.VMEM((stats, BOT), jnp.float32),
        ],
        compiler_params=pltpu.CompilerParams(vmem_limit_bytes=VMEM_LIMIT),
        cost_estimate=LIGHT,
        name="back_mid",
    )(grad, hid_one, rstd, w_mid, gains, shift)


def back_in_kernel(count, *refs):
    grad, x, dres, w_in, dw_in, dx, low = refs

    def cast(frame, rows, lanes):
        low[rows, lanes] = x[rows, lanes].astype(jnp.bfloat16)

    each_chunk(count, D, cast)
    for part in range(D // BOT):
        lanes = pl.ds(part * BOT, BOT)
        dw_in[lanes, :] = dot_rows(low[:, lanes], grad[...]).astype(jnp.bfloat16)
        dx[:, lanes] = dres[:, lanes] + dot_lanes(grad[...], w_in[lanes, :])


def back_in(grad, stream, dres, w_in):
    rows = grad.shape[0]
    return pl.pallas_call(
        functools.partial(back_in_kernel, rows // ROWS),
        out_shape=[bf16(D, BOT), f32(rows, D)],
        in_specs=in_vmem(4),
        out_specs=in_vmem(2),
        scratch_shapes=[pltpu.VMEM((rows, D), jnp.bfloat16)],
        compiler_params=pltpu.CompilerParams(vmem_limit_bytes=VMEM_LIMIT),
        cost_estimate=LIGHT,
        name="back_in",
    )(grad, stream, dres, w_in)


def spread_pixels(devices):
    rows = PATCH_IN // devices
    value = jnp.arange(PATCH_IN)
    at = value // rows * 2 * rows + value % rows
    return jnp.stack(
        [jnp.arange(2 * PATCH_IN)[None, :] == (at + half * rows)[:, None] for half in range(2)]
    ).astype(jnp.bfloat16)


def embed_back_kernel(pixels, spread, grad, out):
    wide = [dot(pixels[...], spread[half]).astype(jnp.bfloat16) for half in range(2)]
    for block in range(2):
        total = None
        for half in range(2):
            lanes = pl.ds((2 * half + block) * WIDTH, WIDTH)
            term = dot_rows(wide[half], grad[:, lanes].astype(jnp.bfloat16))
            total = term if total is None else total + term
        out[block] = total.astype(jnp.bfloat16)


def embed_back(pixels, spread, grad):
    return pl.pallas_call(
        embed_back_kernel,
        out_shape=bf16(2, 2 * PATCH_IN, WIDTH),
        in_specs=in_vmem(3),
        out_specs=in_vmem(1)[0],
        compiler_params=pltpu.CompilerParams(vmem_limit_bytes=VMEM_LIMIT),
        cost_estimate=LIGHT,
        name="embed_back",
    )(pixels, spread, grad)


def head_forward(count, stream, pool, proj, heads, games, pool_t, pooled):
    for part in range(D // ROWS):
        lanes = pl.ds(part * ROWS, ROWS)
        pool_t[:, lanes] = pool[lanes, :].astype(jnp.float32).T
    pooled[...] = jnp.zeros_like(pooled)

    def weigh(frame, rows, lanes):
        value = stream[rows, lanes].astype(jnp.bfloat16).astype(jnp.float32)
        pooled[frame, lanes] = jnp.sum(value * pool_t[:, lanes], axis=0, keepdims=True)

    each_chunk(count, D, weigh)
    before = dot(pooled[...].astype(jnp.bfloat16), proj[...])
    hidden = silu(before).astype(jnp.bfloat16)
    scores = None
    for game in range(GAMES):
        pair = [dot(hidden, heads[2 * game + half]) for half in range(2)]
        term = jnp.where(games == game, jnp.concatenate(pair, axis=1), 0.0)
        scores = term if scores is None else scores + term
    return ([pick_atoms(scores, action) for action in range(ACTIONS)], before, hidden)


def atom_lanes():
    return lax.broadcasted_iota(jnp.int32, (8, ROWS), 1)


def pick_atoms(scores, action):
    offset = action * ATOMS
    moved = pltpu.roll(scores, 2 * WIDTH - offset, 1) if offset else scores
    return jnp.where(atom_lanes() < ATOMS, moved[:, :ROWS], -1e30)


def support_lanes():
    return -10.0 + 20.0 / (ATOMS - 1) * atom_lanes().astype(jnp.float32)


def lane_sum(value):
    return jnp.sum(value, axis=1, keepdims=True)


def target_kernel(count, stream, pool, proj, heads, whole, real, out, pool_t, pooled):
    logits, _, _ = head_forward(
        count, stream, pool, proj, heads, whole[:, 0:1], pool_t, pooled
    )
    chosen = None
    for action in range(ACTIONS):
        term = jnp.where(whole[:, 2:3] == action, logits[action], 0.0)
        chosen = term if chosen is None else chosen + term
    power = jnp.exp(chosen - jnp.max(chosen, axis=1, keepdims=True))
    probs = power / lane_sum(power)
    atoms = support_lanes()
    spacing = 20.0 / (ATOMS - 1)
    moved = jnp.clip(real[:, 0:1] + real[:, 1:2] * atoms, -10.0, 10.0)
    total = jnp.zeros_like(probs)
    for atom in range(ATOMS):
        near = 1.0 - jnp.abs(moved[:, atom : atom + 1] - atoms) / spacing
        total = total + probs[:, atom : atom + 1] * jnp.clip(near, 0.0, 1.0)
    inside = (atom_lanes() < ATOMS) & (lax.broadcasted_iota(jnp.int32, total.shape, 0) < count)
    out[...] = jnp.where(inside, total, 0.0)


def head_target(stream, pool, proj, heads, whole, real):
    count = stream.shape[0] // ROWS
    return pl.pallas_call(
        functools.partial(target_kernel, count),
        out_shape=f32(8, ROWS),
        in_specs=in_vmem(6),
        out_specs=in_vmem(1)[0],
        scratch_shapes=[pltpu.VMEM((ROWS, D), jnp.float32), pltpu.VMEM((8, D), jnp.float32)],
        compiler_params=pltpu.CompilerParams(vmem_limit_bytes=VMEM_LIMIT),
        cost_estimate=LIGHT,
        name="head_target",
    )(stream, pool, proj, heads, whole, real)


def loss_kernel(count, frames_all, *refs):
    stream, pool, proj, heads, target, whole, legal = refs[:7]
    loss, dheads, dproj, dpool, dstream = refs[7:12]
    pool_t, pooled, dpooled = refs[12:]
    games, taken = (whole[:, 0:1], whole[:, 1:2])
    logits, before, hidden = head_forward(count, stream, pool, proj, heads, games, pool_t, pooled)
    atoms = support_lanes()
    inside = atom_lanes() < ATOMS
    logps, probs, values = ([], [], [])
    for value in logits:
        value = value - jnp.max(value, axis=1, keepdims=True)
        power = jnp.where(inside, jnp.exp(value), 0.0)
        mass = lane_sum(power)
        logps.append(value - jnp.log(mass))
        probs.append(power / mass)
        values.append(lane_sum(probs[-1] * atoms))
    masked = [
        jnp.where(legal[:, action : action + 1] > 0, values[action], -1e30)
        for action in range(ACTIONS)
    ]
    largest = functools.reduce(jnp.maximum, masked)
    powers = [jnp.exp(value - largest) for value in masked]
    mass = sum(powers[1:], powers[0])
    goal = target[...]
    goal_mass = lane_sum(goal)
    cross = taken_value = 0.0
    real = lax.broadcasted_iota(jnp.int32, (8, 1), 0) < count
    scale = jnp.where(real, 1.0 / frames_all, 0.0)
    spread = jnp.zeros((8, 2 * WIDTH), jnp.float32)
    for action in range(ACTIONS):
        here = jnp.where(taken == action, 1.0, 0.0)
        cross = cross - here * lane_sum(jnp.where(inside, goal * logps[action], 0.0))
        taken_value = taken_value + here * values[action]
        grad = here * (probs[action] * goal_mass - goal)
        pull = CQL_WEIGHT * (powers[action] / mass - here)
        grad = grad + pull * probs[action] * (atoms - values[action])
        grad = jnp.where(inside, grad * scale, 0.0)
        grad = jnp.concatenate([grad, jnp.zeros((8, 2 * WIDTH - ROWS), jnp.float32)], axis=1)
        offset = action * ATOMS
        spread = spread + (pltpu.roll(grad, offset, 1) if offset else grad)
    losses = cross + CQL_WEIGHT * (jnp.log(mass) + largest - taken_value)
    loss[...] = jnp.sum(jnp.where(real, losses, 0.0), axis=0, keepdims=True)
    dhidden = None
    for game in range(GAMES):
        mine = jnp.where(games == game, spread, 0.0).astype(jnp.bfloat16)
        for half in range(2):
            part = mine[:, half * WIDTH : (half + 1) * WIDTH]
            dheads[2 * game + half] = dot_rows(hidden, part).astype(jnp.bfloat16)
            term = dot_lanes(part, heads[2 * game + half])
            dhidden = term if dhidden is None else dhidden + term
    dbefore = (silu_slope(before) * dhidden).astype(jnp.bfloat16)
    dproj[...] = dot_rows(pooled[...].astype(jnp.bfloat16), dbefore).astype(jnp.bfloat16)
    dpooled[...] = dot_lanes(dbefore, proj[...]).astype(jnp.bfloat16).astype(jnp.float32)

    def push(frame, rows, lanes):
        dstream[rows, lanes] = dpooled[frame, lanes] * pool_t[:, lanes]

    each_chunk(count, D, push)

    def gather_pool(part, carry):
        lanes = pl.ds(pl.multiple_of(part * ROWS, ROWS), ROWS)
        total = None
        for frame in range(count):
            value = stream[pl.ds(frame * ROWS, ROWS), lanes].astype(jnp.bfloat16)
            term = value.astype(jnp.float32) * dpooled[pl.ds(frame, 1), lanes]
            total = term if total is None else total + term
        dpool[lanes, :] = total.T.astype(jnp.bfloat16)
        return carry

    lax.fori_loop(0, D // ROWS, gather_pool, 0)


def head_loss(stream, pool, proj, heads, target, whole, legal, frames_all):
    rows = stream.shape[0]
    return pl.pallas_call(
        functools.partial(loss_kernel, rows // ROWS, frames_all),
        out_shape=[f32(1, 1), bf16(2 * GAMES, DPROJ, WIDTH), bf16(D, DPROJ), bf16(D, ROWS), f32(rows, D)],
        in_specs=in_vmem(7),
        out_specs=in_vmem(5),
        scratch_shapes=[
            pltpu.VMEM((ROWS, D), jnp.float32),
            pltpu.VMEM((8, D), jnp.float32),
            pltpu.VMEM((8, D), jnp.float32),
        ],
        compiler_params=pltpu.CompilerParams(vmem_limit_bytes=VMEM_LIMIT),
        cost_estimate=LIGHT,
        name="head_loss",
    )(stream, pool, proj, heads, target, whole, legal)


WIDTH = 512
TILE = 16
AXES = ("wide", "narrow")


def grid_sizes():
    return (lax.axis_size("wide") // 2, 2, lax.axis_size("narrow") // 2, 2)


def spot():
    sizes = grid_sizes()
    wide, narrow = (lax.axis_index("wide"), lax.axis_index("narrow"))
    return jnp.stack(
        [wide // sizes[1], wide % sizes[1], narrow // sizes[3], narrow % sizes[3]]
    ).astype(jnp.int32)


def hop(array, axis_of_core, step=1):
    sizes = grid_sizes()
    pairs = []
    for place in itertools.product(*[range(size) for size in sizes]):
        axis = axis_of_core[place[3]]
        other = list(place)
        other[axis] = (place[axis] + step) % sizes[axis]
        source, target = [
            ((z * sizes[1] + y) * sizes[2] + x) * sizes[3] + core for z, y, x, core in (place, other)
        ]
        pairs.append((source, target))
    return lax.ppermute(array, AXES, pairs)


ALONG_Z = (0, 0)
ACROSS = (3, 3)
NEAR = (2, 1)
FAR = (1, 2)


def hbm(number):
    return [pl.BlockSpec(memory_space=pl.ANY)] * number


def in_vmem(number):
    return [pl.BlockSpec(memory_space=pltpu.VMEM)] * number


def in_smem():
    return [pl.BlockSpec(memory_space=pltpu.SMEM)]


def copies(pairs, sems):
    started = [
        pltpu.make_async_copy(source, target, sems.at[index])
        for index, (source, target) in enumerate(pairs)
    ]
    for copy in started:
        copy.start()
    for copy in started:
        copy.wait()


class Part:
    def __init__(self, blocks, rows, lanes):
        self.blocks, self.rows, self.lanes = (blocks, rows, lanes)
        self.across = WIDTH // lanes
        self.travel = blocks * rows // self.across

    def moves(self):
        if self.across > 1:
            deep = self.rows // self.across
            return [(0, part * self.lanes, deep, 0, part * deep) for part in range(self.across)]
        return [(block * self.rows, 0, self.rows, block, 0) for block in range(self.blocks)]

    def pack(self, piece):
        if self.across > 1:
            piece = piece.reshape(self.across, self.rows // self.across, self.lanes)
            return piece.transpose(1, 0, 2).reshape(self.travel, WIDTH)
        return piece.reshape(self.travel, WIDTH)

    def unpack(self, rows):
        if self.across > 1:
            rows = rows.reshape(self.rows // self.across, self.across, self.lanes)
            return rows.transpose(1, 0, 2).reshape(1, self.rows, self.lanes)
        return rows.reshape(self.blocks, self.rows, self.lanes)

    def full(self, depth):
        return (self.blocks, depth, 2, 2, 2, self.rows, self.lanes)


def half_rows(parts):
    total = sum(part.travel for part in parts)
    return -(-total // (2 * TILE)) * TILE


def half_moves(parts):
    cut = half_rows(parts)
    halves = ([], [])
    offset = 0
    for index, part in enumerate(parts):
        for row, lane, rows, block, inner in part.moves():
            row = row + offset
            before = max(0, min(rows, cut - row))
            if before:
                halves[0].append((index, row, lane, before, block, inner))
            if rows - before:
                halves[1].append((index, row + before - cut, lane, rows - before, block, inner + before))
        offset += part.travel
    return halves


def unit(parts, depth):
    return (depth, 2, half_rows(parts), WIDTH)


def pack(parts, pieces):
    rows = jnp.concatenate([part.pack(piece) for part, piece in zip(parts, pieces)])
    return jnp.pad(rows, ((0, 2 * half_rows(parts) - rows.shape[0]), (0, 0)))


def stack_kernel(size, place, *refs):
    pairs = [
        (refs[step], refs[size].at[lax.rem(place[0] - step + size, size)]) for step in range(size)
    ]
    copies(pairs, refs[size + 1])


def stack_z(arrays, place):
    size = len(arrays)
    return pl.pallas_call(
        functools.partial(stack_kernel, size),
        out_shape=jax.ShapeDtypeStruct((size,) + arrays[0].shape, arrays[0].dtype),
        in_specs=in_smem() + hbm(size),
        out_specs=in_vmem(1)[0],
        scratch_shapes=[pltpu.SemaphoreType.DMA((size,))],
        cost_estimate=LIGHT,
        name="stack_z",
    )(place, *arrays)


def assemble_pairs(parts, core, y, x, ins, outs):
    pairs = []
    for other, far, near in itertools.product((0, 1), repeat=3):
        half = core ^ other
        step = [0, 0, 0, 0]
        step[NEAR[half]], step[FAR[half]] = (near, far)
        at_y, at_x = (lax.rem(y + step[1], 2), lax.rem(x + step[2], 2))
        for index, row, lane, rows, block, inner in half_moves(parts)[half]:
            pairs.append(
                (
                    index,
                    ins[other].at[far, near, :, :, pl.ds(row, rows), pl.ds(lane, parts[index].lanes)],
                    outs[index].at[block, :, at_y, at_x, :, pl.ds(inner, rows)],
                )
            )
    return pairs


def deal_copies(parts):
    return 4 * sum(len(moves) for moves in half_moves(parts))


def fetch(parts, tuned, place, sources, weights, sems):
    if not tuned:
        for index, (source, weight) in enumerate(zip(sources, weights)):
            pltpu.make_async_copy(source, weight, sems.at[index]).start()
        return
    for core in (0, 1):

        @pl.when(place[3] == core)
        def _():
            pairs = assemble_pairs(parts, core, place[1], place[2], sources, weights)
            for index, source, target in sorted(pairs, key=lambda pair: pair[0]):
                pltpu.make_async_copy(source, target, sems.at[index]).start()


def weight_shapes(parts, buffers, tuned):
    if tuned:
        return [part.full(buffers[0].shape[2]) for part in parts]
    return [item.shape for item in buffers]


def assemble_kernel(parts, place, *refs):
    outs, sems = (refs[2:-1], refs[-1])
    fetch(parts, True, place, refs[:2], outs, sems)
    for index, out in enumerate(outs):
        pltpu.make_async_copy(out, out, sems.at[index]).wait()


def assemble(parts, buffers, place):
    full = pl.pallas_call(
        functools.partial(assemble_kernel, parts),
        out_shape=[bf16(*shape) for shape in weight_shapes(parts, buffers, True)],
        in_specs=in_smem() + hbm(2),
        out_specs=in_vmem(len(parts)),
        scratch_shapes=[pltpu.SemaphoreType.DMA((len(parts),))],
        compiler_params=pltpu.CompilerParams(vmem_limit_bytes=VMEM_LIMIT),
        cost_estimate=LIGHT,
        name="assemble",
    )(place, *buffers)
    return [merged(item) for item in full]


def merged(array):
    return array.reshape(array.shape[0], -1, array.shape[-1])


def both_cores(own, other, core):
    first = jnp.where(core == 0, own, other)
    second = jnp.where(core == 0, other, own)
    return jnp.stack([first, second])


def together(*trees):
    flat, tree = jax.tree.flatten(trees)
    return jax.tree.unflatten(tree, lax.optimization_barrier(flat))


def start_gather(groups, pieces, place):
    core = place[3]
    packed = [pack(parts, items) for parts, items in zip(groups, pieces)]
    halves = [half_rows(parts) for parts in groups]
    kept = [lax.dynamic_slice_in_dim(rows, core * half, half) for rows, half in zip(packed, halves)]
    sent = [
        lax.dynamic_slice_in_dim(rows, (1 - core) * half, half) for rows, half in zip(packed, halves)
    ]
    got = hop(jnp.concatenate(sent), ACROSS)
    held = []
    offset = 0
    for keep, half in zip(kept, halves):
        held.append(both_cores(keep, got[offset : offset + half], core))
        offset += half
    return held


def gather_hop(stage, item):
    if stage == 0:
        return [item] + [hop(item, ALONG_Z, step) for step in range(1, grid_sizes()[0])]
    return [item, hop(item, (NEAR, FAR, ACROSS)[stage - 1])]


def pipelined_gather(groups, pieces, place, state, arrived):
    count = len(groups)
    held = start_gather(groups, pieces, place)
    for tick in range(count + 3):
        live = [index for index in range(tick - 3, tick + 1) if 0 <= index < count]
        items, state = together([held[index] for index in live], state)
        for index, item in zip(live, items):
            held[index] = gather_hop(tick - index, item)
        if tick >= 3:
            state = arrived(tick - 3, held[tick - 3], state)
        live = [index for index in live if index > tick - 3]
        items, state = together([held[index] for index in live], state)
        for index, item in zip(live, items):
            held[index] = stack_z(item, place) if index == tick else jnp.stack(item)
    return state


def deal_kernel(parts, place, *refs):
    number = len(parts)
    ins, outs, sems = (refs[:number], refs[number:-1], refs[-1])
    to_core, to_far, to_near, own = outs
    y, x = (place[1], place[2])
    for core in (0, 1):

        @pl.when(place[3] == core)
        def _():
            pairs = []
            for other, far, near in itertools.product((0, 1), repeat=3):
                half = core ^ other
                step = [0, 0, 0, 0]
                step[NEAR[half]], step[FAR[half]] = (near, far)
                at_y, at_x = (lax.rem(y + step[1], 2), lax.rem(x + step[2], 2))
                if other:
                    target = to_core.at[far, near]
                elif far:
                    target = to_far.at[near]
                else:
                    target = to_near if near else own
                for index, row, lane, rows, block, inner in half_moves(parts)[half]:
                    pairs.append(
                        (
                            ins[index].at[block, :, at_y, at_x, :, pl.ds(inner, rows)],
                            target.at[:, :, pl.ds(row, rows), pl.ds(lane, parts[index].lanes)],
                        )
                    )
            copies(pairs, sems)


def deal(parts, arrays, place):
    depth = arrays[0].shape[1]
    size = unit(parts, depth)
    return pl.pallas_call(
        functools.partial(deal_kernel, parts),
        out_shape=[
            jax.ShapeDtypeStruct(lead + size, jnp.bfloat16) for lead in ((2, 2), (2,), (), ())
        ],
        in_specs=in_smem() + in_vmem(len(parts)),
        out_specs=hbm(4),
        scratch_shapes=[pltpu.SemaphoreType.DMA((deal_copies(parts),))],
        compiler_params=pltpu.CompilerParams(vmem_limit_bytes=VMEM_LIMIT),
        cost_estimate=LIGHT,
        name="deal",
    )(place, *arrays)


def add_up(*terms):
    total = terms[0].astype(jnp.float32)
    for term in terms[1:]:
        total = total + term.astype(jnp.float32)
    return total


def low_add(*terms):
    return add_up(*terms).astype(jnp.bfloat16)


def scatter_stage(stage, parts, items, place):
    depth = grid_sizes()[0]
    z, core = (place[0], place[3])
    if stage == 0:
        arrays = [array.reshape(part.full(depth)) for part, array in zip(parts, items)]
        to_core, *rest = deal(parts, arrays, place)
        return rest + [hop(to_core, ACROSS)]
    to_far, to_near, own, from_core = items[:4]
    if stage == 1:
        return items + [hop(low_add(to_far, from_core[1]), FAR)]
    from_far = items[4]
    if stage == 2:
        return items + [hop(low_add(to_near, from_core[0, 1], from_far[1]), NEAR)]
    pick = [own, from_core[0, 0], from_far[0], items[5]]

    def mine(at):
        return [lax.dynamic_index_in_dim(item, at, 0, False) for item in pick]

    if stage == 3:
        return items + [
            hop(low_add(*mine(lax.rem(z + step, depth))), ALONG_Z, step) for step in range(1, depth)
        ]
    total = add_up(*mine(z), *items[6:])
    keep = lax.dynamic_index_in_dim(total, core, 0, False)
    other = hop(lax.dynamic_index_in_dim(total, 1 - core, 0, False), ACROSS)
    rows = both_cores(keep, other, core).reshape(-1, WIDTH)
    pieces = []
    offset = 0
    for part in parts:
        pieces.append(part.unpack(rows[offset : offset + part.travel]))
        offset += part.travel
    return pieces


SCATTER_STAGES = 5


def pipelined_scatter(groups, place, state, steps):
    count = len(groups)
    held = [None] * count
    for tick in range(count + SCATTER_STAGES):
        live = [index for index in range(tick - SCATTER_STAGES, tick) if 0 <= index < count]
        items, state = together([held[index] for index in live], state)
        for index, item in zip(live, items):
            held[index] = scatter_stage(tick - 1 - index, groups[index], item, place)
        if tick < count:
            held[tick], state = steps[tick](state)
    return (held, state)


CQL_WEIGHT = 0.05
BETA_ONE = 0.5
BETA_TWO = 0.5
LEARNING_RATE = 0.25
WEIGHT_DECAY = 0.01
PATCH_IN = 256
DPROJ = 512
ACTIONS = 18
ATOMS = 51
GAMES = 4
BLOCKS = 2
STEP = 5
PLAYS = ACTIONS * ATOMS


def average_decay():
    return min(0.99, (1.0 + STEP) / (10.0 + STEP))


def segment_lengths():
    top = [PATCH_IN * D, D * PIX, D * DPROJ, DPROJ * GAMES * PLAYS]
    block = [D * BOT, 9 * BOT * BOT, BOT * D, 2 * (2 * BOT + D)]
    return (top, block)


def cut_points(lengths, devices):
    cuts = []
    offset = 0
    for length in lengths:
        width = length // devices
        cuts.append((offset, width))
        offset += width
    return cuts


def pack_top(flat, cuts):
    patch, pool, proj, heads = [flat[start : start + size] for start, size in cuts]
    patch = patch.reshape(-1, 2, 2, WIDTH).transpose(2, 1, 0, 3).reshape(2, -1, WIDTH)
    pool = jnp.pad(pool.reshape(1, -1, PIX), ((0, 0), (0, 0), (0, ROWS - PIX)))
    heads = jnp.pad(heads.reshape(-1, GAMES, PLAYS), ((0, 0), (0, 0), (0, 2 * WIDTH - PLAYS)))
    heads = heads.reshape(-1, 2 * GAMES, WIDTH).transpose(1, 0, 2)
    return [patch, pool, proj.reshape(1, -1, WIDTH), heads]


def flat_top(patch, pool, proj, heads):
    patch = patch.reshape(2, 2, -1, WIDTH).transpose(2, 1, 0, 3)
    heads = heads.transpose(1, 0, 2).reshape(-1, GAMES, 2 * WIDTH)[:, :, :PLAYS]
    return jnp.concatenate(
        [item.reshape(-1) for item in (patch, pool[:, :, :PIX], proj, heads)]
    )


def pack_block(flat, cuts):
    w_in, w_mid, w_out = [flat[start : start + size] for start, size in cuts[:3]]
    w_out = w_out.reshape(-1, D // BOT, BOT).transpose(1, 0, 2)
    return [w_in.reshape(1, -1, BOT), w_mid.reshape(1, -1, BOT), w_out]


def flat_block(w_in, w_mid, w_out, gains):
    return jnp.concatenate(
        [item.reshape(-1) for item in (w_in, w_mid, w_out.transpose(1, 0, 2), gains)]
    )


def parts_for(devices):
    rows = {"patch": 2 * PATCH_IN, "pool": D, "proj": D, "heads": DPROJ}
    rows |= {"w_in": D, "w_mid": TAPS * BOT, "w_out": BOT, "gains": TILE * devices}
    blocks = {"patch": 2, "heads": 2 * GAMES, "w_out": D // BOT}
    return {
        name: Part(blocks.get(name, 1), count // devices, ROWS if name == "pool" else WIDTH)
        for name, count in rows.items()
    }


def is_tuned(devices):
    parts = parts_for(devices).values()
    whole = all(part.rows // part.across % TILE == 0 for part in parts)
    return whole and lax.axis_size("wide") == 8 and lax.axis_size("narrow") == 4


def plain_gather(piece):
    return lax.all_gather(piece, AXES, axis=1, tiled=True)


def plain_scatter(array):
    return lax.psum_scatter(array, AXES, scatter_dimension=1, tiled=True).astype(jnp.float32)


def total(array):
    if lax.axis_size("wide") != 8 or lax.axis_size("narrow") != 4:
        return lax.psum(array, AXES)
    array = array + hop(array, ACROSS)
    array = array + hop(array, (2, 2))
    array = array + hop(array, (1, 1))
    one, two, three = [hop(array, ALONG_Z, step) for step in (1, 2, 3)]
    return (array + two) + (one + three)


def lamb_parts(params, grads, first, second):
    momentum = BETA_ONE * first + (1.0 - BETA_ONE) * grads
    variance = BETA_TWO * second + (1.0 - BETA_TWO) * grads * grads
    direction = (
        momentum / (1.0 - BETA_ONE**STEP) / (jnp.sqrt(variance / (1.0 - BETA_TWO**STEP)) + 1e-06)
        + WEIGHT_DECAY * params
    )
    return (momentum, variance, direction)


def squares(flat, cuts):
    return jnp.stack(
        [jnp.sum(jnp.square(flat[..., start : start + width]), axis=-1) for start, width in cuts],
        axis=-1,
    )


def spread_ratio(ratio, flat, cuts):
    parts = [
        jnp.broadcast_to(ratio[..., index : index + 1], flat.shape[:-1] + (width,))
        for index, (start, width) in enumerate(cuts)
    ]
    return jnp.concatenate(parts, axis=-1)


def frame_rows(frames):
    count = frames.shape[0]
    return jnp.pad(frames, ((0, 0), (0, ROWS - PIX), (0, 0))).reshape(count * ROWS, PATCH_IN)


def on_device(
    observed,
    following,
    game_ids,
    actions,
    legal_mask,
    rewards,
    discounts,
    done_flags,
    params_top,
    params_blocks,
    first_top,
    first_blocks,
    second_top,
    second_blocks,
    average_top,
    average_blocks,
    target_top,
    target_blocks,
):
    devices = lax.axis_size(AXES)
    frames_all = observed.shape[0] * devices
    top_lengths, block_lengths = segment_lengths()
    top_cuts = cut_points(top_lengths, devices)
    block_cuts = cut_points(block_lengths, devices)
    gain_start, gain_width = block_cuts[3]
    parts = parts_for(devices)
    tuned = is_tuned(devices)
    place = spot()
    shift = shifts()
    spread = spread_pixels(devices)
    weight_parts = jnp.concatenate(
        [squares(params_top, top_cuts), squares(params_blocks, block_cuts).reshape(-1)]
    )

    count = observed.shape[0]
    whole = jnp.concatenate([game_ids[:, None], actions], axis=1)
    whole = jnp.pad(whole, ((0, 8 - count), (0, ROWS - 3)), constant_values=-1)
    legal = jnp.pad(legal_mask, ((0, 8 - count), (0, ROWS - ACTIONS)), constant_values=1)
    keep = discounts * (1.0 - done_flags.astype(jnp.float32))
    real = jnp.pad(jnp.stack([rewards, keep], axis=1), ((0, 8 - count), (0, ROWS - 2)))

    low_blocks = params_blocks.astype(jnp.bfloat16)
    own = {}
    for net, top, blocks in (
        ("target", target_top, target_blocks),
        ("online", params_top.astype(jnp.bfloat16), low_blocks),
    ):
        for name, piece in zip(("patch", "pool", "proj", "heads"), pack_top(top, top_cuts)):
            own[net, name] = piece
        for index in range(BLOCKS):
            for name, piece in zip(("w_in", "w_mid", "w_out"), pack_block(blocks[index], block_cuts)):
                own[net, name, index] = piece
    gain_rows = jnp.concatenate([target_blocks, low_blocks])[:, gain_start:]
    own["gains",] = jnp.pad(
        gain_rows, ((0, TILE - 2 * BLOCKS), (0, WIDTH - gain_width))
    ).reshape(1, TILE, WIDTH)
    block_names = ("w_in", "w_mid", "w_out")

    def part_of(key):
        return parts[key[0] if key[0] in parts else key[1]]

    full = {}

    def block_weight(index, name):
        return merged(full["online", name, index]).reshape(-1, BOT)

    def top_weights(net):
        return (full[net, "pool"][0], full[net, "proj"][0], full[net, "heads"])

    def keep_ends(group, buffers, state):
        arrays = assemble([part_of(key) for key in keys[group]], buffers, place) if tuned else buffers
        full.update(zip(keys[group], arrays))
        if ("gains",) not in keys[group]:
            return state
        gains = full["gains",].reshape(devices, TILE, WIDTH)[:, : 2 * BLOCKS, :gain_width]
        gains = gains.transpose(1, 0, 2).reshape(2 * BLOCKS, -1).astype(jnp.float32)
        return state | {"gains": gains}

    def run_block(net, index, group, buffers, state):
        keep = net == "online"
        row = index + (BLOCKS if keep else 0)
        gain = state["gains"][row : row + 1]
        stream = [state["pixels" if keep else "following"], spread]
        if index:
            stream = [state["stream"]]
        kinds = [part_of(key) for key in keys[group]]
        out, *kept = block_forward(stream, gain, shift, kinds, buffers, place, keep, tuned)
        state = state | {"stream": out}
        if keep:
            start = kept.pop(0) if index == 0 else stream[0]
            full.update(zip([(net, name, index) for name in block_names], kept[-3:]))
            state |= {"kept%d" % index: [start, *kept[:-3]]}
        elif index == BLOCKS - 1:
            state |= {"target": head_target(state.pop("stream"), *top_weights(net), whole, real)}
        return state

    keys, then = ([], [])
    ends = ("pool", "proj", "heads")
    for net in ("target", "online"):
        for index in range(BLOCKS):
            keys.append([(net, name, index) for name in block_names])
            if index == 0:
                keys[-1] = [(net, "patch")] + keys[-1]
            then.append(functools.partial(run_block, net, index))
    keys = [[("gains",)] + [("target", name) for name in ends]] + keys
    keys.append([("online", name) for name in ends])
    then = [keep_ends, *then, keep_ends]

    def arrived(group, buffers, state):
        return then[group](group, buffers, dict(state))

    state = {"following": frame_rows(following), "pixels": frame_rows(observed)}
    pieces = [[own[key] for key in group] for group in keys]
    if tuned:
        groups = [[part_of(key) for key in group] for group in keys]
        state = pipelined_gather(groups, pieces, place, state, arrived)
    else:
        for group, items in enumerate(pieces):
            state = arrived(group, [plain_gather(item) for item in items], state)

    def loss_step(state):
        loss, dheads, dproj, dpool, dstream = head_loss(
            state.pop("stream"), *top_weights("online"), state.pop("target"), whole, legal, frames_all
        )
        state |= {"loss": loss[0, 0], "pool": dpool[None], "grad": dstream}
        return ([dheads, dproj[None]], state)

    def back_out_step(index, state):
        stream, hid_one, hid_two, hid_three, rstd = state["kept%d" % index]
        gain = state["gains"][BLOCKS + index : BLOCKS + index + 1]
        dres, dlow, dw_out, late = back_out(
            state["grad"], stream, hid_two, hid_three, rstd, block_weight(index, "w_out"), gain
        )
        state = state | {"grad": dres, "low": dlow, "late%d" % index: late}
        return (dw_out.reshape(D // BOT, BOT, BOT), state)

    def back_mid_step(index, state):
        stream, hid_one, hid_two, hid_three, rstd = state["kept%d" % index]
        gain = state["gains"][BLOCKS + index : BLOCKS + index + 1]
        dlow, dw_mid, early = back_mid(
            state["low"], hid_one, rstd, block_weight(index, "w_mid"), gain, shift
        )
        return ([dw_mid[None]], state | {"low": dlow, "early%d" % index: early})

    def back_in_step(index, state):
        stream = state.pop("kept%d" % index)[0]
        dw_in, dx = back_in(state["low"], stream, state["grad"], block_weight(index, "w_in"))
        return (dw_in[None], state | {"grad": dx})

    def first_step(state):
        dw_out, state = back_out_step(BLOCKS - 1, dict(state))
        return ([dw_out, state.pop("pool")], state)

    def between_step(index, state):
        dw_in, state = back_in_step(index, dict(state))
        dw_out, state = back_out_step(index - 1, state)
        return ([dw_in, dw_out], state)

    def last_step(state):
        dw_in, state = back_in_step(0, dict(state))
        dpatch = embed_back(state.pop("pixels"), spread, state.pop("grad"))
        dgains = [
            jnp.concatenate([state.pop("early%d" % index), state.pop("late%d" % index)], axis=1)
            for index in range(BLOCKS)
        ]
        dgains = jnp.concatenate(dgains).reshape(BLOCKS, devices, gain_width).transpose(1, 0, 2)
        dgains = jnp.pad(dgains, ((0, 0), (0, TILE - BLOCKS), (0, WIDTH - gain_width)))
        return ([dw_in, dpatch, dgains.reshape(1, -1, WIDTH).astype(jnp.bfloat16)], state)

    keys = [[("heads",), ("proj",)], [("w_out", BLOCKS - 1), ("pool",)]]
    steps = [lambda state: loss_step(dict(state)), first_step]
    for index in reversed(range(BLOCKS)):
        keys.append([("w_mid", index)])
        steps.append(functools.partial(back_mid_step, index))
        keys.append([("w_in", index)])
        keys[-1] += [("w_out", index - 1)] if index else [("patch",), ("gains",)]
        steps.append(functools.partial(between_step, index) if index else last_step)
    mine = {}
    if tuned:
        groups = [[parts[key[0]] for key in group] for group in keys]
        sums, state = pipelined_scatter(groups, place, state, steps)
        for group, items in zip(keys, sums):
            mine.update(zip(group, items))
    else:
        for group, step in zip(keys, steps):
            arrays, state = step(state)
            mine.update(zip(group, [plain_scatter(array) for array in arrays]))
    loss_part = state["loss"]
    grad_top = flat_top(*[mine[name,] for name in ("patch", "pool", "proj", "heads")])
    grad_blocks = jnp.stack(
        [
            flat_block(*[mine[name, index] for name in block_names], mine["gains",][0, index, :gain_width])
            for index in range(BLOCKS)
        ]
    )

    momentum_top, variance_top, direction_top = lamb_parts(
        params_top, grad_top, first_top, second_top
    )
    momentum_blocks, variance_blocks, direction_blocks = lamb_parts(
        params_blocks, grad_blocks, first_blocks, second_blocks
    )
    update_parts = jnp.concatenate(
        [squares(direction_top, top_cuts), squares(direction_blocks, block_cuts).reshape(-1)]
    )
    sums = total(jnp.concatenate([weight_parts, update_parts, loss_part[None]])[None])[0]
    count = weight_parts.shape[0]
    weight_sq, update_sq, loss_total = (sums[:count], sums[count : 2 * count], sums[2 * count])
    weight_norm = jnp.sqrt(weight_sq)
    update_norm = jnp.sqrt(update_sq)
    ratio = weight_norm / (update_norm + 1e-06)
    scale_top = spread_ratio(ratio[:4], params_top, top_cuts)
    scale_blocks = spread_ratio(ratio[4:].reshape(BLOCKS, 4), params_blocks, block_cuts)
    updated_top = params_top - LEARNING_RATE * scale_top * direction_top
    updated_blocks = params_blocks - LEARNING_RATE * scale_blocks * direction_blocks
    decay = average_decay()
    averaged_top = decay * average_top + (1.0 - decay) * updated_top
    averaged_blocks = decay * average_blocks + (1.0 - decay) * updated_blocks
    matrix_norms = jnp.stack([weight_norm, update_norm])
    gain_grads = grad_blocks[:, gain_start : gain_start + gain_width]
    return (
        loss_total,
        matrix_norms,
        updated_top,
        updated_top.astype(jnp.bfloat16),
        momentum_top,
        variance_top,
        averaged_top,
        updated_blocks,
        updated_blocks.astype(jnp.bfloat16),
        momentum_blocks,
        variance_blocks,
        averaged_blocks,
        gain_grads,
    )


def solution(mesh):
    one = P(AXES)
    flat = P(None, AXES)
    return jax.shard_map(
        on_device,
        mesh=mesh,
        in_specs=(P(AXES, None, None),) * 2
        + (one, P(AXES, None), P(AXES, None))
        + (one,) * 3
        + (one, flat) * 5,
        out_specs=(P(), P()) + (one,) * 5 + (flat,) * 6,
        check_vma=False,
    )
```

```python
import functools
import itertools

import jax
import jax.numpy as jnp
from jax import lax
from jax.experimental import pallas as pl
from jax.experimental.pallas import tpu as pltpu
from jax.sharding import PartitionSpec as P

D = 2048
BOT = 512
GROUPS = 32
SIDE = 11
PIX = 121
TAPS = 9

ROWS = 128
LANES = 256
VMEM_LIMIT = 60 * 1024 * 1024
LIGHT = pl.CostEstimate(flops=1024, bytes_accessed=1024, transcendentals=0)


def shifts():
    pixel = jnp.arange(ROWS)
    row, col = (pixel // SIDE, pixel % SIDE)
    mats = []
    for tap in range(TAPS):
        at_row, at_col = (row + tap // 3 - 1, col + tap % 3 - 1)
        inside = (at_row >= 0) & (at_row < SIDE) & (at_col >= 0) & (at_col < SIDE) & (pixel < PIX)
        mats.append((inside[:, None] & (pixel[None, :] == (at_row * SIDE + at_col)[:, None])))
    return jnp.concatenate(mats, axis=0).astype(jnp.bfloat16)


def dot(left, right):
    return jnp.dot(left, right, preferred_element_type=jnp.float32)


def dot_rows(left, right):
    return lax.dot_general(
        left, right, (((0,), (0,)), ((), ())), preferred_element_type=jnp.float32
    )


def dot_lanes(left, right):
    return lax.dot_general(
        left, right, (((1,), (1,)), ((), ())), preferred_element_type=jnp.float32
    )


def each_chunk(count, chans, body, unroll=1):
    per = chans // LANES

    def step(index, carry):
        frame = index // per
        rows = pl.ds(pl.multiple_of(frame * ROWS, ROWS), ROWS)
        lanes = pl.ds(pl.multiple_of((index % per) * LANES, LANES), LANES)
        body(pl.ds(frame, 1), rows, lanes)
        return carry

    lax.fori_loop(0, count * per, step, 0, unroll=unroll)


def real_rows():
    return lax.broadcasted_iota(jnp.int32, (ROWS, LANES), 0) < PIX


def group_mean(sums):
    chans = sums.shape[1]
    width = chans // GROUPS
    lane = lax.broadcasted_iota(jnp.int32, sums.shape, 1)
    step = 1
    while step < width:
        ahead = pltpu.roll(sums, chans - step, 1)
        behind = pltpu.roll(sums, step, 1)
        sums = sums + jnp.where((lane & step) == 0, ahead, behind)
        step *= 2
    return sums * (1.0 / (PIX * width))


def silu(value):
    return value / (1.0 + jnp.exp(-value))


def silu_slope(value):
    gate = 1.0 / (1.0 + jnp.exp(-value))
    return gate * (1.0 + value * (1.0 - gate))


def normalise(count, chans, hid, sums, rstd, rstd_at):
    whole = pl.ds(0, chans)
    sums[:, whole] = jnp.zeros((sums.shape[0], chans), jnp.float32)

    def add(frame, rows, lanes):
        sums[frame, lanes] = jnp.sum(hid[rows, lanes], axis=0, keepdims=True)

    each_chunk(count, chans, add, unroll=2)
    sums[:, whole] = group_mean(sums[:, whole])

    def center(frame, rows, lanes):
        value = jnp.where(real_rows(), hid[rows, lanes] - sums[frame, lanes], 0.0)
        hid[rows, lanes] = value
        sums[frame, lanes] = jnp.sum(value * value, axis=0, keepdims=True)

    each_chunk(count, chans, center, unroll=2)
    at = pl.ds(rstd_at, chans)
    rstd[:, at] = lax.rsqrt(group_mean(sums[:, whole]) + 1e-05)


def forward_kernel(count, keep, parts, skip, tuned, *refs):
    refs = list(refs)
    number = len(parts) - skip
    first = number > 3

    def take(number):
        taken = refs[:number]
        del refs[:number]
        return taken

    (place,) = take(1)
    x = take(2 if first else 1)
    gains, shift = take(2)
    sources = take(4 if tuned else len(parts))
    (out,) = take(1)
    if keep:
        if first:
            (start,) = take(1)
        hid_one, hid_two, hid_three, rstd = take(4)
        kept_weights = take(3)
    weights = take(number)
    sems, back_sems, low, act, cols, sums = take(6)
    if not keep:
        hid_one, hid_two, hid_three, rstd = take(4)
        if first:
            (start,) = take(1)
    fetch(parts, tuned, place, sources, dict(enumerate(weights, skip)), sems)

    def arrived(index):
        weight = weights[index]
        pltpu.make_async_copy(weight, weight, sems.at[len(parts) + index]).wait()
        if keep and index >= -3:
            pltpu.make_async_copy(weight, kept_weights[index], back_sems.at[3 + index]).start()
        return weight

    def whole(value):
        return value.reshape(-1, value.shape[-1])

    if first:
        pixels, spread = x
        x = start
        patch = arrived(-4)
        for half in range(2):
            wide = dot(pixels[...], spread[half]).astype(jnp.bfloat16)
            for block in range(2):
                lanes = pl.ds((2 * half + block) * WIDTH, WIDTH)
                x[:, lanes] = dot(wide, whole(patch[block]))
    else:
        (x,) = x

    def cast(frame, rows, lanes):
        low[rows, lanes] = x[rows, lanes].astype(jnp.bfloat16)

    def activate(hid, at, offset):
        def body(frame, rows, lanes):
            gain = gains[:, pl.ds(offset + lanes.start, LANES)]
            bias = gains[:, pl.ds(offset + BOT + lanes.start, LANES)]
            value = hid[rows, lanes] * rstd[frame, pl.ds(at + lanes.start, LANES)]
            hid[rows, lanes] = value
            value = jnp.where(real_rows(), silu(value * gain + bias), 0.0)
            act[rows, lanes] = value.astype(jnp.bfloat16)

        return body

    each_chunk(count, D, cast)
    hid_one[...] = dot(low[...], whole(arrived(-3)[...]))
    normalise(count, BOT, hid_one, sums, rstd, 0)
    each_chunk(count, BOT, activate(hid_one, 0, 0))
    for frame in range(count):
        rows = pl.ds(frame * ROWS, ROWS)
        for tap in range(TAPS):
            picked = dot(shift[pl.ds(tap * ROWS, ROWS), :], act[rows, :])
            cols[rows, pl.ds(tap * BOT, BOT)] = picked.astype(jnp.bfloat16)
    hid_two[...] = dot(cols[...], whole(arrived(-2)[...]))
    normalise(count, BOT, hid_two, sums, rstd, BOT)
    each_chunk(count, BOT, activate(hid_two, BOT, 2 * BOT))
    w_out = arrived(-1)
    for part in range(D // BOT):
        hid_three[:, pl.ds(part * BOT, BOT)] = dot(act[...], whole(w_out[part]))
    normalise(count, D, hid_three, sums, rstd, 2 * BOT)

    def finish(frame, rows, lanes):
        gain = gains[:, pl.ds(4 * BOT + lanes.start, LANES)]
        bias = gains[:, pl.ds(4 * BOT + D + lanes.start, LANES)]
        value = hid_three[rows, lanes] * rstd[frame, pl.ds(2 * BOT + lanes.start, LANES)]
        if keep:
            hid_three[rows, lanes] = value
        value = silu(x[rows, lanes] + value * gain + bias)
        out[rows, lanes] = jnp.where(real_rows(), value, 0.0)

    each_chunk(count, D, finish)
    if keep:
        for index in (-3, -2, -1):
            pltpu.make_async_copy(weights[index], kept_weights[index], back_sems.at[3 + index]).wait()


def f32(*shape):
    return jax.ShapeDtypeStruct(shape, jnp.float32)


def bf16(*shape):
    return jax.ShapeDtypeStruct(shape, jnp.bfloat16)


def stat_rows(count):
    return -(-count // 8) * 8


def block_forward(stream, gains, shift, parts, skip, buffers, place, keep, tuned):
    first = len(parts) - skip > 3
    rows = stream[0].shape[0]
    count = rows // ROWS
    stats = stat_rows(count)
    kept = [
        ((rows, BOT), jnp.float32),
        ((rows, BOT), jnp.float32),
        ((rows, D), jnp.float32),
        ((stats, 2 * BOT + D), jnp.float32),
    ]
    start = [((rows, D), jnp.float32)] if first else []
    weights = weight_shapes(parts, buffers, tuned)[skip:]
    out_shape = [f32(rows, D)]
    out_specs = in_vmem(1)
    scratch = [pltpu.VMEM(shape, jnp.bfloat16) for shape in weights]
    scratch += [
        pltpu.SemaphoreType.DMA((len(parts),)),
        pltpu.SemaphoreType.DMA((3,)),
        pltpu.VMEM((rows, D), jnp.bfloat16),
        pltpu.VMEM((rows, BOT), jnp.bfloat16),
        pltpu.VMEM((rows, TAPS * BOT), jnp.bfloat16),
        pltpu.VMEM((stats, D), jnp.float32),
    ]
    if keep:
        out_shape += [jax.ShapeDtypeStruct(*item) for item in start + kept]
        out_shape += [jax.ShapeDtypeStruct(shape, jnp.bfloat16) for shape in weights[-3:]]
        out_specs += in_vmem(len(start + kept)) + hbm(3)
    else:
        scratch += [pltpu.VMEM(*item) for item in kept + start]
    return pl.pallas_call(
        functools.partial(forward_kernel, count, keep, parts, skip, tuned),
        out_shape=out_shape,
        in_specs=in_smem() + in_vmem(len(stream) + 2) + hbm(len(buffers)),
        out_specs=out_specs,
        scratch_shapes=scratch,
        compiler_params=pltpu.CompilerParams(vmem_limit_bytes=VMEM_LIMIT),
        cost_estimate=LIGHT,
        name="block_forward",
    )(place, *stream, gains, shift, *buffers)


def norm_back(count, chans, slope, hid, sums, more, rstd, rstd_at, gain, grad_gain, grad_bias, store):
    whole = pl.ds(0, chans)
    sums[:, whole] = jnp.zeros((sums.shape[0], chans), jnp.float32)
    more[:, whole] = jnp.zeros((sums.shape[0], chans), jnp.float32)

    def add(frame, rows, lanes):
        value = slope(frame, rows, lanes)
        sums[frame, lanes] = jnp.sum(value, axis=0, keepdims=True)
        more[frame, lanes] = jnp.sum(value * hid[rows, lanes], axis=0, keepdims=True)

    each_chunk(count, chans, add)
    grad_bias[...] = jnp.sum(sums[:, whole], axis=0, keepdims=True)
    grad_gain[...] = jnp.sum(more[:, whole], axis=0, keepdims=True)
    sums[:, whole] = group_mean(sums[:, whole] * gain[...])
    more[:, whole] = group_mean(more[:, whole] * gain[...])

    def spread(frame, rows, lanes):
        store(
            rows,
            lanes,
            lambda value: jnp.where(
                real_rows(),
                rstd[frame, pl.ds(rstd_at + lanes.start, LANES)]
                * (value * gain[:, lanes] - sums[frame, lanes] - hid[rows, lanes] * more[frame, lanes]),
                0.0,
            ).astype(jnp.bfloat16),
        )

    each_chunk(count, chans, spread)


def back_out_body(count, grad, x, hid_two, hid_three, rstd, w_out, gains, dres, dlow, dgains, scratch, dw_out):
    third, act, dact, sums, more = scratch
    gain_three, bias_three = (gains.at[:, pl.ds(4 * BOT, D)], gains.at[:, pl.ds(4 * BOT + D, D)])

    def slope_three(frame, rows, lanes):
        value = x[rows, lanes] + hid_three[rows, lanes] * gain_three[:, lanes] + bias_three[:, lanes]
        value = jnp.where(real_rows(), grad[rows, lanes] * silu_slope(value), 0.0)
        dres[rows, lanes] = value
        return value

    def store_three(rows, lanes, back):
        third[rows, lanes] = back(dres[rows, lanes])

    norm_back(
        count, D, slope_three, hid_three, sums, more, rstd, 2 * BOT, gain_three,
        dgains.at[:, pl.ds(2 * BOT, D)], dgains.at[:, pl.ds(2 * BOT + D, D)], store_three,
    )
    total = None
    for part in range(D // BOT):
        lanes = pl.ds(part * BOT, BOT)
        term = dot_lanes(third[:, lanes], w_out[lanes, :])
        total = term if total is None else total + term
    dact[...] = total
    gain_two, bias_two = (gains.at[:, pl.ds(2 * BOT, BOT)], gains.at[:, pl.ds(3 * BOT, BOT)])

    def slope_two(frame, rows, lanes):
        value = hid_two[rows, lanes] * gain_two[:, lanes] + bias_two[:, lanes]
        gate = 1.0 / (1.0 + jnp.exp(-value))
        act[rows, lanes] = jnp.where(real_rows(), value * gate, 0.0).astype(jnp.bfloat16)
        value = dact[rows, lanes] * (gate * (1.0 + value * (1.0 - gate)))
        value = jnp.where(real_rows(), value, 0.0)
        dact[rows, lanes] = value
        return value

    def store_two(rows, lanes, back):
        dlow[rows, lanes] = back(dact[rows, lanes])

    norm_back(
        count, BOT, slope_two, hid_two, sums, more, rstd, BOT, gain_two,
        dgains.at[:, pl.ds(0, BOT)], dgains.at[:, pl.ds(BOT, BOT)], store_two,
    )
    for part in range(D // BOT):
        lanes = pl.ds(part * BOT, BOT)
        dw_out[part] = dot_rows(act[...], third[:, lanes]).astype(jnp.bfloat16)


def out_scratch(rows):
    stats = stat_rows(rows // ROWS)
    return [
        pltpu.VMEM((rows, D), jnp.bfloat16),
        pltpu.VMEM((rows, BOT), jnp.bfloat16),
        pltpu.VMEM((rows, BOT), jnp.float32),
        pltpu.VMEM((stats, D), jnp.float32),
        pltpu.VMEM((stats, D), jnp.float32),
    ]


def back_mid_body(count, grad, hid_one, rstd, w_mid, gains, shift, dlow, dgains, scratch, dw_mid):
    act, cols, dact, sums, more = scratch
    gain_one, bias_one = (gains.at[:, pl.ds(0, BOT)], gains.at[:, pl.ds(BOT, BOT)])
    for frame in range(count):
        rows = pl.ds(frame * ROWS, ROWS)
        for tap in range(TAPS):
            picked = dot(shift[pl.ds((TAPS - 1 - tap) * ROWS, ROWS), :], grad[rows, :])
            cols[rows, pl.ds(tap * BOT, BOT)] = picked.astype(jnp.bfloat16)
    total = None
    for tap in range(TAPS):
        lanes = pl.ds(tap * BOT, BOT)
        term = dot_lanes(cols[:, lanes], w_mid[lanes, :])
        total = term if total is None else total + term
    dact[...] = total

    def slope_one(frame, rows, lanes):
        value = hid_one[rows, lanes] * gain_one[:, lanes] + bias_one[:, lanes]
        gate = 1.0 / (1.0 + jnp.exp(-value))
        act[rows, lanes] = jnp.where(real_rows(), value * gate, 0.0).astype(jnp.bfloat16)
        value = dact[rows, lanes] * (gate * (1.0 + value * (1.0 - gate)))
        value = jnp.where(real_rows(), value, 0.0)
        dact[rows, lanes] = value
        return value

    def store_one(rows, lanes, back):
        dlow[rows, lanes] = back(dact[rows, lanes])

    norm_back(
        count, BOT, slope_one, hid_one, sums, more, rstd, 0, gain_one,
        dgains.at[:, pl.ds(0, BOT)], dgains.at[:, pl.ds(BOT, BOT)], store_one,
    )
    for tap in range(TAPS):
        lanes = pl.ds(tap * BOT, BOT)
        dw_mid[0, lanes, :] = dot_rows(act[...], cols[:, lanes]).astype(jnp.bfloat16)


def back_in_body(count, grad, x, dres, w_in, dx, low, dw_in):
    def cast(frame, rows, lanes):
        low[rows, lanes] = x[rows, lanes].astype(jnp.bfloat16)

    each_chunk(count, D, cast)
    for part in range(D // BOT):
        lanes = pl.ds(part * BOT, BOT)
        dx[:, lanes] = dres[:, lanes] + dot_lanes(grad[...], w_in[lanes, :])
        dw_in[0, lanes, :] = dot_rows(low[:, lanes], grad[...]).astype(jnp.bfloat16)


def back_kernel(body, parts, tuned, counts, *refs):
    place, refs = (refs[0], list(refs[1:]))
    groups = []
    for number in (*counts[:2], len(dealt_shapes(parts, tuned)), len(parts), 1, counts[2]):
        groups.append(refs[:number])
        refs = refs[number:]
    ins, outs, dealt, made, sems, scratch = groups

    def done(index):
        start_deal(parts, tuned, place, index, made, dealt, sems[0])

    body(ins, outs, made, scratch, done)
    for index, array in enumerate(made):
        pltpu.make_async_copy(array, array, sems[0].at[index]).wait()


def back_call(name, body, ins, out_shape, scratch, parts, tuned, place):
    dealt = dealt_shapes(parts, tuned)
    counts = (len(ins), len(out_shape), len(scratch))
    outs = pl.pallas_call(
        functools.partial(back_kernel, body, parts, tuned, counts),
        out_shape=out_shape + [bf16(*shape) for shape in dealt],
        in_specs=in_smem() + in_vmem(len(ins)),
        out_specs=in_vmem(len(out_shape)) + hbm(len(dealt)),
        scratch_shapes=[pltpu.VMEM(whole_shape(part), jnp.bfloat16) for part in parts]
        + [pltpu.SemaphoreType.DMA((len(parts),))]
        + scratch,
        compiler_params=pltpu.CompilerParams(vmem_limit_bytes=VMEM_LIMIT),
        cost_estimate=LIGHT,
        name=name,
    )(place, *ins)
    return (list(outs[: len(out_shape)]), list(outs[len(out_shape) :]))


def back_out(grad, stream, hid_two, hid_three, rstd, w_out, gains, parts, tuned, place):
    rows = stream.shape[0]

    def body(ins, outs, made, scratch, done):
        back_out_body(rows // ROWS, *ins, *outs, scratch, made[0])
        done(0)

    ins = [grad, stream, hid_two, hid_three, rstd, w_out, gains]
    out_shape = [f32(rows, D), bf16(rows, BOT), f32(1, 2 * BOT + 2 * D)]
    return back_call("back_out", body, ins, out_shape, out_scratch(rows), parts, tuned, place)


def back_mid(grad, hid_one, rstd, w_mid, gains, shift, parts, tuned, place):
    rows = grad.shape[0]
    stats = stat_rows(rows // ROWS)

    def body(ins, outs, made, scratch, done):
        back_mid_body(rows // ROWS, *ins, *outs, scratch, made[0])
        done(0)

    scratch = [
        pltpu.VMEM((rows, BOT), jnp.bfloat16),
        pltpu.VMEM((rows, TAPS * BOT), jnp.bfloat16),
        pltpu.VMEM((rows, BOT), jnp.float32),
        pltpu.VMEM((stats, BOT), jnp.float32),
        pltpu.VMEM((stats, BOT), jnp.float32),
    ]
    ins = [grad, hid_one, rstd, w_mid, gains, shift]
    out_shape = [bf16(rows, BOT), f32(1, 2 * BOT)]
    return back_call("back_mid", body, ins, out_shape, scratch, parts, tuned, place)


def back_between(grad, stream, dres, w_in, later, parts, tuned, place):
    rows = stream.shape[0]

    def body(ins, outs, made, scratch, done):
        dx, low, *rest = scratch
        back_in_body(rows // ROWS, *ins[:4], dx, low, made[0])
        done(0)
        back_out_body(rows // ROWS, dx, *ins[4:], *outs, rest, made[1])
        done(1)

    scratch = [pltpu.VMEM((rows, D), jnp.float32), pltpu.VMEM((rows, D), jnp.bfloat16)]
    scratch += out_scratch(rows)
    ins = [grad, stream, dres, w_in, *later]
    out_shape = [f32(rows, D), bf16(rows, BOT), f32(1, 2 * BOT + 2 * D)]
    return back_call("back_between", body, ins, out_shape, scratch, parts, tuned, place)


def back_first(grad, stream, dres, w_in, pixels, spread, dgains, parts, tuned, place):
    rows = stream.shape[0]

    def body(ins, outs, made, scratch, done):
        dx, low = scratch
        made[2][...] = ins[6][...]
        done(2)
        back_in_body(rows // ROWS, *ins[:4], dx, low, made[0])
        done(0)
        wide = [dot(ins[4][...], ins[5][half]).astype(jnp.bfloat16) for half in range(2)]
        for block in range(2):
            total = None
            for half in range(2):
                lanes = pl.ds((2 * half + block) * WIDTH, WIDTH)
                term = dot_rows(wide[half], dx[:, lanes].astype(jnp.bfloat16))
                total = term if total is None else total + term
            made[1][block] = total.astype(jnp.bfloat16)
        done(1)

    scratch = [pltpu.VMEM((rows, D), jnp.float32), pltpu.VMEM((rows, D), jnp.bfloat16)]
    ins = [grad, stream, dres, w_in, pixels, spread, dgains]
    return back_call("back_first", body, ins, [], scratch, parts, tuned, place)[1]


def spread_pixels(devices):
    rows = PATCH_IN // devices
    value = jnp.arange(PATCH_IN)
    at = value // rows * 2 * rows + value % rows
    return jnp.stack(
        [jnp.arange(2 * PATCH_IN)[None, :] == (at + half * rows)[:, None] for half in range(2)]
    ).astype(jnp.bfloat16)


def head_forward(count, stream, pool, proj, heads, games, pool_t, pooled):
    for part in range(D // ROWS):
        lanes = pl.ds(part * ROWS, ROWS)
        pool_t[:, lanes] = pool[lanes, :].astype(jnp.float32).T
    pooled[...] = jnp.zeros_like(pooled)

    def weigh(frame, rows, lanes):
        value = stream[rows, lanes].astype(jnp.bfloat16).astype(jnp.float32)
        pooled[frame, lanes] = jnp.sum(value * pool_t[:, lanes], axis=0, keepdims=True)

    each_chunk(count, D, weigh)
    before = dot(pooled[...].astype(jnp.bfloat16), proj[...])
    hidden = silu(before).astype(jnp.bfloat16)
    scores = None
    for game in range(GAMES):
        pair = [dot(hidden, heads[2 * game + half]) for half in range(2)]
        term = jnp.where(games == game, jnp.concatenate(pair, axis=1), 0.0)
        scores = term if scores is None else scores + term
    return ([pick_atoms(scores, action) for action in range(ACTIONS)], before, hidden)


def atom_lanes():
    return lax.broadcasted_iota(jnp.int32, (8, ROWS), 1)


def pick_atoms(scores, action):
    offset = action * ATOMS
    moved = pltpu.roll(scores, 2 * WIDTH - offset, 1) if offset else scores
    return jnp.where(atom_lanes() < ATOMS, moved[:, :ROWS], -1e30)


def support_lanes():
    return -10.0 + 20.0 / (ATOMS - 1) * atom_lanes().astype(jnp.float32)


def lane_sum(value):
    return jnp.sum(value, axis=1, keepdims=True)


def target_kernel(count, stream, pool, proj, heads, whole, real, out, pool_t, pooled):
    logits, _, _ = head_forward(
        count, stream, pool, proj, heads, whole[:, 0:1], pool_t, pooled
    )
    chosen = None
    for action in range(ACTIONS):
        term = jnp.where(whole[:, 2:3] == action, logits[action], 0.0)
        chosen = term if chosen is None else chosen + term
    power = jnp.exp(chosen - jnp.max(chosen, axis=1, keepdims=True))
    probs = power / lane_sum(power)
    atoms = support_lanes()
    spacing = 20.0 / (ATOMS - 1)
    moved = jnp.clip(real[:, 0:1] + real[:, 1:2] * atoms, -10.0, 10.0)
    total = jnp.zeros_like(probs)
    for atom in range(ATOMS):
        near = 1.0 - jnp.abs(moved[:, atom : atom + 1] - atoms) / spacing
        total = total + probs[:, atom : atom + 1] * jnp.clip(near, 0.0, 1.0)
    inside = (atom_lanes() < ATOMS) & (lax.broadcasted_iota(jnp.int32, total.shape, 0) < count)
    out[...] = jnp.where(inside, total, 0.0)


def head_target(stream, pool, proj, heads, whole, real):
    count = stream.shape[0] // ROWS
    return pl.pallas_call(
        functools.partial(target_kernel, count),
        out_shape=f32(8, ROWS),
        in_specs=in_vmem(6),
        out_specs=in_vmem(1)[0],
        scratch_shapes=[pltpu.VMEM((ROWS, D), jnp.float32), pltpu.VMEM((8, D), jnp.float32)],
        compiler_params=pltpu.CompilerParams(vmem_limit_bytes=VMEM_LIMIT),
        cost_estimate=LIGHT,
        name="head_target",
    )(stream, pool, proj, heads, whole, real)


def loss_body(count, frames_all, ins, outs, made, scratch, done):
    stream, pool, proj, heads, target, whole, legal = ins
    loss, dstream = outs
    dheads, dproj, dpool = made
    pool_t, pooled, dpooled = scratch
    games, taken = (whole[:, 0:1], whole[:, 1:2])
    logits, before, hidden = head_forward(count, stream, pool, proj, heads, games, pool_t, pooled)
    atoms = support_lanes()
    inside = atom_lanes() < ATOMS
    logps, probs, values = ([], [], [])
    for value in logits:
        value = value - jnp.max(value, axis=1, keepdims=True)
        power = jnp.where(inside, jnp.exp(value), 0.0)
        mass = lane_sum(power)
        logps.append(value - jnp.log(mass))
        probs.append(power / mass)
        values.append(lane_sum(probs[-1] * atoms))
    masked = [
        jnp.where(legal[:, action : action + 1] > 0, values[action], -1e30)
        for action in range(ACTIONS)
    ]
    largest = functools.reduce(jnp.maximum, masked)
    powers = [jnp.exp(value - largest) for value in masked]
    mass = sum(powers[1:], powers[0])
    goal = target[...]
    goal_mass = lane_sum(goal)
    cross = taken_value = 0.0
    real = lax.broadcasted_iota(jnp.int32, (8, 1), 0) < count
    scale = jnp.where(real, 1.0 / frames_all, 0.0)
    spread = jnp.zeros((8, 2 * WIDTH), jnp.float32)
    for action in range(ACTIONS):
        here = jnp.where(taken == action, 1.0, 0.0)
        cross = cross - here * lane_sum(jnp.where(inside, goal * logps[action], 0.0))
        taken_value = taken_value + here * values[action]
        grad = here * (probs[action] * goal_mass - goal)
        pull = CQL_WEIGHT * (powers[action] / mass - here)
        grad = grad + pull * probs[action] * (atoms - values[action])
        grad = jnp.where(inside, grad * scale, 0.0)
        grad = jnp.concatenate([grad, jnp.zeros((8, 2 * WIDTH - ROWS), jnp.float32)], axis=1)
        offset = action * ATOMS
        spread = spread + (pltpu.roll(grad, offset, 1) if offset else grad)
    losses = cross + CQL_WEIGHT * (jnp.log(mass) + largest - taken_value)
    loss[...] = jnp.sum(jnp.where(real, losses, 0.0), axis=0, keepdims=True)
    dhidden = None
    for game in range(GAMES):
        mine = jnp.where(games == game, spread, 0.0).astype(jnp.bfloat16)
        for half in range(2):
            part = mine[:, half * WIDTH : (half + 1) * WIDTH]
            dheads[2 * game + half] = dot_rows(hidden, part).astype(jnp.bfloat16)
            term = dot_lanes(part, heads[2 * game + half])
            dhidden = term if dhidden is None else dhidden + term
    done(0)
    dbefore = (silu_slope(before) * dhidden).astype(jnp.bfloat16)
    dproj[0] = dot_rows(pooled[...].astype(jnp.bfloat16), dbefore).astype(jnp.bfloat16)
    done(1)
    dpooled[...] = dot_lanes(dbefore, proj[...]).astype(jnp.bfloat16).astype(jnp.float32)

    def push(frame, rows, lanes):
        dstream[rows, lanes] = dpooled[frame, lanes] * pool_t[:, lanes]

    each_chunk(count, D, push)

    def gather_pool(part, carry):
        lanes = pl.ds(pl.multiple_of(part * ROWS, ROWS), ROWS)
        total = None
        for frame in range(count):
            value = stream[pl.ds(frame * ROWS, ROWS), lanes].astype(jnp.bfloat16)
            term = value.astype(jnp.float32) * dpooled[pl.ds(frame, 1), lanes]
            total = term if total is None else total + term
        dpool[0, lanes, :] = total.T.astype(jnp.bfloat16)
        return carry

    lax.fori_loop(0, D // ROWS, gather_pool, 0)
    done(2)


def head_loss(stream, pool, proj, heads, target, whole, legal, frames_all, parts, tuned, place):
    rows = stream.shape[0]
    scratch = [
        pltpu.VMEM((ROWS, D), jnp.float32),
        pltpu.VMEM((8, D), jnp.float32),
        pltpu.VMEM((8, D), jnp.float32),
    ]
    ins = [stream, pool, proj, heads, target, whole, legal]
    body = functools.partial(loss_body, rows // ROWS, frames_all)
    return back_call("head_loss", body, ins, [f32(1, 1), f32(rows, D)], scratch, parts, tuned, place)


WIDTH = 512
TILE = 16
AXES = ("wide", "narrow")


def grid_sizes():
    return (lax.axis_size("wide") // 2, 2, lax.axis_size("narrow") // 2, 2)


def spot():
    sizes = grid_sizes()
    wide, narrow = (lax.axis_index("wide"), lax.axis_index("narrow"))
    return jnp.stack(
        [wide // sizes[1], wide % sizes[1], narrow // sizes[3], narrow % sizes[3]]
    ).astype(jnp.int32)


def hop(array, axis_of_core, step=1):
    sizes = grid_sizes()
    pairs = []
    for place in itertools.product(*[range(size) for size in sizes]):
        axis = axis_of_core[place[3]]
        other = list(place)
        other[axis] = (place[axis] + step) % sizes[axis]
        source, target = [
            ((z * sizes[1] + y) * sizes[2] + x) * sizes[3] + core for z, y, x, core in (place, other)
        ]
        pairs.append((source, target))
    return lax.ppermute(array, AXES, pairs)


ALONG_Z = (0, 0)
ACROSS = (3, 3)
NEAR = (2, 1)
FAR = (1, 2)


def hbm(number):
    return [pl.BlockSpec(memory_space=pl.ANY)] * number


def in_vmem(number):
    return [pl.BlockSpec(memory_space=pltpu.VMEM)] * number


def in_smem():
    return [pl.BlockSpec(memory_space=pltpu.SMEM)]


def copies(pairs, sems):
    started = [
        pltpu.make_async_copy(source, target, sems.at[index])
        for index, (source, target) in enumerate(pairs)
    ]
    for copy in started:
        copy.start()
    for copy in started:
        copy.wait()


class Part:
    def __init__(self, blocks, rows, lanes):
        self.blocks, self.rows, self.lanes = (blocks, rows, lanes)
        self.across = WIDTH // lanes
        self.travel = blocks * rows // self.across

    def moves(self):
        if self.across > 1:
            deep = self.rows // self.across
            return [(0, part * self.lanes, deep, 0, part * deep) for part in range(self.across)]
        return [(block * self.rows, 0, self.rows, block, 0) for block in range(self.blocks)]

    def pack(self, piece):
        if self.across > 1:
            piece = piece.reshape(self.across, self.rows // self.across, self.lanes)
            return piece.transpose(1, 0, 2).reshape(self.travel, WIDTH)
        return piece.reshape(self.travel, WIDTH)

    def unpack(self, rows):
        if self.across > 1:
            rows = rows.reshape(self.rows // self.across, self.across, self.lanes)
            return rows.transpose(1, 0, 2).reshape(1, self.rows, self.lanes)
        return rows.reshape(self.blocks, self.rows, self.lanes)

    def full(self, depth):
        return (self.blocks, depth, 2, 2, 2, self.rows, self.lanes)


def half_rows(parts):
    total = sum(part.travel for part in parts)
    return -(-total // (2 * TILE)) * TILE


def half_moves(parts):
    cut = half_rows(parts)
    halves = ([], [])
    offset = 0
    for index, part in enumerate(parts):
        for row, lane, rows, block, inner in part.moves():
            row = row + offset
            before = max(0, min(rows, cut - row))
            if before:
                halves[0].append((index, row, lane, before, block, inner))
            if rows - before:
                halves[1].append((index, row + before - cut, lane, rows - before, block, inner + before))
        offset += part.travel
    return halves


def unit(parts, depth):
    return (depth, 2, half_rows(parts), WIDTH)


def pack(parts, pieces):
    rows = jnp.concatenate([part.pack(piece) for part, piece in zip(parts, pieces)])
    return jnp.pad(rows, ((0, 2 * half_rows(parts) - rows.shape[0]), (0, 0)))


def stack_kernel(size, place, *refs):
    pairs = [
        (refs[step], refs[size].at[lax.rem(place[0] - step + size, size)]) for step in range(size)
    ]
    copies(pairs, refs[size + 1])


def stack_z(arrays, place):
    size = len(arrays)
    return pl.pallas_call(
        functools.partial(stack_kernel, size),
        out_shape=jax.ShapeDtypeStruct((size,) + arrays[0].shape, arrays[0].dtype),
        in_specs=in_smem() + hbm(size),
        out_specs=in_vmem(1)[0],
        scratch_shapes=[pltpu.SemaphoreType.DMA((size,))],
        cost_estimate=LIGHT,
        name="stack_z",
    )(place, *arrays)


def assemble_pairs(parts, core, y, x, ins, outs):
    pairs = []
    for other, far, near in itertools.product((0, 1), repeat=3):
        half = core ^ other
        step = [0, 0, 0, 0]
        step[NEAR[half]], step[FAR[half]] = (near, far)
        at_y, at_x = (lax.rem(y + step[1], 2), lax.rem(x + step[2], 2))
        for index, row, lane, rows, block, inner in half_moves(parts)[half]:
            if index not in outs:
                continue
            pairs.append(
                (
                    index,
                    ins[2 * other + far].at[near, :, :, pl.ds(row, rows), pl.ds(lane, parts[index].lanes)],
                    outs[index].at[block, :, at_y, at_x, :, pl.ds(inner, rows)],
                )
            )
    return pairs


def fetch(parts, tuned, place, sources, weights, sems):
    if not tuned:
        for index, weight in weights.items():
            pltpu.make_async_copy(sources[index], weight, sems.at[index]).start()
        return
    for core in (0, 1):

        @pl.when(place[3] == core)
        def _():
            pairs = assemble_pairs(parts, core, place[1], place[2], sources, weights)
            for index, source, target in sorted(pairs, key=lambda pair: pair[0]):
                pltpu.make_async_copy(source, target, sems.at[index]).start()


def weight_shapes(parts, buffers, tuned):
    if tuned:
        return [part.full(buffers[0].shape[1]) for part in parts]
    return [item.shape for item in buffers]


def assemble_kernel(parts, some, place, *refs):
    outs, sems = (dict(zip(some, refs[4:-1])), refs[-1])
    fetch(parts, True, place, refs[:4], outs, sems)
    for index, out in outs.items():
        pltpu.make_async_copy(out, out, sems.at[index]).wait()


def assemble(parts, buffers, place, some=None):
    some = range(len(parts)) if some is None else some
    shapes = weight_shapes(parts, buffers, True)
    full = pl.pallas_call(
        functools.partial(assemble_kernel, parts, some),
        out_shape=[bf16(*shapes[index]) for index in some],
        in_specs=in_smem() + hbm(4),
        out_specs=in_vmem(len(some)),
        scratch_shapes=[pltpu.SemaphoreType.DMA((len(parts),))],
        compiler_params=pltpu.CompilerParams(vmem_limit_bytes=VMEM_LIMIT),
        cost_estimate=LIGHT,
        name="assemble",
    )(place, *buffers)
    return [merged(item) for item in full]


def merged(array):
    return array.reshape(array.shape[0], -1, array.shape[-1])


def both_cores(own, other, core):
    first = jnp.where(core == 0, own, other)
    second = jnp.where(core == 0, other, own)
    return jnp.stack([first, second])


def together(*trees):
    flat, tree = jax.tree.flatten(trees)
    return jax.tree.unflatten(tree, lax.optimization_barrier(flat))


def start_gather(groups, pieces, place):
    core = place[3]
    packed = [pack(parts, items) for parts, items in zip(groups, pieces)]
    halves = [half_rows(parts) for parts in groups]
    kept = [lax.dynamic_slice_in_dim(rows, core * half, half) for rows, half in zip(packed, halves)]
    sent = [
        lax.dynamic_slice_in_dim(rows, (1 - core) * half, half) for rows, half in zip(packed, halves)
    ]
    got = hop(jnp.concatenate(sent), ACROSS)
    held = []
    offset = 0
    for keep, half in zip(kept, halves):
        held.append(both_cores(keep, got[offset : offset + half], core))
        offset += half
    return held


def pipelined_gather(groups, pieces, place, state, arrived):
    count = len(groups)
    depth = grid_sizes()[0]
    held = start_gather(groups[:1], pieces(None)[:1], place) + [None] * (count - 1)
    for tick in range(count + 3):
        if tick == 1:
            held[1:] = start_gather(groups[1:], pieces(early)[1:], place)
        near, far, last = [index if 0 <= index < count else None for index in range(tick - 1, tick - 4, -1)]
        live = [index for index in (tick, near, far, last) if index is not None and index < count]
        items, state = together([held[index] for index in live], state)
        for index, item in zip(live, items):
            held[index] = item
        if last is not None:
            held[last] = held[last] + [hop(item, ACROSS) for item in held[last]]
        if far is not None:
            held[far] = [held[far], hop(held[far], FAR)]
        if near is not None:
            held[near] = [held[near], hop(held[near], NEAR)]
        if tick < count:
            early = held[tick]
            held[tick] = [held[tick]] + [hop(held[tick], ALONG_Z, step) for step in range(1, depth)]
        if last is not None:
            state = arrived(last, held[last], state)
        if tick < count:
            items, state = together(held[tick], state)
            held[tick] = stack_z(items, place)
        if near is not None:
            items, state = together(held[near], state)
            held[near] = jnp.stack(items)
    return state


def whole_shape(part):
    return (part.blocks, part.rows * lax.axis_size(AXES), part.lanes)


def dealt_shapes(parts, tuned):
    if not tuned:
        return [whole_shape(part) for part in parts]
    size = (grid_sizes()[0], 2, half_rows(parts), WIDTH)
    return [lead + size for lead in ((2, 2), (2,), (), ())]


def start_deal(parts, tuned, place, wanted, arrays, dealt, sems):
    if not tuned:
        pltpu.make_async_copy(arrays[wanted], dealt[wanted], sems.at[wanted]).start()
        return
    array = arrays[wanted].reshape(*parts[wanted].full(grid_sizes()[0]))
    to_core, to_far, to_near, own = dealt
    for core in (0, 1):

        @pl.when(place[3] == core)
        def _():
            for other, far, near in itertools.product((0, 1), repeat=3):
                half = core ^ other
                step = [0, 0, 0, 0]
                step[NEAR[half]], step[FAR[half]] = (near, far)
                at_y, at_x = (lax.rem(place[1] + step[1], 2), lax.rem(place[2] + step[2], 2))
                if other:
                    target = to_core.at[far, near]
                elif far:
                    target = to_far.at[near]
                else:
                    target = to_near if near else own
                for index, row, lane, rows, block, inner in half_moves(parts)[half]:
                    if index == wanted:
                        pltpu.make_async_copy(
                            array.at[block, :, at_y, at_x, :, pl.ds(inner, rows)],
                            target.at[:, :, pl.ds(row, rows), pl.ds(lane, parts[index].lanes)],
                            sems.at[index],
                        ).start()


def add_up(*terms):
    total = terms[0].astype(jnp.float32)
    for term in terms[1:]:
        total = total + term.astype(jnp.float32)
    return total


def low_add(*terms):
    return add_up(*terms).astype(jnp.bfloat16)


def scatter_stage(stage, parts, items, place):
    depth = grid_sizes()[0]
    z, core = (place[0], place[3])
    if stage == 0:
        to_core, *rest = items
        return rest + [hop(to_core, ACROSS)]
    if stage == 1:
        to_far, to_near, own, from_core = items
        return [to_near, own, from_core, hop(low_add(to_far, from_core[1]), FAR)]
    if stage == 2:
        to_near, own, from_core, from_far = items
        from_near = hop(low_add(to_near, from_core[0, 1], from_far[1]), NEAR)
        return [add_up(own, from_core[0, 0], from_far[0]), from_near]
    if stage == 3:
        summed = lax.optimization_barrier(add_up(*items))
        sent = [lax.dynamic_index_in_dim(summed, lax.rem(z + step, depth), 0, False) for step in range(1, depth)]
        along = [hop(item.astype(jnp.bfloat16), ALONG_Z, step + 1) for step, item in enumerate(sent)]
        return [lax.dynamic_index_in_dim(summed, z, 0, False)] + along
    total = add_up(*items)
    keep = lax.dynamic_index_in_dim(total, core, 0, False)
    other = hop(lax.dynamic_index_in_dim(total, 1 - core, 0, False), ACROSS)
    return both_cores(keep, other, core).reshape(-1, WIDTH)


SCATTER_STAGES = 5


def pipelined_scatter(groups, place, state, steps):
    count = len(groups)
    held = [None] * count
    for tick in range(count + SCATTER_STAGES):
        live = [index for index in range(tick - SCATTER_STAGES, tick) if 0 <= index < count]
        if tick <= count:
            items, state = together([held[index] for index in live], state)
            for index, item in zip(live, items):
                held[index] = item
        for index in live:
            held[index] = scatter_stage(tick - 1 - index, groups[index], held[index], place)
        if tick < count:
            held[tick], state = steps[tick](state)
    return (held, state)


CQL_WEIGHT = 0.05
BETA_ONE = 0.5
BETA_TWO = 0.5
LEARNING_RATE = 0.25
WEIGHT_DECAY = 0.01
PATCH_IN = 256
DPROJ = 512
ACTIONS = 18
ATOMS = 51
GAMES = 4
BLOCKS = 2
STEP = 5
PLAYS = ACTIONS * ATOMS


def average_decay():
    return min(0.99, (1.0 + STEP) / (10.0 + STEP))


SWEEP = 1024


def lamb_parts(grads, params, first, second):
    momentum = BETA_ONE * first + (1.0 - BETA_ONE) * grads
    variance = BETA_TWO * second + (1.0 - BETA_TWO) * grads * grads
    direction = (
        momentum / (1.0 - BETA_ONE**STEP) / (jnp.sqrt(variance / (1.0 - BETA_TWO**STEP)) + 1e-06)
        + WEIGHT_DECAY * params
    )
    return (momentum, variance, direction)


def sweep(start, size, body, carry):
    steps = size // SWEEP

    def step(index, carry):
        return body(pl.ds(pl.multiple_of(start + index * SWEEP, ROWS), SWEEP), carry)

    if steps:
        carry = lax.fori_loop(0, steps, step, carry, unroll=2)
    return (carry, start + steps * SWEEP, size - steps * SWEEP)


def row_sum(value):
    return jnp.sum(value, axis=1, keepdims=True)


def put_rows(target, row, source, steps):
    for first, rows, lane, stride in steps:

        def step(index, carry):
            lanes = pl.ds(pl.multiple_of(lane + index * stride, ROWS), WIDTH)
            target[row : row + 1, lanes] = source[pl.ds(first + index, 1), :]
            return carry

        lax.fori_loop(0, rows, step, 0, unroll=4)


def block_rows(name, start, rows, first):
    if name == "w_out":
        count = rows // (D // BOT)
        return [(first + part * count, count, start + part * BOT, D) for part in range(D // BOT)]
    return [(first, rows, start, WIDTH)]


def patch_rows(rows, first):
    count = rows // 4
    return [
        (first + (2 * block + half) * count, count, half * (D // 2) + block * WIDTH, D)
        for block in range(2)
        for half in range(2)
    ]


def direction_kernel(cuts, moves, gain_at, *refs):
    top_cuts, block_cuts = cuts
    number = len(moves)
    sources, refs = (refs[:number], refs[number:])
    late, loss, *refs = refs
    top_ins, block_ins, refs = (refs[:3], refs[3:6], refs[6:])
    sums, *refs = refs
    top_outs, block_outs, (top_grad, block_grad) = (refs[:3], refs[3:6], refs[6:])
    for source, steps in zip(sources, moves):
        for row, placed in steps:
            put_rows(top_grad if row is None else block_grad, row or 0, source, placed)
    patch = top_cuts[0][1]
    top_grad[:, pl.ds(patch, late.shape[1])] = late[...]
    gain_start, gain_width = block_cuts[3]
    source, first = (sources[gain_at[0]], gain_at[1])
    block_grad[:, pl.ds(gain_start, gain_width)] = source[pl.ds(first, 8), :][:BLOCKS, :gain_width]

    def work(lanes, grad, ins, outs):
        param, *moments = [ref[:, lanes] for ref in ins]
        made = lamb_parts(grad[:, lanes], param, *moments)
        for ref, value in zip(outs, made):
            ref[:, lanes] = value
        return (param * param, made[2] * made[2])

    found = []
    width = top_ins[0].shape[1]

    def top_step(lanes, carry):
        size = lanes.size
        squares = work(lanes, top_grad, top_ins, top_outs)
        at = lanes.start + lax.broadcasted_iota(jnp.int32, (1, size), 1)
        masks = [(at >= start) & (at < start + count) for start, count in top_cuts]
        terms = [jnp.where(mask, value, 0.0) for mask in masks for value in squares]
        if size != SWEEP:
            return [row_sum(held) + row_sum(term) for held, term in zip(carry, terms)]
        return [held + term for held, term in zip(carry, terms)]

    zeros = [jnp.zeros((1, SWEEP), jnp.float32)] * (2 * len(top_cuts))
    carry, start, rest = sweep(0, width, top_step, zeros)
    carry = top_step(pl.ds(start, rest), carry) if rest else [row_sum(value) for value in carry]
    found += [(index // 2, index % 2, value) for index, value in enumerate(carry)]

    def block_step(lanes, carry):
        return [held + term for held, term in zip(carry, work(lanes, block_grad, block_ins, block_outs))]

    zeros = [jnp.zeros((BLOCKS, SWEEP), jnp.float32)] * 2
    for index, (start, size) in enumerate(block_cuts):
        carry, start, rest = sweep(start, size, block_step, zeros)
        carry = [row_sum(value) for value in carry]
        if rest:
            terms = work(pl.ds(start, rest), block_grad, block_ins, block_outs)
            carry = [held + row_sum(term) for held, term in zip(carry, terms)]
        for block in range(BLOCKS):
            lane = len(top_cuts) + block * len(block_cuts) + index
            found += [(lane, row, value[block : block + 1]) for row, value in enumerate(carry)]
    rows = lax.broadcasted_iota(jnp.int32, sums.shape, 0)
    lanes = lax.broadcasted_iota(jnp.int32, sums.shape, 1)
    result = jnp.where((rows == 2) & (lanes == 0), loss[...], 0.0)
    for lane, row, value in found:
        result = jnp.where((rows == row) & (lanes == lane), value, result)
    sums[...] = result


def directions(cuts, rows, moves, gain_at, late, loss, top_ins, block_ins):
    shapes = [f32(*top_ins[0].shape)] * 3 + [f32(*block_ins[0].shape)] * 3
    ins = [*rows, late, loss, *top_ins, *block_ins]
    return pl.pallas_call(
        functools.partial(direction_kernel, cuts, moves, gain_at),
        out_shape=[f32(8, ROWS)] + shapes,
        in_specs=in_vmem(len(ins)),
        out_specs=in_vmem(7),
        scratch_shapes=[
            pltpu.VMEM(top_ins[0].shape, jnp.float32),
            pltpu.VMEM(block_ins[0].shape, jnp.float32),
        ],
        compiler_params=pltpu.CompilerParams(vmem_limit_bytes=VMEM_LIMIT),
        cost_estimate=LIGHT,
        name="directions",
    )(*ins)


def update_kernel(cuts, sums, *refs):
    top_cuts, block_cuts = cuts
    top_ins, block_ins, refs = (refs[:3], refs[3:6], refs[6:])
    norms, *refs = refs
    top_outs, block_outs = (refs[:3], refs[3:])
    norm = jnp.sqrt(sums[...])
    norms[...] = norm
    ratio = LEARNING_RATE * (norm[0:1] / (norm[1:2] + 1e-06))
    decay = average_decay()

    def work(lanes, ins, outs, scale):
        param, direction, average = [ref[:, lanes] for ref in ins]
        updated, half, averaged = outs
        value = param - scale * direction
        updated[:, lanes] = value
        half[:, lanes] = value.astype(jnp.bfloat16)
        averaged[:, lanes] = decay * average + (1.0 - decay) * value

    def top_step(lanes, carry):
        at = lanes.start + lax.broadcasted_iota(jnp.int32, (1, lanes.size), 1)
        scale = jnp.broadcast_to(ratio[:, 3:4], at.shape)
        for index in (2, 1, 0):
            scale = jnp.where(at < top_cuts[index + 1][0], ratio[:, index : index + 1], scale)
        work(lanes, top_ins, top_outs, scale)
        return carry

    _, start, rest = sweep(0, top_ins[0].shape[1], top_step, 0)
    if rest:
        top_step(pl.ds(start, rest), 0)
    for index, (start, size) in enumerate(block_cuts):
        scale = jnp.concatenate(
            [
                ratio[:, lane : lane + 1]
                for lane in [4 + block * len(block_cuts) + index for block in range(BLOCKS)]
            ]
        )

        def block_step(lanes, carry):
            work(lanes, block_ins, block_outs, scale)
            return carry

        _, start, rest = sweep(start, size, block_step, 0)
        if rest:
            block_step(pl.ds(start, rest), 0)


def update(cuts, sums, top_ins, block_ins):
    shapes = []
    for array in (top_ins[0], block_ins[0]):
        shapes += [f32(*array.shape), bf16(*array.shape), f32(*array.shape)]
    return pl.pallas_call(
        functools.partial(update_kernel, cuts),
        out_shape=[f32(8, ROWS)] + shapes,
        in_specs=in_vmem(7),
        out_specs=in_vmem(7),
        compiler_params=pltpu.CompilerParams(vmem_limit_bytes=VMEM_LIMIT),
        cost_estimate=LIGHT,
        name="update",
    )(sums, *top_ins, *block_ins)


def segment_lengths():
    top = [PATCH_IN * D, D * PIX, D * DPROJ, DPROJ * GAMES * PLAYS]
    block = [D * BOT, 9 * BOT * BOT, BOT * D, 2 * (2 * BOT + D)]
    return (top, block)


def cut_points(lengths, devices):
    cuts = []
    offset = 0
    for length in lengths:
        width = length // devices
        cuts.append((offset, width))
        offset += width
    return cuts


def pack_top(flat, cuts):
    patch, pool, proj, heads = [flat[start : start + size] for start, size in cuts]
    patch = patch.reshape(-1, 2, 2, WIDTH).transpose(2, 1, 0, 3).reshape(2, -1, WIDTH)
    pool = jnp.pad(pool.reshape(1, -1, PIX), ((0, 0), (0, 0), (0, ROWS - PIX)))
    heads = jnp.pad(heads.reshape(-1, GAMES, PLAYS), ((0, 0), (0, 0), (0, 2 * WIDTH - PLAYS)))
    heads = heads.reshape(-1, 2 * GAMES, WIDTH).transpose(1, 0, 2)
    return [patch, pool, proj.reshape(1, -1, WIDTH), heads]


def flat_late(pool, proj, heads):
    heads = heads.transpose(1, 0, 2).reshape(-1, GAMES, 2 * WIDTH)[:, :, :PLAYS]
    return jnp.concatenate([item.reshape(-1) for item in (pool[:, :, :PIX], proj, heads)])


def pack_block(flat, cuts):
    w_in, w_mid, w_out = [flat[start : start + size] for start, size in cuts[:3]]
    w_out = w_out.reshape(-1, D // BOT, BOT).transpose(1, 0, 2)
    return [w_in.reshape(1, -1, BOT), w_mid.reshape(1, -1, BOT), w_out]


def parts_for(devices):
    rows = {"patch": 2 * PATCH_IN, "pool": D, "proj": D, "heads": DPROJ}
    rows |= {"w_in": D, "w_mid": TAPS * BOT, "w_out": BOT, "gains": TILE * devices}
    blocks = {"patch": 2, "heads": 2 * GAMES, "w_out": D // BOT}
    return {
        name: Part(blocks.get(name, 1), count // devices, ROWS if name == "pool" else WIDTH)
        for name, count in rows.items()
    }


def is_tuned(devices):
    parts = parts_for(devices).values()
    whole = all(part.rows // part.across % TILE == 0 for part in parts)
    return whole and lax.axis_size("wide") == 8 and lax.axis_size("narrow") == 4


def plain_gather(piece):
    return lax.all_gather(piece, AXES, axis=1, tiled=True)


def plain_scatter(array):
    return lax.psum_scatter(array, AXES, scatter_dimension=1, tiled=True).astype(jnp.float32)


def total(array):
    if lax.axis_size("wide") != 8 or lax.axis_size("narrow") != 4:
        return lax.psum(array, AXES)
    array = array + hop(array, ACROSS)
    array = array + hop(array, (2, 2))
    array = array + hop(array, (1, 1))
    one, two, three = [hop(array, ALONG_Z, step) for step in (1, 2, 3)]
    return (array + two) + (one + three)


def frame_rows(frames):
    count = frames.shape[0]
    return jnp.pad(frames, ((0, 0), (0, ROWS - PIX), (0, 0))).reshape(count * ROWS, PATCH_IN)


def on_device(
    observed,
    following,
    game_ids,
    actions,
    legal_mask,
    rewards,
    discounts,
    done_flags,
    params_top,
    params_blocks,
    first_top,
    first_blocks,
    second_top,
    second_blocks,
    average_top,
    average_blocks,
    target_top,
    target_blocks,
):
    devices = lax.axis_size(AXES)
    frames_all = observed.shape[0] * devices
    top_lengths, block_lengths = segment_lengths()
    top_cuts = cut_points(top_lengths, devices)
    block_cuts = cut_points(block_lengths, devices)
    gain_start, gain_width = block_cuts[3]
    parts = parts_for(devices)
    tuned = is_tuned(devices)
    place = spot()
    shift = shifts()
    spread = spread_pixels(devices)
    count = observed.shape[0]
    whole = jnp.concatenate([game_ids[:, None], actions], axis=1)
    whole = jnp.pad(whole, ((0, 8 - count), (0, ROWS - 3)), constant_values=-1)
    legal = jnp.pad(legal_mask, ((0, 8 - count), (0, ROWS - ACTIONS)), constant_values=1)
    keep = discounts * (1.0 - done_flags.astype(jnp.float32))
    real = jnp.pad(jnp.stack([rewards, keep], axis=1), ((0, 8 - count), (0, ROWS - 2)))

    def read_pieces(early):
        sources = (target_top, target_blocks, params_top, params_blocks)
        if early is not None:
            early, sources = together(early, sources)
        tops = (sources[0], sources[2].astype(jnp.bfloat16))
        blocks = (sources[1], sources[3].astype(jnp.bfloat16))
        own = {}
        for net, top, flat in zip(("target", "online"), tops, blocks):
            for name, piece in zip(("patch", "pool", "proj", "heads"), pack_top(top, top_cuts)):
                own[net, name] = piece
            for index in range(BLOCKS):
                for name, piece in zip(block_names, pack_block(flat[index], block_cuts)):
                    own[net, name, index] = piece
        gain_rows = jnp.concatenate(blocks)[:, gain_start:]
        own["gains",] = jnp.pad(
            gain_rows, ((0, TILE - 2 * BLOCKS), (0, WIDTH - gain_width))
        ).reshape(1, TILE, WIDTH)
        return [[own[key] for key in group] for group in keys]

    block_names = ("w_in", "w_mid", "w_out")

    def part_of(key):
        return parts[key[0] if key[0] in parts else key[1]]

    full = {}

    def block_weight(index, name):
        return merged(full["online", name, index]).reshape(-1, BOT)

    def top_weights(net):
        return (full[net, "pool"][0], full[net, "proj"][0], full[net, "heads"])

    def hold(net, index, group, buffers, state):
        full["held", index] = (group, buffers)
        return state

    def read_gains(group, buffers, state):
        gains = assemble(group_parts(group), buffers, place, [0])[0] if tuned else buffers[0]
        gains = gains.reshape(devices, TILE, WIDTH)[:, : 2 * BLOCKS, :gain_width]
        gains = gains.transpose(1, 0, 2).reshape(2 * BLOCKS, -1).astype(jnp.float32)
        return run_block("target", 0, group, buffers, state | {"gains": gains})

    def keep_ends(net, group, buffers, state):
        arrays = assemble(group_parts(group), buffers, place) if tuned else buffers
        full.update(zip(keys[group], arrays))
        if net == "target":
            for index in range(1, BLOCKS):
                state = run_block(net, index, *full["held", index], state)
            stream = state.pop("stream")
            state |= {"target": head_target(stream, *top_weights(net), whole, real)}
        return state

    def run_block(net, index, group, buffers, state):
        keep = net == "online"
        row = index + (BLOCKS if keep else 0)
        gain = state["gains"][row : row + 1]
        stream = [state["pixels" if keep else "following"], spread]
        if index:
            stream = [state["stream"]]
        skip = 1 if keys[group][0] == ("gains",) else 0
        out, *kept = block_forward(
            stream, gain, shift, group_parts(group), skip, buffers, place, keep, tuned
        )
        state = state | {"stream": out}
        if keep:
            start = kept.pop(0) if index == 0 else stream[0]
            full.update(zip([(net, name, index) for name in block_names], kept[-3:]))
            state |= {"kept%d" % index: [start, *kept[:-3]]}
        return state

    keys, then = ([], [])
    ends = ("pool", "proj", "heads")

    def add_group(group, run, *names):
        keys.append(group)
        then.append(functools.partial(run, *names))

    def block_keys(net, index):
        return [(net, name, index) for name in block_names]

    for index in range(1, BLOCKS):
        add_group(block_keys("target", index), hold, "target", index)
    add_group([("gains",), ("target", "patch")] + block_keys("target", 0), read_gains)
    add_group([("target", name) for name in ends], keep_ends, "target")
    for index in range(BLOCKS):
        start = [] if index else [("online", "patch")]
        add_group(start + block_keys("online", index), run_block, "online", index)
    add_group([("online", name) for name in ends], keep_ends, "online")

    def group_parts(group):
        return [part_of(key) for key in keys[group]]

    def arrived(group, buffers, state):
        return then[group](group, buffers, dict(state))

    state = {"following": frame_rows(following), "pixels": frame_rows(observed)}
    if tuned:
        groups = [group_parts(group) for group in range(len(keys))]
        state = pipelined_gather(groups, read_pieces, place, state, arrived)
    else:
        for group, items in enumerate(read_pieces(None)):
            state = arrived(group, [plain_gather(item) for item in items], state)

    keys = []
    steps = []

    def loss_step(group, state):
        (loss, dstream), dealt = head_loss(
            state.pop("stream"), *top_weights("online"), state.pop("target"), whole, legal, frames_all,
            group, tuned, place,
        )
        return (dealt, state | {"loss": loss, "grad": dstream})

    def out_inputs(index, state):
        stream, hid_one, hid_two, hid_three, rstd = state["kept%d" % index]
        gain = state["gains"][BLOCKS + index : BLOCKS + index + 1]
        return [stream, hid_two, hid_three, rstd, block_weight(index, "w_out"), gain]

    def out_step(index, group, state):
        (dres, low, late), dealt = back_out(
            state["grad"], *out_inputs(index, state), group, tuned, place
        )
        return (dealt, state | {"grad": dres, "low": low, "late%d" % index: late})

    def mid_step(index, group, state):
        stream, hid_one, hid_two, hid_three, rstd = state["kept%d" % index]
        gain = state["gains"][BLOCKS + index : BLOCKS + index + 1]
        (low, early), dealt = back_mid(
            state["low"], hid_one, rstd, block_weight(index, "w_mid"), gain, shift, group, tuned, place
        )
        return (dealt, state | {"low": low, "early%d" % index: early})

    def between_step(index, group, state):
        stream = state.pop("kept%d" % index)[0]
        (dres, low, late), dealt = back_between(
            state["low"], stream, state["grad"], block_weight(index, "w_in"),
            out_inputs(index - 1, state), group, tuned, place,
        )
        return (dealt, state | {"grad": dres, "low": low, "late%d" % (index - 1): late})

    def first_step(group, state):
        stream = state.pop("kept0")[0]
        dgains = [
            jnp.concatenate([state.pop("early%d" % index), state.pop("late%d" % index)], axis=1)
            for index in range(BLOCKS)
        ]
        dgains = jnp.concatenate(dgains).reshape(BLOCKS, devices, gain_width).transpose(1, 0, 2)
        dgains = jnp.pad(dgains, ((0, 0), (0, TILE - BLOCKS), (0, WIDTH - gain_width)))
        dgains = dgains.reshape(1, -1, WIDTH).astype(jnp.bfloat16)
        dealt = back_first(
            state.pop("low"), stream, state.pop("grad"), block_weight(0, "w_in"),
            state.pop("pixels"), spread, dgains, group, tuned, place,
        )
        return (dealt, state)

    def add_step(group, run, *names):
        keys.append(group)
        steps.append(
            lambda state: run(*names, [parts[key[0]] for key in group], dict(state))
        )

    add_step([("heads",), ("proj",), ("pool",)], loss_step)
    add_step([("w_out", BLOCKS - 1)], out_step, BLOCKS - 1)
    for index in reversed(range(BLOCKS)):
        add_step([("w_mid", index)], mid_step, index)
        if index:
            add_step([("w_in", index), ("w_out", index - 1)], between_step, index)
    add_step([("w_in", 0), ("patch",), ("gains",)], first_step)
    groups = [[parts[key[0]] for key in group] for group in keys]
    if tuned:
        mine, state = pipelined_scatter(groups, place, state, steps)
    else:
        mine = []
        for group, step in zip(groups, steps):
            arrays, state = step(state)
            mine.append(pack(group, [plain_scatter(array) for array in arrays]))
    loss_part = state["loss"]
    at = {}
    moves = []
    for number, group in enumerate(keys):
        first = 0
        steps = []
        for key in group:
            count = parts[key[0]].travel
            at[key] = (number, first)
            if len(key) > 1:
                start = block_cuts[block_names.index(key[0])][0]
                steps.append((key[1], block_rows(key[0], start, count, first)))
            elif key[0] == "patch":
                steps.append((None, patch_rows(count, first)))
            first += count
        moves.append(steps)
    late = []
    for name in ("pool", "proj", "heads"):
        number, first = at[name,]
        late.append(parts[name].unpack(mine[number][first : first + parts[name].travel]))
    late = flat_late(*late)[None]
    cuts = (top_cuts, block_cuts)
    tops = [array[None] for array in (params_top, first_top, second_top, average_top)]
    sums, *made = directions(
        cuts, mine[1:], moves[1:], (at["gains",][0] - 1, at["gains",][1]), late, loss_part,
        tops[:3], [params_blocks, first_blocks, second_blocks],
    )
    momentum_top, variance_top, direction_top, momentum_blocks, variance_blocks, direction_blocks = made
    sums = total(sums)
    norms, *made = update(
        cuts, sums, [tops[0], direction_top, tops[3]],
        [params_blocks, direction_blocks, average_blocks],
    )
    updated_top, half_top, averaged_top, updated_blocks, half_blocks, averaged_blocks = made
    loss_total = sums[2, 0]
    matrix_norms = norms[:2, : len(top_cuts) + BLOCKS * len(block_cuts)]
    number, first = at["gains",]
    gain_grads = mine[number][first : first + BLOCKS, :gain_width]
    return (
        loss_total,
        matrix_norms,
        updated_top[0],
        half_top[0],
        momentum_top[0],
        variance_top[0],
        averaged_top[0],
        updated_blocks,
        half_blocks,
        momentum_blocks,
        variance_blocks,
        averaged_blocks,
        gain_grads,
    )


def solution(mesh):
    one = P(AXES)
    flat = P(None, AXES)
    return jax.shard_map(
        on_device,
        mesh=mesh,
        in_specs=(P(AXES, None, None),) * 2
        + (one, P(AXES, None), P(AXES, None))
        + (one,) * 3
        + (one, flat) * 5,
        out_specs=(P(), P()) + (one,) * 5 + (flat,) * 6,
        check_vma=False,
    )
```

```python
import functools
import itertools

import jax
import jax.numpy as jnp
from jax import lax
from jax.experimental import pallas as pl
from jax.experimental.pallas import tpu as pltpu
from jax.sharding import PartitionSpec as P

D = 2048
BOT = 512
GROUPS = 32
SIDE = 11
PIX = 121
TAPS = 9

ROWS = 128
LANES = 512
VMEM_LIMIT = 60 * 1024 * 1024
LIGHT = pl.CostEstimate(flops=1024, bytes_accessed=1024, transcendentals=0)


def shifts():
    pixel = jnp.arange(ROWS)
    row, col = (pixel // SIDE, pixel % SIDE)
    mats = []
    for tap in range(TAPS):
        at_row, at_col = (row + tap // 3 - 1, col + tap % 3 - 1)
        inside = (at_row >= 0) & (at_row < SIDE) & (at_col >= 0) & (at_col < SIDE) & (pixel < PIX)
        mats.append((inside[:, None] & (pixel[None, :] == (at_row * SIDE + at_col)[:, None])))
    return jnp.concatenate(mats, axis=0).astype(jnp.bfloat16)


def dot(left, right):
    return jnp.dot(left, right, preferred_element_type=jnp.float32)


def dot_rows(left, right):
    return lax.dot_general(
        left, right, (((0,), (0,)), ((), ())), preferred_element_type=jnp.float32
    )


def dot_lanes(left, right):
    return lax.dot_general(
        left, right, (((1,), (1,)), ((), ())), preferred_element_type=jnp.float32
    )


def each_chunk(count, chans, body, unroll=1):
    per = chans // LANES

    def step(index, carry):
        frame = index // per
        rows = pl.ds(pl.multiple_of(frame * ROWS, ROWS), ROWS)
        lanes = pl.ds(pl.multiple_of((index % per) * LANES, LANES), LANES)
        body(pl.ds(frame, 1), rows, lanes)
        return carry

    lax.fori_loop(0, count * per, step, 0, unroll=unroll)


def real_rows():
    return lax.broadcasted_iota(jnp.int32, (ROWS, LANES), 0) < PIX


def group_mean(sums):
    chans = sums.shape[1]
    width = chans // GROUPS
    lane = lax.broadcasted_iota(jnp.int32, sums.shape, 1)
    step = 1
    while step < width:
        ahead = pltpu.roll(sums, chans - step, 1)
        behind = pltpu.roll(sums, step, 1)
        sums = sums + jnp.where((lane & step) == 0, ahead, behind)
        step *= 2
    return sums * (1.0 / (PIX * width))


def silu(value):
    return value / (1.0 + jnp.exp(-value))


def silu_slope(value):
    gate = 1.0 / (1.0 + jnp.exp(-value))
    return gate * (1.0 + value * (1.0 - gate))


def normalise(count, chans, hid, sums, rstd, rstd_at):
    whole = pl.ds(0, chans)
    sums[:, whole] = jnp.zeros((sums.shape[0], chans), jnp.float32)

    def add(frame, rows, lanes):
        sums[frame, lanes] = jnp.sum(hid[rows, lanes], axis=0, keepdims=True)

    each_chunk(count, chans, add, unroll=2)
    sums[:, whole] = group_mean(sums[:, whole])

    def center(frame, rows, lanes):
        value = jnp.where(real_rows(), hid[rows, lanes] - sums[frame, lanes], 0.0)
        hid[rows, lanes] = value
        sums[frame, lanes] = jnp.sum(value * value, axis=0, keepdims=True)

    each_chunk(count, chans, center, unroll=2)
    at = pl.ds(rstd_at, chans)
    rstd[:, at] = lax.rsqrt(group_mean(sums[:, whole]) + 1e-05)


def forward_kernel(count, keep, parts, skip, tuned, *refs):
    refs = list(refs)
    number = len(parts) - skip
    first = number > 3

    def take(number):
        taken = refs[:number]
        del refs[:number]
        return taken

    (place,) = take(1)
    x = take(2 if first else 1)
    gains, shift = take(2)
    sources = take(4 if tuned else len(parts))
    (out,) = take(1)
    if keep:
        if first:
            (start,) = take(1)
        hid_one, hid_two, hid_three, rstd = take(4)
        kept_weights = take(3)
    weights = take(number)
    sems, back_sems, low, act, cols, sums = take(6)
    if not keep:
        hid_one, hid_two, hid_three, rstd = take(4)
        if first:
            (start,) = take(1)
    fetch(parts, tuned, place, sources, dict(enumerate(weights, skip)), sems)

    def arrived(index):
        weight = weights[index]
        pltpu.make_async_copy(weight, weight, sems.at[len(parts) + index]).wait()
        if keep and index >= -3:
            pltpu.make_async_copy(weight, kept_weights[index], back_sems.at[3 + index]).start()
        return weight

    def whole(value):
        return value.reshape(-1, value.shape[-1])

    if first:
        pixels, spread = x
        x = start
        patch = arrived(-4)
        for half in range(2):
            wide = dot(pixels[...], spread[half]).astype(jnp.bfloat16)
            for block in range(2):
                lanes = pl.ds((2 * half + block) * WIDTH, WIDTH)
                x[:, lanes] = dot(wide, whole(patch[block]))
    else:
        (x,) = x

    def cast(frame, rows, lanes):
        low[rows, lanes] = x[rows, lanes].astype(jnp.bfloat16)

    def activate(hid, at, offset):
        def body(frame, rows, lanes):
            gain = gains[:, pl.ds(offset + lanes.start, LANES)]
            bias = gains[:, pl.ds(offset + BOT + lanes.start, LANES)]
            value = hid[rows, lanes] * rstd[frame, pl.ds(at + lanes.start, LANES)]
            hid[rows, lanes] = value
            value = jnp.where(real_rows(), silu(value * gain + bias), 0.0)
            act[rows, lanes] = value.astype(jnp.bfloat16)

        return body

    each_chunk(count, D, cast)
    hid_one[...] = dot(low[...], whole(arrived(-3)[...]))
    normalise(count, BOT, hid_one, sums, rstd, 0)
    each_chunk(count, BOT, activate(hid_one, 0, 0))
    for frame in range(count):
        rows = pl.ds(frame * ROWS, ROWS)
        for tap in range(TAPS):
            picked = dot(shift[pl.ds(tap * ROWS, ROWS), :], act[rows, :])
            cols[rows, pl.ds(tap * BOT, BOT)] = picked.astype(jnp.bfloat16)
    hid_two[...] = dot(cols[...], whole(arrived(-2)[...]))
    normalise(count, BOT, hid_two, sums, rstd, BOT)
    each_chunk(count, BOT, activate(hid_two, BOT, 2 * BOT))
    w_out = arrived(-1)
    for part in range(D // BOT):
        hid_three[:, pl.ds(part * BOT, BOT)] = dot(act[...], whole(w_out[part]))
    normalise(count, D, hid_three, sums, rstd, 2 * BOT)

    def finish(frame, rows, lanes):
        gain = gains[:, pl.ds(4 * BOT + lanes.start, LANES)]
        bias = gains[:, pl.ds(4 * BOT + D + lanes.start, LANES)]
        value = hid_three[rows, lanes] * rstd[frame, pl.ds(2 * BOT + lanes.start, LANES)]
        if keep:
            hid_three[rows, lanes] = value
        value = silu(x[rows, lanes] + value * gain + bias)
        out[rows, lanes] = jnp.where(real_rows(), value, 0.0)

    each_chunk(count, D, finish)
    if keep:
        for index in (-3, -2, -1):
            pltpu.make_async_copy(weights[index], kept_weights[index], back_sems.at[3 + index]).wait()


def f32(*shape):
    return jax.ShapeDtypeStruct(shape, jnp.float32)


def bf16(*shape):
    return jax.ShapeDtypeStruct(shape, jnp.bfloat16)


def stat_rows(count):
    return -(-count // 8) * 8


def block_forward(stream, gains, shift, parts, skip, buffers, place, keep, tuned):
    first = len(parts) - skip > 3
    rows = stream[0].shape[0]
    count = rows // ROWS
    stats = stat_rows(count)
    kept = [
        ((rows, BOT), jnp.float32),
        ((rows, BOT), jnp.float32),
        ((rows, D), jnp.float32),
        ((stats, 2 * BOT + D), jnp.float32),
    ]
    start = [((rows, D), jnp.float32)] if first else []
    weights = weight_shapes(parts, buffers, tuned)[skip:]
    out_shape = [f32(rows, D)]
    out_specs = in_vmem(1)
    scratch = [pltpu.VMEM(shape, jnp.bfloat16) for shape in weights]
    scratch += [
        pltpu.SemaphoreType.DMA((len(parts),)),
        pltpu.SemaphoreType.DMA((3,)),
        pltpu.VMEM((rows, D), jnp.bfloat16),
        pltpu.VMEM((rows, BOT), jnp.bfloat16),
        pltpu.VMEM((rows, TAPS * BOT), jnp.bfloat16),
        pltpu.VMEM((stats, D), jnp.float32),
    ]
    if keep:
        out_shape += [jax.ShapeDtypeStruct(*item) for item in start + kept]
        out_shape += [jax.ShapeDtypeStruct(shape, jnp.bfloat16) for shape in weights[-3:]]
        out_specs += in_vmem(len(start + kept)) + hbm(3)
    else:
        scratch += [pltpu.VMEM(*item) for item in kept + start]
    return pl.pallas_call(
        functools.partial(forward_kernel, count, keep, parts, skip, tuned),
        out_shape=out_shape,
        in_specs=in_smem() + in_vmem(len(stream) + 2) + hbm(len(buffers)),
        out_specs=out_specs,
        scratch_shapes=scratch,
        compiler_params=pltpu.CompilerParams(vmem_limit_bytes=VMEM_LIMIT),
        cost_estimate=LIGHT,
        name="block_forward",
    )(place, *stream, gains, shift, *buffers)


def norm_back(count, chans, slope, hid, sums, more, rstd, rstd_at, gain, grad_gain, grad_bias, store):
    whole = pl.ds(0, chans)
    sums[:, whole] = jnp.zeros((sums.shape[0], chans), jnp.float32)
    more[:, whole] = jnp.zeros((sums.shape[0], chans), jnp.float32)

    def add(frame, rows, lanes):
        value = slope(frame, rows, lanes)
        sums[frame, lanes] = jnp.sum(value, axis=0, keepdims=True)
        more[frame, lanes] = jnp.sum(value * hid[rows, lanes], axis=0, keepdims=True)

    each_chunk(count, chans, add)
    grad_bias[...] = jnp.sum(sums[:, whole], axis=0, keepdims=True)
    grad_gain[...] = jnp.sum(more[:, whole], axis=0, keepdims=True)
    sums[:, whole] = group_mean(sums[:, whole] * gain[...])
    more[:, whole] = group_mean(more[:, whole] * gain[...])

    def spread(frame, rows, lanes):
        store(
            rows,
            lanes,
            lambda value: jnp.where(
                real_rows(),
                rstd[frame, pl.ds(rstd_at + lanes.start, LANES)]
                * (value * gain[:, lanes] - sums[frame, lanes] - hid[rows, lanes] * more[frame, lanes]),
                0.0,
            ).astype(jnp.bfloat16),
        )

    each_chunk(count, chans, spread)


def back_out_body(count, grad, x, hid_two, hid_three, rstd, w_out, gains, dres, dlow, dgains, scratch, dw_out):
    third, act, dact, sums, more = scratch
    gain_three, bias_three = (gains.at[:, pl.ds(4 * BOT, D)], gains.at[:, pl.ds(4 * BOT + D, D)])

    def slope_three(frame, rows, lanes):
        value = x[rows, lanes] + hid_three[rows, lanes] * gain_three[:, lanes] + bias_three[:, lanes]
        value = jnp.where(real_rows(), grad[rows, lanes] * silu_slope(value), 0.0)
        dres[rows, lanes] = value
        return value

    def store_three(rows, lanes, back):
        third[rows, lanes] = back(dres[rows, lanes])

    norm_back(
        count, D, slope_three, hid_three, sums, more, rstd, 2 * BOT, gain_three,
        dgains.at[:, pl.ds(2 * BOT, D)], dgains.at[:, pl.ds(2 * BOT + D, D)], store_three,
    )
    total = None
    for part in range(D // BOT):
        lanes = pl.ds(part * BOT, BOT)
        term = dot_lanes(third[:, lanes], w_out[lanes, :])
        total = term if total is None else total + term
    dact[...] = total
    gain_two, bias_two = (gains.at[:, pl.ds(2 * BOT, BOT)], gains.at[:, pl.ds(3 * BOT, BOT)])

    def slope_two(frame, rows, lanes):
        value = hid_two[rows, lanes] * gain_two[:, lanes] + bias_two[:, lanes]
        gate = 1.0 / (1.0 + jnp.exp(-value))
        act[rows, lanes] = jnp.where(real_rows(), value * gate, 0.0).astype(jnp.bfloat16)
        value = dact[rows, lanes] * (gate * (1.0 + value * (1.0 - gate)))
        value = jnp.where(real_rows(), value, 0.0)
        dact[rows, lanes] = value
        return value

    def store_two(rows, lanes, back):
        dlow[rows, lanes] = back(dact[rows, lanes])

    norm_back(
        count, BOT, slope_two, hid_two, sums, more, rstd, BOT, gain_two,
        dgains.at[:, pl.ds(0, BOT)], dgains.at[:, pl.ds(BOT, BOT)], store_two,
    )
    for part in range(D // BOT):
        lanes = pl.ds(part * BOT, BOT)
        dw_out[part] = dot_rows(act[...], third[:, lanes]).astype(jnp.bfloat16)


def out_scratch(rows):
    stats = stat_rows(rows // ROWS)
    return [
        pltpu.VMEM((rows, D), jnp.bfloat16),
        pltpu.VMEM((rows, BOT), jnp.bfloat16),
        pltpu.VMEM((rows, BOT), jnp.float32),
        pltpu.VMEM((stats, D), jnp.float32),
        pltpu.VMEM((stats, D), jnp.float32),
    ]


def back_mid_body(count, grad, hid_one, rstd, w_mid, gains, shift, dlow, dgains, scratch, dw_mid):
    act, cols, dact, sums, more = scratch
    gain_one, bias_one = (gains.at[:, pl.ds(0, BOT)], gains.at[:, pl.ds(BOT, BOT)])
    for frame in range(count):
        rows = pl.ds(frame * ROWS, ROWS)
        for tap in range(TAPS):
            picked = dot(shift[pl.ds((TAPS - 1 - tap) * ROWS, ROWS), :], grad[rows, :])
            cols[rows, pl.ds(tap * BOT, BOT)] = picked.astype(jnp.bfloat16)
    total = None
    for tap in range(TAPS):
        lanes = pl.ds(tap * BOT, BOT)
        term = dot_lanes(cols[:, lanes], w_mid[lanes, :])
        total = term if total is None else total + term
    dact[...] = total

    def slope_one(frame, rows, lanes):
        value = hid_one[rows, lanes] * gain_one[:, lanes] + bias_one[:, lanes]
        gate = 1.0 / (1.0 + jnp.exp(-value))
        act[rows, lanes] = jnp.where(real_rows(), value * gate, 0.0).astype(jnp.bfloat16)
        value = dact[rows, lanes] * (gate * (1.0 + value * (1.0 - gate)))
        value = jnp.where(real_rows(), value, 0.0)
        dact[rows, lanes] = value
        return value

    def store_one(rows, lanes, back):
        dlow[rows, lanes] = back(dact[rows, lanes])

    norm_back(
        count, BOT, slope_one, hid_one, sums, more, rstd, 0, gain_one,
        dgains.at[:, pl.ds(0, BOT)], dgains.at[:, pl.ds(BOT, BOT)], store_one,
    )
    for tap in range(TAPS):
        lanes = pl.ds(tap * BOT, BOT)
        dw_mid[0, lanes, :] = dot_rows(act[...], cols[:, lanes]).astype(jnp.bfloat16)


def back_in_body(count, grad, x, dres, w_in, dx, low, dw_in):
    def cast(frame, rows, lanes):
        low[rows, lanes] = x[rows, lanes].astype(jnp.bfloat16)

    each_chunk(count, D, cast)
    for part in range(D // BOT):
        lanes = pl.ds(part * BOT, BOT)
        dx[:, lanes] = dres[:, lanes] + dot_lanes(grad[...], w_in[lanes, :])
        dw_in[0, lanes, :] = dot_rows(low[:, lanes], grad[...]).astype(jnp.bfloat16)


def back_kernel(body, parts, tuned, counts, *refs):
    place, refs = (refs[0], list(refs[1:]))
    groups = []
    for number in (*counts[:2], len(dealt_shapes(parts, tuned)), len(parts), 1, counts[2]):
        groups.append(refs[:number])
        refs = refs[number:]
    ins, outs, dealt, made, sems, scratch = groups

    def done(index):
        start_deal(parts, tuned, place, index, made, dealt, sems[0])

    body(ins, outs, made, scratch, done)
    for index, array in enumerate(made):
        pltpu.make_async_copy(array, array, sems[0].at[index]).wait()


def back_call(name, body, ins, out_shape, scratch, parts, tuned, place):
    dealt = dealt_shapes(parts, tuned)
    counts = (len(ins), len(out_shape), len(scratch))
    outs = pl.pallas_call(
        functools.partial(back_kernel, body, parts, tuned, counts),
        out_shape=out_shape + [bf16(*shape) for shape in dealt],
        in_specs=in_smem() + in_vmem(len(ins)),
        out_specs=in_vmem(len(out_shape)) + hbm(len(dealt)),
        scratch_shapes=[pltpu.VMEM(whole_shape(part), jnp.bfloat16) for part in parts]
        + [pltpu.SemaphoreType.DMA((len(parts),))]
        + scratch,
        compiler_params=pltpu.CompilerParams(vmem_limit_bytes=VMEM_LIMIT),
        cost_estimate=LIGHT,
        name=name,
    )(place, *ins)
    return (list(outs[: len(out_shape)]), list(outs[len(out_shape) :]))


def back_out(grad, stream, hid_two, hid_three, rstd, w_out, gains, parts, tuned, place):
    rows = stream.shape[0]

    def body(ins, outs, made, scratch, done):
        back_out_body(rows // ROWS, *ins, *outs, scratch, made[0])
        done(0)

    ins = [grad, stream, hid_two, hid_three, rstd, w_out, gains]
    out_shape = [f32(rows, D), bf16(rows, BOT), f32(1, 2 * BOT + 2 * D)]
    return back_call("back_out", body, ins, out_shape, out_scratch(rows), parts, tuned, place)


def back_mid(grad, hid_one, rstd, w_mid, gains, shift, parts, tuned, place):
    rows = grad.shape[0]
    stats = stat_rows(rows // ROWS)

    def body(ins, outs, made, scratch, done):
        back_mid_body(rows // ROWS, *ins, *outs, scratch, made[0])
        done(0)

    scratch = [
        pltpu.VMEM((rows, BOT), jnp.bfloat16),
        pltpu.VMEM((rows, TAPS * BOT), jnp.bfloat16),
        pltpu.VMEM((rows, BOT), jnp.float32),
        pltpu.VMEM((stats, BOT), jnp.float32),
        pltpu.VMEM((stats, BOT), jnp.float32),
    ]
    ins = [grad, hid_one, rstd, w_mid, gains, shift]
    out_shape = [bf16(rows, BOT), f32(1, 2 * BOT)]
    return back_call("back_mid", body, ins, out_shape, scratch, parts, tuned, place)


def back_between(grad, stream, dres, w_in, later, parts, tuned, place):
    rows = stream.shape[0]

    def body(ins, outs, made, scratch, done):
        dx, low, *rest = scratch
        back_in_body(rows // ROWS, *ins[:4], dx, low, made[0])
        done(0)
        back_out_body(rows // ROWS, dx, *ins[4:], *outs, rest, made[1])
        done(1)

    scratch = [pltpu.VMEM((rows, D), jnp.float32), pltpu.VMEM((rows, D), jnp.bfloat16)]
    scratch += out_scratch(rows)
    ins = [grad, stream, dres, w_in, *later]
    out_shape = [f32(rows, D), bf16(rows, BOT), f32(1, 2 * BOT + 2 * D)]
    return back_call("back_between", body, ins, out_shape, scratch, parts, tuned, place)


def back_first(grad, stream, dres, w_in, pixels, spread, dgains, parts, tuned, place):
    rows = stream.shape[0]

    def body(ins, outs, made, scratch, done):
        dx, low = scratch
        made[2][...] = ins[6][...]
        done(2)
        back_in_body(rows // ROWS, *ins[:4], dx, low, made[0])
        done(0)
        wide = [dot(ins[4][...], ins[5][half]).astype(jnp.bfloat16) for half in range(2)]
        for block in range(2):
            total = None
            for half in range(2):
                lanes = pl.ds((2 * half + block) * WIDTH, WIDTH)
                term = dot_rows(wide[half], dx[:, lanes].astype(jnp.bfloat16))
                total = term if total is None else total + term
            made[1][block] = total.astype(jnp.bfloat16)
        done(1)

    scratch = [pltpu.VMEM((rows, D), jnp.float32), pltpu.VMEM((rows, D), jnp.bfloat16)]
    ins = [grad, stream, dres, w_in, pixels, spread, dgains]
    return back_call("back_first", body, ins, [], scratch, parts, tuned, place)[1]


def spread_pixels(devices):
    rows = PATCH_IN // devices
    value = jnp.arange(PATCH_IN)
    at = value // rows * 2 * rows + value % rows
    return jnp.stack(
        [jnp.arange(2 * PATCH_IN)[None, :] == (at + half * rows)[:, None] for half in range(2)]
    ).astype(jnp.bfloat16)


def head_forward(count, stream, pool, proj, heads, games, pool_t, pooled):
    for part in range(D // ROWS):
        lanes = pl.ds(part * ROWS, ROWS)
        pool_t[:, lanes] = pool[lanes, :].astype(jnp.float32).T
    pooled[...] = jnp.zeros_like(pooled)

    def weigh(frame, rows, lanes):
        value = stream[rows, lanes].astype(jnp.bfloat16).astype(jnp.float32)
        pooled[frame, lanes] = jnp.sum(value * pool_t[:, lanes], axis=0, keepdims=True)

    each_chunk(count, D, weigh)
    before = dot(pooled[...].astype(jnp.bfloat16), proj[...])
    hidden = silu(before).astype(jnp.bfloat16)
    scores = None
    for game in range(GAMES):
        pair = [dot(hidden, heads[2 * game + half]) for half in range(2)]
        term = jnp.where(games == game, jnp.concatenate(pair, axis=1), 0.0)
        scores = term if scores is None else scores + term
    return ([pick_atoms(scores, action) for action in range(ACTIONS)], before, hidden)


def atom_lanes():
    return lax.broadcasted_iota(jnp.int32, (8, ROWS), 1)


def pick_atoms(scores, action):
    offset = action * ATOMS
    moved = pltpu.roll(scores, 2 * WIDTH - offset, 1) if offset else scores
    return jnp.where(atom_lanes() < ATOMS, moved[:, :ROWS], -1e30)


def support_lanes():
    return -10.0 + 20.0 / (ATOMS - 1) * atom_lanes().astype(jnp.float32)


def lane_sum(value):
    return jnp.sum(value, axis=1, keepdims=True)


def target_kernel(count, stream, pool, proj, heads, whole, real, out, pool_t, pooled):
    logits, _, _ = head_forward(
        count, stream, pool, proj, heads, whole[:, 0:1], pool_t, pooled
    )
    chosen = None
    for action in range(ACTIONS):
        term = jnp.where(whole[:, 2:3] == action, logits[action], 0.0)
        chosen = term if chosen is None else chosen + term
    power = jnp.exp(chosen - jnp.max(chosen, axis=1, keepdims=True))
    probs = power / lane_sum(power)
    atoms = support_lanes()
    spacing = 20.0 / (ATOMS - 1)
    moved = jnp.clip(real[:, 0:1] + real[:, 1:2] * atoms, -10.0, 10.0)
    total = jnp.zeros_like(probs)
    for atom in range(ATOMS):
        near = 1.0 - jnp.abs(moved[:, atom : atom + 1] - atoms) / spacing
        total = total + probs[:, atom : atom + 1] * jnp.clip(near, 0.0, 1.0)
    inside = (atom_lanes() < ATOMS) & (lax.broadcasted_iota(jnp.int32, total.shape, 0) < count)
    out[...] = jnp.where(inside, total, 0.0)


def head_target(stream, pool, proj, heads, whole, real):
    count = stream.shape[0] // ROWS
    return pl.pallas_call(
        functools.partial(target_kernel, count),
        out_shape=f32(8, ROWS),
        in_specs=in_vmem(6),
        out_specs=in_vmem(1)[0],
        scratch_shapes=[pltpu.VMEM((ROWS, D), jnp.float32), pltpu.VMEM((8, D), jnp.float32)],
        compiler_params=pltpu.CompilerParams(vmem_limit_bytes=VMEM_LIMIT),
        cost_estimate=LIGHT,
        name="head_target",
    )(stream, pool, proj, heads, whole, real)


def loss_body(count, frames_all, ins, outs, made, scratch, done):
    stream, pool, proj, heads, target, whole, legal = ins
    loss, dstream = outs
    dheads, dproj, dpool = made
    pool_t, pooled, dpooled = scratch
    games, taken = (whole[:, 0:1], whole[:, 1:2])
    logits, before, hidden = head_forward(count, stream, pool, proj, heads, games, pool_t, pooled)
    atoms = support_lanes()
    inside = atom_lanes() < ATOMS
    logps, probs, values = ([], [], [])
    for value in logits:
        value = value - jnp.max(value, axis=1, keepdims=True)
        power = jnp.where(inside, jnp.exp(value), 0.0)
        mass = lane_sum(power)
        logps.append(value - jnp.log(mass))
        probs.append(power / mass)
        values.append(lane_sum(probs[-1] * atoms))
    masked = [
        jnp.where(legal[:, action : action + 1] > 0, values[action], -1e30)
        for action in range(ACTIONS)
    ]
    largest = functools.reduce(jnp.maximum, masked)
    powers = [jnp.exp(value - largest) for value in masked]
    mass = sum(powers[1:], powers[0])
    goal = target[...]
    goal_mass = lane_sum(goal)
    cross = taken_value = 0.0
    real = lax.broadcasted_iota(jnp.int32, (8, 1), 0) < count
    scale = jnp.where(real, 1.0 / frames_all, 0.0)
    spread = jnp.zeros((8, 2 * WIDTH), jnp.float32)
    for action in range(ACTIONS):
        here = jnp.where(taken == action, 1.0, 0.0)
        cross = cross - here * lane_sum(jnp.where(inside, goal * logps[action], 0.0))
        taken_value = taken_value + here * values[action]
        grad = here * (probs[action] * goal_mass - goal)
        pull = CQL_WEIGHT * (powers[action] / mass - here)
        grad = grad + pull * probs[action] * (atoms - values[action])
        grad = jnp.where(inside, grad * scale, 0.0)
        grad = jnp.concatenate([grad, jnp.zeros((8, 2 * WIDTH - ROWS), jnp.float32)], axis=1)
        offset = action * ATOMS
        spread = spread + (pltpu.roll(grad, offset, 1) if offset else grad)
    losses = cross + CQL_WEIGHT * (jnp.log(mass) + largest - taken_value)
    loss[...] = jnp.sum(jnp.where(real, losses, 0.0), axis=0, keepdims=True)
    dhidden = None
    for game in range(GAMES):
        mine = jnp.where(games == game, spread, 0.0).astype(jnp.bfloat16)
        for half in range(2):
            part = mine[:, half * WIDTH : (half + 1) * WIDTH]
            dheads[2 * game + half] = dot_rows(hidden, part).astype(jnp.bfloat16)
            term = dot_lanes(part, heads[2 * game + half])
            dhidden = term if dhidden is None else dhidden + term
    done(0)
    dbefore = (silu_slope(before) * dhidden).astype(jnp.bfloat16)
    dproj[0] = dot_rows(pooled[...].astype(jnp.bfloat16), dbefore).astype(jnp.bfloat16)
    done(1)
    dpooled[...] = dot_lanes(dbefore, proj[...]).astype(jnp.bfloat16).astype(jnp.float32)

    def push(frame, rows, lanes):
        dstream[rows, lanes] = dpooled[frame, lanes] * pool_t[:, lanes]

    each_chunk(count, D, push)

    def gather_pool(part, carry):
        lanes = pl.ds(pl.multiple_of(part * ROWS, ROWS), ROWS)
        total = None
        for frame in range(count):
            value = stream[pl.ds(frame * ROWS, ROWS), lanes].astype(jnp.bfloat16)
            term = value.astype(jnp.float32) * dpooled[pl.ds(frame, 1), lanes]
            total = term if total is None else total + term
        dpool[0, lanes, :] = total.T.astype(jnp.bfloat16)
        return carry

    lax.fori_loop(0, D // ROWS, gather_pool, 0)
    done(2)


def head_loss(stream, pool, proj, heads, target, whole, legal, frames_all, parts, tuned, place):
    rows = stream.shape[0]
    scratch = [
        pltpu.VMEM((ROWS, D), jnp.float32),
        pltpu.VMEM((8, D), jnp.float32),
        pltpu.VMEM((8, D), jnp.float32),
    ]
    ins = [stream, pool, proj, heads, target, whole, legal]
    body = functools.partial(loss_body, rows // ROWS, frames_all)
    return back_call("head_loss", body, ins, [f32(1, 1), f32(rows, D)], scratch, parts, tuned, place)


WIDTH = 512
TILE = 16
AXES = ("wide", "narrow")


def grid_sizes():
    return (lax.axis_size("wide") // 2, 2, lax.axis_size("narrow") // 2, 2)


def spot():
    sizes = grid_sizes()
    wide, narrow = (lax.axis_index("wide"), lax.axis_index("narrow"))
    return jnp.stack(
        [wide // sizes[1], wide % sizes[1], narrow // sizes[3], narrow % sizes[3]]
    ).astype(jnp.int32)


def hop(array, axis_of_core, step=1, swap=0):
    sizes = grid_sizes()
    pairs = []
    for place in itertools.product(*[range(size) for size in sizes]):
        axis = axis_of_core[place[3]]
        other = list(place)
        other[axis] = place[axis] ^ swap if swap else (place[axis] + step) % sizes[axis]
        source, target = [
            ((z * sizes[1] + y) * sizes[2] + x) * sizes[3] + core for z, y, x, core in (place, other)
        ]
        pairs.append((source, target))
    return lax.ppermute(array, AXES, pairs)


ALONG_Z = (0, 0)
ACROSS = (3, 3)
NEAR = (2, 1)
FAR = (1, 2)


def hbm(number):
    return [pl.BlockSpec(memory_space=pl.ANY)] * number


def in_vmem(number):
    return [pl.BlockSpec(memory_space=pltpu.VMEM)] * number


def in_smem():
    return [pl.BlockSpec(memory_space=pltpu.SMEM)]


def copies(pairs, sems):
    started = [
        pltpu.make_async_copy(source, target, sems.at[index])
        for index, (source, target) in enumerate(pairs)
    ]
    for copy in started:
        copy.start()
    for copy in started:
        copy.wait()


class Part:
    def __init__(self, blocks, rows, lanes):
        self.blocks, self.rows, self.lanes = (blocks, rows, lanes)
        self.across = WIDTH // lanes
        self.travel = blocks * rows // self.across

    def moves(self):
        if self.across > 1:
            deep = self.rows // self.across
            return [(0, part * self.lanes, deep, 0, part * deep) for part in range(self.across)]
        return [(block * self.rows, 0, self.rows, block, 0) for block in range(self.blocks)]

    def pack(self, piece):
        if self.across > 1:
            piece = piece.reshape(self.across, self.rows // self.across, self.lanes)
            return piece.transpose(1, 0, 2).reshape(self.travel, WIDTH)
        return piece.reshape(self.travel, WIDTH)

    def unpack(self, rows):
        if self.across > 1:
            rows = rows.reshape(self.rows // self.across, self.across, self.lanes)
            return rows.transpose(1, 0, 2).reshape(1, self.rows, self.lanes)
        return rows.reshape(self.blocks, self.rows, self.lanes)

    def full(self, depth):
        return (self.blocks, depth, 2, 2, 2, self.rows, self.lanes)


def half_rows(parts):
    total = sum(part.travel for part in parts)
    return -(-total // (2 * TILE)) * TILE


def half_moves(parts):
    cut = half_rows(parts)
    halves = ([], [])
    offset = 0
    for index, part in enumerate(parts):
        for row, lane, rows, block, inner in part.moves():
            row = row + offset
            before = max(0, min(rows, cut - row))
            if before:
                halves[0].append((index, row, lane, before, block, inner))
            if rows - before:
                halves[1].append((index, row + before - cut, lane, rows - before, block, inner + before))
        offset += part.travel
    return halves


def unit(parts, depth):
    return (depth, 2, half_rows(parts), WIDTH)


def pack(parts, pieces):
    rows = jnp.concatenate([part.pack(piece) for part, piece in zip(parts, pieces)])
    return jnp.pad(rows, ((0, 2 * half_rows(parts) - rows.shape[0]), (0, 0)))


def assemble_pairs(parts, core, y, x, ins, outs):
    pairs = []
    for other, far, near in itertools.product((0, 1), repeat=3):
        half = core ^ other
        step = [0, 0, 0, 0]
        step[NEAR[half]], step[FAR[half]] = (near, far)
        at_y, at_x = (lax.rem(y + step[1], 2), lax.rem(x + step[2], 2))
        for index, row, lane, rows, block, inner in half_moves(parts)[half]:
            if index not in outs:
                continue
            pairs.append(
                (
                    index,
                    ins[2 * other + far].at[near, :, :, pl.ds(row, rows), pl.ds(lane, parts[index].lanes)],
                    outs[index].at[block, :, at_y, at_x, :, pl.ds(inner, rows)],
                )
            )
    return pairs


def fetch(parts, tuned, place, sources, weights, sems):
    if not tuned:
        for index, weight in weights.items():
            pltpu.make_async_copy(sources[index], weight, sems.at[index]).start()
        return
    for core in (0, 1):

        @pl.when(place[3] == core)
        def _():
            pairs = assemble_pairs(parts, core, place[1], place[2], sources, weights)
            for index, source, target in sorted(pairs, key=lambda pair: pair[0]):
                pltpu.make_async_copy(source, target, sems.at[index]).start()


def weight_shapes(parts, buffers, tuned):
    if tuned:
        return [part.full(buffers[0].shape[1]) for part in parts]
    return [item.shape for item in buffers]


def assemble_kernel(parts, some, place, *refs):
    outs, sems = (dict(zip(some, refs[4:-1])), refs[-1])
    fetch(parts, True, place, refs[:4], outs, sems)
    for index, out in outs.items():
        pltpu.make_async_copy(out, out, sems.at[index]).wait()


def assemble(parts, buffers, place, some=None):
    some = range(len(parts)) if some is None else some
    shapes = weight_shapes(parts, buffers, True)
    full = pl.pallas_call(
        functools.partial(assemble_kernel, parts, some),
        out_shape=[bf16(*shapes[index]) for index in some],
        in_specs=in_smem() + hbm(4),
        out_specs=in_vmem(len(some)),
        scratch_shapes=[pltpu.SemaphoreType.DMA((len(parts),))],
        compiler_params=pltpu.CompilerParams(vmem_limit_bytes=VMEM_LIMIT),
        cost_estimate=LIGHT,
        name="assemble",
    )(place, *buffers)
    return [merged(item) for item in full]


def merged(array):
    return array.reshape(array.shape[0], -1, array.shape[-1])


def in_order(own, other, bit):
    first = jnp.where(bit == 0, own, other)
    second = jnp.where(bit == 0, other, own)
    return jnp.stack([first, second])


def together(*trees):
    flat, tree = jax.tree.flatten(trees)
    return jax.tree.unflatten(tree, lax.optimization_barrier(flat))


def start_gather(groups, pieces, place):
    core = place[3]
    packed = [pack(parts, items) for parts, items in zip(groups, pieces)]
    halves = [half_rows(parts) for parts in groups]
    kept = [lax.dynamic_slice_in_dim(rows, core * half, half) for rows, half in zip(packed, halves)]
    sent = [
        lax.dynamic_slice_in_dim(rows, (1 - core) * half, half) for rows, half in zip(packed, halves)
    ]
    got = hop(jnp.concatenate(sent), ACROSS)
    held = []
    offset = 0
    for keep, half in zip(kept, halves):
        held.append(in_order(keep, got[offset : offset + half], core))
        offset += half
    return held


def pipelined_gather(groups, pieces, place, state, arrived):
    count = len(groups)
    low, high = (place[0] % 2, place[0] // 2)
    held = start_gather(groups[:1], pieces(None)[:1], place) + [None] * (count - 1)
    held[0] = in_order(held[0], hop(held[0], ALONG_Z, swap=1), low)
    for tick in range(count + 3):
        near, far, last = [index if 0 <= index < count else None for index in range(tick - 1, tick - 4, -1)]
        live = [index for index in (tick, near, far, last) if index is not None and index < count]
        if tick == 1:
            live += range(2, count)
        items, state = together([held[index] for index in live], state)
        for index, item in zip(live, items):
            held[index] = item
        if tick == 0:
            held[1:] = start_gather(groups[1:], pieces(held[0])[1:], place)
        if last is not None:
            own, arrived_far, other = held[last]
            held[last] = [own, arrived_far, other, hop(arrived_far, ACROSS)]
        if far is not None:
            held[far] = [held[far], hop(held[far], FAR), hop(held[far], ACROSS)]
        if near is not None:
            held[near] = [held[near], hop(held[near], NEAR)]
        if tick < count:
            held[tick] = [held[tick], hop(held[tick], ALONG_Z, swap=2)]
        if tick < 2:
            early = slice(1, 2) if tick == 0 else slice(2, count)
            got = hop(jnp.concatenate(held[early], axis=1), ALONG_Z, swap=1)
            ends = list(itertools.accumulate(half_rows(parts) for parts in groups[early]))
            got = jnp.split(got, ends[:-1], axis=1)
            held[early] = [in_order(item, other, low) for item, other in zip(held[early], got)]
        if last is not None:
            state = arrived(last, held[last], state)
        if tick < count:
            (own, other), state = together(held[tick], state)
            both = in_order(own, other, high)
            held[tick] = both.reshape(-1, *both.shape[2:])
        if near is not None:
            items, state = together(held[near], state)
            held[near] = jnp.stack(items)
    return state


def whole_shape(part):
    return (part.blocks, part.rows * lax.axis_size(AXES), part.lanes)


def dealt_shapes(parts, tuned):
    if not tuned:
        return [whole_shape(part) for part in parts]
    size = (grid_sizes()[0], 2, half_rows(parts), WIDTH)
    return [lead + size for lead in ((2, 2), (2,), (), ())]


def start_deal(parts, tuned, place, wanted, arrays, dealt, sems):
    if not tuned:
        pltpu.make_async_copy(arrays[wanted], dealt[wanted], sems.at[wanted]).start()
        return
    array = arrays[wanted].reshape(*parts[wanted].full(grid_sizes()[0]))
    to_core, to_far, to_near, own = dealt
    for core in (0, 1):

        @pl.when(place[3] == core)
        def _():
            for other, far, near in itertools.product((0, 1), repeat=3):
                half = core ^ other
                step = [0, 0, 0, 0]
                step[NEAR[half]], step[FAR[half]] = (near, far)
                at_y, at_x = (lax.rem(place[1] + step[1], 2), lax.rem(place[2] + step[2], 2))
                if other:
                    target = to_core.at[far, near]
                elif far:
                    target = to_far.at[near]
                else:
                    target = to_near if near else own
                for index, row, lane, rows, block, inner in half_moves(parts)[half]:
                    if index == wanted:
                        pltpu.make_async_copy(
                            array.at[block, :, at_y, at_x, :, pl.ds(inner, rows)],
                            target.at[:, :, pl.ds(row, rows), pl.ds(lane, parts[index].lanes)],
                            sems.at[index],
                        ).start()


def add_up(*terms):
    total = terms[0].astype(jnp.float32)
    for term in terms[1:]:
        total = total + term.astype(jnp.float32)
    return total


def low_add(*terms):
    return add_up(*terms).astype(jnp.bfloat16)


def scatter_stage(stage, parts, items, place):
    depth = grid_sizes()[0]
    z, core = (place[0], place[3])
    if stage == 0:
        to_core, *rest = items
        return rest + [hop(to_core, ACROSS)]
    if stage == 1:
        to_far, to_near, own, from_core = items
        return [to_near, own, from_core, hop(low_add(to_far, from_core[1]), FAR)]
    if stage == 2:
        to_near, own, from_core, from_far = items
        from_near = hop(low_add(to_near, from_core[0, 1], from_far[1]), NEAR)
        return [add_up(own, from_core[0, 0], from_far[0]), from_near]
    if stage == 3:
        summed = lax.optimization_barrier(add_up(*items))
        sent = [lax.dynamic_index_in_dim(summed, lax.rem(z + step, depth), 0, False) for step in range(1, depth)]
        along = [hop(item.astype(jnp.bfloat16), ALONG_Z, step + 1) for step, item in enumerate(sent)]
        return [lax.dynamic_index_in_dim(summed, z, 0, False)] + along
    total = add_up(*items)
    keep = lax.dynamic_index_in_dim(total, core, 0, False)
    other = hop(lax.dynamic_index_in_dim(total, 1 - core, 0, False), ACROSS)
    return in_order(keep, other, core).reshape(-1, WIDTH)


SCATTER_STAGES = 5


def pipelined_scatter(groups, place, state, steps):
    count = len(groups)
    held = [None] * count
    for tick in range(count + SCATTER_STAGES):
        live = [index for index in range(tick - SCATTER_STAGES, tick) if 0 <= index < count]
        if tick <= count:
            items, state = together([held[index] for index in live], state)
            for index, item in zip(live, items):
                held[index] = item
        for index in live:
            held[index] = scatter_stage(tick - 1 - index, groups[index], held[index], place)
        if tick < count:
            held[tick], state = steps[tick](state)
    return (held, state)


CQL_WEIGHT = 0.05
BETA_ONE = 0.5
BETA_TWO = 0.5
LEARNING_RATE = 0.25
WEIGHT_DECAY = 0.01
PATCH_IN = 256
DPROJ = 512
ACTIONS = 18
ATOMS = 51
GAMES = 4
BLOCKS = 2
STEP = 5
PLAYS = ACTIONS * ATOMS


def average_decay():
    return min(0.99, (1.0 + STEP) / (10.0 + STEP))


SWEEP = 8192


def lamb_parts(grads, params, first, second):
    momentum = BETA_ONE * first + (1.0 - BETA_ONE) * grads
    variance = BETA_TWO * second + (1.0 - BETA_TWO) * grads * grads
    direction = (
        momentum / (1.0 - BETA_ONE**STEP) / (jnp.sqrt(variance / (1.0 - BETA_TWO**STEP)) + 1e-06)
        + WEIGHT_DECAY * params
    )
    return (momentum, variance, direction)


def stretches(cuts):
    found = []
    at = 0
    for index, (start, size) in enumerate(cuts):
        end = start + size
        last = index == len(cuts) - 1
        whole = end if last else end // ROWS * ROWS
        found.append((at, whole - at, [index]))
        at = whole
        if end != whole:
            found.append((whole, ROWS, [index, index + 1]))
            at = whole + ROWS
    return found


def sweep(start, size, body, carry):
    steps = size // SWEEP

    def step(index, carry):
        return body(pl.ds(pl.multiple_of(start + index * SWEEP, ROWS), SWEEP), carry)

    if steps:
        carry = lax.fori_loop(0, steps, step, carry)
    return (carry, start + steps * SWEEP, size - steps * SWEEP)


def row_sum(value):
    return jnp.sum(value, axis=1, keepdims=True)


def put_rows(target, row, source, steps):
    for first, rows, lane, stride in steps:

        def step(index, carry):
            lanes = pl.ds(pl.multiple_of(lane + index * stride, ROWS), WIDTH)
            target[row : row + 1, lanes] = source[pl.ds(first + index, 1), :]
            return carry

        lax.fori_loop(0, rows, step, 0, unroll=4)


def block_rows(name, start, rows, first):
    if name == "w_out":
        count = rows // (D // BOT)
        return [(first + part * count, count, start + part * BOT, D) for part in range(D // BOT)]
    return [(first, rows, start, WIDTH)]


def patch_rows(rows, first):
    count = rows // 4
    return [
        (first + (2 * block + half) * count, count, half * (D // 2) + block * WIDTH, D)
        for block in range(2)
        for half in range(2)
    ]


def direction_kernel(cuts, moves, gain_at, *refs):
    top_cuts, block_cuts = cuts
    number = len(moves)
    sources, refs = (refs[:number], refs[number:])
    late, loss, *refs = refs
    top_ins, block_ins, refs = (refs[:3], refs[3:6], refs[6:])
    sums, *refs = refs
    top_outs, block_outs, (top_grad, block_grad) = (refs[:3], refs[3:6], refs[6:])
    for source, steps in zip(sources, moves):
        for row, placed in steps:
            put_rows(top_grad if row is None else block_grad, row or 0, source, placed)
    patch = top_cuts[0][1]
    top_grad[:, pl.ds(patch, late.shape[1])] = late[...]
    gain_start, gain_width = block_cuts[3]
    source, first = (sources[gain_at[0]], gain_at[1])
    block_grad[:, pl.ds(gain_start, gain_width)] = source[pl.ds(first, 8), :][:BLOCKS, :gain_width]

    def work(lanes, grad, ins, outs):
        param, *moments = [ref[:, lanes] for ref in ins]
        made = lamb_parts(grad[:, lanes], param, *moments)
        for ref, value in zip(outs, made):
            ref[:, lanes] = value
        return (param * param, made[2] * made[2])

    found = []

    def run(cuts, grad, ins, outs, first_lane, height):
        for start, size, segments in stretches(cuts):

            def step(lanes, carry):
                terms = work(lanes, grad, ins, outs)
                return [held + term for held, term in zip(carry, terms)]

            zeros = [jnp.zeros((height, SWEEP), jnp.float32)] * 2
            carry, begin, rest = sweep(start, size, step, zeros)
            sizes = [row_sum(value) for value in carry] if rest != size else None
            if rest:
                terms = work(pl.ds(begin, rest), grad, ins, outs)
                at = begin + lax.broadcasted_iota(jnp.int32, terms[0].shape, 1)
                if len(segments) > 1:
                    edge = cuts[segments[1]][0]
                    after = [row_sum(jnp.where(at >= edge, term, 0.0)) for term in terms]
                    found.extend((first_lane, segments[1], *item) for item in enumerate(after))
                    terms = [jnp.where(at < edge, term, 0.0) for term in terms]
                more = [row_sum(term) for term in terms]
                sizes = more if sizes is None else [held + term for held, term in zip(sizes, more)]
            found.extend((first_lane, segments[0], *item) for item in enumerate(sizes))

    run(top_cuts, top_grad, top_ins, top_outs, 0, 1)
    run(block_cuts, block_grad, block_ins, block_outs, len(top_cuts), BLOCKS)
    rows = lax.broadcasted_iota(jnp.int32, sums.shape, 0)
    lanes = lax.broadcasted_iota(jnp.int32, sums.shape, 1)
    result = jnp.where((rows == 2) & (lanes == 0), loss[...], 0.0)
    for first, segment, row, value in found:
        for part in range(value.shape[0]):
            lane = first + part * len(block_cuts) + segment
            here = (rows == row) & (lanes == lane)
            result = result + jnp.where(here, value[part : part + 1], 0.0)
    sums[...] = result


def directions(cuts, rows, moves, gain_at, late, loss, top_ins, block_ins):
    shapes = [f32(*top_ins[0].shape)] * 3 + [f32(*block_ins[0].shape)] * 3
    ins = [*rows, late, loss, *top_ins, *block_ins]
    return pl.pallas_call(
        functools.partial(direction_kernel, cuts, moves, gain_at),
        out_shape=[f32(8, ROWS)] + shapes,
        in_specs=in_vmem(len(ins)),
        out_specs=in_vmem(7),
        scratch_shapes=[
            pltpu.VMEM(top_ins[0].shape, jnp.float32),
            pltpu.VMEM(block_ins[0].shape, jnp.float32),
        ],
        compiler_params=pltpu.CompilerParams(vmem_limit_bytes=VMEM_LIMIT),
        cost_estimate=LIGHT,
        name="directions",
    )(*ins)


def update_kernel(cuts, sums, *refs):
    top_cuts, block_cuts = cuts
    top_ins, block_ins, refs = (refs[:3], refs[3:6], refs[6:])
    norms, *refs = refs
    top_outs, block_outs = (refs[:3], refs[3:])
    norm = jnp.sqrt(sums[...])
    norms[...] = norm
    ratio = LEARNING_RATE * (norm[0:1] / (norm[1:2] + 1e-06))
    decay = average_decay()

    def work(lanes, ins, outs, scale):
        param, direction, average = [ref[:, lanes] for ref in ins]
        updated, half, averaged = outs
        value = param - scale * direction
        updated[:, lanes] = value
        half[:, lanes] = value.astype(jnp.bfloat16)
        averaged[:, lanes] = decay * average + (1.0 - decay) * value

    def run(cuts, ins, outs, scales):
        for start, size, segments in stretches(cuts):
            scale = scales[segments[0]]

            def step(lanes, carry):
                work(lanes, ins, outs, scale)
                return carry

            _, begin, rest = sweep(start, size, step, 0)
            if rest:
                if len(segments) > 1:
                    at = begin + lax.broadcasted_iota(jnp.int32, (1, rest), 1)
                    scale = jnp.where(at < cuts[segments[1]][0], scale, scales[segments[1]])
                work(pl.ds(begin, rest), ins, outs, scale)

    lanes = [ratio[:, lane : lane + 1] for lane in range(len(top_cuts) + BLOCKS * len(block_cuts))]
    run(top_cuts, top_ins, top_outs, lanes[: len(top_cuts)])
    rest = lanes[len(top_cuts) :]
    scales = [jnp.concatenate(rest[index :: len(block_cuts)]) for index in range(len(block_cuts))]
    run(block_cuts, block_ins, block_outs, scales)


def update(cuts, sums, top_ins, block_ins):
    shapes = []
    for array in (top_ins[0], block_ins[0]):
        shapes += [f32(*array.shape), bf16(*array.shape), f32(*array.shape)]
    return pl.pallas_call(
        functools.partial(update_kernel, cuts),
        out_shape=[f32(8, ROWS)] + shapes,
        in_specs=in_vmem(7),
        out_specs=in_vmem(7),
        compiler_params=pltpu.CompilerParams(vmem_limit_bytes=VMEM_LIMIT),
        cost_estimate=LIGHT,
        name="update",
    )(sums, *top_ins, *block_ins)


def segment_lengths():
    top = [PATCH_IN * D, D * PIX, D * DPROJ, DPROJ * GAMES * PLAYS]
    block = [D * BOT, 9 * BOT * BOT, BOT * D, 2 * (2 * BOT + D)]
    return (top, block)


def cut_points(lengths, devices):
    cuts = []
    offset = 0
    for length in lengths:
        width = length // devices
        cuts.append((offset, width))
        offset += width
    return cuts


def pack_top(flat, cuts):
    patch, pool, proj, heads = [flat[start : start + size] for start, size in cuts]
    patch = patch.reshape(-1, 2, 2, WIDTH).transpose(2, 1, 0, 3).reshape(2, -1, WIDTH)
    pool = jnp.pad(pool.reshape(1, -1, PIX), ((0, 0), (0, 0), (0, ROWS - PIX)))
    heads = jnp.pad(heads.reshape(-1, GAMES, PLAYS), ((0, 0), (0, 0), (0, 2 * WIDTH - PLAYS)))
    heads = heads.reshape(-1, 2 * GAMES, WIDTH).transpose(1, 0, 2)
    return [patch, pool, proj.reshape(1, -1, WIDTH), heads]


def flat_late(pool, proj, heads):
    heads = heads.transpose(1, 0, 2).reshape(-1, GAMES, 2 * WIDTH)[:, :, :PLAYS]
    return jnp.concatenate([item.reshape(-1) for item in (pool[:, :, :PIX], proj, heads)])


def pack_block(flat, cuts):
    w_in, w_mid, w_out = [flat[start : start + size] for start, size in cuts[:3]]
    w_out = w_out.reshape(-1, D // BOT, BOT).transpose(1, 0, 2)
    return [w_in.reshape(1, -1, BOT), w_mid.reshape(1, -1, BOT), w_out]


def parts_for(devices):
    rows = {"patch": 2 * PATCH_IN, "pool": D, "proj": D, "heads": DPROJ}
    rows |= {"w_in": D, "w_mid": TAPS * BOT, "w_out": BOT, "gains": TILE * devices}
    blocks = {"patch": 2, "heads": 2 * GAMES, "w_out": D // BOT}
    return {
        name: Part(blocks.get(name, 1), count // devices, ROWS if name == "pool" else WIDTH)
        for name, count in rows.items()
    }


def is_tuned(devices):
    parts = parts_for(devices).values()
    whole = all(part.rows // part.across % TILE == 0 for part in parts)
    return whole and lax.axis_size("wide") == 8 and lax.axis_size("narrow") == 4


def plain_gather(piece):
    return lax.all_gather(piece, AXES, axis=1, tiled=True)


def plain_scatter(array):
    return lax.psum_scatter(array, AXES, scatter_dimension=1, tiled=True).astype(jnp.float32)


def total(array):
    if lax.axis_size("wide") != 8 or lax.axis_size("narrow") != 4:
        return lax.psum(array, AXES)
    array = array + hop(array, ACROSS)
    array = array + hop(array, (2, 2))
    array = array + hop(array, (1, 1))
    one, two, three = [hop(array, ALONG_Z, step) for step in (1, 2, 3)]
    return (array + two) + (one + three)


def frame_rows(frames):
    count = frames.shape[0]
    return jnp.pad(frames, ((0, 0), (0, ROWS - PIX), (0, 0))).reshape(count * ROWS, PATCH_IN)


def on_device(
    observed,
    following,
    game_ids,
    actions,
    legal_mask,
    rewards,
    discounts,
    done_flags,
    params_top,
    params_blocks,
    first_top,
    first_blocks,
    second_top,
    second_blocks,
    average_top,
    average_blocks,
    target_top,
    target_blocks,
):
    devices = lax.axis_size(AXES)
    frames_all = observed.shape[0] * devices
    top_lengths, block_lengths = segment_lengths()
    top_cuts = cut_points(top_lengths, devices)
    block_cuts = cut_points(block_lengths, devices)
    gain_start, gain_width = block_cuts[3]
    parts = parts_for(devices)
    tuned = is_tuned(devices)
    place = spot()
    shift = shifts()
    spread = spread_pixels(devices)
    count = observed.shape[0]
    whole = jnp.concatenate([game_ids[:, None], actions], axis=1)
    whole = jnp.pad(whole, ((0, 8 - count), (0, ROWS - 3)), constant_values=-1)
    legal = jnp.pad(legal_mask, ((0, 8 - count), (0, ROWS - ACTIONS)), constant_values=1)
    keep = discounts * (1.0 - done_flags.astype(jnp.float32))
    real = jnp.pad(jnp.stack([rewards, keep], axis=1), ((0, 8 - count), (0, ROWS - 2)))

    def read_pieces(early):
        sources = (target_top, target_blocks, params_top, params_blocks)
        if early is not None:
            early, sources = together(early, sources)
        tops = (sources[0], sources[2].astype(jnp.bfloat16))
        blocks = (sources[1], sources[3].astype(jnp.bfloat16))
        own = {}
        for net, top, flat in zip(("target", "online"), tops, blocks):
            for name, piece in zip(("patch", "pool", "proj", "heads"), pack_top(top, top_cuts)):
                own[net, name] = piece
            for index in range(BLOCKS):
                for name, piece in zip(block_names, pack_block(flat[index], block_cuts)):
                    own[net, name, index] = piece
        gain_rows = jnp.concatenate(blocks)[:, gain_start:]
        own["gains",] = jnp.pad(
            gain_rows, ((0, TILE - 2 * BLOCKS), (0, WIDTH - gain_width))
        ).reshape(1, TILE, WIDTH)
        return [[own[key] for key in group] for group in keys]

    block_names = ("w_in", "w_mid", "w_out")

    def part_of(key):
        return parts[key[0] if key[0] in parts else key[1]]

    full = {}

    def block_weight(index, name):
        return merged(full["online", name, index]).reshape(-1, BOT)

    def top_weights(net):
        return (full[net, "pool"][0], full[net, "proj"][0], full[net, "heads"])

    def hold(net, index, group, buffers, state):
        full["held", index] = (group, buffers)
        return state

    def read_gains(group, buffers, state):
        gains = assemble(group_parts(group), buffers, place, [0])[0] if tuned else buffers[0]
        gains = gains.reshape(devices, TILE, WIDTH)[:, : 2 * BLOCKS, :gain_width]
        gains = gains.transpose(1, 0, 2).reshape(2 * BLOCKS, -1).astype(jnp.float32)
        return run_block("target", 0, group, buffers, state | {"gains": gains})

    def keep_ends(net, group, buffers, state):
        arrays = assemble(group_parts(group), buffers, place) if tuned else buffers
        full.update(zip(keys[group], arrays))
        if net == "target":
            for index in range(1, BLOCKS):
                state = run_block(net, index, *full["held", index], state)
            stream = state.pop("stream")
            state |= {"target": head_target(stream, *top_weights(net), whole, real)}
        return state

    def run_block(net, index, group, buffers, state):
        keep = net == "online"
        row = index + (BLOCKS if keep else 0)
        gain = state["gains"][row : row + 1]
        stream = [state["pixels" if keep else "following"], spread]
        if index:
            stream = [state["stream"]]
        skip = 1 if keys[group][0] == ("gains",) else 0
        out, *kept = block_forward(
            stream, gain, shift, group_parts(group), skip, buffers, place, keep, tuned
        )
        state = state | {"stream": out}
        if keep:
            start = kept.pop(0) if index == 0 else stream[0]
            full.update(zip([(net, name, index) for name in block_names], kept[-3:]))
            state |= {"kept%d" % index: [start, *kept[:-3]]}
        return state

    keys, then = ([], [])
    ends = ("pool", "proj", "heads")

    def add_group(group, run, *names):
        keys.append(group)
        then.append(functools.partial(run, *names))

    def block_keys(net, index):
        return [(net, name, index) for name in block_names]

    for index in range(1, BLOCKS):
        add_group(block_keys("target", index), hold, "target", index)
    add_group([("gains",), ("target", "patch")] + block_keys("target", 0), read_gains)
    add_group([("target", name) for name in ends], keep_ends, "target")
    for index in range(BLOCKS):
        start = [] if index else [("online", "patch")]
        add_group(start + block_keys("online", index), run_block, "online", index)
    add_group([("online", name) for name in ends], keep_ends, "online")

    def group_parts(group):
        return [part_of(key) for key in keys[group]]

    def arrived(group, buffers, state):
        return then[group](group, buffers, dict(state))

    state = {"following": frame_rows(following), "pixels": frame_rows(observed)}
    if tuned:
        groups = [group_parts(group) for group in range(len(keys))]
        state = pipelined_gather(groups, read_pieces, place, state, arrived)
    else:
        for group, items in enumerate(read_pieces(None)):
            state = arrived(group, [plain_gather(item) for item in items], state)

    keys = []
    steps = []

    def loss_step(group, state):
        (loss, dstream), dealt = head_loss(
            state.pop("stream"), *top_weights("online"), state.pop("target"), whole, legal, frames_all,
            group, tuned, place,
        )
        return (dealt, state | {"loss": loss, "grad": dstream})

    def out_inputs(index, state):
        stream, hid_one, hid_two, hid_three, rstd = state["kept%d" % index]
        gain = state["gains"][BLOCKS + index : BLOCKS + index + 1]
        return [stream, hid_two, hid_three, rstd, block_weight(index, "w_out"), gain]

    def out_step(index, group, state):
        (dres, low, late), dealt = back_out(
            state["grad"], *out_inputs(index, state), group, tuned, place
        )
        return (dealt, state | {"grad": dres, "low": low, "late%d" % index: late})

    def mid_step(index, group, state):
        stream, hid_one, hid_two, hid_three, rstd = state["kept%d" % index]
        gain = state["gains"][BLOCKS + index : BLOCKS + index + 1]
        (low, early), dealt = back_mid(
            state["low"], hid_one, rstd, block_weight(index, "w_mid"), gain, shift, group, tuned, place
        )
        return (dealt, state | {"low": low, "early%d" % index: early})

    def between_step(index, group, state):
        stream = state.pop("kept%d" % index)[0]
        (dres, low, late), dealt = back_between(
            state["low"], stream, state["grad"], block_weight(index, "w_in"),
            out_inputs(index - 1, state), group, tuned, place,
        )
        return (dealt, state | {"grad": dres, "low": low, "late%d" % (index - 1): late})

    def first_step(group, state):
        stream = state.pop("kept0")[0]
        dgains = [
            jnp.concatenate([state.pop("early%d" % index), state.pop("late%d" % index)], axis=1)
            for index in range(BLOCKS)
        ]
        dgains = jnp.concatenate(dgains).reshape(BLOCKS, devices, gain_width).transpose(1, 0, 2)
        dgains = jnp.pad(dgains, ((0, 0), (0, TILE - BLOCKS), (0, WIDTH - gain_width)))
        dgains = dgains.reshape(1, -1, WIDTH).astype(jnp.bfloat16)
        dealt = back_first(
            state.pop("low"), stream, state.pop("grad"), block_weight(0, "w_in"),
            state.pop("pixels"), spread, dgains, group, tuned, place,
        )
        return (dealt, state)

    def add_step(group, run, *names):
        keys.append(group)
        steps.append(
            lambda state: run(*names, [parts[key[0]] for key in group], dict(state))
        )

    add_step([("heads",), ("proj",), ("pool",)], loss_step)
    add_step([("w_out", BLOCKS - 1)], out_step, BLOCKS - 1)
    for index in reversed(range(BLOCKS)):
        add_step([("w_mid", index)], mid_step, index)
        if index:
            add_step([("w_in", index), ("w_out", index - 1)], between_step, index)
    add_step([("w_in", 0), ("patch",), ("gains",)], first_step)
    groups = [[parts[key[0]] for key in group] for group in keys]
    if tuned:
        mine, state = pipelined_scatter(groups, place, state, steps)
    else:
        mine = []
        for group, step in zip(groups, steps):
            arrays, state = step(state)
            mine.append(pack(group, [plain_scatter(array) for array in arrays]))
    loss_part = state["loss"]
    at = {}
    moves = []
    for number, group in enumerate(keys):
        first = 0
        steps = []
        for key in group:
            count = parts[key[0]].travel
            at[key] = (number, first)
            if len(key) > 1:
                start = block_cuts[block_names.index(key[0])][0]
                steps.append((key[1], block_rows(key[0], start, count, first)))
            elif key[0] == "patch":
                steps.append((None, patch_rows(count, first)))
            first += count
        moves.append(steps)
    late = []
    for name in ("pool", "proj", "heads"):
        number, first = at[name,]
        late.append(parts[name].unpack(mine[number][first : first + parts[name].travel]))
    late = flat_late(*late)[None]
    cuts = (top_cuts, block_cuts)
    tops = [array[None] for array in (params_top, first_top, second_top, average_top)]
    sums, *made = directions(
        cuts, mine[1:], moves[1:], (at["gains",][0] - 1, at["gains",][1]), late, loss_part,
        tops[:3], [params_blocks, first_blocks, second_blocks],
    )
    momentum_top, variance_top, direction_top, momentum_blocks, variance_blocks, direction_blocks = made
    sums = total(sums)
    norms, *made = update(
        cuts, sums, [tops[0], direction_top, tops[3]],
        [params_blocks, direction_blocks, average_blocks],
    )
    updated_top, half_top, averaged_top, updated_blocks, half_blocks, averaged_blocks = made
    loss_total = sums[2, 0]
    matrix_norms = norms[:2, : len(top_cuts) + BLOCKS * len(block_cuts)]
    number, first = at["gains",]
    gain_grads = mine[number][first : first + BLOCKS, :gain_width]
    return (
        loss_total,
        matrix_norms,
        updated_top[0],
        half_top[0],
        momentum_top[0],
        variance_top[0],
        averaged_top[0],
        updated_blocks,
        half_blocks,
        momentum_blocks,
        variance_blocks,
        averaged_blocks,
        gain_grads,
    )


def solution(mesh):
    one = P(AXES)
    flat = P(None, AXES)
    return jax.shard_map(
        on_device,
        mesh=mesh,
        in_specs=(P(AXES, None, None),) * 2
        + (one, P(AXES, None), P(AXES, None))
        + (one,) * 3
        + (one, flat) * 5,
        out_specs=(P(), P()) + (one,) * 5 + (flat,) * 6,
        check_vma=False,
    )
```

```python
import functools
import itertools

import jax
import jax.numpy as jnp
from jax import lax
from jax.experimental import pallas as pl
from jax.experimental.pallas import tpu as pltpu
from jax.sharding import PartitionSpec as P

D = 2048
BOT = 512
GROUPS = 32
SIDE = 11
PIX = 121
TAPS = 9

ROWS = 128
LANES = 512
VMEM_LIMIT = 60 * 1024 * 1024
LIGHT = pl.CostEstimate(flops=1024, bytes_accessed=1024, transcendentals=0)


def shifts():
    pixel = jnp.arange(ROWS)
    row, col = (pixel // SIDE, pixel % SIDE)
    mats = []
    for tap in range(TAPS):
        at_row, at_col = (row + tap // 3 - 1, col + tap % 3 - 1)
        inside = (at_row >= 0) & (at_row < SIDE) & (at_col >= 0) & (at_col < SIDE) & (pixel < PIX)
        mats.append((inside[:, None] & (pixel[None, :] == (at_row * SIDE + at_col)[:, None])))
    return jnp.concatenate(mats, axis=0).astype(jnp.bfloat16)


def dot(left, right):
    return jnp.dot(left, right, preferred_element_type=jnp.float32)


def dot_rows(left, right):
    return lax.dot_general(
        left, right, (((0,), (0,)), ((), ())), preferred_element_type=jnp.float32
    )


def dot_lanes(left, right):
    return lax.dot_general(
        left, right, (((1,), (1,)), ((), ())), preferred_element_type=jnp.float32
    )


def each_chunk(count, chans, body, unroll=1):
    per = chans // LANES

    def step(index, carry):
        frame = index // per
        rows = pl.ds(pl.multiple_of(frame * ROWS, ROWS), ROWS)
        lanes = pl.ds(pl.multiple_of((index % per) * LANES, LANES), LANES)
        body(pl.ds(frame, 1), rows, lanes)
        return carry

    lax.fori_loop(0, count * per, step, 0, unroll=unroll)


def real_rows():
    return lax.broadcasted_iota(jnp.int32, (ROWS, LANES), 0) < PIX


def group_mean(sums):
    chans = sums.shape[1]
    width = chans // GROUPS
    lane = lax.broadcasted_iota(jnp.int32, sums.shape, 1)
    step = 1
    while step < width:
        ahead = pltpu.roll(sums, chans - step, 1)
        behind = pltpu.roll(sums, step, 1)
        sums = sums + jnp.where((lane & step) == 0, ahead, behind)
        step *= 2
    return sums * (1.0 / (PIX * width))


def silu(value):
    return value / (1.0 + jnp.exp(-value))


def silu_slope(value):
    gate = 1.0 / (1.0 + jnp.exp(-value))
    return gate * (1.0 + value * (1.0 - gate))


def normalise(count, chans, hid, sums, rstd, rstd_at):
    whole = pl.ds(0, chans)
    sums[:, whole] = jnp.zeros((sums.shape[0], chans), jnp.float32)

    def add(frame, rows, lanes):
        sums[frame, lanes] = jnp.sum(hid[rows, lanes], axis=0, keepdims=True)

    each_chunk(count, chans, add, unroll=2)
    sums[:, whole] = group_mean(sums[:, whole])

    def center(frame, rows, lanes):
        value = jnp.where(real_rows(), hid[rows, lanes] - sums[frame, lanes], 0.0)
        hid[rows, lanes] = value
        sums[frame, lanes] = jnp.sum(value * value, axis=0, keepdims=True)

    each_chunk(count, chans, center, unroll=2)
    at = pl.ds(rstd_at, chans)
    rstd[:, at] = lax.rsqrt(group_mean(sums[:, whole]) + 1e-05)


def forward_kernel(count, keep, parts, skip, tuned, *refs):
    refs = list(refs)
    number = len(parts) - skip
    first = number > 3

    def take(number):
        taken = refs[:number]
        del refs[:number]
        return taken

    (place,) = take(1)
    x = take(2 if first else 1)
    gains, shift = take(2)
    sources = take(4 if tuned else len(parts))
    (out,) = take(1)
    if keep:
        if first:
            (start,) = take(1)
        hid_one, hid_two, hid_three, rstd = take(4)
        kept_weights = take(3)
    weights = take(number)
    sems, back_sems, low, act, cols, sums = take(6)
    if not keep:
        hid_one, hid_two, hid_three, rstd = take(4)
        if first:
            (start,) = take(1)
    fetch(parts, tuned, place, sources, dict(enumerate(weights, skip)), sems)

    def arrived(index):
        weight = weights[index]
        pltpu.make_async_copy(weight, weight, sems.at[len(parts) + index]).wait()
        if keep and index >= -3:
            pltpu.make_async_copy(weight, kept_weights[index], back_sems.at[3 + index]).start()
        return weight

    def whole(value):
        return value.reshape(-1, value.shape[-1])

    if first:
        pixels, spread = x
        x = start
        patch = arrived(-4)
        for half in range(2):
            wide = dot(pixels[...], spread[half]).astype(jnp.bfloat16)
            for block in range(2):
                lanes = pl.ds((2 * half + block) * WIDTH, WIDTH)
                x[:, lanes] = dot(wide, whole(patch[block]))
    else:
        (x,) = x

    def cast(frame, rows, lanes):
        low[rows, lanes] = x[rows, lanes].astype(jnp.bfloat16)

    def activate(hid, at, offset):
        def body(frame, rows, lanes):
            gain = gains[:, pl.ds(offset + lanes.start, LANES)]
            bias = gains[:, pl.ds(offset + BOT + lanes.start, LANES)]
            value = hid[rows, lanes] * rstd[frame, pl.ds(at + lanes.start, LANES)]
            hid[rows, lanes] = value
            value = jnp.where(real_rows(), silu(value * gain + bias), 0.0)
            act[rows, lanes] = value.astype(jnp.bfloat16)

        return body

    each_chunk(count, D, cast)
    hid_one[...] = dot(low[...], whole(arrived(-3)[...]))
    normalise(count, BOT, hid_one, sums, rstd, 0)
    each_chunk(count, BOT, activate(hid_one, 0, 0))
    for frame in range(count):
        rows = pl.ds(frame * ROWS, ROWS)
        for tap in range(TAPS):
            picked = dot(shift[pl.ds(tap * ROWS, ROWS), :], act[rows, :])
            cols[rows, pl.ds(tap * BOT, BOT)] = picked.astype(jnp.bfloat16)
    hid_two[...] = dot(cols[...], whole(arrived(-2)[...]))
    normalise(count, BOT, hid_two, sums, rstd, BOT)
    each_chunk(count, BOT, activate(hid_two, BOT, 2 * BOT))
    w_out = arrived(-1)
    for part in range(D // BOT):
        hid_three[:, pl.ds(part * BOT, BOT)] = dot(act[...], whole(w_out[part]))
    normalise(count, D, hid_three, sums, rstd, 2 * BOT)

    def finish(frame, rows, lanes):
        gain = gains[:, pl.ds(4 * BOT + lanes.start, LANES)]
        bias = gains[:, pl.ds(4 * BOT + D + lanes.start, LANES)]
        value = hid_three[rows, lanes] * rstd[frame, pl.ds(2 * BOT + lanes.start, LANES)]
        if keep:
            hid_three[rows, lanes] = value
        value = silu(x[rows, lanes] + value * gain + bias)
        out[rows, lanes] = jnp.where(real_rows(), value, 0.0)

    each_chunk(count, D, finish)
    if keep:
        for index in (-3, -2, -1):
            pltpu.make_async_copy(weights[index], kept_weights[index], back_sems.at[3 + index]).wait()


def f32(*shape):
    return jax.ShapeDtypeStruct(shape, jnp.float32)


def bf16(*shape):
    return jax.ShapeDtypeStruct(shape, jnp.bfloat16)


def stat_rows(count):
    return -(-count // 8) * 8


def block_forward(stream, gains, shift, parts, skip, buffers, place, keep, tuned):
    first = len(parts) - skip > 3
    rows = stream[0].shape[0]
    count = rows // ROWS
    stats = stat_rows(count)
    kept = [
        ((rows, BOT), jnp.float32),
        ((rows, BOT), jnp.float32),
        ((rows, D), jnp.float32),
        ((stats, 2 * BOT + D), jnp.float32),
    ]
    start = [((rows, D), jnp.float32)] if first else []
    weights = weight_shapes(parts, buffers, tuned)[skip:]
    out_shape = [f32(rows, D)]
    out_specs = in_vmem(1)
    scratch = [pltpu.VMEM(shape, jnp.bfloat16) for shape in weights]
    scratch += [
        pltpu.SemaphoreType.DMA((len(parts),)),
        pltpu.SemaphoreType.DMA((3,)),
        pltpu.VMEM((rows, D), jnp.bfloat16),
        pltpu.VMEM((rows, BOT), jnp.bfloat16),
        pltpu.VMEM((rows, TAPS * BOT), jnp.bfloat16),
        pltpu.VMEM((stats, D), jnp.float32),
    ]
    if keep:
        out_shape += [jax.ShapeDtypeStruct(*item) for item in start + kept]
        out_shape += [jax.ShapeDtypeStruct(shape, jnp.bfloat16) for shape in weights[-3:]]
        out_specs += in_vmem(len(start + kept)) + hbm(3)
    else:
        scratch += [pltpu.VMEM(*item) for item in kept + start]
    return pl.pallas_call(
        functools.partial(forward_kernel, count, keep, parts, skip, tuned),
        out_shape=out_shape,
        in_specs=in_smem() + in_vmem(len(stream) + 2) + hbm(len(buffers)),
        out_specs=out_specs,
        scratch_shapes=scratch,
        compiler_params=pltpu.CompilerParams(vmem_limit_bytes=VMEM_LIMIT),
        cost_estimate=LIGHT,
        name="block_forward",
    )(place, *stream, gains, shift, *buffers)


def norm_back(count, chans, slope, hid, sums, more, rstd, rstd_at, gain, grad_gain, grad_bias, store):
    whole = pl.ds(0, chans)
    sums[:, whole] = jnp.zeros((sums.shape[0], chans), jnp.float32)
    more[:, whole] = jnp.zeros((sums.shape[0], chans), jnp.float32)

    def add(frame, rows, lanes):
        value = slope(frame, rows, lanes)
        sums[frame, lanes] = jnp.sum(value, axis=0, keepdims=True)
        more[frame, lanes] = jnp.sum(value * hid[rows, lanes], axis=0, keepdims=True)

    each_chunk(count, chans, add)
    grad_bias[...] = jnp.sum(sums[:, whole], axis=0, keepdims=True)
    grad_gain[...] = jnp.sum(more[:, whole], axis=0, keepdims=True)
    sums[:, whole] = group_mean(sums[:, whole] * gain[...])
    more[:, whole] = group_mean(more[:, whole] * gain[...])

    def spread(frame, rows, lanes):
        store(
            rows,
            lanes,
            lambda value: jnp.where(
                real_rows(),
                rstd[frame, pl.ds(rstd_at + lanes.start, LANES)]
                * (value * gain[:, lanes] - sums[frame, lanes] - hid[rows, lanes] * more[frame, lanes]),
                0.0,
            ).astype(jnp.bfloat16),
        )

    each_chunk(count, chans, spread)


def back_out_body(count, grad, x, hid_two, hid_three, rstd, w_out, gains, dres, dlow, dgains, scratch, dw_out):
    third, act, dact, sums, more = scratch
    gain_three, bias_three = (gains.at[:, pl.ds(4 * BOT, D)], gains.at[:, pl.ds(4 * BOT + D, D)])

    def slope_three(frame, rows, lanes):
        value = x[rows, lanes] + hid_three[rows, lanes] * gain_three[:, lanes] + bias_three[:, lanes]
        value = jnp.where(real_rows(), grad[rows, lanes] * silu_slope(value), 0.0)
        dres[rows, lanes] = value
        return value

    def store_three(rows, lanes, back):
        third[rows, lanes] = back(dres[rows, lanes])

    norm_back(
        count, D, slope_three, hid_three, sums, more, rstd, 2 * BOT, gain_three,
        dgains.at[:, pl.ds(2 * BOT, D)], dgains.at[:, pl.ds(2 * BOT + D, D)], store_three,
    )
    total = None
    for part in range(D // BOT):
        lanes = pl.ds(part * BOT, BOT)
        term = dot_lanes(third[:, lanes], w_out[lanes, :])
        total = term if total is None else total + term
    dact[...] = total
    gain_two, bias_two = (gains.at[:, pl.ds(2 * BOT, BOT)], gains.at[:, pl.ds(3 * BOT, BOT)])

    def slope_two(frame, rows, lanes):
        value = hid_two[rows, lanes] * gain_two[:, lanes] + bias_two[:, lanes]
        gate = 1.0 / (1.0 + jnp.exp(-value))
        act[rows, lanes] = jnp.where(real_rows(), value * gate, 0.0).astype(jnp.bfloat16)
        value = dact[rows, lanes] * (gate * (1.0 + value * (1.0 - gate)))
        value = jnp.where(real_rows(), value, 0.0)
        dact[rows, lanes] = value
        return value

    def store_two(rows, lanes, back):
        dlow[rows, lanes] = back(dact[rows, lanes])

    norm_back(
        count, BOT, slope_two, hid_two, sums, more, rstd, BOT, gain_two,
        dgains.at[:, pl.ds(0, BOT)], dgains.at[:, pl.ds(BOT, BOT)], store_two,
    )
    for part in range(D // BOT):
        lanes = pl.ds(part * BOT, BOT)
        dw_out[part] = dot_rows(act[...], third[:, lanes]).astype(jnp.bfloat16)


def out_scratch(rows):
    stats = stat_rows(rows // ROWS)
    return [
        pltpu.VMEM((rows, D), jnp.bfloat16),
        pltpu.VMEM((rows, BOT), jnp.bfloat16),
        pltpu.VMEM((rows, BOT), jnp.float32),
        pltpu.VMEM((stats, D), jnp.float32),
        pltpu.VMEM((stats, D), jnp.float32),
    ]


def back_mid_body(count, grad, hid_one, rstd, w_mid, gains, shift, dlow, dgains, scratch, dw_mid):
    act, cols, dact, sums, more = scratch
    gain_one, bias_one = (gains.at[:, pl.ds(0, BOT)], gains.at[:, pl.ds(BOT, BOT)])
    for frame in range(count):
        rows = pl.ds(frame * ROWS, ROWS)
        for tap in range(TAPS):
            picked = dot(shift[pl.ds((TAPS - 1 - tap) * ROWS, ROWS), :], grad[rows, :])
            cols[rows, pl.ds(tap * BOT, BOT)] = picked.astype(jnp.bfloat16)
    total = None
    for tap in range(TAPS):
        lanes = pl.ds(tap * BOT, BOT)
        term = dot_lanes(cols[:, lanes], w_mid[lanes, :])
        total = term if total is None else total + term
    dact[...] = total

    def slope_one(frame, rows, lanes):
        value = hid_one[rows, lanes] * gain_one[:, lanes] + bias_one[:, lanes]
        gate = 1.0 / (1.0 + jnp.exp(-value))
        act[rows, lanes] = jnp.where(real_rows(), value * gate, 0.0).astype(jnp.bfloat16)
        value = dact[rows, lanes] * (gate * (1.0 + value * (1.0 - gate)))
        value = jnp.where(real_rows(), value, 0.0)
        dact[rows, lanes] = value
        return value

    def store_one(rows, lanes, back):
        dlow[rows, lanes] = back(dact[rows, lanes])

    norm_back(
        count, BOT, slope_one, hid_one, sums, more, rstd, 0, gain_one,
        dgains.at[:, pl.ds(0, BOT)], dgains.at[:, pl.ds(BOT, BOT)], store_one,
    )
    for tap in range(TAPS):
        lanes = pl.ds(tap * BOT, BOT)
        dw_mid[0, lanes, :] = dot_rows(act[...], cols[:, lanes]).astype(jnp.bfloat16)


def back_in_body(count, grad, x, dres, w_in, dx, low, dw_in):
    def cast(frame, rows, lanes):
        low[rows, lanes] = x[rows, lanes].astype(jnp.bfloat16)

    each_chunk(count, D, cast)
    for part in range(D // BOT):
        lanes = pl.ds(part * BOT, BOT)
        dx[:, lanes] = dres[:, lanes] + dot_lanes(grad[...], w_in[lanes, :])
        dw_in[0, lanes, :] = dot_rows(low[:, lanes], grad[...]).astype(jnp.bfloat16)


def back_kernel(body, parts, tuned, counts, *refs):
    place, refs = (refs[0], list(refs[1:]))
    groups = []
    for number in (*counts[:2], len(dealt_shapes(parts, tuned)), len(parts), 1, counts[2]):
        groups.append(refs[:number])
        refs = refs[number:]
    ins, outs, dealt, made, sems, scratch = groups

    def done(index):
        start_deal(parts, tuned, place, index, made, dealt, sems[0])

    body(ins, outs, made, scratch, done)
    for index, array in enumerate(made):
        pltpu.make_async_copy(array, array, sems[0].at[index]).wait()


def back_call(name, body, ins, out_shape, scratch, parts, tuned, place):
    dealt = dealt_shapes(parts, tuned)
    counts = (len(ins), len(out_shape), len(scratch))
    outs = pl.pallas_call(
        functools.partial(back_kernel, body, parts, tuned, counts),
        out_shape=out_shape + [bf16(*shape) for shape in dealt],
        in_specs=in_smem() + in_vmem(len(ins)),
        out_specs=in_vmem(len(out_shape)) + hbm(len(dealt)),
        scratch_shapes=[pltpu.VMEM(whole_shape(part), jnp.bfloat16) for part in parts]
        + [pltpu.SemaphoreType.DMA((len(parts),))]
        + scratch,
        compiler_params=pltpu.CompilerParams(vmem_limit_bytes=VMEM_LIMIT),
        cost_estimate=LIGHT,
        name=name,
    )(place, *ins)
    return (list(outs[: len(out_shape)]), list(outs[len(out_shape) :]))


def back_out(grad, stream, hid_two, hid_three, rstd, w_out, gains, dpool, parts, tuned, place):
    rows = stream.shape[0]

    def body(ins, outs, made, scratch, done):
        made[1][...] = ins[7][...]
        done(1)
        back_out_body(rows // ROWS, *ins[:7], *outs, scratch, made[0])
        done(0)

    ins = [grad, stream, hid_two, hid_three, rstd, w_out, gains, dpool]
    out_shape = [f32(rows, D), bf16(rows, BOT), f32(1, 2 * BOT + 2 * D)]
    return back_call("back_out", body, ins, out_shape, out_scratch(rows), parts, tuned, place)


def back_mid(grad, hid_one, rstd, w_mid, gains, shift, parts, tuned, place):
    rows = grad.shape[0]
    stats = stat_rows(rows // ROWS)

    def body(ins, outs, made, scratch, done):
        back_mid_body(rows // ROWS, *ins, *outs, scratch, made[0])
        done(0)

    scratch = [
        pltpu.VMEM((rows, BOT), jnp.bfloat16),
        pltpu.VMEM((rows, TAPS * BOT), jnp.bfloat16),
        pltpu.VMEM((rows, BOT), jnp.float32),
        pltpu.VMEM((stats, BOT), jnp.float32),
        pltpu.VMEM((stats, BOT), jnp.float32),
    ]
    ins = [grad, hid_one, rstd, w_mid, gains, shift]
    out_shape = [bf16(rows, BOT), f32(1, 2 * BOT)]
    return back_call("back_mid", body, ins, out_shape, scratch, parts, tuned, place)


def back_between(grad, stream, dres, w_in, later, parts, tuned, place):
    rows = stream.shape[0]

    def body(ins, outs, made, scratch, done):
        dx, low, *rest = scratch
        back_in_body(rows // ROWS, *ins[:4], dx, low, made[0])
        done(0)
        back_out_body(rows // ROWS, dx, *ins[4:], *outs, rest, made[1])
        done(1)

    scratch = [pltpu.VMEM((rows, D), jnp.float32), pltpu.VMEM((rows, D), jnp.bfloat16)]
    scratch += out_scratch(rows)
    ins = [grad, stream, dres, w_in, *later]
    out_shape = [f32(rows, D), bf16(rows, BOT), f32(1, 2 * BOT + 2 * D)]
    return back_call("back_between", body, ins, out_shape, scratch, parts, tuned, place)


def back_first(grad, stream, dres, w_in, pixels, spread, dgains, parts, tuned, place):
    rows = stream.shape[0]

    def body(ins, outs, made, scratch, done):
        dx, low = scratch
        made[2][...] = ins[6][...]
        done(2)
        back_in_body(rows // ROWS, *ins[:4], dx, low, made[0])
        done(0)
        wide = [dot(ins[4][...], ins[5][half]).astype(jnp.bfloat16) for half in range(2)]
        for block in range(2):
            total = None
            for half in range(2):
                lanes = pl.ds((2 * half + block) * WIDTH, WIDTH)
                term = dot_rows(wide[half], dx[:, lanes].astype(jnp.bfloat16))
                total = term if total is None else total + term
            made[1][block] = total.astype(jnp.bfloat16)
        done(1)

    scratch = [pltpu.VMEM((rows, D), jnp.float32), pltpu.VMEM((rows, D), jnp.bfloat16)]
    ins = [grad, stream, dres, w_in, pixels, spread, dgains]
    return back_call("back_first", body, ins, [], scratch, parts, tuned, place)[1]


def spread_pixels(devices):
    rows = PATCH_IN // devices
    value = jnp.arange(PATCH_IN)
    at = value // rows * 2 * rows + value % rows
    return jnp.stack(
        [jnp.arange(2 * PATCH_IN)[None, :] == (at + half * rows)[:, None] for half in range(2)]
    ).astype(jnp.bfloat16)


def merge(value):
    return value.reshape(-1, value.shape[-1])


def fetch_ends(parts, tuned, place, sources, weights, sems):
    first = len(parts) - 3
    fetch(parts, tuned, place, sources, dict(enumerate(weights, first)), sems)

    def arrived(index):
        weight = weights[index]
        pltpu.make_async_copy(weight, weight, sems.at[first + index]).wait()
        return weight

    return arrived


def head_forward(count, stream, arrived, games, pool_t, pooled):
    pool = merge(arrived(0)[...]).astype(jnp.float32)
    for part in range(D // ROWS):
        pool_t[:, pl.ds(part * ROWS, ROWS)] = pool[part * ROWS : (part + 1) * ROWS].T
    pooled[...] = jnp.zeros_like(pooled)

    def weigh(frame, rows, lanes):
        value = stream[rows, lanes].astype(jnp.bfloat16).astype(jnp.float32)
        pooled[frame, lanes] = jnp.sum(value * pool_t[:, lanes], axis=0, keepdims=True)

    each_chunk(count, D, weigh)
    before = dot(pooled[...].astype(jnp.bfloat16), merge(arrived(1)[...]))
    hidden = silu(before).astype(jnp.bfloat16)
    heads = arrived(2)
    scores = None
    for game in range(GAMES):
        pair = [dot(hidden, merge(heads[2 * game + half])) for half in range(2)]
        term = jnp.where(games == game, jnp.concatenate(pair, axis=1), 0.0)
        scores = term if scores is None else scores + term
    return ([pick_atoms(scores, action) for action in range(ACTIONS)], before, hidden)


def atom_lanes():
    return lax.broadcasted_iota(jnp.int32, (8, ROWS), 1)


def pick_atoms(scores, action):
    offset = action * ATOMS
    moved = pltpu.roll(scores, 2 * WIDTH - offset, 1) if offset else scores
    return jnp.where(atom_lanes() < ATOMS, moved[:, :ROWS], -1e30)


def support_lanes():
    return -10.0 + 20.0 / (ATOMS - 1) * atom_lanes().astype(jnp.float32)


def lane_sum(value):
    return jnp.sum(value, axis=1, keepdims=True)


def target_kernel(count, parts, tuned, place, stream, whole, real, *refs):
    sources, (out, *weights, sems, pool_t, pooled) = (refs[:-7], refs[-7:])
    arrived = fetch_ends(parts, tuned, place, sources, weights, sems)
    logits, _, _ = head_forward(count, stream, arrived, whole[:, 0:1], pool_t, pooled)
    chosen = None
    for action in range(ACTIONS):
        term = jnp.where(whole[:, 2:3] == action, logits[action], 0.0)
        chosen = term if chosen is None else chosen + term
    power = jnp.exp(chosen - jnp.max(chosen, axis=1, keepdims=True))
    probs = power / lane_sum(power)
    atoms = support_lanes()
    spacing = 20.0 / (ATOMS - 1)
    moved = jnp.clip(real[:, 0:1] + real[:, 1:2] * atoms, -10.0, 10.0)
    total = jnp.zeros_like(probs)
    for atom in range(ATOMS):
        near = 1.0 - jnp.abs(moved[:, atom : atom + 1] - atoms) / spacing
        total = total + probs[:, atom : atom + 1] * jnp.clip(near, 0.0, 1.0)
    inside = (atom_lanes() < ATOMS) & (lax.broadcasted_iota(jnp.int32, total.shape, 0) < count)
    out[...] = jnp.where(inside, total, 0.0)


def ends_scratch(parts, buffers, tuned):
    scratch = [pltpu.VMEM(shape, jnp.bfloat16) for shape in weight_shapes(parts, buffers, tuned)[-3:]]
    scratch += [pltpu.SemaphoreType.DMA((len(parts),))]
    return scratch + [pltpu.VMEM((ROWS, D), jnp.float32), pltpu.VMEM((8, D), jnp.float32)]


def head_target(stream, whole, real, parts, buffers, tuned, place):
    count = stream.shape[0] // ROWS
    return pl.pallas_call(
        functools.partial(target_kernel, count, parts, tuned),
        out_shape=f32(8, ROWS),
        in_specs=in_smem() + in_vmem(3) + hbm(len(buffers)),
        out_specs=in_vmem(1)[0],
        scratch_shapes=ends_scratch(parts, buffers, tuned),
        compiler_params=pltpu.CompilerParams(vmem_limit_bytes=VMEM_LIMIT),
        cost_estimate=LIGHT,
        name="head_target",
    )(place, stream, whole, real, *buffers)


def loss_kernel(count, frames_all, parts, tuned, place, stream, target, whole, legal, *refs):
    sources, refs = (refs[:-11], refs[-11:])
    loss, dstream, dpool, acts, *weights, sems, pool_t, pooled, dpooled = refs
    arrived = fetch_ends(parts, tuned, place, sources, weights, sems)
    _, proj, heads = weights
    games, taken = (whole[:, 0:1], whole[:, 1:2])
    logits, before, hidden = head_forward(count, stream, arrived, games, pool_t, pooled)
    atoms = support_lanes()
    inside = atom_lanes() < ATOMS
    logps, probs, values = ([], [], [])
    for value in logits:
        value = value - jnp.max(value, axis=1, keepdims=True)
        power = jnp.where(inside, jnp.exp(value), 0.0)
        mass = lane_sum(power)
        logps.append(value - jnp.log(mass))
        probs.append(power / mass)
        values.append(lane_sum(probs[-1] * atoms))
    masked = [
        jnp.where(legal[:, action : action + 1] > 0, values[action], -1e30)
        for action in range(ACTIONS)
    ]
    largest = functools.reduce(jnp.maximum, masked)
    powers = [jnp.exp(value - largest) for value in masked]
    mass = sum(powers[1:], powers[0])
    goal = target[...]
    goal_mass = lane_sum(goal)
    cross = taken_value = 0.0
    real = lax.broadcasted_iota(jnp.int32, (8, 1), 0) < count
    scale = jnp.where(real, 1.0 / frames_all, 0.0)
    spread = jnp.zeros((8, 2 * WIDTH), jnp.float32)
    for action in range(ACTIONS):
        here = jnp.where(taken == action, 1.0, 0.0)
        cross = cross - here * lane_sum(jnp.where(inside, goal * logps[action], 0.0))
        taken_value = taken_value + here * values[action]
        grad = here * (probs[action] * goal_mass - goal)
        pull = CQL_WEIGHT * (powers[action] / mass - here)
        grad = grad + pull * probs[action] * (atoms - values[action])
        grad = jnp.where(inside, grad * scale, 0.0)
        grad = jnp.concatenate([grad, jnp.zeros((8, 2 * WIDTH - ROWS), jnp.float32)], axis=1)
        offset = action * ATOMS
        spread = spread + (pltpu.roll(grad, offset, 1) if offset else grad)
    losses = cross + CQL_WEIGHT * (jnp.log(mass) + largest - taken_value)
    loss[...] = jnp.sum(jnp.where(real, losses, 0.0), axis=0, keepdims=True)
    dhidden = None
    spread = spread.astype(jnp.bfloat16)
    for game in range(GAMES):
        mine = jnp.where(games == game, spread, 0.0).astype(jnp.bfloat16)
        for half in range(2):
            part = mine[:, half * WIDTH : (half + 1) * WIDTH]
            term = dot_lanes(part, merge(heads[2 * game + half]))
            dhidden = term if dhidden is None else dhidden + term
    dbefore = (silu_slope(before) * dhidden).astype(jnp.bfloat16)
    pieces = [hidden, dbefore]
    pieces += [pooled[:, part * WIDTH : (part + 1) * WIDTH] for part in range(D // WIDTH)]
    lanes = lax.broadcasted_iota(jnp.int32, (8, WIDTH), 1)
    marked = jnp.where(lanes == WIDTH - 1, games.astype(jnp.float32), spread[:, WIDTH:].astype(jnp.float32))
    pieces += [spread[:, :WIDTH], marked]
    acts[...] = jnp.concatenate([piece.astype(jnp.float32) for piece in pieces]).astype(jnp.bfloat16)
    dpooled[...] = dot_lanes(dbefore, merge(proj[...])).astype(jnp.bfloat16).astype(jnp.float32)

    def push(frame, rows, lanes):
        dstream[rows, lanes] = dpooled[frame, lanes] * pool_t[:, lanes]

    each_chunk(count, D, push)

    def gather_pool(part, carry):
        lanes = pl.ds(pl.multiple_of(part * ROWS, ROWS), ROWS)
        total = None
        for frame in range(count):
            value = stream[pl.ds(frame * ROWS, ROWS), lanes].astype(jnp.bfloat16)
            term = value.astype(jnp.float32) * dpooled[pl.ds(frame, 1), lanes]
            total = term if total is None else total + term
        dpool[0, lanes, :] = total.T.astype(jnp.bfloat16)
        return carry

    lax.fori_loop(0, D // ROWS, gather_pool, 0)


def head_loss(stream, target, whole, legal, frames_all, parts, buffers, tuned, place):
    rows = stream.shape[0]
    return pl.pallas_call(
        functools.partial(loss_kernel, rows // ROWS, frames_all, parts, tuned),
        out_shape=[f32(1, 1), f32(rows, D), bf16(1, D, ROWS), bf16(ACTS, WIDTH)],
        in_specs=in_smem() + in_vmem(4) + hbm(len(buffers)),
        out_specs=in_vmem(4),
        scratch_shapes=ends_scratch(parts, buffers, tuned) + [pltpu.VMEM((8, D), jnp.float32)],
        compiler_params=pltpu.CompilerParams(vmem_limit_bytes=VMEM_LIMIT),
        cost_estimate=LIGHT,
        name="head_loss",
    )(place, stream, target, whole, legal, *buffers)


ACTS = 64


def own_heads_kernel(parts, tuned, place, *refs):
    sources, (heads, proj, acts, sems) = (refs[:-4], refs[-4:])
    fetch(parts, tuned, place, sources, {0: acts}, sems)
    pltpu.make_async_copy(acts, acts, sems.at[0]).wait()
    value = acts[...].reshape(-1, ACTS, WIDTH).astype(jnp.float32)
    pieces = [value[:, first : first + 8].reshape(-1, WIDTH) for first in range(0, ACTS, 8)]
    pieces = [piece.astype(jnp.bfloat16) for piece in pieces]
    hidden, dbefore, scores = (pieces[0], pieces[1], pieces[-2:])
    games = scores[1][:, WIDTH - 1 :].astype(jnp.float32)
    lanes = lax.broadcasted_iota(jnp.int32, scores[1].shape, 1)
    scores[1] = jnp.where(lanes < WIDTH - 1, scores[1].astype(jnp.float32), 0.0).astype(jnp.bfloat16)
    row = lax.broadcasted_iota(jnp.int32, (WIDTH, ROWS), 0)
    lane = lax.broadcasted_iota(jnp.int32, (WIDTH, ROWS), 1)

    def own(items, count):
        total = None
        for block, item in enumerate(items):
            wanted = (row + block * WIDTH == place[4] * count + lane) & (lane < count)
            term = dot(item, jnp.where(wanted, 1.0, 0.0).astype(jnp.bfloat16))
            total = term if total is None else total + term
        return total.astype(jnp.bfloat16)

    count = heads.shape[1]
    mine = own([hidden], count)
    for game in range(GAMES):
        for half in range(2):
            chosen = jnp.where(games == game, scores[half].astype(jnp.float32), 0.0)
            heads[2 * game + half] = dot_rows(mine, chosen.astype(jnp.bfloat16))[:count]
    count = proj.shape[1]
    proj[0] = dot_rows(own(pieces[2:-2], count), dbefore)[:count]


def own_heads(buffers, heads, proj, tuned, place):
    parts = [Part(1, ACTS, WIDTH)]
    return pl.pallas_call(
        functools.partial(own_heads_kernel, parts, tuned),
        out_shape=[f32(part.blocks, part.rows, part.lanes) for part in (heads, proj)],
        in_specs=in_smem() + hbm(len(buffers)),
        out_specs=in_vmem(2),
        scratch_shapes=[
            pltpu.VMEM(weight_shapes(parts, buffers, tuned)[0], jnp.bfloat16),
            pltpu.SemaphoreType.DMA((1,)),
        ],
        compiler_params=pltpu.CompilerParams(vmem_limit_bytes=VMEM_LIMIT),
        cost_estimate=LIGHT,
        name="own_heads",
    )(place, *buffers)


WIDTH = 512
TILE = 16
AXES = ("wide", "narrow")


def grid_sizes():
    return (lax.axis_size("wide") // 2, 2, lax.axis_size("narrow") // 2, 2)


def spot():
    sizes = grid_sizes()
    wide, narrow = (lax.axis_index("wide"), lax.axis_index("narrow"))
    place = [wide // sizes[1], wide % sizes[1], narrow // sizes[3], narrow % sizes[3]]
    return jnp.stack(place + [wide * lax.axis_size("narrow") + narrow]).astype(jnp.int32)


def hop(array, axis_of_core, step=1, swap=0):
    sizes = grid_sizes()

    def target(place):
        axis = axis_of_core[place[3]]
        other = list(place)
        other[axis] = place[axis] ^ swap if swap else (place[axis] + step) % sizes[axis]
        return other

    return send(array, target)


def flip(array, *bits):
    return send(array, lambda place: [value ^ bit for value, bit in zip(place, bits)])


def send(array, target):
    sizes = grid_sizes()
    pairs = []
    for place in itertools.product(*[range(size) for size in sizes]):
        pairs.append(
            tuple(
                ((z * sizes[1] + y) * sizes[2] + x) * sizes[3] + core
                for z, y, x, core in (place, target(place))
            )
        )
    return lax.ppermute(array, AXES, pairs)


ALONG_Z = (0, 0)
ACROSS = (3, 3)
NEAR = (2, 1)
FAR = (1, 2)


def hbm(number):
    return [pl.BlockSpec(memory_space=pl.ANY)] * number


def in_vmem(number):
    return [pl.BlockSpec(memory_space=pltpu.VMEM)] * number


def in_smem():
    return [pl.BlockSpec(memory_space=pltpu.SMEM)]


def copies(pairs, sems):
    started = [
        pltpu.make_async_copy(source, target, sems.at[index])
        for index, (source, target) in enumerate(pairs)
    ]
    for copy in started:
        copy.start()
    for copy in started:
        copy.wait()


class Part:
    def __init__(self, blocks, rows, lanes):
        self.blocks, self.rows, self.lanes = (blocks, rows, lanes)
        self.across = WIDTH // lanes
        self.travel = blocks * rows // self.across

    def moves(self):
        if self.across > 1:
            deep = self.rows // self.across
            return [(0, part * self.lanes, deep, 0, part * deep) for part in range(self.across)]
        return [(block * self.rows, 0, self.rows, block, 0) for block in range(self.blocks)]

    def pack(self, piece):
        if self.across > 1:
            piece = piece.reshape(self.across, self.rows // self.across, self.lanes)
            return piece.transpose(1, 0, 2).reshape(self.travel, WIDTH)
        return piece.reshape(self.travel, WIDTH)

    def unpack(self, rows):
        if self.across > 1:
            rows = rows.reshape(self.rows // self.across, self.across, self.lanes)
            return rows.transpose(1, 0, 2).reshape(1, self.rows, self.lanes)
        return rows.reshape(self.blocks, self.rows, self.lanes)

    def full(self, depth):
        return (self.blocks, depth, 2, 2, 2, self.rows, self.lanes)


def half_rows(parts):
    total = sum(part.travel for part in parts)
    return -(-total // (2 * TILE)) * TILE


def half_moves(parts):
    cut = half_rows(parts)
    halves = ([], [])
    offset = 0
    for index, part in enumerate(parts):
        for row, lane, rows, block, inner in part.moves():
            row = row + offset
            before = max(0, min(rows, cut - row))
            if before:
                halves[0].append((index, row, lane, before, block, inner))
            if rows - before:
                halves[1].append((index, row + before - cut, lane, rows - before, block, inner + before))
        offset += part.travel
    return halves


def unit(parts, depth):
    return (depth, 2, half_rows(parts), WIDTH)


def pack(parts, pieces):
    rows = jnp.concatenate([part.pack(piece) for part, piece in zip(parts, pieces)])
    return jnp.pad(rows, ((0, 2 * half_rows(parts) - rows.shape[0]), (0, 0)))


def assemble_pairs(parts, core, y, x, ins, outs):
    pairs = []
    for other, far, near in itertools.product((0, 1), repeat=3):
        half = core ^ other
        step = [0, 0, 0, 0]
        step[NEAR[half]], step[FAR[half]] = (near, far)
        at_y, at_x = (lax.rem(y + step[1], 2), lax.rem(x + step[2], 2))
        for index, row, lane, rows, block, inner in half_moves(parts)[half]:
            if index not in outs:
                continue
            pairs.append(
                (
                    index,
                    ins[2 * other + far].at[near, :, :, pl.ds(row, rows), pl.ds(lane, parts[index].lanes)],
                    outs[index].at[block, :, at_y, at_x, :, pl.ds(inner, rows)],
                )
            )
    return pairs


def fetch(parts, tuned, place, sources, weights, sems):
    if not tuned:
        for index, weight in weights.items():
            pltpu.make_async_copy(sources[index], weight, sems.at[index]).start()
        return
    for core in (0, 1):

        @pl.when(place[3] == core)
        def _():
            pairs = assemble_pairs(parts, core, place[1], place[2], sources, weights)
            for index, source, target in sorted(pairs, key=lambda pair: pair[0]):
                pltpu.make_async_copy(source, target, sems.at[index]).start()


def weight_shapes(parts, buffers, tuned):
    if tuned:
        return [part.full(buffers[0].shape[1]) for part in parts]
    return [item.shape for item in buffers]


def assemble_kernel(parts, some, place, *refs):
    outs, sems = (dict(zip(some, refs[4:-1])), refs[-1])
    fetch(parts, True, place, refs[:4], outs, sems)
    for index, out in outs.items():
        pltpu.make_async_copy(out, out, sems.at[index]).wait()


def assemble(parts, buffers, place, some=None):
    some = range(len(parts)) if some is None else some
    shapes = weight_shapes(parts, buffers, True)
    full = pl.pallas_call(
        functools.partial(assemble_kernel, parts, some),
        out_shape=[bf16(*shapes[index]) for index in some],
        in_specs=in_smem() + hbm(4),
        out_specs=in_vmem(len(some)),
        scratch_shapes=[pltpu.SemaphoreType.DMA((len(parts),))],
        compiler_params=pltpu.CompilerParams(vmem_limit_bytes=VMEM_LIMIT),
        cost_estimate=LIGHT,
        name="assemble",
    )(place, *buffers)
    return [merged(item) for item in full]


def merged(array):
    return array.reshape(array.shape[0], -1, array.shape[-1])


def in_order(own, other, bit):
    first = jnp.where(bit == 0, own, other)
    second = jnp.where(bit == 0, other, own)
    return jnp.stack([first, second])


def together(*trees):
    flat, tree = jax.tree.flatten(trees)
    return jax.tree.unflatten(tree, lax.optimization_barrier(flat))


def start_gather(groups, pieces, place):
    core = place[3]
    packed = [pack(parts, items) for parts, items in zip(groups, pieces)]
    halves = [half_rows(parts) for parts in groups]
    kept = [lax.dynamic_slice_in_dim(rows, core * half, half) for rows, half in zip(packed, halves)]
    sent = [
        lax.dynamic_slice_in_dim(rows, (1 - core) * half, half) for rows, half in zip(packed, halves)
    ]
    got = hop(jnp.concatenate(sent), ACROSS)
    held = []
    offset = 0
    for keep, half in zip(kept, halves):
        held.append(in_order(keep, got[offset : offset + half], core))
        offset += half
    return held


def pipelined_gather(groups, pieces, place, state, arrived):
    count = len(groups)
    low, high = (place[0] % 2, place[0] // 2)
    held = start_gather(groups[:1], pieces(None)[:1], place) + [None] * (count - 1)
    held[0] = in_order(held[0], hop(held[0], ALONG_Z, swap=1), low)
    for tick in range(count + 3):
        near, far, last = [index if 0 <= index < count else None for index in range(tick - 1, tick - 4, -1)]
        live = [index for index in (tick, near, far, last) if index is not None and index < count]
        if tick == 1:
            live += range(2, count)
        items, state = together([held[index] for index in live], state)
        for index, item in zip(live, items):
            held[index] = item
        if tick == 0:
            held[1:] = start_gather(groups[1:], pieces(held[0])[1:], place)
        if last is not None:
            own, arrived_far, other = held[last]
            held[last] = [own, arrived_far, other, hop(arrived_far, ACROSS)]
        if far is not None:
            held[far] = [held[far], hop(held[far], FAR), hop(held[far], ACROSS)]
        if near is not None:
            held[near] = [held[near], hop(held[near], NEAR)]
        if tick < count:
            held[tick] = [held[tick], hop(held[tick], ALONG_Z, swap=2)]
        if tick < 2:
            early = slice(1, 2) if tick == 0 else slice(2, count)
            got = hop(jnp.concatenate(held[early], axis=1), ALONG_Z, swap=1)
            ends = list(itertools.accumulate(half_rows(parts) for parts in groups[early]))
            got = jnp.split(got, ends[:-1], axis=1)
            held[early] = [in_order(item, other, low) for item, other in zip(held[early], got)]
        if last is not None:
            state = arrived(last, held[last], state)
        if tick < count:
            (own, other), state = together(held[tick], state)
            both = in_order(own, other, high)
            held[tick] = both.reshape(-1, *both.shape[2:])
        if near is not None:
            items, state = together(held[near], state)
            held[near] = jnp.stack(items)
    return state


def whole_shape(part):
    return (part.blocks, part.rows * lax.axis_size(AXES), part.lanes)


def dealt_shapes(parts, tuned):
    if not tuned:
        return [whole_shape(part) for part in parts]
    size = (grid_sizes()[0], 2, half_rows(parts), WIDTH)
    return [lead + size for lead in ((2, 2), (2,), (), ())]


def start_deal(parts, tuned, place, wanted, arrays, dealt, sems):
    if not tuned:
        pltpu.make_async_copy(arrays[wanted], dealt[wanted], sems.at[wanted]).start()
        return
    array = arrays[wanted].reshape(*parts[wanted].full(grid_sizes()[0]))
    to_core, to_far, to_near, own = dealt
    for core in (0, 1):

        @pl.when(place[3] == core)
        def _():
            for other, far, near in itertools.product((0, 1), repeat=3):
                half = core ^ other
                step = [0, 0, 0, 0]
                step[NEAR[half]], step[FAR[half]] = (near, far)
                at_y, at_x = (lax.rem(place[1] + step[1], 2), lax.rem(place[2] + step[2], 2))
                if other:
                    target = to_core.at[far, near]
                elif far:
                    target = to_far.at[near]
                else:
                    target = to_near if near else own
                for index, row, lane, rows, block, inner in half_moves(parts)[half]:
                    if index == wanted:
                        pltpu.make_async_copy(
                            array.at[block, :, at_y, at_x, :, pl.ds(inner, rows)],
                            target.at[:, :, pl.ds(row, rows), pl.ds(lane, parts[index].lanes)],
                            sems.at[index],
                        ).start()


def add_up(*terms):
    total = terms[0].astype(jnp.float32)
    for term in terms[1:]:
        total = total + term.astype(jnp.float32)
    return total


def low_add(*terms):
    return add_up(*terms).astype(jnp.bfloat16)


def scatter_stages(place, direct):
    depth = grid_sizes()[0]
    z, core = (place[0], place[3])
    low, high = (z % 2, z // 2)

    def across(items):
        to_core, *rest = items
        return rest + [hop(to_core, ACROSS)]

    def far(items):
        to_far, to_near, own, from_core = items
        return [to_near, own, from_core, hop(low_add(to_far, from_core[1]), FAR)]

    def near(items):
        to_near, own, from_core, from_far = items
        from_near = hop(low_add(to_near, from_core[0, 1], from_far[1]), NEAR)
        return [add_up(own, from_core[0, 0], from_far[0]), from_near]

    def pick(array, at):
        return lax.dynamic_index_in_dim(array, at, 0, False)

    def along(items):
        summed = lax.optimization_barrier(add_up(*items))
        sent = [pick(summed, lax.rem(z + step, depth)) for step in range(1, depth)]
        got = [hop(item.astype(jnp.bfloat16), ALONG_Z, step + 1) for step, item in enumerate(sent)]
        return [pick(summed, z)] + got

    def pairs(items):
        summed = lax.optimization_barrier(add_up(*items))
        summed = summed.reshape(2, 2, *summed.shape[1:])
        return [pick(summed, high), hop(pick(summed, 1 - high).astype(jnp.bfloat16), ALONG_Z, swap=2)]

    def neighbours(items):
        summed = add_up(*items)
        return [pick(summed, low), hop(pick(summed, 1 - low).astype(jnp.bfloat16), ALONG_Z, swap=1)]

    def finish(items):
        total = add_up(*items)
        other = hop(pick(total, 1 - core), ACROSS)
        return in_order(pick(total, core), other, core).reshape(-1, WIDTH)

    return [across, far, near] + ([along] if direct else [pairs, neighbours]) + [finish]


def share_stages(part, place):
    low, high = (place[0] % 2, place[0] // 2)

    def along(item):
        one, two, three = [hop(item, ALONG_Z, swap=bits) for bits in (1, 2, 3)]
        both = in_order(in_order(item, one, low), in_order(two, three, low), high)
        return both.reshape(-1, *both.shape[2:])

    return [
        lambda item: start_gather([[part]], [[item]], place)[0],
        along,
        lambda item: jnp.stack([item, hop(item, NEAR)]),
        lambda item: [item, hop(item, FAR), hop(item, ACROSS)],
        lambda items: items + [hop(items[1], ACROSS)],
    ]


def pipelined_scatter(count, place, state, steps, shared):
    held, todo = ([], [])
    part, piece, more = shared
    share = share_stages(part, place)
    for tick in range(count + 5):
        live = [index for index in range(len(held)) if todo[index]]
        items, state, piece = together([held[index] for index in live], state, piece)
        for index, item in zip(live, items):
            held[index] = item
            for _ in range(2 if index == tick - 1 else 1):
                held[index] = todo[index].pop(0)(held[index])
        if share:
            piece = share.pop(0)(piece)
        elif more:
            piece = more.pop(0)(piece, held)
        if tick < count:
            dealt, state = steps[tick](state)
            held.append(dealt)
            todo.append(scatter_stages(place, tick >= count - 2))
    return (held, piece, state)


CQL_WEIGHT = 0.05
BETA_ONE = 0.5
BETA_TWO = 0.5
LEARNING_RATE = 0.25
WEIGHT_DECAY = 0.01
PATCH_IN = 256
DPROJ = 512
ACTIONS = 18
ATOMS = 51
GAMES = 4
BLOCKS = 2
STEP = 5
PLAYS = ACTIONS * ATOMS


def average_decay():
    return min(0.99, (1.0 + STEP) / (10.0 + STEP))


SWEEP = 8192


def lamb_parts(grads, params, first, second):
    momentum = BETA_ONE * first + (1.0 - BETA_ONE) * grads
    variance = BETA_TWO * second + (1.0 - BETA_TWO) * grads * grads
    direction = (
        momentum / (1.0 - BETA_ONE**STEP) / (jnp.sqrt(variance / (1.0 - BETA_TWO**STEP)) + 1e-06)
        + WEIGHT_DECAY * params
    )
    return (momentum, variance, direction)


def stretches(cuts):
    found = []
    at = 0
    for index, (start, size) in enumerate(cuts):
        end = start + size
        last = index == len(cuts) - 1
        whole = end if last else end // ROWS * ROWS
        found.append((at, whole - at, [index]))
        at = whole
        if end != whole:
            found.append((whole, ROWS, [index, index + 1]))
            at = whole + ROWS
    return found


def sweep(start, size, body, carry):
    steps = size // SWEEP

    def step(index, carry):
        return body(pl.ds(pl.multiple_of(start + index * SWEEP, ROWS), SWEEP), carry)

    if steps:
        carry = lax.fori_loop(0, steps, step, carry)
    return (carry, start + steps * SWEEP, size - steps * SWEEP)


def row_sum(value):
    return jnp.sum(value, axis=1, keepdims=True)


def put_rows(target, row, source, steps):
    for first, rows, lane, stride in steps:

        def step(index, carry):
            lanes = pl.ds(pl.multiple_of(lane + index * stride, ROWS), WIDTH)
            target[row : row + 1, lanes] = source[pl.ds(first + index, 1), :]
            return carry

        lax.fori_loop(0, rows, step, 0, unroll=4)


def block_rows(name, start, rows, first):
    if name == "w_out":
        count = rows // (D // BOT)
        return [(first + part * count, count, start + part * BOT, D) for part in range(D // BOT)]
    return [(first, rows, start, WIDTH)]


def patch_rows(rows, first):
    count = rows // 4
    return [
        (first + (2 * block + half) * count, count, half * (D // 2) + block * WIDTH, D)
        for block in range(2)
        for half in range(2)
    ]


def direction_kernel(cuts, moves, gain_at, *refs):
    top_cuts, block_cuts = cuts
    number = len(moves)
    sources, refs = (refs[:number], refs[number:])
    late, loss, *refs = refs
    top_ins, block_ins, refs = (refs[:3], refs[3:6], refs[6:])
    sums, *refs = refs
    top_outs, block_outs, (top_grad, block_grad) = (refs[:3], refs[3:6], refs[6:])
    for source, steps in zip(sources, moves):
        for row, placed in steps:
            put_rows(top_grad if row is None else block_grad, row or 0, source, placed)
    patch = top_cuts[0][1]
    top_grad[:, pl.ds(patch, late.shape[1])] = late[...]
    gain_start, gain_width = block_cuts[3]
    source, first = (sources[gain_at[0]], gain_at[1])
    block_grad[:, pl.ds(gain_start, gain_width)] = source[pl.ds(first, 8), :][:BLOCKS, :gain_width]

    def work(lanes, grad, ins, outs):
        param, *moments = [ref[:, lanes] for ref in ins]
        made = lamb_parts(grad[:, lanes], param, *moments)
        for ref, value in zip(outs, made):
            ref[:, lanes] = value
        return (param * param, made[2] * made[2])

    found = []

    def run(cuts, grad, ins, outs, first_lane, height):
        for start, size, segments in stretches(cuts):

            def step(lanes, carry):
                terms = work(lanes, grad, ins, outs)
                return [held + term for held, term in zip(carry, terms)]

            zeros = [jnp.zeros((height, SWEEP), jnp.float32)] * 2
            carry, begin, rest = sweep(start, size, step, zeros)
            sizes = [row_sum(value) for value in carry] if rest != size else None
            if rest:
                terms = work(pl.ds(begin, rest), grad, ins, outs)
                at = begin + lax.broadcasted_iota(jnp.int32, terms[0].shape, 1)
                if len(segments) > 1:
                    edge = cuts[segments[1]][0]
                    after = [row_sum(jnp.where(at >= edge, term, 0.0)) for term in terms]
                    found.extend((first_lane, segments[1], *item) for item in enumerate(after))
                    terms = [jnp.where(at < edge, term, 0.0) for term in terms]
                more = [row_sum(term) for term in terms]
                sizes = more if sizes is None else [held + term for held, term in zip(sizes, more)]
            found.extend((first_lane, segments[0], *item) for item in enumerate(sizes))

    run(top_cuts, top_grad, top_ins, top_outs, 0, 1)
    run(block_cuts, block_grad, block_ins, block_outs, len(top_cuts), BLOCKS)
    rows = lax.broadcasted_iota(jnp.int32, sums.shape, 0)
    lanes = lax.broadcasted_iota(jnp.int32, sums.shape, 1)
    result = jnp.where((rows == 2) & (lanes == 0), loss[...], 0.0)
    for first, segment, row, value in found:
        for part in range(value.shape[0]):
            lane = first + part * len(block_cuts) + segment
            here = (rows == row) & (lanes == lane)
            result = result + jnp.where(here, value[part : part + 1], 0.0)
    sums[...] = result


def directions(cuts, rows, moves, gain_at, late, loss, top_ins, block_ins):
    shapes = [f32(*top_ins[0].shape)] * 3 + [f32(*block_ins[0].shape)] * 3
    ins = [*rows, late, loss, *top_ins, *block_ins]
    return pl.pallas_call(
        functools.partial(direction_kernel, cuts, moves, gain_at),
        out_shape=[f32(8, ROWS)] + shapes,
        in_specs=in_vmem(len(ins)),
        out_specs=in_vmem(7),
        scratch_shapes=[
            pltpu.VMEM(top_ins[0].shape, jnp.float32),
            pltpu.VMEM(block_ins[0].shape, jnp.float32),
        ],
        compiler_params=pltpu.CompilerParams(vmem_limit_bytes=VMEM_LIMIT),
        cost_estimate=LIGHT,
        name="directions",
    )(*ins)


def update_kernel(cuts, sums, *refs):
    top_cuts, block_cuts = cuts
    top_ins, block_ins, refs = (refs[:3], refs[3:6], refs[6:])
    norms, *refs = refs
    top_outs, block_outs = (refs[:2], refs[2:])
    norm = jnp.sqrt(sums[...])
    norms[...] = norm
    ratio = LEARNING_RATE * (norm[0:1] / (norm[1:2] + 1e-06))
    decay = average_decay()

    def work(lanes, ins, outs, scale):
        param, direction, average = [ref[:, lanes] for ref in ins]
        updated, averaged, *half = outs
        value = param - scale * direction
        updated[:, lanes] = value
        averaged[:, lanes] = decay * average + (1.0 - decay) * value
        for ref in half:
            ref[:, lanes] = value.astype(jnp.bfloat16)

    def run(cuts, ins, outs, scales):
        for start, size, segments in stretches(cuts):
            scale = scales[segments[0]]

            def step(lanes, carry):
                work(lanes, ins, outs, scale)
                return carry

            _, begin, rest = sweep(start, size, step, 0)
            if rest:
                if len(segments) > 1:
                    at = begin + lax.broadcasted_iota(jnp.int32, (1, rest), 1)
                    scale = jnp.where(at < cuts[segments[1]][0], scale, scales[segments[1]])
                work(pl.ds(begin, rest), ins, outs, scale)

    lanes = [ratio[:, lane : lane + 1] for lane in range(len(top_cuts) + BLOCKS * len(block_cuts))]
    run(top_cuts, top_ins, top_outs, lanes[: len(top_cuts)])
    rest = lanes[len(top_cuts) :]
    scales = [jnp.concatenate(rest[index :: len(block_cuts)]) for index in range(len(block_cuts))]
    run(block_cuts, block_ins, block_outs, scales)


def update(cuts, sums, top_ins, block_ins):
    shapes = [f32(*array.shape) for array in [top_ins[0]] * 2 + [block_ins[0]] * 2]
    shapes.append(bf16(*block_ins[0].shape))
    return pl.pallas_call(
        functools.partial(update_kernel, cuts),
        out_shape=[f32(8, ROWS)] + shapes,
        in_specs=in_vmem(7),
        out_specs=in_vmem(6),
        compiler_params=pltpu.CompilerParams(vmem_limit_bytes=VMEM_LIMIT),
        cost_estimate=LIGHT,
        name="update",
    )(sums, *top_ins, *block_ins)


def segment_lengths():
    top = [PATCH_IN * D, D * PIX, D * DPROJ, DPROJ * GAMES * PLAYS]
    block = [D * BOT, 9 * BOT * BOT, BOT * D, 2 * (2 * BOT + D)]
    return (top, block)


def cut_points(lengths, devices):
    cuts = []
    offset = 0
    for length in lengths:
        width = length // devices
        cuts.append((offset, width))
        offset += width
    return cuts


def pack_top(flat, cuts):
    patch, pool, proj, heads = [flat[start : start + size] for start, size in cuts]
    patch = patch.reshape(-1, 2, 2, WIDTH).transpose(2, 1, 0, 3).reshape(2, -1, WIDTH)
    pool = jnp.pad(pool.reshape(1, -1, PIX), ((0, 0), (0, 0), (0, ROWS - PIX)))
    heads = jnp.pad(heads.reshape(-1, GAMES, PLAYS), ((0, 0), (0, 0), (0, 2 * WIDTH - PLAYS)))
    heads = heads.reshape(-1, 2 * GAMES, WIDTH).transpose(1, 0, 2)
    return [patch, pool, proj.reshape(1, -1, WIDTH), heads]


def flat_late(pool, proj, heads):
    heads = heads.transpose(1, 0, 2).reshape(-1, GAMES, 2 * WIDTH)[:, :, :PLAYS]
    return jnp.concatenate([item.reshape(-1) for item in (pool[:, :, :PIX], proj, heads)])


def pack_block(flat, cuts):
    w_in, w_mid, w_out = [flat[start : start + size] for start, size in cuts[:3]]
    w_out = w_out.reshape(-1, D // BOT, BOT).transpose(1, 0, 2)
    return [w_in.reshape(1, -1, BOT), w_mid.reshape(1, -1, BOT), w_out]


def parts_for(devices):
    rows = {"patch": 2 * PATCH_IN, "pool": D, "proj": D, "heads": DPROJ}
    rows |= {"w_in": D, "w_mid": TAPS * BOT, "w_out": BOT, "gains": TILE * devices}
    blocks = {"patch": 2, "heads": 2 * GAMES, "w_out": D // BOT}
    return {
        name: Part(blocks.get(name, 1), count // devices, ROWS if name == "pool" else WIDTH)
        for name, count in rows.items()
    }


def is_tuned(devices):
    parts = parts_for(devices).values()
    whole = all(part.rows // part.across % TILE == 0 for part in parts)
    return whole and lax.axis_size("wide") == 8 and lax.axis_size("narrow") == 4


def plain_gather(piece):
    return lax.all_gather(piece, AXES, axis=1, tiled=True)


def plain_scatter(array):
    return lax.psum_scatter(array, AXES, scatter_dimension=1, tiled=True).astype(jnp.float32)


def total(array):
    if lax.axis_size("wide") != 8 or lax.axis_size("narrow") != 4:
        return lax.psum(array, AXES)
    array = array + flip(array, 0, 0, 0, 1)
    array = (array + flip(array, 0, 0, 1, 0)) + (flip(array, 0, 1, 0, 0) + flip(array, 0, 1, 1, 0))
    one, two, three = [flip(array, bits, 0, 0, 0) for bits in (1, 2, 3)]
    return (array + two) + (one + three)


def frame_rows(frames):
    count = frames.shape[0]
    return jnp.pad(frames, ((0, 0), (0, ROWS - PIX), (0, 0))).reshape(count * ROWS, PATCH_IN)


def on_device(
    observed,
    following,
    game_ids,
    actions,
    legal_mask,
    rewards,
    discounts,
    done_flags,
    params_top,
    params_blocks,
    first_top,
    first_blocks,
    second_top,
    second_blocks,
    average_top,
    average_blocks,
    target_top,
    target_blocks,
):
    devices = lax.axis_size(AXES)
    frames_all = observed.shape[0] * devices
    top_lengths, block_lengths = segment_lengths()
    top_cuts = cut_points(top_lengths, devices)
    block_cuts = cut_points(block_lengths, devices)
    gain_start, gain_width = block_cuts[3]
    parts = parts_for(devices)
    tuned = is_tuned(devices)
    place = spot()
    shift = shifts()
    spread = spread_pixels(devices)
    count = observed.shape[0]
    whole = jnp.concatenate([game_ids[:, None], actions], axis=1)
    whole = jnp.pad(whole, ((0, 8 - count), (0, ROWS - 3)), constant_values=-1)
    legal = jnp.pad(legal_mask, ((0, 8 - count), (0, ROWS - ACTIONS)), constant_values=1)
    keep = discounts * (1.0 - done_flags.astype(jnp.float32))
    real = jnp.pad(jnp.stack([rewards, keep], axis=1), ((0, 8 - count), (0, ROWS - 2)))

    def read_pieces(early):
        sources = (target_top, target_blocks, params_top, params_blocks)
        if early is not None:
            early, sources = together(early, sources)
        tops = (sources[0], sources[2].astype(jnp.bfloat16))
        blocks = (sources[1], sources[3].astype(jnp.bfloat16))
        own = {}
        for net, top, flat in zip(("target", "online"), tops, blocks):
            for name, piece in zip(("patch", "pool", "proj", "heads"), pack_top(top, top_cuts)):
                own[net, name] = piece
            for index in range(BLOCKS):
                for name, piece in zip(block_names, pack_block(flat[index], block_cuts)):
                    own[net, name, index] = piece
        gain_rows = jnp.concatenate(blocks)[:, gain_start:]
        own["gains",] = jnp.pad(
            gain_rows, ((0, TILE - 2 * BLOCKS), (0, WIDTH - gain_width))
        ).reshape(1, TILE, WIDTH)
        return [[own[key] for key in group] for group in keys]

    block_names = ("w_in", "w_mid", "w_out")

    def part_of(key):
        return parts[key[0] if key[0] in parts else key[1]]

    full = {}

    def block_weight(index, name):
        return merged(full["online", name, index]).reshape(-1, BOT)

    def hold(net, index, group, buffers, state):
        full["held", index] = (group, buffers)
        return state

    def read_gains(group, buffers, state):
        gains = assemble(group_parts(group), buffers, place, [0])[0] if tuned else buffers[0]
        gains = gains.reshape(devices, TILE, WIDTH)[:, : 2 * BLOCKS, :gain_width]
        gains = gains.transpose(1, 0, 2).reshape(2 * BLOCKS, -1).astype(jnp.float32)
        return run_block("target", 0, group, buffers, state | {"gains": gains})

    def target_ends(group, buffers, state):
        for index in range(1, BLOCKS):
            state = run_block("target", index, *full["held", index], state)
        target = head_target(
            state.pop("stream"), whole, real, group_parts(group), buffers, tuned, place
        )
        return state | {"target": target}

    def online_ends(group, buffers, state):
        loss, dstream, dpool, acts = head_loss(
            state.pop("stream"), state.pop("target"), whole, legal, frames_all,
            group_parts(group), buffers, tuned, place,
        )
        return state | {"loss": loss, "grad": dstream, "pool": dpool, "acts": acts}

    def run_block(net, index, group, buffers, state):
        keep = net == "online"
        row = index + (BLOCKS if keep else 0)
        gain = state["gains"][row : row + 1]
        stream = [state["pixels" if keep else "following"], spread]
        if index:
            stream = [state["stream"]]
        skip = 1 if keys[group][0] == ("gains",) else 0
        out, *kept = block_forward(
            stream, gain, shift, group_parts(group), skip, buffers, place, keep, tuned
        )
        state = state | {"stream": out}
        if keep:
            start = kept.pop(0) if index == 0 else stream[0]
            full.update(zip([(net, name, index) for name in block_names], kept[-3:]))
            state |= {"kept%d" % index: [start, *kept[:-3]]}
        return state

    keys, then = ([], [])
    ends = ("pool", "proj", "heads")

    def add_group(group, run, *names):
        keys.append(group)
        then.append(functools.partial(run, *names))

    def block_keys(net, index):
        return [(net, name, index) for name in block_names]

    for index in range(1, BLOCKS):
        add_group(block_keys("target", index), hold, "target", index)
    add_group([("gains",), ("target", "patch")] + block_keys("target", 0), read_gains)
    add_group([("target", name) for name in ends], target_ends)
    for index in range(BLOCKS):
        start = [] if index else [("online", "patch")]
        add_group(start + block_keys("online", index), run_block, "online", index)
    add_group([("online", name) for name in ends], online_ends)

    def group_parts(group):
        return [part_of(key) for key in keys[group]]

    def arrived(group, buffers, state):
        return then[group](group, buffers, dict(state))

    state = {"following": frame_rows(following), "pixels": frame_rows(observed)}
    if tuned:
        groups = [group_parts(group) for group in range(len(keys))]
        state = pipelined_gather(groups, read_pieces, place, state, arrived)
    else:
        for group, items in enumerate(read_pieces(None)):
            state = arrived(group, [plain_gather(item) for item in items], state)

    keys = []
    steps = []

    def out_inputs(index, state):
        stream, hid_one, hid_two, hid_three, rstd = state["kept%d" % index]
        gain = state["gains"][BLOCKS + index : BLOCKS + index + 1]
        return [stream, hid_two, hid_three, rstd, block_weight(index, "w_out"), gain]

    def out_step(index, group, state):
        (dres, low, late), dealt = back_out(
            state.pop("grad"), *out_inputs(index, state), state.pop("pool"), group, tuned, place
        )
        return (dealt, state | {"grad": dres, "low": low, "late%d" % index: late})

    def mid_step(index, group, state):
        stream, hid_one, hid_two, hid_three, rstd = state["kept%d" % index]
        gain = state["gains"][BLOCKS + index : BLOCKS + index + 1]
        (low, early), dealt = back_mid(
            state["low"], hid_one, rstd, block_weight(index, "w_mid"), gain, shift, group, tuned, place
        )
        return (dealt, state | {"low": low, "early%d" % index: early})

    def between_step(index, group, state):
        stream = state.pop("kept%d" % index)[0]
        (dres, low, late), dealt = back_between(
            state["low"], stream, state["grad"], block_weight(index, "w_in"),
            out_inputs(index - 1, state), group, tuned, place,
        )
        return (dealt, state | {"grad": dres, "low": low, "late%d" % (index - 1): late})

    def first_step(group, state):
        stream = state.pop("kept0")[0]
        dgains = [
            jnp.concatenate([state.pop("early%d" % index), state.pop("late%d" % index)], axis=1)
            for index in range(BLOCKS)
        ]
        dgains = jnp.concatenate(dgains).reshape(BLOCKS, devices, gain_width).transpose(1, 0, 2)
        dgains = jnp.pad(dgains, ((0, 0), (0, TILE - BLOCKS), (0, WIDTH - gain_width)))
        dgains = dgains.reshape(1, -1, WIDTH).astype(jnp.bfloat16)
        dealt = back_first(
            state.pop("low"), stream, state.pop("grad"), block_weight(0, "w_in"),
            state.pop("pixels"), spread, dgains, group, tuned, place,
        )
        return (dealt, state)

    def add_step(group, run, *names):
        keys.append(group)
        steps.append(
            lambda state: run(*names, [parts[key[0]] for key in group], dict(state))
        )

    loss_part, acts = (state.pop("loss"), state.pop("acts"))
    add_step([("w_out", BLOCKS - 1), ("pool",)], out_step, BLOCKS - 1)
    for index in reversed(range(BLOCKS)):
        add_step([("w_mid", index)], mid_step, index)
        if index:
            add_step([("w_in", index), ("w_out", index - 1)], between_step, index)
    add_step([("w_in", 0), ("patch",), ("gains",)], first_step)
    def read_heads(buffers, rows):
        return own_heads(buffers, parts["heads"], parts["proj"], tuned, place)

    def read_late(pair, rows):
        pool = parts["pool"]
        first = parts["w_out"].travel
        return flat_late(pool.unpack(rows[0][first : first + pool.travel]), pair[1], pair[0])[None]

    groups = [[parts[key[0]] for key in group] for group in keys]
    if tuned:
        shared = (Part(1, ACTS, WIDTH), acts[None], [read_heads, read_late])
        mine, late, state = pipelined_scatter(len(groups), place, state, steps, shared)
    else:
        mine = []
        for group, step in zip(groups, steps):
            arrays, state = step(state)
            mine.append(pack(group, [plain_scatter(array) for array in arrays]))
        late = read_late(read_heads([plain_gather(acts[None])], mine), mine)
    at = {}
    moves = []
    for number, group in enumerate(keys):
        first = 0
        steps = []
        for key in group:
            count = parts[key[0]].travel
            at[key] = (number, first)
            if len(key) > 1:
                start = block_cuts[block_names.index(key[0])][0]
                steps.append((key[1], block_rows(key[0], start, count, first)))
            elif key[0] == "patch":
                steps.append((None, patch_rows(count, first)))
            first += count
        moves.append(steps)
    cuts = (top_cuts, block_cuts)
    tops = [array[None] for array in (params_top, first_top, second_top, average_top)]
    sums, *made = directions(
        cuts, mine, moves, at["gains",], late, loss_part,
        tops[:3], [params_blocks, first_blocks, second_blocks],
    )
    momentum_top, variance_top, direction_top, momentum_blocks, variance_blocks, direction_blocks = made
    sums = total(sums)
    norms, *made = update(
        cuts, sums, [tops[0], direction_top, tops[3]],
        [params_blocks, direction_blocks, average_blocks],
    )
    updated_top, averaged_top, updated_blocks, averaged_blocks, half_blocks = made
    loss_total = sums[2, 0]
    matrix_norms = norms[:2, : len(top_cuts) + BLOCKS * len(block_cuts)]
    number, first = at["gains",]
    gain_grads = mine[number][first : first + BLOCKS, :gain_width]
    return (
        loss_total,
        matrix_norms,
        updated_top[0],
        updated_top[0].astype(jnp.bfloat16),
        momentum_top[0],
        variance_top[0],
        averaged_top[0],
        updated_blocks,
        half_blocks,
        momentum_blocks,
        variance_blocks,
        averaged_blocks,
        gain_grads,
    )


def solution(mesh):
    one = P(AXES)
    flat = P(None, AXES)
    return jax.shard_map(
        on_device,
        mesh=mesh,
        in_specs=(P(AXES, None, None),) * 2
        + (one, P(AXES, None), P(AXES, None))
        + (one,) * 3
        + (one, flat) * 5,
        out_specs=(P(), P()) + (one,) * 5 + (flat,) * 6,
        check_vma=False,
    )
```

```python
import functools
import itertools

import jax
import jax.numpy as jnp
from jax import lax
from jax.experimental import pallas as pl
from jax.experimental.pallas import tpu as pltpu
from jax.sharding import PartitionSpec as P

D = 2048
BOT = 512
GROUPS = 32
SIDE = 11
PIX = 121
TAPS = 9

ROWS = 128
LANES = 512
VMEM_LIMIT = 44 * 1024 * 1024
LIGHT = pl.CostEstimate(flops=1024, bytes_accessed=1024, transcendentals=0)


def shifts():
    pixel = jnp.arange(ROWS)
    row, col = (pixel // SIDE, pixel % SIDE)
    mats = []
    for tap in range(TAPS):
        at_row, at_col = (row + tap // 3 - 1, col + tap % 3 - 1)
        inside = (at_row >= 0) & (at_row < SIDE) & (at_col >= 0) & (at_col < SIDE) & (pixel < PIX)
        mats.append((inside[:, None] & (pixel[None, :] == (at_row * SIDE + at_col)[:, None])))
    return jnp.concatenate(mats, axis=0).astype(jnp.bfloat16)


def dot(left, right):
    return jnp.dot(left, right, preferred_element_type=jnp.float32)


def dot_rows(left, right):
    return lax.dot_general(
        left, right, (((0,), (0,)), ((), ())), preferred_element_type=jnp.float32
    )


def dot_lanes(left, right):
    return lax.dot_general(
        left, right, (((1,), (1,)), ((), ())), preferred_element_type=jnp.float32
    )


def each_chunk(count, chans, body, unroll=1):
    per = chans // LANES

    def step(index, carry):
        frame = index // per
        rows = pl.ds(pl.multiple_of(frame * ROWS, ROWS), ROWS)
        lanes = pl.ds(pl.multiple_of((index % per) * LANES, LANES), LANES)
        body(pl.ds(frame, 1), rows, lanes)
        return carry

    lax.fori_loop(0, count * per, step, 0, unroll=unroll)


def real_rows():
    return lax.broadcasted_iota(jnp.int32, (ROWS, LANES), 0) < PIX


def group_mean(sums):
    chans = sums.shape[1]
    width = chans // GROUPS
    lane = lax.broadcasted_iota(jnp.int32, sums.shape, 1)
    step = 1
    while step < width:
        ahead = pltpu.roll(sums, chans - step, 1)
        behind = pltpu.roll(sums, step, 1)
        sums = sums + jnp.where((lane & step) == 0, ahead, behind)
        step *= 2
    return sums * (1.0 / (PIX * width))


def silu(value):
    return value / (1.0 + jnp.exp(-value))


def silu_slope(value):
    gate = 1.0 / (1.0 + jnp.exp(-value))
    return gate * (1.0 + value * (1.0 - gate))


def normalise(count, chans, hid, sums, rstd, rstd_at):
    whole = pl.ds(0, chans)
    sums[:, whole] = jnp.zeros((sums.shape[0], chans), jnp.float32)

    def add(frame, rows, lanes):
        sums[frame, lanes] = jnp.sum(hid[rows, lanes], axis=0, keepdims=True)

    each_chunk(count, chans, add, unroll=2)
    sums[:, whole] = group_mean(sums[:, whole])

    def center(frame, rows, lanes):
        value = jnp.where(real_rows(), hid[rows, lanes] - sums[frame, lanes], 0.0)
        hid[rows, lanes] = value
        sums[frame, lanes] = jnp.sum(value * value, axis=0, keepdims=True)

    each_chunk(count, chans, center, unroll=2)
    at = pl.ds(rstd_at, chans)
    rstd[:, at] = lax.rsqrt(group_mean(sums[:, whole]) + 1e-05)


def forward_kernel(count, keep, parts, skip, tuned, *refs):
    refs = list(refs)
    number = len(parts) - skip
    first = number > 3

    def take(number):
        taken = refs[:number]
        del refs[:number]
        return taken

    (place,) = take(1)
    x = take(2 if first else 1)
    gains, shift = take(2)
    sources = take(4 if tuned else len(parts))
    (out,) = take(1)
    if keep:
        if first:
            (start,) = take(1)
        hid_one, hid_two, hid_three, rstd = take(4)
        kept_weights = take(3)
    weights = take(number)
    sems, back_sems, low, act, cols, sums = take(6)
    if not keep:
        hid_one, hid_two, hid_three, rstd = take(4)
        if first:
            (start,) = take(1)
    fetch(parts, tuned, place, sources, dict(enumerate(weights, skip)), sems)

    def arrived(index):
        weight = weights[index]
        pltpu.make_async_copy(weight, weight, sems.at[len(parts) + index]).wait()
        if keep and index >= -3:
            pltpu.make_async_copy(weight, kept_weights[index], back_sems.at[3 + index]).start()
        return weight

    def whole(value):
        return value.reshape(-1, value.shape[-1])

    if first:
        pixels, spread = x
        x = start
        patch = arrived(-4)
        for half in range(2):
            wide = dot(pixels[...], spread[half]).astype(jnp.bfloat16)
            for block in range(2):
                lanes = pl.ds((2 * half + block) * WIDTH, WIDTH)
                x[:, lanes] = dot(wide, whole(patch[block]))
    else:
        (x,) = x

    def cast(frame, rows, lanes):
        low[rows, lanes] = x[rows, lanes].astype(jnp.bfloat16)

    def activate(hid, at, offset):
        def body(frame, rows, lanes):
            gain = gains[:, pl.ds(offset + lanes.start, LANES)]
            bias = gains[:, pl.ds(offset + BOT + lanes.start, LANES)]
            value = hid[rows, lanes] * rstd[frame, pl.ds(at + lanes.start, LANES)]
            hid[rows, lanes] = value
            value = jnp.where(real_rows(), silu(value * gain + bias), 0.0)
            act[rows, lanes] = value.astype(jnp.bfloat16)

        return body

    each_chunk(count, D, cast)
    hid_one[...] = dot(low[...], whole(arrived(-3)[...]))
    normalise(count, BOT, hid_one, sums, rstd, 0)
    each_chunk(count, BOT, activate(hid_one, 0, 0))
    for frame in range(count):
        rows = pl.ds(frame * ROWS, ROWS)
        for tap in range(TAPS):
            picked = dot(shift[pl.ds(tap * ROWS, ROWS), :], act[rows, :])
            cols[rows, pl.ds(tap * BOT, BOT)] = picked.astype(jnp.bfloat16)
    hid_two[...] = dot(cols[...], whole(arrived(-2)[...]))
    normalise(count, BOT, hid_two, sums, rstd, BOT)
    each_chunk(count, BOT, activate(hid_two, BOT, 2 * BOT))
    w_out = arrived(-1)
    for part in range(D // BOT):
        hid_three[:, pl.ds(part * BOT, BOT)] = dot(act[...], whole(w_out[part]))
    normalise(count, D, hid_three, sums, rstd, 2 * BOT)

    def finish(frame, rows, lanes):
        gain = gains[:, pl.ds(4 * BOT + lanes.start, LANES)]
        bias = gains[:, pl.ds(4 * BOT + D + lanes.start, LANES)]
        value = hid_three[rows, lanes] * rstd[frame, pl.ds(2 * BOT + lanes.start, LANES)]
        if keep:
            hid_three[rows, lanes] = value
        value = silu(x[rows, lanes] + value * gain + bias)
        out[rows, lanes] = jnp.where(real_rows(), value, 0.0)

    each_chunk(count, D, finish)
    if keep:
        for index in (-3, -2, -1):
            pltpu.make_async_copy(weights[index], kept_weights[index], back_sems.at[3 + index]).wait()


def f32(*shape):
    return jax.ShapeDtypeStruct(shape, jnp.float32)


def bf16(*shape):
    return jax.ShapeDtypeStruct(shape, jnp.bfloat16)


def stat_rows(count):
    return -(-count // 8) * 8


def block_forward(stream, gains, shift, parts, skip, buffers, place, keep, tuned):
    first = len(parts) - skip > 3
    rows = stream[0].shape[0]
    count = rows // ROWS
    stats = stat_rows(count)
    kept = [
        ((rows, BOT), jnp.float32),
        ((rows, BOT), jnp.float32),
        ((rows, D), jnp.float32),
        ((stats, 2 * BOT + D), jnp.float32),
    ]
    start = [((rows, D), jnp.float32)] if first else []
    weights = weight_shapes(parts, buffers, tuned)[skip:]
    out_shape = [f32(rows, D)]
    out_specs = in_vmem(1)
    scratch = [pltpu.VMEM(shape, jnp.bfloat16) for shape in weights]
    scratch += [
        pltpu.SemaphoreType.DMA((len(parts),)),
        pltpu.SemaphoreType.DMA((3,)),
        pltpu.VMEM((rows, D), jnp.bfloat16),
        pltpu.VMEM((rows, BOT), jnp.bfloat16),
        pltpu.VMEM((rows, TAPS * BOT), jnp.bfloat16),
        pltpu.VMEM((stats, D), jnp.float32),
    ]
    if keep:
        out_shape += [jax.ShapeDtypeStruct(*item) for item in start + kept]
        out_shape += [jax.ShapeDtypeStruct(shape, jnp.bfloat16) for shape in weights[-3:]]
        out_specs += in_vmem(len(start + kept)) + hbm(3)
    else:
        scratch += [pltpu.VMEM(*item) for item in kept + start]
    return pl.pallas_call(
        functools.partial(forward_kernel, count, keep, parts, skip, tuned),
        out_shape=out_shape,
        in_specs=in_smem() + in_vmem(len(stream) + 2) + hbm(len(buffers)),
        out_specs=out_specs,
        scratch_shapes=scratch,
        compiler_params=pltpu.CompilerParams(vmem_limit_bytes=VMEM_LIMIT),
        cost_estimate=LIGHT,
        name="block_forward",
    )(place, *stream, gains, shift, *buffers)


def norm_back(count, chans, slope, hid, sums, more, rstd, rstd_at, gain, grad_gain, grad_bias, store):
    whole = pl.ds(0, chans)
    sums[:, whole] = jnp.zeros((sums.shape[0], chans), jnp.float32)
    more[:, whole] = jnp.zeros((sums.shape[0], chans), jnp.float32)

    def add(frame, rows, lanes):
        value = slope(frame, rows, lanes)
        sums[frame, lanes] = jnp.sum(value, axis=0, keepdims=True)
        more[frame, lanes] = jnp.sum(value * hid[rows, lanes], axis=0, keepdims=True)

    each_chunk(count, chans, add)
    grad_bias[...] = jnp.sum(sums[:, whole], axis=0, keepdims=True)
    grad_gain[...] = jnp.sum(more[:, whole], axis=0, keepdims=True)
    sums[:, whole] = group_mean(sums[:, whole] * gain[...])
    more[:, whole] = group_mean(more[:, whole] * gain[...])

    def spread(frame, rows, lanes):
        store(
            rows,
            lanes,
            lambda value: jnp.where(
                real_rows(),
                rstd[frame, pl.ds(rstd_at + lanes.start, LANES)]
                * (value * gain[:, lanes] - sums[frame, lanes] - hid[rows, lanes] * more[frame, lanes]),
                0.0,
            ).astype(jnp.bfloat16),
        )

    each_chunk(count, chans, spread)


def back_out_body(count, grad, x, hid_two, hid_three, rstd, w_out, gains, dres, dlow, dgains, scratch, dw_out):
    third, act, dact, sums, more = scratch
    gain_three, bias_three = (gains.at[:, pl.ds(4 * BOT, D)], gains.at[:, pl.ds(4 * BOT + D, D)])

    def slope_three(frame, rows, lanes):
        value = x[rows, lanes] + hid_three[rows, lanes] * gain_three[:, lanes] + bias_three[:, lanes]
        value = jnp.where(real_rows(), grad[rows, lanes] * silu_slope(value), 0.0)
        dres[rows, lanes] = value
        return value

    def store_three(rows, lanes, back):
        third[rows, lanes] = back(dres[rows, lanes])

    norm_back(
        count, D, slope_three, hid_three, sums, more, rstd, 2 * BOT, gain_three,
        dgains.at[:, pl.ds(2 * BOT, D)], dgains.at[:, pl.ds(2 * BOT + D, D)], store_three,
    )
    total = None
    for part in range(D // BOT):
        lanes = pl.ds(part * BOT, BOT)
        term = dot_lanes(third[:, lanes], w_out[lanes, :])
        total = term if total is None else total + term
    dact[...] = total
    gain_two, bias_two = (gains.at[:, pl.ds(2 * BOT, BOT)], gains.at[:, pl.ds(3 * BOT, BOT)])

    def slope_two(frame, rows, lanes):
        value = hid_two[rows, lanes] * gain_two[:, lanes] + bias_two[:, lanes]
        gate = 1.0 / (1.0 + jnp.exp(-value))
        act[rows, lanes] = jnp.where(real_rows(), value * gate, 0.0).astype(jnp.bfloat16)
        value = dact[rows, lanes] * (gate * (1.0 + value * (1.0 - gate)))
        value = jnp.where(real_rows(), value, 0.0)
        dact[rows, lanes] = value
        return value

    def store_two(rows, lanes, back):
        dlow[rows, lanes] = back(dact[rows, lanes])

    norm_back(
        count, BOT, slope_two, hid_two, sums, more, rstd, BOT, gain_two,
        dgains.at[:, pl.ds(0, BOT)], dgains.at[:, pl.ds(BOT, BOT)], store_two,
    )
    for part in range(D // BOT):
        lanes = pl.ds(part * BOT, BOT)
        dw_out[part] = dot_rows(act[...], third[:, lanes]).astype(jnp.bfloat16)


def out_scratch(rows):
    stats = stat_rows(rows // ROWS)
    return [
        pltpu.VMEM((rows, D), jnp.bfloat16),
        pltpu.VMEM((rows, BOT), jnp.bfloat16),
        pltpu.VMEM((rows, BOT), jnp.float32),
        pltpu.VMEM((stats, D), jnp.float32),
        pltpu.VMEM((stats, D), jnp.float32),
    ]


def back_mid_body(count, grad, hid_one, rstd, w_mid, gains, shift, dlow, dgains, scratch, dw_mid):
    act, cols, dact, sums, more = scratch
    gain_one, bias_one = (gains.at[:, pl.ds(0, BOT)], gains.at[:, pl.ds(BOT, BOT)])
    for frame in range(count):
        rows = pl.ds(frame * ROWS, ROWS)
        for tap in range(TAPS):
            picked = dot(shift[pl.ds((TAPS - 1 - tap) * ROWS, ROWS), :], grad[rows, :])
            cols[rows, pl.ds(tap * BOT, BOT)] = picked.astype(jnp.bfloat16)
    total = None
    for tap in range(TAPS):
        lanes = pl.ds(tap * BOT, BOT)
        term = dot_lanes(cols[:, lanes], w_mid[lanes, :])
        total = term if total is None else total + term
    dact[...] = total

    def slope_one(frame, rows, lanes):
        value = hid_one[rows, lanes] * gain_one[:, lanes] + bias_one[:, lanes]
        gate = 1.0 / (1.0 + jnp.exp(-value))
        act[rows, lanes] = jnp.where(real_rows(), value * gate, 0.0).astype(jnp.bfloat16)
        value = dact[rows, lanes] * (gate * (1.0 + value * (1.0 - gate)))
        value = jnp.where(real_rows(), value, 0.0)
        dact[rows, lanes] = value
        return value

    def store_one(rows, lanes, back):
        dlow[rows, lanes] = back(dact[rows, lanes])

    norm_back(
        count, BOT, slope_one, hid_one, sums, more, rstd, 0, gain_one,
        dgains.at[:, pl.ds(0, BOT)], dgains.at[:, pl.ds(BOT, BOT)], store_one,
    )
    for tap in range(TAPS):
        lanes = pl.ds(tap * BOT, BOT)
        dw_mid[0, lanes, :] = dot_rows(act[...], cols[:, lanes]).astype(jnp.bfloat16)


def back_in_body(count, grad, x, dres, w_in, dx, low, dw_in):
    def cast(frame, rows, lanes):
        low[rows, lanes] = x[rows, lanes].astype(jnp.bfloat16)

    each_chunk(count, D, cast)
    for part in range(D // BOT):
        lanes = pl.ds(part * BOT, BOT)
        dx[:, lanes] = dres[:, lanes] + dot_lanes(grad[...], w_in[lanes, :])
        dw_in[0, lanes, :] = dot_rows(low[:, lanes], grad[...]).astype(jnp.bfloat16)


def back_kernel(body, parts, tuned, counts, *refs):
    place, refs = (refs[0], list(refs[1:]))
    groups = []
    for number in (*counts[:2], len(dealt_shapes(parts, tuned)), len(parts), 1, counts[2]):
        groups.append(refs[:number])
        refs = refs[number:]
    ins, outs, dealt, made, sems, scratch = groups

    def done(index):
        start_deal(parts, tuned, place, index, made, dealt, sems[0])

    body(ins, outs, made, scratch, done)
    for index, array in enumerate(made):
        pltpu.make_async_copy(array, array, sems[0].at[index]).wait()


def back_call(name, body, ins, out_shape, scratch, parts, tuned, place):
    dealt = dealt_shapes(parts, tuned)
    counts = (len(ins), len(out_shape), len(scratch))
    outs = pl.pallas_call(
        functools.partial(back_kernel, body, parts, tuned, counts),
        out_shape=out_shape + [bf16(*shape) for shape in dealt],
        in_specs=in_smem() + in_vmem(len(ins)),
        out_specs=in_vmem(len(out_shape)) + hbm(len(dealt)),
        scratch_shapes=[pltpu.VMEM(whole_shape(part), jnp.bfloat16) for part in parts]
        + [pltpu.SemaphoreType.DMA((len(parts),))]
        + scratch,
        compiler_params=pltpu.CompilerParams(vmem_limit_bytes=VMEM_LIMIT),
        cost_estimate=LIGHT,
        name=name,
    )(place, *ins)
    return (list(outs[: len(out_shape)]), list(outs[len(out_shape) :]))


def back_out(grad, stream, hid_two, hid_three, rstd, w_out, gains, dpool, parts, tuned, place):
    rows = stream.shape[0]

    def body(ins, outs, made, scratch, done):
        made[1][...] = ins[7][...]
        done(1)
        back_out_body(rows // ROWS, *ins[:7], *outs, scratch, made[0])
        done(0)

    ins = [grad, stream, hid_two, hid_three, rstd, w_out, gains, dpool]
    out_shape = [f32(rows, D), bf16(rows, BOT), f32(1, 2 * BOT + 2 * D)]
    return back_call("back_out", body, ins, out_shape, out_scratch(rows), parts, tuned, place)


def back_mid(grad, hid_one, rstd, w_mid, gains, shift, parts, tuned, place):
    rows = grad.shape[0]
    stats = stat_rows(rows // ROWS)

    def body(ins, outs, made, scratch, done):
        back_mid_body(rows // ROWS, *ins, *outs, scratch, made[0])
        done(0)

    scratch = [
        pltpu.VMEM((rows, BOT), jnp.bfloat16),
        pltpu.VMEM((rows, TAPS * BOT), jnp.bfloat16),
        pltpu.VMEM((rows, BOT), jnp.float32),
        pltpu.VMEM((stats, BOT), jnp.float32),
        pltpu.VMEM((stats, BOT), jnp.float32),
    ]
    ins = [grad, hid_one, rstd, w_mid, gains, shift]
    out_shape = [bf16(rows, BOT), f32(1, 2 * BOT)]
    return back_call("back_mid", body, ins, out_shape, scratch, parts, tuned, place)


def back_between(grad, stream, dres, w_in, later, parts, tuned, place):
    rows = stream.shape[0]

    def body(ins, outs, made, scratch, done):
        dx, low, *rest = scratch
        back_in_body(rows // ROWS, *ins[:4], dx, low, made[0])
        done(0)
        back_out_body(rows // ROWS, dx, *ins[4:], *outs, rest, made[1])
        done(1)

    scratch = [pltpu.VMEM((rows, D), jnp.float32), pltpu.VMEM((rows, D), jnp.bfloat16)]
    scratch += out_scratch(rows)
    ins = [grad, stream, dres, w_in, *later]
    out_shape = [f32(rows, D), bf16(rows, BOT), f32(1, 2 * BOT + 2 * D)]
    return back_call("back_between", body, ins, out_shape, scratch, parts, tuned, place)


def back_first(grad, stream, dres, w_in, pixels, spread, dgains, parts, tuned, place):
    rows = stream.shape[0]

    def body(ins, outs, made, scratch, done):
        dx, low = scratch
        made[2][...] = ins[6][...]
        done(2)
        back_in_body(rows // ROWS, *ins[:4], dx, low, made[0])
        done(0)
        wide = [dot(ins[4][...], ins[5][half]).astype(jnp.bfloat16) for half in range(2)]
        for block in range(2):
            total = None
            for half in range(2):
                lanes = pl.ds((2 * half + block) * WIDTH, WIDTH)
                term = dot_rows(wide[half], dx[:, lanes].astype(jnp.bfloat16))
                total = term if total is None else total + term
            made[1][block] = total.astype(jnp.bfloat16)
        done(1)

    scratch = [pltpu.VMEM((rows, D), jnp.float32), pltpu.VMEM((rows, D), jnp.bfloat16)]
    ins = [grad, stream, dres, w_in, pixels, spread, dgains]
    return back_call("back_first", body, ins, [], scratch, parts, tuned, place)[1]


def spread_pixels(devices):
    rows = PATCH_IN // devices
    value = jnp.arange(PATCH_IN)
    at = value // rows * 2 * rows + value % rows
    return jnp.stack(
        [jnp.arange(2 * PATCH_IN)[None, :] == (at + half * rows)[:, None] for half in range(2)]
    ).astype(jnp.bfloat16)


def merge(value):
    return value.reshape(-1, value.shape[-1])


def fetch_ends(parts, tuned, place, sources, weights, sems):
    first = len(parts) - 3
    fetch(parts, tuned, place, sources, dict(enumerate(weights, first)), sems)

    def arrived(index):
        weight = weights[index]
        pltpu.make_async_copy(weight, weight, sems.at[first + index]).wait()
        return weight

    return arrived


def head_forward(count, stream, arrived, games, pool_t, pooled):
    pool = merge(arrived(0)[...]).astype(jnp.float32)
    for part in range(D // ROWS):
        pool_t[:, pl.ds(part * ROWS, ROWS)] = pool[part * ROWS : (part + 1) * ROWS].T
    pooled[...] = jnp.zeros_like(pooled)

    def weigh(frame, rows, lanes):
        value = stream[rows, lanes].astype(jnp.bfloat16).astype(jnp.float32)
        pooled[frame, lanes] = jnp.sum(value * pool_t[:, lanes], axis=0, keepdims=True)

    each_chunk(count, D, weigh)
    before = dot(pooled[...].astype(jnp.bfloat16), merge(arrived(1)[...]))
    hidden = silu(before).astype(jnp.bfloat16)
    heads = arrived(2)
    scores = None
    for game in range(GAMES):
        pair = [dot(hidden, merge(heads[2 * game + half])) for half in range(2)]
        term = jnp.where(games == game, jnp.concatenate(pair, axis=1), 0.0)
        scores = term if scores is None else scores + term
    return ([pick_atoms(scores, action) for action in range(ACTIONS)], before, hidden)


def atom_lanes():
    return lax.broadcasted_iota(jnp.int32, (8, ROWS), 1)


def pick_atoms(scores, action):
    offset = action * ATOMS
    moved = pltpu.roll(scores, 2 * WIDTH - offset, 1) if offset else scores
    return jnp.where(atom_lanes() < ATOMS, moved[:, :ROWS], -1e30)


def support_lanes():
    return -10.0 + 20.0 / (ATOMS - 1) * atom_lanes().astype(jnp.float32)


def lane_sum(value):
    return jnp.sum(value, axis=1, keepdims=True)


def target_kernel(count, parts, tuned, place, stream, whole, real, *refs):
    sources, (out, *weights, sems, pool_t, pooled) = (refs[:-7], refs[-7:])
    arrived = fetch_ends(parts, tuned, place, sources, weights, sems)
    logits, _, _ = head_forward(count, stream, arrived, whole[:, 0:1], pool_t, pooled)
    chosen = None
    for action in range(ACTIONS):
        term = jnp.where(whole[:, 2:3] == action, logits[action], 0.0)
        chosen = term if chosen is None else chosen + term
    power = jnp.exp(chosen - jnp.max(chosen, axis=1, keepdims=True))
    probs = power / lane_sum(power)
    atoms = support_lanes()
    spacing = 20.0 / (ATOMS - 1)
    moved = jnp.clip(real[:, 0:1] + real[:, 1:2] * atoms, -10.0, 10.0)
    total = jnp.zeros_like(probs)
    for atom in range(ATOMS):
        near = 1.0 - jnp.abs(moved[:, atom : atom + 1] - atoms) / spacing
        total = total + probs[:, atom : atom + 1] * jnp.clip(near, 0.0, 1.0)
    inside = (atom_lanes() < ATOMS) & (lax.broadcasted_iota(jnp.int32, total.shape, 0) < count)
    out[...] = jnp.where(inside, total, 0.0)


def ends_scratch(parts, buffers, tuned):
    scratch = [pltpu.VMEM(shape, jnp.bfloat16) for shape in weight_shapes(parts, buffers, tuned)[-3:]]
    scratch += [pltpu.SemaphoreType.DMA((len(parts),))]
    return scratch + [pltpu.VMEM((ROWS, D), jnp.float32), pltpu.VMEM((8, D), jnp.float32)]


def head_target(stream, whole, real, parts, buffers, tuned, place):
    count = stream.shape[0] // ROWS
    return pl.pallas_call(
        functools.partial(target_kernel, count, parts, tuned),
        out_shape=f32(8, ROWS),
        in_specs=in_smem() + in_vmem(3) + hbm(len(buffers)),
        out_specs=in_vmem(1)[0],
        scratch_shapes=ends_scratch(parts, buffers, tuned),
        compiler_params=pltpu.CompilerParams(vmem_limit_bytes=VMEM_LIMIT),
        cost_estimate=LIGHT,
        name="head_target",
    )(place, stream, whole, real, *buffers)


def loss_kernel(count, frames_all, parts, tuned, place, stream, target, whole, legal, *refs):
    sources, refs = (refs[:-11], refs[-11:])
    loss, dstream, dpool, acts, *weights, sems, pool_t, pooled, dpooled = refs
    arrived = fetch_ends(parts, tuned, place, sources, weights, sems)
    _, proj, heads = weights
    games, taken = (whole[:, 0:1], whole[:, 1:2])
    logits, before, hidden = head_forward(count, stream, arrived, games, pool_t, pooled)
    atoms = support_lanes()
    inside = atom_lanes() < ATOMS
    logps, probs, values = ([], [], [])
    for value in logits:
        value = value - jnp.max(value, axis=1, keepdims=True)
        power = jnp.where(inside, jnp.exp(value), 0.0)
        mass = lane_sum(power)
        logps.append(value - jnp.log(mass))
        probs.append(power / mass)
        values.append(lane_sum(probs[-1] * atoms))
    masked = [
        jnp.where(legal[:, action : action + 1] > 0, values[action], -1e30)
        for action in range(ACTIONS)
    ]
    largest = functools.reduce(jnp.maximum, masked)
    powers = [jnp.exp(value - largest) for value in masked]
    mass = sum(powers[1:], powers[0])
    goal = target[...]
    goal_mass = lane_sum(goal)
    cross = taken_value = 0.0
    real = lax.broadcasted_iota(jnp.int32, (8, 1), 0) < count
    scale = jnp.where(real, 1.0 / frames_all, 0.0)
    spread = jnp.zeros((8, 2 * WIDTH), jnp.float32)
    for action in range(ACTIONS):
        here = jnp.where(taken == action, 1.0, 0.0)
        cross = cross - here * lane_sum(jnp.where(inside, goal * logps[action], 0.0))
        taken_value = taken_value + here * values[action]
        grad = here * (probs[action] * goal_mass - goal)
        pull = CQL_WEIGHT * (powers[action] / mass - here)
        grad = grad + pull * probs[action] * (atoms - values[action])
        grad = jnp.where(inside, grad * scale, 0.0)
        grad = jnp.concatenate([grad, jnp.zeros((8, 2 * WIDTH - ROWS), jnp.float32)], axis=1)
        offset = action * ATOMS
        spread = spread + (pltpu.roll(grad, offset, 1) if offset else grad)
    losses = cross + CQL_WEIGHT * (jnp.log(mass) + largest - taken_value)
    loss[...] = jnp.sum(jnp.where(real, losses, 0.0), axis=0, keepdims=True)
    dhidden = None
    spread = spread.astype(jnp.bfloat16)
    for game in range(GAMES):
        mine = jnp.where(games == game, spread, 0.0).astype(jnp.bfloat16)
        for half in range(2):
            part = mine[:, half * WIDTH : (half + 1) * WIDTH]
            term = dot_lanes(part, merge(heads[2 * game + half]))
            dhidden = term if dhidden is None else dhidden + term
    dbefore = (silu_slope(before) * dhidden).astype(jnp.bfloat16)
    pieces = [hidden, dbefore]
    pieces += [pooled[:, part * WIDTH : (part + 1) * WIDTH] for part in range(D // WIDTH)]
    lanes = lax.broadcasted_iota(jnp.int32, (8, WIDTH), 1)
    marked = jnp.where(lanes == WIDTH - 1, games.astype(jnp.float32), spread[:, WIDTH:].astype(jnp.float32))
    pieces += [spread[:, :WIDTH], marked]
    acts[...] = jnp.concatenate([piece.astype(jnp.float32) for piece in pieces]).astype(jnp.bfloat16)
    dpooled[...] = dot_lanes(dbefore, merge(proj[...])).astype(jnp.bfloat16).astype(jnp.float32)

    def push(frame, rows, lanes):
        dstream[rows, lanes] = dpooled[frame, lanes] * pool_t[:, lanes]

    each_chunk(count, D, push)

    def gather_pool(part, carry):
        lanes = pl.ds(pl.multiple_of(part * ROWS, ROWS), ROWS)
        total = None
        for frame in range(count):
            value = stream[pl.ds(frame * ROWS, ROWS), lanes].astype(jnp.bfloat16)
            term = value.astype(jnp.float32) * dpooled[pl.ds(frame, 1), lanes]
            total = term if total is None else total + term
        dpool[0, lanes, :] = total.T.astype(jnp.bfloat16)
        return carry

    lax.fori_loop(0, D // ROWS, gather_pool, 0)


def head_loss(stream, target, whole, legal, frames_all, parts, buffers, tuned, place):
    rows = stream.shape[0]
    return pl.pallas_call(
        functools.partial(loss_kernel, rows // ROWS, frames_all, parts, tuned),
        out_shape=[f32(1, 1), f32(rows, D), bf16(1, D, ROWS), bf16(ACTS, WIDTH)],
        in_specs=in_smem() + in_vmem(4) + hbm(len(buffers)),
        out_specs=in_vmem(4),
        scratch_shapes=ends_scratch(parts, buffers, tuned) + [pltpu.VMEM((8, D), jnp.float32)],
        compiler_params=pltpu.CompilerParams(vmem_limit_bytes=VMEM_LIMIT),
        cost_estimate=LIGHT,
        name="head_loss",
    )(place, stream, target, whole, legal, *buffers)


ACTS = 64


def own_heads_kernel(parts, tuned, place, *refs):
    sources, (heads, proj, acts, sems) = (refs[:-4], refs[-4:])
    fetch(parts, tuned, place, sources, {0: acts}, sems)
    pltpu.make_async_copy(acts, acts, sems.at[0]).wait()
    value = acts[...].reshape(-1, ACTS, WIDTH).astype(jnp.float32)
    pieces = [value[:, first : first + 8].reshape(-1, WIDTH) for first in range(0, ACTS, 8)]
    pieces = [piece.astype(jnp.bfloat16) for piece in pieces]
    hidden, dbefore, scores = (pieces[0], pieces[1], pieces[-2:])
    games = scores[1][:, WIDTH - 1 :].astype(jnp.float32)
    lanes = lax.broadcasted_iota(jnp.int32, scores[1].shape, 1)
    scores[1] = jnp.where(lanes < WIDTH - 1, scores[1].astype(jnp.float32), 0.0).astype(jnp.bfloat16)
    row = lax.broadcasted_iota(jnp.int32, (WIDTH, ROWS), 0)
    lane = lax.broadcasted_iota(jnp.int32, (WIDTH, ROWS), 1)

    def own(items, count):
        total = None
        for block, item in enumerate(items):
            wanted = (row + block * WIDTH == place[4] * count + lane) & (lane < count)
            term = dot(item, jnp.where(wanted, 1.0, 0.0).astype(jnp.bfloat16))
            total = term if total is None else total + term
        return total.astype(jnp.bfloat16)

    count = heads.shape[1]
    mine = own([hidden], count)
    for game in range(GAMES):
        for half in range(2):
            chosen = jnp.where(games == game, scores[half].astype(jnp.float32), 0.0)
            heads[2 * game + half] = dot_rows(mine, chosen.astype(jnp.bfloat16))[:count]
    count = proj.shape[1]
    proj[0] = dot_rows(own(pieces[2:-2], count), dbefore)[:count]


def own_heads(buffers, heads, proj, tuned, place):
    parts = [Part(1, ACTS, WIDTH)]
    return pl.pallas_call(
        functools.partial(own_heads_kernel, parts, tuned),
        out_shape=[f32(part.blocks, part.rows, part.lanes) for part in (heads, proj)],
        in_specs=in_smem() + hbm(len(buffers)),
        out_specs=in_vmem(2),
        scratch_shapes=[
            pltpu.VMEM(weight_shapes(parts, buffers, tuned)[0], jnp.bfloat16),
            pltpu.SemaphoreType.DMA((1,)),
        ],
        compiler_params=pltpu.CompilerParams(vmem_limit_bytes=VMEM_LIMIT),
        cost_estimate=LIGHT,
        name="own_heads",
    )(place, *buffers)


WIDTH = 512
TILE = 16
AXES = ("wide", "narrow")


def grid_sizes():
    return (lax.axis_size("wide") // 2, 2, lax.axis_size("narrow") // 2, 2)


def spot():
    sizes = grid_sizes()
    wide, narrow = (lax.axis_index("wide"), lax.axis_index("narrow"))
    place = [wide // sizes[1], wide % sizes[1], narrow // sizes[3], narrow % sizes[3]]
    return jnp.stack(place + [wide * lax.axis_size("narrow") + narrow]).astype(jnp.int32)


def hop(array, axis_of_core, step=1, swap=0):
    sizes = grid_sizes()

    def target(place):
        axis = axis_of_core[place[3]]
        other = list(place)
        other[axis] = place[axis] ^ swap if swap else (place[axis] + step) % sizes[axis]
        return other

    return send(array, target)


def flip(array, *bits):
    return send(array, lambda place: [value ^ bit for value, bit in zip(place, bits)])


def send(array, target):
    sizes = grid_sizes()
    pairs = []
    for place in itertools.product(*[range(size) for size in sizes]):
        pairs.append(
            tuple(
                ((z * sizes[1] + y) * sizes[2] + x) * sizes[3] + core
                for z, y, x, core in (place, target(place))
            )
        )
    return lax.ppermute(array, AXES, pairs)


ALONG_Z = (0, 0)
ACROSS = (3, 3)
NEAR = (2, 1)
FAR = (1, 2)


def hbm(number):
    return [pl.BlockSpec(memory_space=pl.ANY)] * number


def in_vmem(number):
    return [pl.BlockSpec(memory_space=pltpu.VMEM)] * number


def in_smem():
    return [pl.BlockSpec(memory_space=pltpu.SMEM)]


def copies(pairs, sems):
    started = [
        pltpu.make_async_copy(source, target, sems.at[index])
        for index, (source, target) in enumerate(pairs)
    ]
    for copy in started:
        copy.start()
    for copy in started:
        copy.wait()


class Part:
    def __init__(self, blocks, rows, lanes):
        self.blocks, self.rows, self.lanes = (blocks, rows, lanes)
        self.across = WIDTH // lanes
        self.travel = blocks * rows // self.across

    def moves(self):
        if self.across > 1:
            deep = self.rows // self.across
            return [(0, part * self.lanes, deep, 0, part * deep) for part in range(self.across)]
        return [(block * self.rows, 0, self.rows, block, 0) for block in range(self.blocks)]

    def pack(self, piece):
        if self.across > 1:
            piece = piece.reshape(self.across, self.rows // self.across, self.lanes)
            return piece.transpose(1, 0, 2).reshape(self.travel, WIDTH)
        return piece.reshape(self.travel, WIDTH)

    def unpack(self, rows):
        if self.across > 1:
            rows = rows.reshape(self.rows // self.across, self.across, self.lanes)
            return rows.transpose(1, 0, 2).reshape(1, self.rows, self.lanes)
        return rows.reshape(self.blocks, self.rows, self.lanes)

    def full(self, depth):
        return (self.blocks, depth, 2, 2, 2, self.rows, self.lanes)


def half_rows(parts):
    total = sum(part.travel for part in parts)
    return -(-total // (2 * TILE)) * TILE


def half_moves(parts):
    cut = half_rows(parts)
    halves = ([], [])
    offset = 0
    for index, part in enumerate(parts):
        for row, lane, rows, block, inner in part.moves():
            row = row + offset
            before = max(0, min(rows, cut - row))
            if before:
                halves[0].append((index, row, lane, before, block, inner))
            if rows - before:
                halves[1].append((index, row + before - cut, lane, rows - before, block, inner + before))
        offset += part.travel
    return halves


def unit(parts, depth):
    return (depth, 2, half_rows(parts), WIDTH)


def pack(parts, pieces):
    rows = jnp.concatenate([part.pack(piece) for part, piece in zip(parts, pieces)])
    return jnp.pad(rows, ((0, 2 * half_rows(parts) - rows.shape[0]), (0, 0)))


def assemble_pairs(parts, core, y, x, ins, outs):
    pairs = []
    for other, far, near in itertools.product((0, 1), repeat=3):
        half = core ^ other
        step = [0, 0, 0, 0]
        step[NEAR[half]], step[FAR[half]] = (near, far)
        at_y, at_x = (lax.rem(y + step[1], 2), lax.rem(x + step[2], 2))
        for index, row, lane, rows, block, inner in half_moves(parts)[half]:
            if index not in outs:
                continue
            pairs.append(
                (
                    index,
                    ins[2 * other + far].at[near, :, :, pl.ds(row, rows), pl.ds(lane, parts[index].lanes)],
                    outs[index].at[block, :, at_y, at_x, :, pl.ds(inner, rows)],
                )
            )
    return pairs


def fetch(parts, tuned, place, sources, weights, sems):
    if not tuned:
        for index, weight in weights.items():
            pltpu.make_async_copy(sources[index], weight, sems.at[index]).start()
        return
    for core in (0, 1):

        @pl.when(place[3] == core)
        def _():
            pairs = assemble_pairs(parts, core, place[1], place[2], sources, weights)
            for index, source, target in sorted(pairs, key=lambda pair: pair[0]):
                pltpu.make_async_copy(source, target, sems.at[index]).start()


def weight_shapes(parts, buffers, tuned):
    if tuned:
        return [part.full(buffers[0].shape[1]) for part in parts]
    return [item.shape for item in buffers]


def assemble_kernel(parts, some, place, *refs):
    outs, sems = (dict(zip(some, refs[4:-1])), refs[-1])
    fetch(parts, True, place, refs[:4], outs, sems)
    for index, out in outs.items():
        pltpu.make_async_copy(out, out, sems.at[index]).wait()


def assemble(parts, buffers, place, some=None):
    some = range(len(parts)) if some is None else some
    shapes = weight_shapes(parts, buffers, True)
    full = pl.pallas_call(
        functools.partial(assemble_kernel, parts, some),
        out_shape=[bf16(*shapes[index]) for index in some],
        in_specs=in_smem() + hbm(4),
        out_specs=in_vmem(len(some)),
        scratch_shapes=[pltpu.SemaphoreType.DMA((len(parts),))],
        compiler_params=pltpu.CompilerParams(vmem_limit_bytes=VMEM_LIMIT),
        cost_estimate=LIGHT,
        name="assemble",
    )(place, *buffers)
    return [merged(item) for item in full]


def merged(array):
    return array.reshape(array.shape[0], -1, array.shape[-1])


def in_order(own, other, bit):
    first = jnp.where(bit == 0, own, other)
    second = jnp.where(bit == 0, other, own)
    return jnp.stack([first, second])


def together(*trees):
    flat, tree = jax.tree.flatten(trees)
    return jax.tree.unflatten(tree, lax.optimization_barrier(flat))


def start_gather(groups, pieces, place):
    core = place[3]
    packed = [pack(parts, items) for parts, items in zip(groups, pieces)]
    halves = [half_rows(parts) for parts in groups]
    kept = [lax.dynamic_slice_in_dim(rows, core * half, half) for rows, half in zip(packed, halves)]
    sent = [
        lax.dynamic_slice_in_dim(rows, (1 - core) * half, half) for rows, half in zip(packed, halves)
    ]
    got = hop(jnp.concatenate(sent), ACROSS)
    held = []
    offset = 0
    for keep, half in zip(kept, halves):
        held.append(in_order(keep, got[offset : offset + half], core))
        offset += half
    return held


def pipelined_gather(groups, pieces, place, state, arrived):
    count = len(groups)
    low, high = (place[0] % 2, place[0] // 2)
    held = start_gather(groups[:1], pieces(None)[:1], place)
    for tick in range(count + 3):
        near, far, last = [index if 0 <= index < count else None for index in range(tick - 1, tick - 4, -1)]
        live = [index for index in (tick, near, far, last) if index is not None and index < count]
        if tick in (1, 2):
            live += range(tick + 1, count)
        items, state = together([held[index] for index in live], state)
        for index, item in zip(live, items):
            held[index] = item
        if tick == 0:
            held += start_gather(groups[1:2], pieces(held[0])[1:2], place)
            held += start_gather(groups[2:], pieces(held[1])[2:], place)
        if last is not None:
            own, arrived_far, other = held[last]
            held[last] = [own, arrived_far, other, hop(arrived_far, ACROSS)]
        if far is not None:
            held[far] = [held[far], hop(held[far], FAR), hop(held[far], ACROSS)]
        if near is not None:
            held[near] = [held[near], hop(held[near], NEAR)]
        if tick == 0:
            held[0] = [held[0]] + [hop(held[0], ALONG_Z, swap=bits) for bits in (1, 2, 3)]
        elif tick < count:
            held[tick] = [held[tick], hop(held[tick], ALONG_Z, swap=2)]
        if tick < 3:
            early = slice(tick + 1, tick + 2 if tick < 2 else count)
            got = hop(jnp.concatenate(held[early], axis=1), ALONG_Z, swap=1)
            ends = list(itertools.accumulate(half_rows(parts) for parts in groups[early]))
            got = jnp.split(got, ends[:-1], axis=1)
            held[early] = [in_order(item, other, low) for item, other in zip(held[early], got)]
        if last is not None:
            state = arrived(last, held[last], state)
        if tick < count:
            items, state = together(held[tick], state)
            if tick == 0:
                items = [in_order(*items[:2], low), in_order(*items[2:], low)]
            both = in_order(*items, high)
            held[tick] = both.reshape(-1, *both.shape[2:])
        if near is not None:
            items, state = together(held[near], state)
            held[near] = jnp.stack(items)
    return state


def whole_shape(part):
    return (part.blocks, part.rows * lax.axis_size(AXES), part.lanes)


def dealt_shapes(parts, tuned):
    if not tuned:
        return [whole_shape(part) for part in parts]
    size = (grid_sizes()[0], 2, half_rows(parts), WIDTH)
    return [lead + size for lead in ((2, 2), (2,), (), ())]


def start_deal(parts, tuned, place, wanted, arrays, dealt, sems):
    if not tuned:
        pltpu.make_async_copy(arrays[wanted], dealt[wanted], sems.at[wanted]).start()
        return
    array = arrays[wanted].reshape(*parts[wanted].full(grid_sizes()[0]))
    to_core, to_far, to_near, own = dealt
    for core in (0, 1):

        @pl.when(place[3] == core)
        def _():
            for other, far, near in itertools.product((0, 1), repeat=3):
                half = core ^ other
                step = [0, 0, 0, 0]
                step[NEAR[half]], step[FAR[half]] = (near, far)
                at_y, at_x = (lax.rem(place[1] + step[1], 2), lax.rem(place[2] + step[2], 2))
                if other:
                    target = to_core.at[far, near]
                elif far:
                    target = to_far.at[near]
                else:
                    target = to_near if near else own
                for index, row, lane, rows, block, inner in half_moves(parts)[half]:
                    if index == wanted:
                        pltpu.make_async_copy(
                            array.at[block, :, at_y, at_x, :, pl.ds(inner, rows)],
                            target.at[:, :, pl.ds(row, rows), pl.ds(lane, parts[index].lanes)],
                            sems.at[index],
                        ).start()


def add_up(*terms):
    total = terms[0].astype(jnp.float32)
    for term in terms[1:]:
        total = total + term.astype(jnp.float32)
    return total


def low_add(*terms):
    return add_up(*terms).astype(jnp.bfloat16)


def scatter_stages(place, direct):
    depth = grid_sizes()[0]
    z, core = (place[0], place[3])
    low, high = (z % 2, z // 2)

    def across(items):
        to_core, *rest = items
        return rest + [hop(to_core, ACROSS)]

    def far(items):
        to_far, to_near, own, from_core = items
        return [to_near, own, from_core, hop(low_add(to_far, from_core[1]), FAR)]

    def near(items):
        to_near, own, from_core, from_far = items
        from_near = hop(low_add(to_near, from_core[0, 1], from_far[1]), NEAR)
        return [own, from_core[0, 0], from_far[0], from_near]

    def pick(array, at):
        return lax.dynamic_index_in_dim(array, at, 0, False)

    def along(items):
        summed = lax.optimization_barrier(add_up(*items))
        sent = [pick(summed, lax.rem(z + step, depth)) for step in range(1, depth)]
        got = [hop(item.astype(jnp.bfloat16), ALONG_Z, step + 1) for step, item in enumerate(sent)]
        return [pick(summed, z)] + got

    def pairs(items):
        summed = lax.optimization_barrier(add_up(*items))
        summed = summed.reshape(2, 2, *summed.shape[1:])
        return [pick(summed, high), hop(pick(summed, 1 - high).astype(jnp.bfloat16), ALONG_Z, swap=2)]

    def neighbours(items):
        summed = add_up(*items)
        return [pick(summed, low), hop(pick(summed, 1 - low).astype(jnp.bfloat16), ALONG_Z, swap=1)]

    def finish(items):
        total = add_up(*items)
        other = hop(pick(total, 1 - core), ACROSS)
        return in_order(pick(total, core), other, core).reshape(-1, WIDTH)

    return [across, far, near] + ([along] if direct else [pairs, neighbours]) + [finish]


def share_stages(part, place):
    low, high = (place[0] % 2, place[0] // 2)

    def along(item):
        one, two, three = [hop(item, ALONG_Z, swap=bits) for bits in (1, 2, 3)]
        both = in_order(in_order(item, one, low), in_order(two, three, low), high)
        return both.reshape(-1, *both.shape[2:])

    return [
        lambda item: start_gather([[part]], [[item]], place)[0],
        along,
        lambda item: jnp.stack([item, hop(item, NEAR)]),
        lambda item: [item, hop(item, FAR), hop(item, ACROSS)],
        lambda items: items + [hop(items[1], ACROSS)],
    ]


def pipelined_scatter(count, place, state, steps, shared):
    held, todo = ([], [])
    part, piece, more = shared
    share = share_stages(part, place)
    for tick in range(count + 5):
        live = [index for index in range(len(held)) if todo[index]]
        items, state, piece = together([held[index] for index in live], state, piece)
        for index, item in zip(live, items):
            held[index] = item
            for _ in range(2 if index == tick - 1 else 1):
                held[index] = todo[index].pop(0)(held[index])
        if share:
            piece = share.pop(0)(piece)
        elif more:
            piece = more.pop(0)(piece, held)
        if tick < count:
            dealt, state = steps[tick](state)
            held.append(dealt)
            todo.append(scatter_stages(place, tick >= count - 2))
    return (held, piece, state)


CQL_WEIGHT = 0.05
BETA_ONE = 0.5
BETA_TWO = 0.5
LEARNING_RATE = 0.25
WEIGHT_DECAY = 0.01
PATCH_IN = 256
DPROJ = 512
ACTIONS = 18
ATOMS = 51
GAMES = 4
BLOCKS = 2
STEP = 5
PLAYS = ACTIONS * ATOMS


def average_decay():
    return min(0.99, (1.0 + STEP) / (10.0 + STEP))


SWEEP = 8192


def lamb_parts(grads, params, first, second):
    momentum = BETA_ONE * first + (1.0 - BETA_ONE) * grads
    variance = BETA_TWO * second + (1.0 - BETA_TWO) * grads * grads
    direction = (
        momentum / (1.0 - BETA_ONE**STEP) / (jnp.sqrt(variance / (1.0 - BETA_TWO**STEP)) + 1e-06)
        + WEIGHT_DECAY * params
    )
    return (momentum, variance, direction)


def stretches(cuts):
    found = []
    at = 0
    for index, (start, size) in enumerate(cuts):
        end = start + size
        last = index == len(cuts) - 1
        whole = end if last else end // ROWS * ROWS
        found.append((at, whole - at, [index]))
        at = whole
        if end != whole:
            found.append((whole, ROWS, [index, index + 1]))
            at = whole + ROWS
    return found


def sweep(start, size, body, carry):
    steps = size // SWEEP

    def step(index, carry):
        return body(pl.ds(pl.multiple_of(start + index * SWEEP, ROWS), SWEEP), carry)

    if steps:
        carry = lax.fori_loop(0, steps, step, carry)
    return (carry, start + steps * SWEEP, size - steps * SWEEP)


def row_sum(value):
    return jnp.sum(value, axis=1, keepdims=True)


def put_rows(target, row, source, steps):
    for first, rows, lane, stride in steps:

        def step(index, carry):
            lanes = pl.ds(pl.multiple_of(lane + index * stride, ROWS), WIDTH)
            target[row : row + 1, lanes] = source[pl.ds(first + index, 1), :]
            return carry

        lax.fori_loop(0, rows, step, 0, unroll=4)


def block_rows(name, start, rows, first):
    if name == "w_out":
        count = rows // (D // BOT)
        return [(first + part * count, count, start + part * BOT, D) for part in range(D // BOT)]
    return [(first, rows, start, WIDTH)]


def patch_rows(rows, first):
    count = rows // 4
    return [
        (first + (2 * block + half) * count, count, half * (D // 2) + block * WIDTH, D)
        for block in range(2)
        for half in range(2)
    ]


def direction_kernel(cuts, moves, gain_at, *refs):
    top_cuts, block_cuts = cuts
    number = len(moves)
    sources, refs = (refs[:number], refs[number:])
    late, loss, *refs = refs
    top_ins, block_ins, refs = (refs[:3], refs[3:6], refs[6:])
    sums, *refs = refs
    top_outs, block_outs, (top_grad, block_grad) = (refs[:3], refs[3:6], refs[6:])
    for source, steps in zip(sources, moves):
        for row, placed in steps:
            put_rows(top_grad if row is None else block_grad, row or 0, source, placed)
    patch = top_cuts[0][1]
    top_grad[:, pl.ds(patch, late.shape[1])] = late[...]
    gain_start, gain_width = block_cuts[3]
    source, first = (sources[gain_at[0]], gain_at[1])
    block_grad[:, pl.ds(gain_start, gain_width)] = source[pl.ds(first, 8), :][:BLOCKS, :gain_width]

    def work(lanes, grad, ins, outs):
        param, *moments = [ref[:, lanes] for ref in ins]
        made = lamb_parts(grad[:, lanes], param, *moments)
        for ref, value in zip(outs, made):
            ref[:, lanes] = value
        return (param * param, made[2] * made[2])

    found = []

    def run(cuts, grad, ins, outs, first_lane, height):
        for start, size, segments in stretches(cuts):

            def step(lanes, carry):
                terms = work(lanes, grad, ins, outs)
                return [held + term for held, term in zip(carry, terms)]

            zeros = [jnp.zeros((height, SWEEP), jnp.float32)] * 2
            carry, begin, rest = sweep(start, size, step, zeros)
            sizes = [row_sum(value) for value in carry] if rest != size else None
            if rest:
                terms = work(pl.ds(begin, rest), grad, ins, outs)
                at = begin + lax.broadcasted_iota(jnp.int32, terms[0].shape, 1)
                if len(segments) > 1:
                    edge = cuts[segments[1]][0]
                    after = [row_sum(jnp.where(at >= edge, term, 0.0)) for term in terms]
                    found.extend((first_lane, segments[1], *item) for item in enumerate(after))
                    terms = [jnp.where(at < edge, term, 0.0) for term in terms]
                more = [row_sum(term) for term in terms]
                sizes = more if sizes is None else [held + term for held, term in zip(sizes, more)]
            found.extend((first_lane, segments[0], *item) for item in enumerate(sizes))

    run(top_cuts, top_grad, top_ins, top_outs, 0, 1)
    run(block_cuts, block_grad, block_ins, block_outs, len(top_cuts), BLOCKS)
    rows = lax.broadcasted_iota(jnp.int32, sums.shape, 0)
    lanes = lax.broadcasted_iota(jnp.int32, sums.shape, 1)
    result = jnp.where((rows == 2) & (lanes == 0), loss[...], 0.0)
    for first, segment, row, value in found:
        for part in range(value.shape[0]):
            lane = first + part * len(block_cuts) + segment
            here = (rows == row) & (lanes == lane)
            result = result + jnp.where(here, value[part : part + 1], 0.0)
    sums[...] = result


def directions(cuts, rows, moves, gain_at, late, loss, top_ins, block_ins):
    shapes = [f32(*top_ins[0].shape)] * 3 + [f32(*block_ins[0].shape)] * 3
    ins = [*rows, late, loss, *top_ins, *block_ins]
    return pl.pallas_call(
        functools.partial(direction_kernel, cuts, moves, gain_at),
        out_shape=[f32(8, ROWS)] + shapes,
        in_specs=in_vmem(len(ins)),
        out_specs=in_vmem(7),
        scratch_shapes=[
            pltpu.VMEM(top_ins[0].shape, jnp.float32),
            pltpu.VMEM(block_ins[0].shape, jnp.float32),
        ],
        compiler_params=pltpu.CompilerParams(vmem_limit_bytes=VMEM_LIMIT),
        cost_estimate=LIGHT,
        name="directions",
    )(*ins)


def update_kernel(cuts, sums, *refs):
    top_cuts, block_cuts = cuts
    top_ins, block_ins, refs = (refs[:3], refs[3:6], refs[6:])
    norms, *refs = refs
    top_outs, block_outs = (refs[:2], refs[2:])
    norm = jnp.sqrt(sums[...])
    norms[...] = norm
    ratio = LEARNING_RATE * (norm[0:1] / (norm[1:2] + 1e-06))
    decay = average_decay()

    def work(lanes, ins, outs, scale):
        param, direction, average = [ref[:, lanes] for ref in ins]
        updated, averaged, *half = outs
        value = param - scale * direction
        updated[:, lanes] = value
        averaged[:, lanes] = decay * average + (1.0 - decay) * value
        for ref in half:
            ref[:, lanes] = value.astype(jnp.bfloat16)

    def run(cuts, ins, outs, scales):
        for start, size, segments in stretches(cuts):
            scale = scales[segments[0]]

            def step(lanes, carry):
                work(lanes, ins, outs, scale)
                return carry

            _, begin, rest = sweep(start, size, step, 0)
            if rest:
                if len(segments) > 1:
                    at = begin + lax.broadcasted_iota(jnp.int32, (1, rest), 1)
                    scale = jnp.where(at < cuts[segments[1]][0], scale, scales[segments[1]])
                work(pl.ds(begin, rest), ins, outs, scale)

    lanes = [ratio[:, lane : lane + 1] for lane in range(len(top_cuts) + BLOCKS * len(block_cuts))]
    run(top_cuts, top_ins, top_outs, lanes[: len(top_cuts)])
    rest = lanes[len(top_cuts) :]
    scales = [jnp.concatenate(rest[index :: len(block_cuts)]) for index in range(len(block_cuts))]
    run(block_cuts, block_ins, block_outs, scales)


def update(cuts, sums, top_ins, block_ins):
    shapes = [f32(*array.shape) for array in [top_ins[0]] * 2 + [block_ins[0]] * 2]
    shapes.append(bf16(*block_ins[0].shape))
    return pl.pallas_call(
        functools.partial(update_kernel, cuts),
        out_shape=[f32(8, ROWS)] + shapes,
        in_specs=in_vmem(7),
        out_specs=in_vmem(6),
        compiler_params=pltpu.CompilerParams(vmem_limit_bytes=VMEM_LIMIT),
        cost_estimate=LIGHT,
        name="update",
    )(sums, *top_ins, *block_ins)


def segment_lengths():
    top = [PATCH_IN * D, D * PIX, D * DPROJ, DPROJ * GAMES * PLAYS]
    block = [D * BOT, 9 * BOT * BOT, BOT * D, 2 * (2 * BOT + D)]
    return (top, block)


def cut_points(lengths, devices):
    cuts = []
    offset = 0
    for length in lengths:
        width = length // devices
        cuts.append((offset, width))
        offset += width
    return cuts


def pack_top(flat, cuts):
    patch, pool, proj, heads = [flat[start : start + size] for start, size in cuts]
    patch = patch.reshape(-1, 2, 2, WIDTH).transpose(2, 1, 0, 3).reshape(2, -1, WIDTH)
    pool = jnp.pad(pool.reshape(1, -1, PIX), ((0, 0), (0, 0), (0, ROWS - PIX)))
    heads = jnp.pad(heads.reshape(-1, GAMES, PLAYS), ((0, 0), (0, 0), (0, 2 * WIDTH - PLAYS)))
    heads = heads.reshape(-1, 2 * GAMES, WIDTH).transpose(1, 0, 2)
    return [patch, pool, proj.reshape(1, -1, WIDTH), heads]


def flat_late(pool, proj, heads):
    heads = heads.transpose(1, 0, 2).reshape(-1, GAMES, 2 * WIDTH)[:, :, :PLAYS]
    return jnp.concatenate([item.reshape(-1) for item in (pool[:, :, :PIX], proj, heads)])


def pack_block(flat, cuts):
    w_in, w_mid, w_out = [flat[start : start + size] for start, size in cuts[:3]]
    w_out = w_out.reshape(-1, D // BOT, BOT).transpose(1, 0, 2)
    return [w_in.reshape(1, -1, BOT), w_mid.reshape(1, -1, BOT), w_out]


def parts_for(devices):
    rows = {"patch": 2 * PATCH_IN, "pool": D, "proj": D, "heads": DPROJ}
    rows |= {"w_in": D, "w_mid": TAPS * BOT, "w_out": BOT, "gains": TILE * devices}
    blocks = {"patch": 2, "heads": 2 * GAMES, "w_out": D // BOT}
    return {
        name: Part(blocks.get(name, 1), count // devices, ROWS if name == "pool" else WIDTH)
        for name, count in rows.items()
    }


def is_tuned(devices):
    parts = parts_for(devices).values()
    whole = all(part.rows // part.across % TILE == 0 for part in parts)
    return whole and lax.axis_size("wide") == 8 and lax.axis_size("narrow") == 4


def plain_gather(piece):
    return lax.all_gather(piece, AXES, axis=1, tiled=True)


def plain_scatter(array):
    return lax.psum_scatter(array, AXES, scatter_dimension=1, tiled=True).astype(jnp.float32)


def total(array):
    if lax.axis_size("wide") != 8 or lax.axis_size("narrow") != 4:
        return lax.psum(array, AXES)
    array = array + flip(array, 0, 0, 0, 1)
    array = (array + flip(array, 0, 0, 1, 0)) + (flip(array, 0, 1, 0, 0) + flip(array, 0, 1, 1, 0))
    one, two, three = [flip(array, bits, 0, 0, 0) for bits in (1, 2, 3)]
    return (array + two) + (one + three)


def frame_rows(frames):
    count = frames.shape[0]
    return jnp.pad(frames, ((0, 0), (0, ROWS - PIX), (0, 0))).reshape(count * ROWS, PATCH_IN)


def on_device(
    observed,
    following,
    game_ids,
    actions,
    legal_mask,
    rewards,
    discounts,
    done_flags,
    params_top,
    params_blocks,
    first_top,
    first_blocks,
    second_top,
    second_blocks,
    average_top,
    average_blocks,
    target_top,
    target_blocks,
):
    devices = lax.axis_size(AXES)
    frames_all = observed.shape[0] * devices
    top_lengths, block_lengths = segment_lengths()
    top_cuts = cut_points(top_lengths, devices)
    block_cuts = cut_points(block_lengths, devices)
    gain_start, gain_width = block_cuts[3]
    parts = parts_for(devices)
    tuned = is_tuned(devices)
    place = spot()
    shift = shifts()
    spread = spread_pixels(devices)
    count = observed.shape[0]
    whole = jnp.concatenate([game_ids[:, None], actions], axis=1)
    whole = jnp.pad(whole, ((0, 8 - count), (0, ROWS - 3)), constant_values=-1)
    legal = jnp.pad(legal_mask, ((0, 8 - count), (0, ROWS - ACTIONS)), constant_values=1)
    keep = discounts * (1.0 - done_flags.astype(jnp.float32))
    real = jnp.pad(jnp.stack([rewards, keep], axis=1), ((0, 8 - count), (0, ROWS - 2)))

    def read_pieces(early):
        sources = (target_top, target_blocks, params_top, params_blocks)
        if early is not None:
            early, sources = together(early, sources)
        tops = (sources[0], sources[2].astype(jnp.bfloat16))
        blocks = (sources[1], sources[3].astype(jnp.bfloat16))
        own = {}
        for net, top, flat in zip(("target", "online"), tops, blocks):
            for name, piece in zip(("patch", "pool", "proj", "heads"), pack_top(top, top_cuts)):
                own[net, name] = piece
            for index in range(BLOCKS):
                for name, piece in zip(block_names, pack_block(flat[index], block_cuts)):
                    own[net, name, index] = piece
        gain_rows = jnp.concatenate(blocks)[:, gain_start:]
        own["gains",] = jnp.pad(
            gain_rows, ((0, TILE - 2 * BLOCKS), (0, WIDTH - gain_width))
        ).reshape(1, TILE, WIDTH)
        return [[own[key] for key in group] for group in keys]

    block_names = ("w_in", "w_mid", "w_out")

    def part_of(key):
        return parts[key[0] if key[0] in parts else key[1]]

    full = {}

    def block_weight(index, name):
        return merged(full["online", name, index]).reshape(-1, BOT)

    def hold(net, index, group, buffers, state):
        full["held", index] = (group, buffers)
        return state

    def read_gains(group, buffers, state):
        gains = assemble(group_parts(group), buffers, place, [0])[0] if tuned else buffers[0]
        gains = gains.reshape(devices, TILE, WIDTH)[:, : 2 * BLOCKS, :gain_width]
        gains = gains.transpose(1, 0, 2).reshape(2 * BLOCKS, -1).astype(jnp.float32)
        return run_block("target", 0, group, buffers, state | {"gains": gains})

    def target_ends(group, buffers, state):
        for index in range(1, BLOCKS):
            state = run_block("target", index, *full["held", index], state)
        target = head_target(
            state.pop("stream"), whole, real, group_parts(group), buffers, tuned, place
        )
        return state | {"target": target}

    def online_ends(group, buffers, state):
        loss, dstream, dpool, acts = head_loss(
            state.pop("stream"), state.pop("target"), whole, legal, frames_all,
            group_parts(group), buffers, tuned, place,
        )
        return state | {"loss": loss, "grad": dstream, "pool": dpool, "acts": acts}

    def run_block(net, index, group, buffers, state):
        keep = net == "online"
        row = index + (BLOCKS if keep else 0)
        gain = state["gains"][row : row + 1]
        stream = [state["pixels" if keep else "following"], spread]
        if index:
            stream = [state["stream"]]
        skip = 1 if keys[group][0] == ("gains",) else 0
        out, *kept = block_forward(
            stream, gain, shift, group_parts(group), skip, buffers, place, keep, tuned
        )
        state = state | {"stream": out}
        if keep:
            start = kept.pop(0) if index == 0 else stream[0]
            full.update(zip([(net, name, index) for name in block_names], kept[-3:]))
            state |= {"kept%d" % index: [start, *kept[:-3]]}
        return state

    keys, then = ([], [])
    ends = ("pool", "proj", "heads")

    def add_group(group, run, *names):
        keys.append(group)
        then.append(functools.partial(run, *names))

    def block_keys(net, index):
        return [(net, name, index) for name in block_names]

    for index in range(1, BLOCKS):
        add_group(block_keys("target", index), hold, "target", index)
    add_group([("gains",), ("target", "patch")] + block_keys("target", 0), read_gains)
    add_group([("target", name) for name in ends], target_ends)
    for index in range(BLOCKS):
        start = [] if index else [("online", "patch")]
        add_group(start + block_keys("online", index), run_block, "online", index)
    add_group([("online", name) for name in ends], online_ends)

    def group_parts(group):
        return [part_of(key) for key in keys[group]]

    def arrived(group, buffers, state):
        return then[group](group, buffers, dict(state))

    state = {"following": frame_rows(following), "pixels": frame_rows(observed)}
    if tuned:
        groups = [group_parts(group) for group in range(len(keys))]
        state = pipelined_gather(groups, read_pieces, place, state, arrived)
    else:
        for group, items in enumerate(read_pieces(None)):
            state = arrived(group, [plain_gather(item) for item in items], state)

    keys = []
    steps = []

    def out_inputs(index, state):
        stream, hid_one, hid_two, hid_three, rstd = state["kept%d" % index]
        gain = state["gains"][BLOCKS + index : BLOCKS + index + 1]
        return [stream, hid_two, hid_three, rstd, block_weight(index, "w_out"), gain]

    def out_step(index, group, state):
        (dres, low, late), dealt = back_out(
            state.pop("grad"), *out_inputs(index, state), state.pop("pool"), group, tuned, place
        )
        return (dealt, state | {"grad": dres, "low": low, "late%d" % index: late})

    def mid_step(index, group, state):
        stream, hid_one, hid_two, hid_three, rstd = state["kept%d" % index]
        gain = state["gains"][BLOCKS + index : BLOCKS + index + 1]
        (low, early), dealt = back_mid(
            state["low"], hid_one, rstd, block_weight(index, "w_mid"), gain, shift, group, tuned, place
        )
        return (dealt, state | {"low": low, "early%d" % index: early})

    def between_step(index, group, state):
        stream = state.pop("kept%d" % index)[0]
        (dres, low, late), dealt = back_between(
            state["low"], stream, state["grad"], block_weight(index, "w_in"),
            out_inputs(index - 1, state), group, tuned, place,
        )
        return (dealt, state | {"grad": dres, "low": low, "late%d" % (index - 1): late})

    def first_step(group, state):
        stream = state.pop("kept0")[0]
        dgains = [
            jnp.concatenate([state.pop("early%d" % index), state.pop("late%d" % index)], axis=1)
            for index in range(BLOCKS)
        ]
        dgains = jnp.concatenate(dgains).reshape(BLOCKS, devices, gain_width).transpose(1, 0, 2)
        dgains = jnp.pad(dgains, ((0, 0), (0, TILE - BLOCKS), (0, WIDTH - gain_width)))
        dgains = dgains.reshape(1, -1, WIDTH).astype(jnp.bfloat16)
        dealt = back_first(
            state.pop("low"), stream, state.pop("grad"), block_weight(0, "w_in"),
            state.pop("pixels"), spread, dgains, group, tuned, place,
        )
        return (dealt, state)

    def add_step(group, run, *names):
        keys.append(group)
        steps.append(
            lambda state: run(*names, [parts[key[0]] for key in group], dict(state))
        )

    loss_part, acts = (state.pop("loss"), state.pop("acts"))
    add_step([("w_out", BLOCKS - 1), ("pool",)], out_step, BLOCKS - 1)
    for index in reversed(range(BLOCKS)):
        add_step([("w_mid", index)], mid_step, index)
        if index:
            add_step([("w_in", index), ("w_out", index - 1)], between_step, index)
    add_step([("w_in", 0), ("patch",), ("gains",)], first_step)
    def read_heads(buffers, rows):
        return own_heads(buffers, parts["heads"], parts["proj"], tuned, place)

    def read_late(pair, rows):
        pool = parts["pool"]
        first = parts["w_out"].travel
        return flat_late(pool.unpack(rows[0][first : first + pool.travel]), pair[1], pair[0])[None]

    groups = [[parts[key[0]] for key in group] for group in keys]
    if tuned:
        shared = (Part(1, ACTS, WIDTH), acts[None], [read_heads, read_late])
        mine, late, state = pipelined_scatter(len(groups), place, state, steps, shared)
    else:
        mine = []
        for group, step in zip(groups, steps):
            arrays, state = step(state)
            mine.append(pack(group, [plain_scatter(array) for array in arrays]))
        late = read_late(read_heads([plain_gather(acts[None])], mine), mine)
    at = {}
    moves = []
    for number, group in enumerate(keys):
        first = 0
        steps = []
        for key in group:
            count = parts[key[0]].travel
            at[key] = (number, first)
            if len(key) > 1:
                start = block_cuts[block_names.index(key[0])][0]
                steps.append((key[1], block_rows(key[0], start, count, first)))
            elif key[0] == "patch":
                steps.append((None, patch_rows(count, first)))
            first += count
        moves.append(steps)
    cuts = (top_cuts, block_cuts)
    tops = [array[None] for array in (params_top, first_top, second_top, average_top)]
    sums, *made = directions(
        cuts, mine, moves, at["gains",], late, loss_part,
        tops[:3], [params_blocks, first_blocks, second_blocks],
    )
    momentum_top, variance_top, direction_top, momentum_blocks, variance_blocks, direction_blocks = made
    sums = total(sums)
    norms, *made = update(
        cuts, sums, [tops[0], direction_top, tops[3]],
        [params_blocks, direction_blocks, average_blocks],
    )
    updated_top, averaged_top, updated_blocks, averaged_blocks, half_blocks = made
    loss_total = sums[2, 0]
    matrix_norms = norms[:2, : len(top_cuts) + BLOCKS * len(block_cuts)]
    number, first = at["gains",]
    gain_grads = mine[number][first : first + BLOCKS, :gain_width]
    return (
        loss_total,
        matrix_norms,
        updated_top[0],
        updated_top[0].astype(jnp.bfloat16),
        momentum_top[0],
        variance_top[0],
        averaged_top[0],
        updated_blocks,
        half_blocks,
        momentum_blocks,
        variance_blocks,
        averaged_blocks,
        gain_grads,
    )


def solution(mesh):
    one = P(AXES)
    flat = P(None, AXES)
    return jax.shard_map(
        on_device,
        mesh=mesh,
        in_specs=(P(AXES, None, None),) * 2
        + (one, P(AXES, None), P(AXES, None))
        + (one,) * 3
        + (one, flat) * 5,
        out_specs=(P(), P()) + (one,) * 5 + (flat,) * 6,
        check_vma=False,
    )
```

```python
import functools
import itertools

import jax
import jax.numpy as jnp
from jax import lax
from jax.experimental import pallas as pl
from jax.experimental.pallas import tpu as pltpu
from jax.sharding import PartitionSpec as P

D = 2048
BOT = 512
GROUPS = 32
SIDE = 11
PIX = 121
TAPS = 9

ROWS = 128
LANES = 512
VMEM_LIMIT = 44 * 1024 * 1024
LIGHT = pl.CostEstimate(flops=1024, bytes_accessed=1024, transcendentals=0)


def shifts():
    pixel = jnp.arange(ROWS)
    row, col = (pixel // SIDE, pixel % SIDE)
    mats = []
    for tap in range(TAPS):
        at_row, at_col = (row + tap // 3 - 1, col + tap % 3 - 1)
        inside = (at_row >= 0) & (at_row < SIDE) & (at_col >= 0) & (at_col < SIDE) & (pixel < PIX)
        mats.append((inside[:, None] & (pixel[None, :] == (at_row * SIDE + at_col)[:, None])))
    return jnp.concatenate(mats, axis=0).astype(jnp.bfloat16)


def dot(left, right):
    return jnp.dot(left, right, preferred_element_type=jnp.float32)


def dot_rows(left, right):
    return lax.dot_general(
        left, right, (((0,), (0,)), ((), ())), preferred_element_type=jnp.float32
    )


def dot_lanes(left, right):
    return lax.dot_general(
        left, right, (((1,), (1,)), ((), ())), preferred_element_type=jnp.float32
    )


def each_chunk(count, chans, body, unroll=1):
    per = chans // LANES

    def step(index, carry):
        frame = index // per
        rows = pl.ds(pl.multiple_of(frame * ROWS, ROWS), ROWS)
        lanes = pl.ds(pl.multiple_of((index % per) * LANES, LANES), LANES)
        body(pl.ds(frame, 1), rows, lanes)
        return carry

    lax.fori_loop(0, count * per, step, 0, unroll=unroll)


def real_rows():
    return lax.broadcasted_iota(jnp.int32, (ROWS, LANES), 0) < PIX


def group_mean(sums):
    chans = sums.shape[1]
    width = chans // GROUPS
    lane = lax.broadcasted_iota(jnp.int32, sums.shape, 1)
    step = 1
    while step < width:
        ahead = pltpu.roll(sums, chans - step, 1)
        behind = pltpu.roll(sums, step, 1)
        sums = sums + jnp.where((lane & step) == 0, ahead, behind)
        step *= 2
    return sums * (1.0 / (PIX * width))


def silu(value):
    return value / (1.0 + jnp.exp(-value))


def silu_slope(value):
    gate = 1.0 / (1.0 + jnp.exp(-value))
    return gate * (1.0 + value * (1.0 - gate))


def normalise(count, chans, hid, sums, rstd, rstd_at):
    whole = pl.ds(0, chans)
    sums[:, whole] = jnp.zeros((sums.shape[0], chans), jnp.float32)

    def add(frame, rows, lanes):
        sums[frame, lanes] = jnp.sum(hid[rows, lanes], axis=0, keepdims=True)

    each_chunk(count, chans, add, unroll=2)
    sums[:, whole] = group_mean(sums[:, whole])

    def center(frame, rows, lanes):
        value = jnp.where(real_rows(), hid[rows, lanes] - sums[frame, lanes], 0.0)
        hid[rows, lanes] = value
        sums[frame, lanes] = jnp.sum(value * value, axis=0, keepdims=True)

    each_chunk(count, chans, center, unroll=2)
    at = pl.ds(rstd_at, chans)
    rstd[:, at] = lax.rsqrt(group_mean(sums[:, whole]) + 1e-05)


def forward_kernel(count, keep, parts, skip, tuned, *refs):
    refs = list(refs)
    number = len(parts) - skip
    first = number > 3

    def take(number):
        taken = refs[:number]
        del refs[:number]
        return taken

    (place,) = take(1)
    x = take(2 if first else 1)
    gains, shift = take(2)
    sources = take(4 if tuned else len(parts))
    (out,) = take(1)
    if keep:
        if first:
            (start,) = take(1)
        hid_one, hid_two, hid_three, rstd = take(4)
        kept_weights = take(3)
    weights = take(number)
    sems, back_sems, low, act, cols, sums = take(6)
    if not keep:
        hid_one, hid_two, hid_three, rstd = take(4)
        if first:
            (start,) = take(1)
    fetch(parts, tuned, place, sources, dict(enumerate(weights, skip)), sems)

    def arrived(index):
        weight = weights[index]
        pltpu.make_async_copy(weight, weight, sems.at[len(parts) + index]).wait()
        if keep and index >= -3:
            pltpu.make_async_copy(weight, kept_weights[index], back_sems.at[3 + index]).start()
        return weight

    def whole(value):
        return value.reshape(-1, value.shape[-1])

    if first:
        pixels, spread = x
        x = start
        patch = arrived(-4)
        for half in range(2):
            wide = dot(pixels[...], spread[half]).astype(jnp.bfloat16)
            for block in range(2):
                lanes = pl.ds((2 * half + block) * WIDTH, WIDTH)
                x[:, lanes] = dot(wide, whole(patch[block]))
    else:
        (x,) = x

    def cast(frame, rows, lanes):
        low[rows, lanes] = x[rows, lanes].astype(jnp.bfloat16)

    def activate(hid, at, offset):
        def body(frame, rows, lanes):
            gain = gains[:, pl.ds(offset + lanes.start, LANES)]
            bias = gains[:, pl.ds(offset + BOT + lanes.start, LANES)]
            value = hid[rows, lanes] * rstd[frame, pl.ds(at + lanes.start, LANES)]
            hid[rows, lanes] = value
            value = jnp.where(real_rows(), silu(value * gain + bias), 0.0)
            act[rows, lanes] = value.astype(jnp.bfloat16)

        return body

    each_chunk(count, D, cast)
    hid_one[...] = dot(low[...], whole(arrived(-3)[...]))
    normalise(count, BOT, hid_one, sums, rstd, 0)
    each_chunk(count, BOT, activate(hid_one, 0, 0))
    for frame in range(count):
        rows = pl.ds(frame * ROWS, ROWS)
        for tap in range(TAPS):
            picked = dot(shift[pl.ds(tap * ROWS, ROWS), :], act[rows, :])
            cols[rows, pl.ds(tap * BOT, BOT)] = picked.astype(jnp.bfloat16)
    hid_two[...] = dot(cols[...], whole(arrived(-2)[...]))
    normalise(count, BOT, hid_two, sums, rstd, BOT)
    each_chunk(count, BOT, activate(hid_two, BOT, 2 * BOT))
    w_out = arrived(-1)
    for part in range(D // BOT):
        hid_three[:, pl.ds(part * BOT, BOT)] = dot(act[...], whole(w_out[part]))
    normalise(count, D, hid_three, sums, rstd, 2 * BOT)

    def finish(frame, rows, lanes):
        gain = gains[:, pl.ds(4 * BOT + lanes.start, LANES)]
        bias = gains[:, pl.ds(4 * BOT + D + lanes.start, LANES)]
        value = hid_three[rows, lanes] * rstd[frame, pl.ds(2 * BOT + lanes.start, LANES)]
        if keep:
            hid_three[rows, lanes] = value
        value = silu(x[rows, lanes] + value * gain + bias)
        out[rows, lanes] = jnp.where(real_rows(), value, 0.0)

    each_chunk(count, D, finish)
    if keep:
        for index in (-3, -2, -1):
            pltpu.make_async_copy(weights[index], kept_weights[index], back_sems.at[3 + index]).wait()


def f32(*shape):
    return jax.ShapeDtypeStruct(shape, jnp.float32)


def bf16(*shape):
    return jax.ShapeDtypeStruct(shape, jnp.bfloat16)


def stat_rows(count):
    return -(-count // 8) * 8


def block_forward(stream, gains, shift, parts, skip, buffers, place, keep, tuned):
    first = len(parts) - skip > 3
    rows = stream[0].shape[0]
    count = rows // ROWS
    stats = stat_rows(count)
    kept = [
        ((rows, BOT), jnp.float32),
        ((rows, BOT), jnp.float32),
        ((rows, D), jnp.float32),
        ((stats, 2 * BOT + D), jnp.float32),
    ]
    start = [((rows, D), jnp.float32)] if first else []
    weights = weight_shapes(parts, buffers, tuned)[skip:]
    out_shape = [f32(rows, D)]
    out_specs = in_vmem(1)
    scratch = [pltpu.VMEM(shape, jnp.bfloat16) for shape in weights]
    scratch += [
        pltpu.SemaphoreType.DMA((len(parts),)),
        pltpu.SemaphoreType.DMA((3,)),
        pltpu.VMEM((rows, D), jnp.bfloat16),
        pltpu.VMEM((rows, BOT), jnp.bfloat16),
        pltpu.VMEM((rows, TAPS * BOT), jnp.bfloat16),
        pltpu.VMEM((stats, D), jnp.float32),
    ]
    if keep:
        out_shape += [jax.ShapeDtypeStruct(*item) for item in start + kept]
        out_shape += [jax.ShapeDtypeStruct(shape, jnp.bfloat16) for shape in weights[-3:]]
        out_specs += in_vmem(len(start + kept)) + hbm(3)
    else:
        scratch += [pltpu.VMEM(*item) for item in kept + start]
    return pl.pallas_call(
        functools.partial(forward_kernel, count, keep, parts, skip, tuned),
        out_shape=out_shape,
        in_specs=in_smem() + in_vmem(len(stream) + 2) + hbm(len(buffers)),
        out_specs=out_specs,
        scratch_shapes=scratch,
        compiler_params=pltpu.CompilerParams(vmem_limit_bytes=VMEM_LIMIT),
        cost_estimate=LIGHT,
        name="block_forward",
    )(place, *stream, gains, shift, *buffers)


def norm_back(count, chans, slope, hid, sums, more, rstd, rstd_at, gain, grad_gain, grad_bias, store):
    whole = pl.ds(0, chans)
    sums[:, whole] = jnp.zeros((sums.shape[0], chans), jnp.float32)
    more[:, whole] = jnp.zeros((sums.shape[0], chans), jnp.float32)

    def add(frame, rows, lanes):
        value = slope(frame, rows, lanes)
        sums[frame, lanes] = jnp.sum(value, axis=0, keepdims=True)
        more[frame, lanes] = jnp.sum(value * hid[rows, lanes], axis=0, keepdims=True)

    each_chunk(count, chans, add)
    grad_bias[...] = jnp.sum(sums[:, whole], axis=0, keepdims=True)
    grad_gain[...] = jnp.sum(more[:, whole], axis=0, keepdims=True)
    sums[:, whole] = group_mean(sums[:, whole] * gain[...])
    more[:, whole] = group_mean(more[:, whole] * gain[...])

    def spread(frame, rows, lanes):
        store(
            rows,
            lanes,
            lambda value: jnp.where(
                real_rows(),
                rstd[frame, pl.ds(rstd_at + lanes.start, LANES)]
                * (value * gain[:, lanes] - sums[frame, lanes] - hid[rows, lanes] * more[frame, lanes]),
                0.0,
            ).astype(jnp.bfloat16),
        )

    each_chunk(count, chans, spread)


def back_out_body(count, grad, x, hid_two, hid_three, rstd, w_out, gains, dres, dlow, dgains, scratch, dw_out):
    third, act, dact, sums, more = scratch
    gain_three, bias_three = (gains.at[:, pl.ds(4 * BOT, D)], gains.at[:, pl.ds(4 * BOT + D, D)])

    def slope_three(frame, rows, lanes):
        value = x[rows, lanes] + hid_three[rows, lanes] * gain_three[:, lanes] + bias_three[:, lanes]
        value = jnp.where(real_rows(), grad[rows, lanes] * silu_slope(value), 0.0)
        dres[rows, lanes] = value
        return value

    def store_three(rows, lanes, back):
        third[rows, lanes] = back(dres[rows, lanes])

    norm_back(
        count, D, slope_three, hid_three, sums, more, rstd, 2 * BOT, gain_three,
        dgains.at[:, pl.ds(2 * BOT, D)], dgains.at[:, pl.ds(2 * BOT + D, D)], store_three,
    )
    total = None
    for part in range(D // BOT):
        lanes = pl.ds(part * BOT, BOT)
        term = dot_lanes(third[:, lanes], w_out[lanes, :])
        total = term if total is None else total + term
    dact[...] = total
    gain_two, bias_two = (gains.at[:, pl.ds(2 * BOT, BOT)], gains.at[:, pl.ds(3 * BOT, BOT)])

    def slope_two(frame, rows, lanes):
        value = hid_two[rows, lanes] * gain_two[:, lanes] + bias_two[:, lanes]
        gate = 1.0 / (1.0 + jnp.exp(-value))
        act[rows, lanes] = jnp.where(real_rows(), value * gate, 0.0).astype(jnp.bfloat16)
        value = dact[rows, lanes] * (gate * (1.0 + value * (1.0 - gate)))
        value = jnp.where(real_rows(), value, 0.0)
        dact[rows, lanes] = value
        return value

    def store_two(rows, lanes, back):
        dlow[rows, lanes] = back(dact[rows, lanes])

    norm_back(
        count, BOT, slope_two, hid_two, sums, more, rstd, BOT, gain_two,
        dgains.at[:, pl.ds(0, BOT)], dgains.at[:, pl.ds(BOT, BOT)], store_two,
    )
    for part in range(D // BOT):
        lanes = pl.ds(part * BOT, BOT)
        dw_out[part] = dot_rows(act[...], third[:, lanes]).astype(jnp.bfloat16)


def out_scratch(rows):
    stats = stat_rows(rows // ROWS)
    return [
        pltpu.VMEM((rows, D), jnp.bfloat16),
        pltpu.VMEM((rows, BOT), jnp.bfloat16),
        pltpu.VMEM((rows, BOT), jnp.float32),
        pltpu.VMEM((stats, D), jnp.float32),
        pltpu.VMEM((stats, D), jnp.float32),
    ]


def back_mid_body(count, grad, hid_one, rstd, w_mid, gains, shift, dlow, dgains, scratch, dw_mid):
    act, cols, dact, sums, more = scratch
    gain_one, bias_one = (gains.at[:, pl.ds(0, BOT)], gains.at[:, pl.ds(BOT, BOT)])
    for frame in range(count):
        rows = pl.ds(frame * ROWS, ROWS)
        for tap in range(TAPS):
            picked = dot(shift[pl.ds((TAPS - 1 - tap) * ROWS, ROWS), :], grad[rows, :])
            cols[rows, pl.ds(tap * BOT, BOT)] = picked.astype(jnp.bfloat16)
    total = None
    for tap in range(TAPS):
        lanes = pl.ds(tap * BOT, BOT)
        term = dot_lanes(cols[:, lanes], w_mid[lanes, :])
        total = term if total is None else total + term
    dact[...] = total

    def slope_one(frame, rows, lanes):
        value = hid_one[rows, lanes] * gain_one[:, lanes] + bias_one[:, lanes]
        gate = 1.0 / (1.0 + jnp.exp(-value))
        act[rows, lanes] = jnp.where(real_rows(), value * gate, 0.0).astype(jnp.bfloat16)
        value = dact[rows, lanes] * (gate * (1.0 + value * (1.0 - gate)))
        value = jnp.where(real_rows(), value, 0.0)
        dact[rows, lanes] = value
        return value

    def store_one(rows, lanes, back):
        dlow[rows, lanes] = back(dact[rows, lanes])

    norm_back(
        count, BOT, slope_one, hid_one, sums, more, rstd, 0, gain_one,
        dgains.at[:, pl.ds(0, BOT)], dgains.at[:, pl.ds(BOT, BOT)], store_one,
    )
    for tap in range(TAPS):
        lanes = pl.ds(tap * BOT, BOT)
        dw_mid[0, lanes, :] = dot_rows(act[...], cols[:, lanes]).astype(jnp.bfloat16)


def back_in_body(count, grad, x, dres, w_in, dx, low, dw_in):
    def cast(frame, rows, lanes):
        low[rows, lanes] = x[rows, lanes].astype(jnp.bfloat16)

    each_chunk(count, D, cast)
    for part in range(D // BOT):
        lanes = pl.ds(part * BOT, BOT)
        dx[:, lanes] = dres[:, lanes] + dot_lanes(grad[...], w_in[lanes, :])
        dw_in[0, lanes, :] = dot_rows(low[:, lanes], grad[...]).astype(jnp.bfloat16)


def back_kernel(body, parts, tuned, counts, *refs):
    place, refs = (refs[0], list(refs[1:]))
    groups = []
    for number in (*counts[:2], len(dealt_shapes(parts, tuned)), len(parts), 1, counts[2]):
        groups.append(refs[:number])
        refs = refs[number:]
    ins, outs, dealt, made, sems, scratch = groups

    def done(index):
        start_deal(parts, tuned, place, index, made, dealt, sems[0])

    body(ins, outs, made, scratch, done)
    for index, array in enumerate(made):
        pltpu.make_async_copy(array, array, sems[0].at[index]).wait()


def back_call(name, body, ins, out_shape, scratch, parts, tuned, place):
    dealt = dealt_shapes(parts, tuned)
    counts = (len(ins), len(out_shape), len(scratch))
    outs = pl.pallas_call(
        functools.partial(back_kernel, body, parts, tuned, counts),
        out_shape=out_shape + [bf16(*shape) for shape in dealt],
        in_specs=in_smem() + in_vmem(len(ins)),
        out_specs=in_vmem(len(out_shape)) + hbm(len(dealt)),
        scratch_shapes=[pltpu.VMEM(whole_shape(part), jnp.bfloat16) for part in parts]
        + [pltpu.SemaphoreType.DMA((len(parts),))]
        + scratch,
        compiler_params=pltpu.CompilerParams(vmem_limit_bytes=VMEM_LIMIT),
        cost_estimate=LIGHT,
        name=name,
    )(place, *ins)
    return (list(outs[: len(out_shape)]), list(outs[len(out_shape) :]))


def back_out(grad, stream, hid_two, hid_three, rstd, w_out, gains, parts, tuned, place):
    rows = stream.shape[0]

    def body(ins, outs, made, scratch, done):
        back_out_body(rows // ROWS, *ins, *outs, scratch, made[0])
        done(0)

    ins = [grad, stream, hid_two, hid_three, rstd, w_out, gains]
    out_shape = [f32(rows, D), bf16(rows, BOT), f32(1, 2 * BOT + 2 * D)]
    return back_call("back_out", body, ins, out_shape, out_scratch(rows), parts, tuned, place)


def back_mid(grad, hid_one, rstd, w_mid, gains, shift, more, parts, tuned, place):
    rows = grad.shape[0]
    stats = stat_rows(rows // ROWS)

    def body(ins, outs, made, scratch, done):
        for index in range(1, len(made)):
            made[index][...] = ins[5 + index][...]
            done(index)
        back_mid_body(rows // ROWS, *ins[:6], *outs, scratch, made[0])
        done(0)

    scratch = [
        pltpu.VMEM((rows, BOT), jnp.bfloat16),
        pltpu.VMEM((rows, TAPS * BOT), jnp.bfloat16),
        pltpu.VMEM((rows, BOT), jnp.float32),
        pltpu.VMEM((stats, BOT), jnp.float32),
        pltpu.VMEM((stats, BOT), jnp.float32),
    ]
    ins = [grad, hid_one, rstd, w_mid, gains, shift, *more]
    out_shape = [bf16(rows, BOT), f32(1, 2 * BOT)]
    return back_call("back_mid", body, ins, out_shape, scratch, parts, tuned, place)


def back_between(grad, stream, dres, w_in, later, parts, tuned, place):
    rows = stream.shape[0]

    def body(ins, outs, made, scratch, done):
        dx, low, *rest = scratch
        back_in_body(rows // ROWS, *ins[:4], dx, low, made[0])
        done(0)
        back_out_body(rows // ROWS, dx, *ins[4:], *outs, rest, made[1])
        done(1)

    scratch = [pltpu.VMEM((rows, D), jnp.float32), pltpu.VMEM((rows, D), jnp.bfloat16)]
    scratch += out_scratch(rows)
    ins = [grad, stream, dres, w_in, *later]
    out_shape = [f32(rows, D), bf16(rows, BOT), f32(1, 2 * BOT + 2 * D)]
    return back_call("back_between", body, ins, out_shape, scratch, parts, tuned, place)


def back_first(grad, stream, dres, w_in, pixels, spread, dgains, parts, tuned, place):
    rows = stream.shape[0]

    def body(ins, outs, made, scratch, done):
        dx, low = scratch
        made[2][...] = ins[6][...]
        done(2)
        back_in_body(rows // ROWS, *ins[:4], dx, low, made[0])
        done(0)
        wide = [dot(ins[4][...], ins[5][half]).astype(jnp.bfloat16) for half in range(2)]
        for block in range(2):
            total = None
            for half in range(2):
                lanes = pl.ds((2 * half + block) * WIDTH, WIDTH)
                term = dot_rows(wide[half], dx[:, lanes].astype(jnp.bfloat16))
                total = term if total is None else total + term
            made[1][block] = total.astype(jnp.bfloat16)
        done(1)

    scratch = [pltpu.VMEM((rows, D), jnp.float32), pltpu.VMEM((rows, D), jnp.bfloat16)]
    ins = [grad, stream, dres, w_in, pixels, spread, dgains]
    return back_call("back_first", body, ins, [], scratch, parts, tuned, place)[1]


def spread_pixels(devices):
    rows = PATCH_IN // devices
    value = jnp.arange(PATCH_IN)
    at = value // rows * 2 * rows + value % rows
    return jnp.stack(
        [jnp.arange(2 * PATCH_IN)[None, :] == (at + half * rows)[:, None] for half in range(2)]
    ).astype(jnp.bfloat16)


def merge(value):
    return value.reshape(-1, value.shape[-1])


def fetch_ends(parts, tuned, place, sources, weights, sems):
    first = len(parts) - 2
    fetch(parts, tuned, place, sources, dict(enumerate(weights, first)), sems)

    def arrived(index):
        weight = weights[index]
        pltpu.make_async_copy(weight, weight, sems.at[first + index]).wait()
        return weight

    return arrived


def head_forward(count, stream, pool, arrived, games, pool_t, pooled):
    for part in range(D // ROWS):
        lanes = pl.ds(part * ROWS, ROWS)
        pool_t[:, lanes] = pool[lanes, :].astype(jnp.float32).T
    pooled[...] = jnp.zeros_like(pooled)

    def weigh(frame, rows, lanes):
        value = stream[rows, lanes].astype(jnp.bfloat16).astype(jnp.float32)
        pooled[frame, lanes] = jnp.sum(value * pool_t[:, lanes], axis=0, keepdims=True)

    each_chunk(count, D, weigh)
    before = dot(pooled[...].astype(jnp.bfloat16), merge(arrived(0)[...]))
    hidden = silu(before).astype(jnp.bfloat16)
    heads = arrived(1)
    scores = None
    for game in range(GAMES):
        pair = [dot(hidden, merge(heads[2 * game + half])) for half in range(2)]
        term = jnp.where(games == game, jnp.concatenate(pair, axis=1), 0.0)
        scores = term if scores is None else scores + term
    return ([pick_atoms(scores, action) for action in range(ACTIONS)], before, hidden)


def atom_lanes():
    return lax.broadcasted_iota(jnp.int32, (8, ROWS), 1)


def pick_atoms(scores, action):
    offset = action * ATOMS
    moved = pltpu.roll(scores, 2 * WIDTH - offset, 1) if offset else scores
    return jnp.where(atom_lanes() < ATOMS, moved[:, :ROWS], -1e30)


def support_lanes():
    return -10.0 + 20.0 / (ATOMS - 1) * atom_lanes().astype(jnp.float32)


def lane_sum(value):
    return jnp.sum(value, axis=1, keepdims=True)


def target_kernel(count, parts, tuned, place, stream, pool, whole, real, *refs):
    sources, (out, *weights, sems, pool_t, pooled) = (refs[:-6], refs[-6:])
    arrived = fetch_ends(parts, tuned, place, sources, weights, sems)
    logits, _, _ = head_forward(count, stream, pool, arrived, whole[:, 0:1], pool_t, pooled)
    chosen = None
    for action in range(ACTIONS):
        term = jnp.where(whole[:, 2:3] == action, logits[action], 0.0)
        chosen = term if chosen is None else chosen + term
    power = jnp.exp(chosen - jnp.max(chosen, axis=1, keepdims=True))
    probs = power / lane_sum(power)
    atoms = support_lanes()
    spacing = 20.0 / (ATOMS - 1)
    moved = jnp.clip(real[:, 0:1] + real[:, 1:2] * atoms, -10.0, 10.0)
    total = jnp.zeros_like(probs)
    for atom in range(ATOMS):
        near = 1.0 - jnp.abs(moved[:, atom : atom + 1] - atoms) / spacing
        total = total + probs[:, atom : atom + 1] * jnp.clip(near, 0.0, 1.0)
    inside = (atom_lanes() < ATOMS) & (lax.broadcasted_iota(jnp.int32, total.shape, 0) < count)
    out[...] = jnp.where(inside, total, 0.0)


def ends_scratch(parts, buffers, tuned):
    scratch = [pltpu.VMEM(shape, jnp.bfloat16) for shape in weight_shapes(parts, buffers, tuned)[-2:]]
    scratch += [pltpu.SemaphoreType.DMA((len(parts),))]
    return scratch + [pltpu.VMEM((ROWS, D), jnp.float32), pltpu.VMEM((8, D), jnp.float32)]


def head_target(stream, pool, whole, real, parts, buffers, tuned, place):
    count = stream.shape[0] // ROWS
    return pl.pallas_call(
        functools.partial(target_kernel, count, parts, tuned),
        out_shape=f32(8, ROWS),
        in_specs=in_smem() + in_vmem(4) + hbm(len(buffers)),
        out_specs=in_vmem(1)[0],
        scratch_shapes=ends_scratch(parts, buffers, tuned),
        compiler_params=pltpu.CompilerParams(vmem_limit_bytes=VMEM_LIMIT),
        cost_estimate=LIGHT,
        name="head_target",
    )(place, stream, pool, whole, real, *buffers)


def loss_kernel(count, frames_all, parts, tuned, place, stream, pool, target, whole, legal, *refs):
    sources, refs = (refs[:-10], refs[-10:])
    loss, dstream, dpool, acts, *weights, sems, pool_t, pooled, dpooled = refs
    arrived = fetch_ends(parts, tuned, place, sources, weights, sems)
    proj, heads = weights
    games, taken = (whole[:, 0:1], whole[:, 1:2])
    logits, before, hidden = head_forward(count, stream, pool, arrived, games, pool_t, pooled)
    atoms = support_lanes()
    inside = atom_lanes() < ATOMS
    logps, probs, values = ([], [], [])
    for value in logits:
        value = value - jnp.max(value, axis=1, keepdims=True)
        power = jnp.where(inside, jnp.exp(value), 0.0)
        mass = lane_sum(power)
        logps.append(value - jnp.log(mass))
        probs.append(power / mass)
        values.append(lane_sum(probs[-1] * atoms))
    masked = [
        jnp.where(legal[:, action : action + 1] > 0, values[action], -1e30)
        for action in range(ACTIONS)
    ]
    largest = functools.reduce(jnp.maximum, masked)
    powers = [jnp.exp(value - largest) for value in masked]
    mass = sum(powers[1:], powers[0])
    goal = target[...]
    goal_mass = lane_sum(goal)
    cross = taken_value = 0.0
    real = lax.broadcasted_iota(jnp.int32, (8, 1), 0) < count
    scale = jnp.where(real, 1.0 / frames_all, 0.0)
    spread = jnp.zeros((8, 2 * WIDTH), jnp.float32)
    for action in range(ACTIONS):
        here = jnp.where(taken == action, 1.0, 0.0)
        cross = cross - here * lane_sum(jnp.where(inside, goal * logps[action], 0.0))
        taken_value = taken_value + here * values[action]
        grad = here * (probs[action] * goal_mass - goal)
        pull = CQL_WEIGHT * (powers[action] / mass - here)
        grad = grad + pull * probs[action] * (atoms - values[action])
        grad = jnp.where(inside, grad * scale, 0.0)
        grad = jnp.concatenate([grad, jnp.zeros((8, 2 * WIDTH - ROWS), jnp.float32)], axis=1)
        offset = action * ATOMS
        spread = spread + (pltpu.roll(grad, offset, 1) if offset else grad)
    losses = cross + CQL_WEIGHT * (jnp.log(mass) + largest - taken_value)
    loss[...] = jnp.sum(jnp.where(real, losses, 0.0), axis=0, keepdims=True)
    dhidden = None
    spread = spread.astype(jnp.bfloat16)
    for game in range(GAMES):
        mine = jnp.where(games == game, spread, 0.0).astype(jnp.bfloat16)
        for half in range(2):
            part = mine[:, half * WIDTH : (half + 1) * WIDTH]
            term = dot_lanes(part, merge(heads[2 * game + half]))
            dhidden = term if dhidden is None else dhidden + term
    dbefore = (silu_slope(before) * dhidden).astype(jnp.bfloat16)
    pieces = [hidden, dbefore]
    pieces += [pooled[:, part * WIDTH : (part + 1) * WIDTH] for part in range(D // WIDTH)]
    lanes = lax.broadcasted_iota(jnp.int32, (8, WIDTH), 1)
    marked = jnp.where(lanes == WIDTH - 1, games.astype(jnp.float32), spread[:, WIDTH:].astype(jnp.float32))
    pieces += [spread[:, :WIDTH], marked]
    acts[...] = jnp.concatenate([piece.astype(jnp.float32) for piece in pieces]).astype(jnp.bfloat16)
    dpooled[...] = dot_lanes(dbefore, merge(proj[...])).astype(jnp.bfloat16).astype(jnp.float32)

    def push(frame, rows, lanes):
        dstream[rows, lanes] = dpooled[frame, lanes] * pool_t[:, lanes]

    each_chunk(count, D, push)

    def gather_pool(part, carry):
        lanes = pl.ds(pl.multiple_of(part * ROWS, ROWS), ROWS)
        total = None
        for frame in range(count):
            value = stream[pl.ds(frame * ROWS, ROWS), lanes].astype(jnp.bfloat16)
            term = value.astype(jnp.float32) * dpooled[pl.ds(frame, 1), lanes]
            total = term if total is None else total + term
        dpool[0, lanes, :] = total.T.astype(jnp.bfloat16)
        return carry

    lax.fori_loop(0, D // ROWS, gather_pool, 0)


def head_loss(stream, pool, target, whole, legal, frames_all, parts, buffers, tuned, place):
    rows = stream.shape[0]
    return pl.pallas_call(
        functools.partial(loss_kernel, rows // ROWS, frames_all, parts, tuned),
        out_shape=[f32(1, 1), f32(rows, D), bf16(1, D, ROWS), bf16(ACTS, WIDTH)],
        in_specs=in_smem() + in_vmem(5) + hbm(len(buffers)),
        out_specs=in_vmem(4),
        scratch_shapes=ends_scratch(parts, buffers, tuned) + [pltpu.VMEM((8, D), jnp.float32)],
        compiler_params=pltpu.CompilerParams(vmem_limit_bytes=VMEM_LIMIT),
        cost_estimate=LIGHT,
        name="head_loss",
    )(place, stream, pool, target, whole, legal, *buffers)


ACTS = 64


def own_heads_kernel(parts, tuned, place, *refs):
    sources, (heads, proj, acts, sems) = (refs[:-4], refs[-4:])
    fetch(parts, tuned, place, sources, {0: acts}, sems)
    pltpu.make_async_copy(acts, acts, sems.at[0]).wait()
    value = acts[...].reshape(-1, ACTS, WIDTH).astype(jnp.float32)
    pieces = [value[:, first : first + 8].reshape(-1, WIDTH) for first in range(0, ACTS, 8)]
    pieces = [piece.astype(jnp.bfloat16) for piece in pieces]
    hidden, dbefore, scores = (pieces[0], pieces[1], pieces[-2:])
    games = scores[1][:, WIDTH - 1 :].astype(jnp.float32)
    lanes = lax.broadcasted_iota(jnp.int32, scores[1].shape, 1)
    scores[1] = jnp.where(lanes < WIDTH - 1, scores[1].astype(jnp.float32), 0.0).astype(jnp.bfloat16)
    row = lax.broadcasted_iota(jnp.int32, (WIDTH, ROWS), 0)
    lane = lax.broadcasted_iota(jnp.int32, (WIDTH, ROWS), 1)

    def own(items, count):
        total = None
        for block, item in enumerate(items):
            wanted = (row + block * WIDTH == place[4] * count + lane) & (lane < count)
            term = dot(item, jnp.where(wanted, 1.0, 0.0).astype(jnp.bfloat16))
            total = term if total is None else total + term
        return total.astype(jnp.bfloat16)

    count = heads.shape[1]
    mine = own([hidden], count)
    for game in range(GAMES):
        for half in range(2):
            chosen = jnp.where(games == game, scores[half].astype(jnp.float32), 0.0)
            heads[2 * game + half] = dot_rows(mine, chosen.astype(jnp.bfloat16))[:count]
    count = proj.shape[1]
    proj[0] = dot_rows(own(pieces[2:-2], count), dbefore)[:count]


def own_heads(buffers, heads, proj, tuned, place):
    parts = [Part(1, ACTS, WIDTH)]
    return pl.pallas_call(
        functools.partial(own_heads_kernel, parts, tuned),
        out_shape=[f32(part.blocks, part.rows, part.lanes) for part in (heads, proj)],
        in_specs=in_smem() + hbm(len(buffers)),
        out_specs=in_vmem(2),
        scratch_shapes=[
            pltpu.VMEM(weight_shapes(parts, buffers, tuned)[0], jnp.bfloat16),
            pltpu.SemaphoreType.DMA((1,)),
        ],
        compiler_params=pltpu.CompilerParams(vmem_limit_bytes=VMEM_LIMIT),
        cost_estimate=LIGHT,
        name="own_heads",
    )(place, *buffers)


WIDTH = 512
TILE = 16
AXES = ("wide", "narrow")


def grid_sizes():
    return (lax.axis_size("wide") // 2, 2, lax.axis_size("narrow") // 2, 2)


def spot():
    sizes = grid_sizes()
    wide, narrow = (lax.axis_index("wide"), lax.axis_index("narrow"))
    place = [wide // sizes[1], wide % sizes[1], narrow // sizes[3], narrow % sizes[3]]
    return jnp.stack(place + [wide * lax.axis_size("narrow") + narrow]).astype(jnp.int32)


def hop(array, axis_of_core, step=1, swap=0):
    sizes = grid_sizes()

    def target(place):
        axis = axis_of_core[place[3]]
        other = list(place)
        other[axis] = place[axis] ^ swap if swap else (place[axis] + step) % sizes[axis]
        return other

    return send(array, target)


def flip(array, *bits):
    return send(array, lambda place: [value ^ bit for value, bit in zip(place, bits)])


def send(array, target):
    sizes = grid_sizes()
    pairs = []
    for place in itertools.product(*[range(size) for size in sizes]):
        pairs.append(
            tuple(
                ((z * sizes[1] + y) * sizes[2] + x) * sizes[3] + core
                for z, y, x, core in (place, target(place))
            )
        )
    return lax.ppermute(array, AXES, pairs)


ALONG_Z = (0, 0)
ACROSS = (3, 3)
NEAR = (2, 1)
FAR = (1, 2)


def hbm(number):
    return [pl.BlockSpec(memory_space=pl.ANY)] * number


def in_vmem(number):
    return [pl.BlockSpec(memory_space=pltpu.VMEM)] * number


def in_smem():
    return [pl.BlockSpec(memory_space=pltpu.SMEM)]


def copies(pairs, sems):
    started = [
        pltpu.make_async_copy(source, target, sems.at[index])
        for index, (source, target) in enumerate(pairs)
    ]
    for copy in started:
        copy.start()
    for copy in started:
        copy.wait()


class Part:
    def __init__(self, blocks, rows, lanes):
        self.blocks, self.rows, self.lanes = (blocks, rows, lanes)
        self.across = WIDTH // lanes
        self.travel = blocks * rows // self.across

    def moves(self):
        if self.across > 1:
            deep = self.rows // self.across
            return [(0, part * self.lanes, deep, 0, part * deep) for part in range(self.across)]
        return [(block * self.rows, 0, self.rows, block, 0) for block in range(self.blocks)]

    def pack(self, piece):
        if self.across > 1:
            piece = piece.reshape(self.across, self.rows // self.across, self.lanes)
            return piece.transpose(1, 0, 2).reshape(self.travel, WIDTH)
        return piece.reshape(self.travel, WIDTH)

    def unpack(self, rows):
        if self.across > 1:
            rows = rows.reshape(self.rows // self.across, self.across, self.lanes)
            return rows.transpose(1, 0, 2).reshape(1, self.rows, self.lanes)
        return rows.reshape(self.blocks, self.rows, self.lanes)

    def full(self, depth):
        return (self.blocks, depth, 2, 2, 2, self.rows, self.lanes)


def half_rows(parts):
    total = sum(part.travel for part in parts)
    return -(-total // (2 * TILE)) * TILE


def half_moves(parts):
    cut = half_rows(parts)
    halves = ([], [])
    offset = 0
    for index, part in enumerate(parts):
        for row, lane, rows, block, inner in part.moves():
            row = row + offset
            before = max(0, min(rows, cut - row))
            if before:
                halves[0].append((index, row, lane, before, block, inner))
            if rows - before:
                halves[1].append((index, row + before - cut, lane, rows - before, block, inner + before))
        offset += part.travel
    return halves


def unit(parts, depth):
    return (depth, 2, half_rows(parts), WIDTH)


def pack(parts, pieces):
    rows = jnp.concatenate([part.pack(piece) for part, piece in zip(parts, pieces)])
    return jnp.pad(rows, ((0, 2 * half_rows(parts) - rows.shape[0]), (0, 0)))


def assemble_pairs(parts, core, y, x, ins, outs):
    pairs = []
    for other, far, near in itertools.product((0, 1), repeat=3):
        half = core ^ other
        step = [0, 0, 0, 0]
        step[NEAR[half]], step[FAR[half]] = (near, far)
        at_y, at_x = (lax.rem(y + step[1], 2), lax.rem(x + step[2], 2))
        for index, row, lane, rows, block, inner in half_moves(parts)[half]:
            if index not in outs:
                continue
            pairs.append(
                (
                    index,
                    ins[2 * other + far].at[near, :, :, pl.ds(row, rows), pl.ds(lane, parts[index].lanes)],
                    outs[index].at[block, :, at_y, at_x, :, pl.ds(inner, rows)],
                )
            )
    return pairs


def fetch(parts, tuned, place, sources, weights, sems):
    if not tuned:
        for index, weight in weights.items():
            pltpu.make_async_copy(sources[index], weight, sems.at[index]).start()
        return
    for core in (0, 1):

        @pl.when(place[3] == core)
        def _():
            pairs = assemble_pairs(parts, core, place[1], place[2], sources, weights)
            for index, source, target in sorted(pairs, key=lambda pair: pair[0]):
                pltpu.make_async_copy(source, target, sems.at[index]).start()


def weight_shapes(parts, buffers, tuned):
    if tuned:
        return [part.full(buffers[0].shape[1]) for part in parts]
    return [item.shape for item in buffers]


def assemble_kernel(parts, some, place, *refs):
    outs, sems = (dict(zip(some, refs[4:-1])), refs[-1])
    fetch(parts, True, place, refs[:4], outs, sems)
    for index, out in outs.items():
        pltpu.make_async_copy(out, out, sems.at[index]).wait()


def assemble(parts, buffers, place, some=None):
    some = range(len(parts)) if some is None else some
    shapes = weight_shapes(parts, buffers, True)
    full = pl.pallas_call(
        functools.partial(assemble_kernel, parts, some),
        out_shape=[bf16(*shapes[index]) for index in some],
        in_specs=in_smem() + hbm(4),
        out_specs=in_vmem(len(some)),
        scratch_shapes=[pltpu.SemaphoreType.DMA((len(parts),))],
        compiler_params=pltpu.CompilerParams(vmem_limit_bytes=VMEM_LIMIT),
        cost_estimate=LIGHT,
        name="assemble",
    )(place, *buffers)
    return [merged(item) for item in full]


def merged(array):
    return array.reshape(array.shape[0], -1, array.shape[-1])


def in_order(own, other, bit):
    first = jnp.where(bit == 0, own, other)
    second = jnp.where(bit == 0, other, own)
    return jnp.stack([first, second])


def together(*trees):
    flat, tree = jax.tree.flatten(trees)
    return jax.tree.unflatten(tree, lax.optimization_barrier(flat))


def start_gather(groups, pieces, place):
    core = place[3]
    packed = [pack(parts, items) for parts, items in zip(groups, pieces)]
    halves = [half_rows(parts) for parts in groups]
    kept = [lax.dynamic_slice_in_dim(rows, core * half, half) for rows, half in zip(packed, halves)]
    sent = [
        lax.dynamic_slice_in_dim(rows, (1 - core) * half, half) for rows, half in zip(packed, halves)
    ]
    got = hop(jnp.concatenate(sent), ACROSS)
    held = []
    offset = 0
    for keep, half in zip(kept, halves):
        held.append(in_order(keep, got[offset : offset + half], core))
        offset += half
    return held


def pipelined_gather(groups, pieces, place, state, arrived):
    count = len(groups)
    low, high = (place[0] % 2, place[0] // 2)
    held = start_gather(groups[:1], pieces(None)[:1], place)
    for tick in range(count + 3):
        near, far, last = [index if 0 <= index < count else None for index in range(tick - 1, tick - 4, -1)]
        live = [index for index in (tick, near, far, last) if index is not None and index < count]
        if tick in (1, 2):
            live += range(tick + 1, count)
        items, state = together([held[index] for index in live], state)
        for index, item in zip(live, items):
            held[index] = item
        if tick == 0:
            held += start_gather(groups[1:2], pieces(held[0])[1:2], place)
            held += start_gather(groups[2:], pieces(held[1])[2:], place)
        if last is not None:
            own, arrived_far, other = held[last]
            held[last] = [own, arrived_far, other, hop(arrived_far, ACROSS)]
        if far is not None:
            held[far] = [held[far], hop(held[far], FAR), hop(held[far], ACROSS)]
        if near is not None:
            held[near] = [held[near], hop(held[near], NEAR)]
        if tick == 0:
            held[0] = [held[0]] + [hop(held[0], ALONG_Z, swap=bits) for bits in (1, 2, 3)]
        elif tick < count:
            held[tick] = [held[tick], hop(held[tick], ALONG_Z, swap=2)]
        if tick < 3:
            early = slice(tick + 1, tick + 2 if tick < 2 else count)
            got = hop(jnp.concatenate(held[early], axis=1), ALONG_Z, swap=1)
            ends = list(itertools.accumulate(half_rows(parts) for parts in groups[early]))
            got = jnp.split(got, ends[:-1], axis=1)
            held[early] = [in_order(item, other, low) for item, other in zip(held[early], got)]
        if last is not None:
            state = arrived(last, held[last], state)
        if tick < count:
            items, state = together(held[tick], state)
            if tick == 0:
                items = [in_order(*items[:2], low), in_order(*items[2:], low)]
            both = in_order(*items, high)
            held[tick] = both.reshape(-1, *both.shape[2:])
        if near is not None:
            items, state = together(held[near], state)
            held[near] = jnp.stack(items)
    return state


def whole_shape(part):
    return (part.blocks, part.rows * lax.axis_size(AXES), part.lanes)


def dealt_shapes(parts, tuned):
    if not tuned:
        return [whole_shape(part) for part in parts]
    size = (grid_sizes()[0], 2, half_rows(parts), WIDTH)
    return [lead + size for lead in ((2, 2), (2,), (), ())]


def start_deal(parts, tuned, place, wanted, arrays, dealt, sems):
    if not tuned:
        pltpu.make_async_copy(arrays[wanted], dealt[wanted], sems.at[wanted]).start()
        return
    array = arrays[wanted].reshape(*parts[wanted].full(grid_sizes()[0]))
    to_core, to_far, to_near, own = dealt
    for core in (0, 1):

        @pl.when(place[3] == core)
        def _():
            for other, far, near in itertools.product((0, 1), repeat=3):
                half = core ^ other
                step = [0, 0, 0, 0]
                step[NEAR[half]], step[FAR[half]] = (near, far)
                at_y, at_x = (lax.rem(place[1] + step[1], 2), lax.rem(place[2] + step[2], 2))
                if other:
                    target = to_core.at[far, near]
                elif far:
                    target = to_far.at[near]
                else:
                    target = to_near if near else own
                for index, row, lane, rows, block, inner in half_moves(parts)[half]:
                    if index == wanted:
                        pltpu.make_async_copy(
                            array.at[block, :, at_y, at_x, :, pl.ds(inner, rows)],
                            target.at[:, :, pl.ds(row, rows), pl.ds(lane, parts[index].lanes)],
                            sems.at[index],
                        ).start()


def add_up(*terms):
    total = terms[0].astype(jnp.float32)
    for term in terms[1:]:
        total = total + term.astype(jnp.float32)
    return total


def low_add(*terms):
    return add_up(*terms).astype(jnp.bfloat16)


def scatter_stages(place, direct):
    depth = grid_sizes()[0]
    z, core = (place[0], place[3])
    low, high = (z % 2, z // 2)

    def across(items):
        to_core, *rest = items
        return rest + [hop(to_core, ACROSS)]

    def far(items):
        to_far, to_near, own, from_core = items
        return [to_near, own, from_core, hop(low_add(to_far, from_core[1]), FAR)]

    def near(items):
        to_near, own, from_core, from_far = items
        from_near = hop(low_add(to_near, from_core[0, 1], from_far[1]), NEAR)
        return [own, from_core[0, 0], from_far[0], from_near]

    def pick(array, at):
        return lax.dynamic_index_in_dim(array, at, 0, False)

    def along(items):
        summed = lax.optimization_barrier(add_up(*items))
        sent = [pick(summed, lax.rem(z + step, depth)) for step in range(1, depth)]
        got = [hop(item.astype(jnp.bfloat16), ALONG_Z, step + 1) for step, item in enumerate(sent)]
        return [pick(summed, z)] + got

    def pairs(items):
        summed = lax.optimization_barrier(add_up(*items))
        summed = summed.reshape(2, 2, *summed.shape[1:])
        return [pick(summed, high), hop(pick(summed, 1 - high).astype(jnp.bfloat16), ALONG_Z, swap=2)]

    def neighbours(items):
        summed = add_up(*items)
        return [pick(summed, low), hop(pick(summed, 1 - low).astype(jnp.bfloat16), ALONG_Z, swap=1)]

    def finish(items):
        total = add_up(*items)
        other = hop(pick(total, 1 - core), ACROSS)
        return in_order(pick(total, core), other, core).reshape(-1, WIDTH)

    return [across, far, near] + ([along] if direct else [pairs, neighbours]) + [finish]


def share_stages(part, place):
    low, high = (place[0] % 2, place[0] // 2)

    def along(item):
        one, two, three = [hop(item, ALONG_Z, swap=bits) for bits in (1, 2, 3)]
        both = in_order(in_order(item, one, low), in_order(two, three, low), high)
        return both.reshape(-1, *both.shape[2:])

    return [
        lambda item: start_gather([[part]], [[item]], place)[0],
        along,
        lambda item: jnp.stack([item, hop(item, NEAR)]),
        lambda item: [item, hop(item, FAR), hop(item, ACROSS)],
        lambda items: items + [hop(items[1], ACROSS)],
    ]


def pipelined_scatter(count, place, state, steps, shared):
    held, todo = ([], [])
    part, piece, more = shared
    share = share_stages(part, place)
    for tick in range(count + 5):
        live = [index for index in range(len(held)) if todo[index]]
        items, state, piece = together([held[index] for index in live], state, piece)
        for index, item in zip(live, items):
            held[index] = item
            for _ in range(2 if index == tick - 1 else 1):
                held[index] = todo[index].pop(0)(held[index])
        if share:
            piece = share.pop(0)(piece)
        elif more:
            piece = more.pop(0)(piece, held)
        if tick < count:
            dealt, state = steps[tick](state)
            held.append(dealt)
            todo.append(scatter_stages(place, tick >= count - 2))
    return (held, piece, state)


CQL_WEIGHT = 0.05
BETA_ONE = 0.5
BETA_TWO = 0.5
LEARNING_RATE = 0.25
WEIGHT_DECAY = 0.01
PATCH_IN = 256
DPROJ = 512
ACTIONS = 18
ATOMS = 51
GAMES = 4
BLOCKS = 2
STEP = 5
PLAYS = ACTIONS * ATOMS


def average_decay():
    return min(0.99, (1.0 + STEP) / (10.0 + STEP))


SWEEP = 8192


def lamb_parts(grads, params, first, second):
    momentum = BETA_ONE * first + (1.0 - BETA_ONE) * grads
    variance = BETA_TWO * second + (1.0 - BETA_TWO) * grads * grads
    direction = (
        momentum / (1.0 - BETA_ONE**STEP) / (jnp.sqrt(variance / (1.0 - BETA_TWO**STEP)) + 1e-06)
        + WEIGHT_DECAY * params
    )
    return (momentum, variance, direction)


def stretches(cuts):
    found = []
    at = 0
    for index, (start, size) in enumerate(cuts):
        end = start + size
        last = index == len(cuts) - 1
        whole = end if last else end // ROWS * ROWS
        found.append((at, whole - at, [index]))
        at = whole
        if end != whole:
            found.append((whole, ROWS, [index, index + 1]))
            at = whole + ROWS
    return found


def sweep(start, size, body, carry):
    steps = size // SWEEP

    def step(index, carry):
        return body(pl.ds(pl.multiple_of(start + index * SWEEP, ROWS), SWEEP), carry)

    if steps:
        carry = lax.fori_loop(0, steps, step, carry)
    return (carry, start + steps * SWEEP, size - steps * SWEEP)


def row_sum(value):
    return jnp.sum(value, axis=1, keepdims=True)


def put_rows(target, row, source, steps):
    for first, rows, lane, stride in steps:

        def step(index, carry):
            lanes = pl.ds(pl.multiple_of(lane + index * stride, ROWS), WIDTH)
            target[row : row + 1, lanes] = source[pl.ds(first + index, 1), :]
            return carry

        lax.fori_loop(0, rows, step, 0, unroll=4)


def block_rows(name, start, rows, first):
    if name == "w_out":
        count = rows // (D // BOT)
        return [(first + part * count, count, start + part * BOT, D) for part in range(D // BOT)]
    return [(first, rows, start, WIDTH)]


def patch_rows(rows, first):
    count = rows // 4
    return [
        (first + (2 * block + half) * count, count, half * (D // 2) + block * WIDTH, D)
        for block in range(2)
        for half in range(2)
    ]


def direction_kernel(cuts, moves, gain_at, *refs):
    top_cuts, block_cuts = cuts
    number = len(moves)
    sources, refs = (refs[:number], refs[number:])
    late, loss, *refs = refs
    top_ins, block_ins, refs = (refs[:3], refs[3:6], refs[6:])
    sums, *refs = refs
    top_outs, block_outs, (top_grad, block_grad) = (refs[:3], refs[3:6], refs[6:])
    for source, steps in zip(sources, moves):
        for row, placed in steps:
            put_rows(top_grad if row is None else block_grad, row or 0, source, placed)
    patch = top_cuts[0][1]
    top_grad[:, pl.ds(patch, late.shape[1])] = late[...]
    gain_start, gain_width = block_cuts[3]
    source, first = (sources[gain_at[0]], gain_at[1])
    block_grad[:, pl.ds(gain_start, gain_width)] = source[pl.ds(first, 8), :][:BLOCKS, :gain_width]

    def work(lanes, grad, ins, outs):
        param, *moments = [ref[:, lanes] for ref in ins]
        made = lamb_parts(grad[:, lanes], param, *moments)
        for ref, value in zip(outs, made):
            ref[:, lanes] = value
        return (param * param, made[2] * made[2])

    found = []

    def run(cuts, grad, ins, outs, first_lane, height):
        for start, size, segments in stretches(cuts):

            def step(lanes, carry):
                terms = work(lanes, grad, ins, outs)
                return [held + term for held, term in zip(carry, terms)]

            zeros = [jnp.zeros((height, SWEEP), jnp.float32)] * 2
            carry, begin, rest = sweep(start, size, step, zeros)
            sizes = [row_sum(value) for value in carry] if rest != size else None
            if rest:
                terms = work(pl.ds(begin, rest), grad, ins, outs)
                at = begin + lax.broadcasted_iota(jnp.int32, terms[0].shape, 1)
                if len(segments) > 1:
                    edge = cuts[segments[1]][0]
                    after = [row_sum(jnp.where(at >= edge, term, 0.0)) for term in terms]
                    found.extend((first_lane, segments[1], *item) for item in enumerate(after))
                    terms = [jnp.where(at < edge, term, 0.0) for term in terms]
                more = [row_sum(term) for term in terms]
                sizes = more if sizes is None else [held + term for held, term in zip(sizes, more)]
            found.extend((first_lane, segments[0], *item) for item in enumerate(sizes))

    run(top_cuts, top_grad, top_ins, top_outs, 0, 1)
    run(block_cuts, block_grad, block_ins, block_outs, len(top_cuts), BLOCKS)
    rows = lax.broadcasted_iota(jnp.int32, sums.shape, 0)
    lanes = lax.broadcasted_iota(jnp.int32, sums.shape, 1)
    result = jnp.where((rows == 2) & (lanes == 0), loss[...], 0.0)
    for first, segment, row, value in found:
        for part in range(value.shape[0]):
            lane = first + part * len(block_cuts) + segment
            here = (rows == row) & (lanes == lane)
            result = result + jnp.where(here, value[part : part + 1], 0.0)
    sums[...] = result


def directions(cuts, rows, moves, gain_at, late, loss, top_ins, block_ins):
    shapes = [f32(*top_ins[0].shape)] * 3 + [f32(*block_ins[0].shape)] * 3
    ins = [*rows, late, loss, *top_ins, *block_ins]
    return pl.pallas_call(
        functools.partial(direction_kernel, cuts, moves, gain_at),
        out_shape=[f32(8, ROWS)] + shapes,
        in_specs=in_vmem(len(ins)),
        out_specs=in_vmem(7),
        scratch_shapes=[
            pltpu.VMEM(top_ins[0].shape, jnp.float32),
            pltpu.VMEM(block_ins[0].shape, jnp.float32),
        ],
        compiler_params=pltpu.CompilerParams(vmem_limit_bytes=VMEM_LIMIT),
        cost_estimate=LIGHT,
        name="directions",
    )(*ins)


def update_kernel(cuts, sums, *refs):
    top_cuts, block_cuts = cuts
    top_ins, block_ins, refs = (refs[:3], refs[3:6], refs[6:])
    norms, *refs = refs
    top_outs, block_outs = (refs[:2], refs[2:])
    norm = jnp.sqrt(sums[...])
    norms[...] = norm
    ratio = LEARNING_RATE * (norm[0:1] / (norm[1:2] + 1e-06))
    decay = average_decay()

    def work(lanes, ins, outs, scale):
        param, direction, average = [ref[:, lanes] for ref in ins]
        updated, averaged, *half = outs
        value = param - scale * direction
        updated[:, lanes] = value
        averaged[:, lanes] = decay * average + (1.0 - decay) * value
        for ref in half:
            ref[:, lanes] = value.astype(jnp.bfloat16)

    def run(cuts, ins, outs, scales):
        for start, size, segments in stretches(cuts):
            scale = scales[segments[0]]

            def step(lanes, carry):
                work(lanes, ins, outs, scale)
                return carry

            _, begin, rest = sweep(start, size, step, 0)
            if rest:
                if len(segments) > 1:
                    at = begin + lax.broadcasted_iota(jnp.int32, (1, rest), 1)
                    scale = jnp.where(at < cuts[segments[1]][0], scale, scales[segments[1]])
                work(pl.ds(begin, rest), ins, outs, scale)

    lanes = [ratio[:, lane : lane + 1] for lane in range(len(top_cuts) + BLOCKS * len(block_cuts))]
    run(top_cuts, top_ins, top_outs, lanes[: len(top_cuts)])
    rest = lanes[len(top_cuts) :]
    scales = [jnp.concatenate(rest[index :: len(block_cuts)]) for index in range(len(block_cuts))]
    run(block_cuts, block_ins, block_outs, scales)


def update(cuts, sums, top_ins, block_ins):
    shapes = [f32(*array.shape) for array in [top_ins[0]] * 2 + [block_ins[0]] * 2]
    shapes.append(bf16(*block_ins[0].shape))
    return pl.pallas_call(
        functools.partial(update_kernel, cuts),
        out_shape=[f32(8, ROWS)] + shapes,
        in_specs=in_vmem(7),
        out_specs=in_vmem(6),
        compiler_params=pltpu.CompilerParams(vmem_limit_bytes=VMEM_LIMIT),
        cost_estimate=LIGHT,
        name="update",
    )(sums, *top_ins, *block_ins)


def segment_lengths():
    top = [PATCH_IN * D, D * PIX, D * DPROJ, DPROJ * GAMES * PLAYS]
    block = [D * BOT, 9 * BOT * BOT, BOT * D, 2 * (2 * BOT + D)]
    return (top, block)


def cut_points(lengths, devices):
    cuts = []
    offset = 0
    for length in lengths:
        width = length // devices
        cuts.append((offset, width))
        offset += width
    return cuts


def pack_top(flat, cuts):
    patch, pool, proj, heads = [flat[start : start + size] for start, size in cuts]
    patch = patch.reshape(-1, 2, 2, WIDTH).transpose(2, 1, 0, 3).reshape(2, -1, WIDTH)
    pool = jnp.pad(pool.reshape(1, -1, PIX), ((0, 0), (0, 0), (0, ROWS - PIX)))
    heads = jnp.pad(heads.reshape(-1, GAMES, PLAYS), ((0, 0), (0, 0), (0, 2 * WIDTH - PLAYS)))
    heads = heads.reshape(-1, 2 * GAMES, WIDTH).transpose(1, 0, 2)
    return [patch, pool, proj.reshape(1, -1, WIDTH), heads]


def flat_late(pool, proj, heads):
    heads = heads.transpose(1, 0, 2).reshape(-1, GAMES, 2 * WIDTH)[:, :, :PLAYS]
    return jnp.concatenate([item.reshape(-1) for item in (pool[:, :, :PIX], proj, heads)])


def pack_block(flat, cuts):
    w_in, w_mid, w_out = [flat[start : start + size] for start, size in cuts[:3]]
    w_out = w_out.reshape(-1, D // BOT, BOT).transpose(1, 0, 2)
    return [w_in.reshape(1, -1, BOT), w_mid.reshape(1, -1, BOT), w_out]


def parts_for(devices):
    rows = {"patch": 2 * PATCH_IN, "pool": D, "proj": D, "heads": DPROJ}
    rows |= {"w_in": D, "w_mid": TAPS * BOT, "w_out": BOT, "gains": TILE * devices}
    blocks = {"patch": 2, "heads": 2 * GAMES, "w_out": D // BOT}
    return {
        name: Part(blocks.get(name, 1), count // devices, ROWS if name == "pool" else WIDTH)
        for name, count in rows.items()
    }


def is_tuned(devices):
    parts = parts_for(devices).values()
    whole = all(part.rows // part.across % TILE == 0 for part in parts)
    return whole and lax.axis_size("wide") == 8 and lax.axis_size("narrow") == 4


def plain_gather(piece):
    return lax.all_gather(piece, AXES, axis=1, tiled=True)


def plain_scatter(array):
    return lax.psum_scatter(array, AXES, scatter_dimension=1, tiled=True).astype(jnp.float32)


def total(array):
    if lax.axis_size("wide") != 8 or lax.axis_size("narrow") != 4:
        return lax.psum(array, AXES)
    array = array + flip(array, 0, 0, 0, 1)
    array = (array + flip(array, 0, 0, 1, 0)) + (flip(array, 0, 1, 0, 0) + flip(array, 0, 1, 1, 0))
    one, two, three = [flip(array, bits, 0, 0, 0) for bits in (1, 2, 3)]
    return (array + two) + (one + three)


def frame_rows(frames):
    count = frames.shape[0]
    return jnp.pad(frames, ((0, 0), (0, ROWS - PIX), (0, 0))).reshape(count * ROWS, PATCH_IN)


def on_device(
    observed,
    following,
    game_ids,
    actions,
    legal_mask,
    rewards,
    discounts,
    done_flags,
    params_top,
    params_blocks,
    first_top,
    first_blocks,
    second_top,
    second_blocks,
    average_top,
    average_blocks,
    target_top,
    target_blocks,
):
    devices = lax.axis_size(AXES)
    frames_all = observed.shape[0] * devices
    top_lengths, block_lengths = segment_lengths()
    top_cuts = cut_points(top_lengths, devices)
    block_cuts = cut_points(block_lengths, devices)
    gain_start, gain_width = block_cuts[3]
    parts = parts_for(devices)
    tuned = is_tuned(devices)
    place = spot()
    shift = shifts()
    spread = spread_pixels(devices)
    count = observed.shape[0]
    whole = jnp.concatenate([game_ids[:, None], actions], axis=1)
    whole = jnp.pad(whole, ((0, 8 - count), (0, ROWS - 3)), constant_values=-1)
    legal = jnp.pad(legal_mask, ((0, 8 - count), (0, ROWS - ACTIONS)), constant_values=1)
    keep = discounts * (1.0 - done_flags.astype(jnp.float32))
    real = jnp.pad(jnp.stack([rewards, keep], axis=1), ((0, 8 - count), (0, ROWS - 2)))

    def read_pieces(early):
        sources = (target_top, target_blocks, params_top, params_blocks)
        if early is not None:
            early, sources = together(early, sources)
        tops = (sources[0], sources[2].astype(jnp.bfloat16))
        blocks = (sources[1], sources[3].astype(jnp.bfloat16))
        own = {}
        for net, top, flat in zip(("target", "online"), tops, blocks):
            for name, piece in zip(("patch", "pool", "proj", "heads"), pack_top(top, top_cuts)):
                own[net, name] = piece
            for index in range(BLOCKS):
                for name, piece in zip(block_names, pack_block(flat[index], block_cuts)):
                    own[net, name, index] = piece
        gain_rows = jnp.concatenate(blocks)[:, gain_start:]
        own["gains",] = jnp.pad(
            gain_rows, ((0, TILE - 2 * BLOCKS), (0, WIDTH - gain_width))
        ).reshape(1, TILE, WIDTH)
        return [[own[key] for key in group] for group in keys]

    block_names = ("w_in", "w_mid", "w_out")

    def part_of(key):
        return parts[key[0] if key[0] in parts else key[1]]

    full = {}

    def block_weight(index, name):
        return merged(full["online", name, index]).reshape(-1, BOT)

    def lead(group, buffers):
        return assemble(group_parts(group), buffers, place, [0])[0] if tuned else buffers[0]

    def hold(index, group, buffers, state):
        full["held", index] = (group, buffers)
        if index > 1:
            return state
        return state | {"target_pool": lead(group, buffers)[0]}

    def read_gains(group, buffers, state):
        gains = lead(group, buffers).reshape(devices, TILE, WIDTH)[:, : 2 * BLOCKS, :gain_width]
        gains = gains.transpose(1, 0, 2).reshape(2 * BLOCKS, -1).astype(jnp.float32)
        return run_block("target", 0, group, buffers, state | {"gains": gains})

    def target_ends(group, buffers, state):
        for index in range(1, BLOCKS):
            state = run_block("target", index, *full["held", index], state)
        target = head_target(
            state.pop("stream"), state.pop("target_pool"), whole, real,
            group_parts(group), buffers, tuned, place,
        )
        return state | {"target": target}

    def online_ends(group, buffers, state):
        loss, dstream, dpool, acts = head_loss(
            state.pop("stream"), state.pop("online_pool"), state.pop("target"), whole, legal, frames_all,
            group_parts(group), buffers, tuned, place,
        )
        return state | {"loss": loss, "grad": dstream, "pool": dpool, "acts": acts}

    def run_block(net, index, group, buffers, state):
        keep = net == "online"
        row = index + (BLOCKS if keep else 0)
        gain = state["gains"][row : row + 1]
        stream = [state["pixels" if keep else "following"], spread]
        if index:
            stream = [state["stream"]]
        skip = 1 if keys[group][0][-1] in ("gains", "pool") else 0
        out, *kept = block_forward(
            stream, gain, shift, group_parts(group), skip, buffers, place, keep, tuned
        )
        state = state | {"stream": out}
        if keep:
            start = kept.pop(0) if index == 0 else stream[0]
            full.update(zip([(net, name, index) for name in block_names], kept[-3:]))
            state |= {"kept%d" % index: [start, *kept[:-3]]}
            if index == 0:
                state |= {"online_pool": lead(group, buffers)[0]}
        return state

    keys, then = ([], [])
    ends = ("proj", "heads")

    def add_group(group, run, *names):
        keys.append(group)
        then.append(functools.partial(run, *names))

    def block_keys(net, index):
        return [(net, name, index) for name in block_names]

    for index in range(1, BLOCKS):
        start = [("target", "pool")] if index == 1 else []
        add_group(start + block_keys("target", index), hold, index)
    add_group([("gains",), ("target", "patch")] + block_keys("target", 0), read_gains)
    add_group([("target", name) for name in ends], target_ends)
    for index in range(BLOCKS):
        start = [] if index else [("online", "pool"), ("online", "patch")]
        add_group(start + block_keys("online", index), run_block, "online", index)
    add_group([("online", name) for name in ends], online_ends)

    def group_parts(group):
        return [part_of(key) for key in keys[group]]

    def arrived(group, buffers, state):
        return then[group](group, buffers, dict(state))

    state = {"following": frame_rows(following), "pixels": frame_rows(observed)}
    if tuned:
        groups = [group_parts(group) for group in range(len(keys))]
        state = pipelined_gather(groups, read_pieces, place, state, arrived)
    else:
        for group, items in enumerate(read_pieces(None)):
            state = arrived(group, [plain_gather(item) for item in items], state)

    keys = []
    steps = []

    def out_inputs(index, state):
        stream, hid_one, hid_two, hid_three, rstd = state["kept%d" % index]
        gain = state["gains"][BLOCKS + index : BLOCKS + index + 1]
        return [stream, hid_two, hid_three, rstd, block_weight(index, "w_out"), gain]

    def out_step(index, group, state):
        (dres, low, late), dealt = back_out(
            state.pop("grad"), *out_inputs(index, state), group, tuned, place
        )
        return (dealt, state | {"grad": dres, "low": low, "late%d" % index: late})

    def mid_step(index, group, state):
        stream, hid_one, hid_two, hid_three, rstd = state["kept%d" % index]
        gain = state["gains"][BLOCKS + index : BLOCKS + index + 1]
        more = [state.pop("pool")] if len(group) > 1 else []
        (low, early), dealt = back_mid(
            state["low"], hid_one, rstd, block_weight(index, "w_mid"), gain, shift, more,
            group, tuned, place,
        )
        return (dealt, state | {"low": low, "early%d" % index: early})

    def between_step(index, group, state):
        stream = state.pop("kept%d" % index)[0]
        (dres, low, late), dealt = back_between(
            state["low"], stream, state["grad"], block_weight(index, "w_in"),
            out_inputs(index - 1, state), group, tuned, place,
        )
        return (dealt, state | {"grad": dres, "low": low, "late%d" % (index - 1): late})

    def first_step(group, state):
        stream = state.pop("kept0")[0]
        dgains = [
            jnp.concatenate([state.pop("early%d" % index), state.pop("late%d" % index)], axis=1)
            for index in range(BLOCKS)
        ]
        dgains = jnp.concatenate(dgains).reshape(BLOCKS, devices, gain_width).transpose(1, 0, 2)
        dgains = jnp.pad(dgains, ((0, 0), (0, TILE - BLOCKS), (0, WIDTH - gain_width)))
        dgains = dgains.reshape(1, -1, WIDTH).astype(jnp.bfloat16)
        dealt = back_first(
            state.pop("low"), stream, state.pop("grad"), block_weight(0, "w_in"),
            state.pop("pixels"), spread, dgains, group, tuned, place,
        )
        return (dealt, state)

    def add_step(group, run, *names):
        keys.append(group)
        steps.append(
            lambda state: run(*names, [parts[key[0]] for key in group], dict(state))
        )

    loss_part, acts = (state.pop("loss"), state.pop("acts"))
    add_step([("w_out", BLOCKS - 1)], out_step, BLOCKS - 1)
    for index in reversed(range(BLOCKS)):
        more = [("pool",)] if index == BLOCKS - 1 else []
        add_step([("w_mid", index)] + more, mid_step, index)
        if index:
            add_step([("w_in", index), ("w_out", index - 1)], between_step, index)
    add_step([("w_in", 0), ("patch",), ("gains",)], first_step)
    def read_heads(buffers, rows):
        return own_heads(buffers, parts["heads"], parts["proj"], tuned, place)

    def read_late(pair, rows):
        pool = parts["pool"]
        first = parts["w_mid"].travel
        return flat_late(pool.unpack(rows[1][first : first + pool.travel]), pair[1], pair[0])[None]

    groups = [[parts[key[0]] for key in group] for group in keys]
    if tuned:
        shared = (Part(1, ACTS, WIDTH), acts[None], [read_heads, read_late])
        mine, late, state = pipelined_scatter(len(groups), place, state, steps, shared)
    else:
        mine = []
        for group, step in zip(groups, steps):
            arrays, state = step(state)
            mine.append(pack(group, [plain_scatter(array) for array in arrays]))
        late = read_late(read_heads([plain_gather(acts[None])], mine), mine)
    at = {}
    moves = []
    for number, group in enumerate(keys):
        first = 0
        steps = []
        for key in group:
            count = parts[key[0]].travel
            at[key] = (number, first)
            if len(key) > 1:
                start = block_cuts[block_names.index(key[0])][0]
                steps.append((key[1], block_rows(key[0], start, count, first)))
            elif key[0] == "patch":
                steps.append((None, patch_rows(count, first)))
            first += count
        moves.append(steps)
    cuts = (top_cuts, block_cuts)
    tops = [array[None] for array in (params_top, first_top, second_top, average_top)]
    sums, *made = directions(
        cuts, mine, moves, at["gains",], late, loss_part,
        tops[:3], [params_blocks, first_blocks, second_blocks],
    )
    momentum_top, variance_top, direction_top, momentum_blocks, variance_blocks, direction_blocks = made
    sums = total(sums)
    norms, *made = update(
        cuts, sums, [tops[0], direction_top, tops[3]],
        [params_blocks, direction_blocks, average_blocks],
    )
    updated_top, averaged_top, updated_blocks, averaged_blocks, half_blocks = made
    loss_total = sums[2, 0]
    matrix_norms = norms[:2, : len(top_cuts) + BLOCKS * len(block_cuts)]
    number, first = at["gains",]
    gain_grads = mine[number][first : first + BLOCKS, :gain_width]
    return (
        loss_total,
        matrix_norms,
        updated_top[0],
        updated_top[0].astype(jnp.bfloat16),
        momentum_top[0],
        variance_top[0],
        averaged_top[0],
        updated_blocks,
        half_blocks,
        momentum_blocks,
        variance_blocks,
        averaged_blocks,
        gain_grads,
    )


def solution(mesh):
    one = P(AXES)
    flat = P(None, AXES)
    return jax.shard_map(
        on_device,
        mesh=mesh,
        in_specs=(P(AXES, None, None),) * 2
        + (one, P(AXES, None), P(AXES, None))
        + (one,) * 3
        + (one, flat) * 5,
        out_specs=(P(), P()) + (one,) * 5 + (flat,) * 6,
        check_vma=False,
    )
```

```python
import functools
import itertools

import jax
import jax.numpy as jnp
from jax import lax
from jax.experimental import pallas as pl
from jax.experimental.pallas import tpu as pltpu
from jax.sharding import PartitionSpec as P

D = 2048
BOT = 512
GROUPS = 32
SIDE = 11
PIX = 121
TAPS = 9

ROWS = 128
LANES = 512
VMEM_LIMIT = 44 * 1024 * 1024
LIGHT = pl.CostEstimate(flops=1024, bytes_accessed=1024, transcendentals=0)


def shifts():
    pixel = jnp.arange(ROWS)
    row, col = (pixel // SIDE, pixel % SIDE)
    mats = []
    for tap in range(TAPS):
        at_row, at_col = (row + tap // 3 - 1, col + tap % 3 - 1)
        inside = (at_row >= 0) & (at_row < SIDE) & (at_col >= 0) & (at_col < SIDE) & (pixel < PIX)
        mats.append((inside[:, None] & (pixel[None, :] == (at_row * SIDE + at_col)[:, None])))
    return jnp.concatenate(mats, axis=0).astype(jnp.bfloat16)


def dot(left, right):
    return jnp.dot(left, right, preferred_element_type=jnp.float32)


def dot_rows(left, right):
    return lax.dot_general(
        left, right, (((0,), (0,)), ((), ())), preferred_element_type=jnp.float32
    )


def dot_lanes(left, right):
    return lax.dot_general(
        left, right, (((1,), (1,)), ((), ())), preferred_element_type=jnp.float32
    )


def each_chunk(count, chans, body, unroll=1):
    per = chans // LANES

    def step(index, carry):
        frame = index // per
        rows = pl.ds(pl.multiple_of(frame * ROWS, ROWS), ROWS)
        lanes = pl.ds(pl.multiple_of((index % per) * LANES, LANES), LANES)
        body(pl.ds(frame, 1), rows, lanes)
        return carry

    lax.fori_loop(0, count * per, step, 0, unroll=unroll)


def real_rows():
    return lax.broadcasted_iota(jnp.int32, (ROWS, LANES), 0) < PIX


def group_mean(sums):
    chans = sums.shape[1]
    width = chans // GROUPS
    lane = lax.broadcasted_iota(jnp.int32, sums.shape, 1)
    step = 1
    while step < width:
        ahead = pltpu.roll(sums, chans - step, 1)
        behind = pltpu.roll(sums, step, 1)
        sums = sums + jnp.where((lane & step) == 0, ahead, behind)
        step *= 2
    return sums * (1.0 / (PIX * width))


def silu(value):
    return value / (1.0 + jnp.exp(-value))


def silu_slope(value):
    gate = 1.0 / (1.0 + jnp.exp(-value))
    return gate * (1.0 + value * (1.0 - gate))


def normalise(count, chans, hid, sums, rstd, rstd_at):
    whole = pl.ds(0, chans)
    sums[:, whole] = jnp.zeros((sums.shape[0], chans), jnp.float32)

    def add(frame, rows, lanes):
        sums[frame, lanes] = jnp.sum(hid[rows, lanes], axis=0, keepdims=True)

    each_chunk(count, chans, add, unroll=2)
    sums[:, whole] = group_mean(sums[:, whole])

    def center(frame, rows, lanes):
        value = jnp.where(real_rows(), hid[rows, lanes] - sums[frame, lanes], 0.0)
        hid[rows, lanes] = value
        sums[frame, lanes] = jnp.sum(value * value, axis=0, keepdims=True)

    each_chunk(count, chans, center, unroll=2)
    at = pl.ds(rstd_at, chans)
    rstd[:, at] = lax.rsqrt(group_mean(sums[:, whole]) + 1e-05)


def forward_kernel(count, keep, parts, skip, tuned, *refs):
    refs = list(refs)
    number = len(parts) - skip
    first = number > 3

    def take(number):
        taken = refs[:number]
        del refs[:number]
        return taken

    (place,) = take(1)
    x = take(2 if first else 1)
    gains, shift = take(2)
    sources = take(4 if tuned else len(parts))
    (out,) = take(1)
    if keep:
        if first:
            (start,) = take(1)
        hid_one, hid_two, hid_three, rstd = take(4)
        kept_weights = take(3)
    weights = take(number)
    sems, back_sems, low, act, cols, sums = take(6)
    if not keep:
        hid_one, hid_two, hid_three, rstd = take(4)
        if first:
            (start,) = take(1)
    fetch(parts, tuned, place, sources, dict(enumerate(weights, skip)), sems)

    def arrived(index):
        weight = weights[index]
        pltpu.make_async_copy(weight, weight, sems.at[len(parts) + index]).wait()
        if keep and index >= -3:
            pltpu.make_async_copy(weight, kept_weights[index], back_sems.at[3 + index]).start()
        return weight

    def whole(value):
        return value.reshape(-1, value.shape[-1])

    if first:
        pixels, spread = x
        x = start
        patch = arrived(-4)
        for half in range(2):
            wide = dot(pixels[...], spread[half]).astype(jnp.bfloat16)
            for block in range(2):
                lanes = pl.ds((2 * half + block) * WIDTH, WIDTH)
                x[:, lanes] = dot(wide, whole(patch[block]))
    else:
        (x,) = x

    def cast(frame, rows, lanes):
        low[rows, lanes] = x[rows, lanes].astype(jnp.bfloat16)

    def activate(hid, at, offset):
        def body(frame, rows, lanes):
            gain = gains[:, pl.ds(offset + lanes.start, LANES)]
            bias = gains[:, pl.ds(offset + BOT + lanes.start, LANES)]
            value = hid[rows, lanes] * rstd[frame, pl.ds(at + lanes.start, LANES)]
            hid[rows, lanes] = value
            value = jnp.where(real_rows(), silu(value * gain + bias), 0.0)
            act[rows, lanes] = value.astype(jnp.bfloat16)

        return body

    each_chunk(count, D, cast)
    hid_one[...] = dot(low[...], whole(arrived(-3)[...]))
    normalise(count, BOT, hid_one, sums, rstd, 0)
    each_chunk(count, BOT, activate(hid_one, 0, 0))
    for frame in range(count):
        rows = pl.ds(frame * ROWS, ROWS)
        for tap in range(TAPS):
            picked = dot(shift[pl.ds(tap * ROWS, ROWS), :], act[rows, :])
            cols[rows, pl.ds(tap * BOT, BOT)] = picked.astype(jnp.bfloat16)
    hid_two[...] = dot(cols[...], whole(arrived(-2)[...]))
    normalise(count, BOT, hid_two, sums, rstd, BOT)
    each_chunk(count, BOT, activate(hid_two, BOT, 2 * BOT))
    w_out = arrived(-1)
    for part in range(D // BOT):
        hid_three[:, pl.ds(part * BOT, BOT)] = dot(act[...], whole(w_out[part]))
    normalise(count, D, hid_three, sums, rstd, 2 * BOT)

    def finish(frame, rows, lanes):
        gain = gains[:, pl.ds(4 * BOT + lanes.start, LANES)]
        bias = gains[:, pl.ds(4 * BOT + D + lanes.start, LANES)]
        value = hid_three[rows, lanes] * rstd[frame, pl.ds(2 * BOT + lanes.start, LANES)]
        if keep:
            hid_three[rows, lanes] = value
        value = silu(x[rows, lanes] + value * gain + bias)
        out[rows, lanes] = jnp.where(real_rows(), value, 0.0)

    each_chunk(count, D, finish)
    if keep:
        for index in (-3, -2, -1):
            pltpu.make_async_copy(weights[index], kept_weights[index], back_sems.at[3 + index]).wait()


def f32(*shape):
    return jax.ShapeDtypeStruct(shape, jnp.float32)


def bf16(*shape):
    return jax.ShapeDtypeStruct(shape, jnp.bfloat16)


def stat_rows(count):
    return -(-count // 8) * 8


def block_forward(stream, gains, shift, parts, skip, buffers, place, keep, tuned):
    first = len(parts) - skip > 3
    rows = stream[0].shape[0]
    count = rows // ROWS
    stats = stat_rows(count)
    kept = [
        ((rows, BOT), jnp.float32),
        ((rows, BOT), jnp.float32),
        ((rows, D), jnp.float32),
        ((stats, 2 * BOT + D), jnp.float32),
    ]
    start = [((rows, D), jnp.float32)] if first else []
    weights = weight_shapes(parts, buffers, tuned)[skip:]
    out_shape = [f32(rows, D)]
    out_specs = in_vmem(1)
    scratch = [pltpu.VMEM(shape, jnp.bfloat16) for shape in weights]
    scratch += [
        pltpu.SemaphoreType.DMA((len(parts),)),
        pltpu.SemaphoreType.DMA((3,)),
        pltpu.VMEM((rows, D), jnp.bfloat16),
        pltpu.VMEM((rows, BOT), jnp.bfloat16),
        pltpu.VMEM((rows, TAPS * BOT), jnp.bfloat16),
        pltpu.VMEM((stats, D), jnp.float32),
    ]
    if keep:
        out_shape += [jax.ShapeDtypeStruct(*item) for item in start + kept]
        out_shape += [jax.ShapeDtypeStruct(shape, jnp.bfloat16) for shape in weights[-3:]]
        out_specs += in_vmem(len(start + kept)) + hbm(3)
    else:
        scratch += [pltpu.VMEM(*item) for item in kept + start]
    return pl.pallas_call(
        functools.partial(forward_kernel, count, keep, parts, skip, tuned),
        out_shape=out_shape,
        in_specs=in_smem() + in_vmem(len(stream) + 2) + hbm(len(buffers)),
        out_specs=out_specs,
        scratch_shapes=scratch,
        compiler_params=pltpu.CompilerParams(vmem_limit_bytes=VMEM_LIMIT),
        cost_estimate=LIGHT,
        name="block_forward",
    )(place, *stream, gains, shift, *buffers)


def norm_back(count, chans, slope, hid, sums, more, rstd, rstd_at, gain, grad_gain, grad_bias, store):
    whole = pl.ds(0, chans)
    sums[:, whole] = jnp.zeros((sums.shape[0], chans), jnp.float32)
    more[:, whole] = jnp.zeros((sums.shape[0], chans), jnp.float32)

    def add(frame, rows, lanes):
        value = slope(frame, rows, lanes)
        sums[frame, lanes] = jnp.sum(value, axis=0, keepdims=True)
        more[frame, lanes] = jnp.sum(value * hid[rows, lanes], axis=0, keepdims=True)

    each_chunk(count, chans, add)
    grad_bias[...] = jnp.sum(sums[:, whole], axis=0, keepdims=True)
    grad_gain[...] = jnp.sum(more[:, whole], axis=0, keepdims=True)
    sums[:, whole] = group_mean(sums[:, whole] * gain[...])
    more[:, whole] = group_mean(more[:, whole] * gain[...])

    def spread(frame, rows, lanes):
        store(
            rows,
            lanes,
            lambda value: jnp.where(
                real_rows(),
                rstd[frame, pl.ds(rstd_at + lanes.start, LANES)]
                * (value * gain[:, lanes] - sums[frame, lanes] - hid[rows, lanes] * more[frame, lanes]),
                0.0,
            ).astype(jnp.bfloat16),
        )

    each_chunk(count, chans, spread)


def back_out_body(count, grad, x, hid_two, hid_three, rstd, w_out, gains, dres, dlow, dgains, scratch, dw_out):
    third, act, dact, sums, more = scratch
    gain_three, bias_three = (gains.at[:, pl.ds(4 * BOT, D)], gains.at[:, pl.ds(4 * BOT + D, D)])

    def slope_three(frame, rows, lanes):
        value = x[rows, lanes] + hid_three[rows, lanes] * gain_three[:, lanes] + bias_three[:, lanes]
        value = jnp.where(real_rows(), grad[rows, lanes] * silu_slope(value), 0.0)
        dres[rows, lanes] = value
        return value

    def store_three(rows, lanes, back):
        third[rows, lanes] = back(dres[rows, lanes])

    norm_back(
        count, D, slope_three, hid_three, sums, more, rstd, 2 * BOT, gain_three,
        dgains.at[:, pl.ds(2 * BOT, D)], dgains.at[:, pl.ds(2 * BOT + D, D)], store_three,
    )
    total = None
    for part in range(D // BOT):
        lanes = pl.ds(part * BOT, BOT)
        term = dot_lanes(third[:, lanes], w_out[lanes, :])
        total = term if total is None else total + term
    dact[...] = total
    gain_two, bias_two = (gains.at[:, pl.ds(2 * BOT, BOT)], gains.at[:, pl.ds(3 * BOT, BOT)])

    def slope_two(frame, rows, lanes):
        value = hid_two[rows, lanes] * gain_two[:, lanes] + bias_two[:, lanes]
        gate = 1.0 / (1.0 + jnp.exp(-value))
        act[rows, lanes] = jnp.where(real_rows(), value * gate, 0.0).astype(jnp.bfloat16)
        value = dact[rows, lanes] * (gate * (1.0 + value * (1.0 - gate)))
        value = jnp.where(real_rows(), value, 0.0)
        dact[rows, lanes] = value
        return value

    def store_two(rows, lanes, back):
        dlow[rows, lanes] = back(dact[rows, lanes])

    norm_back(
        count, BOT, slope_two, hid_two, sums, more, rstd, BOT, gain_two,
        dgains.at[:, pl.ds(0, BOT)], dgains.at[:, pl.ds(BOT, BOT)], store_two,
    )
    for part in range(D // BOT):
        lanes = pl.ds(part * BOT, BOT)
        dw_out[part] = dot_rows(act[...], third[:, lanes]).astype(jnp.bfloat16)


def out_scratch(rows):
    stats = stat_rows(rows // ROWS)
    return [
        pltpu.VMEM((rows, D), jnp.bfloat16),
        pltpu.VMEM((rows, BOT), jnp.bfloat16),
        pltpu.VMEM((rows, BOT), jnp.float32),
        pltpu.VMEM((stats, D), jnp.float32),
        pltpu.VMEM((stats, D), jnp.float32),
    ]


def back_mid_body(count, grad, hid_one, rstd, w_mid, gains, shift, dlow, dgains, scratch, dw_mid):
    act, cols, dact, sums, more = scratch
    gain_one, bias_one = (gains.at[:, pl.ds(0, BOT)], gains.at[:, pl.ds(BOT, BOT)])
    for frame in range(count):
        rows = pl.ds(frame * ROWS, ROWS)
        for tap in range(TAPS):
            picked = dot(shift[pl.ds((TAPS - 1 - tap) * ROWS, ROWS), :], grad[rows, :])
            cols[rows, pl.ds(tap * BOT, BOT)] = picked.astype(jnp.bfloat16)
    total = None
    for tap in range(TAPS):
        lanes = pl.ds(tap * BOT, BOT)
        term = dot_lanes(cols[:, lanes], w_mid[lanes, :])
        total = term if total is None else total + term
    dact[...] = total

    def slope_one(frame, rows, lanes):
        value = hid_one[rows, lanes] * gain_one[:, lanes] + bias_one[:, lanes]
        gate = 1.0 / (1.0 + jnp.exp(-value))
        act[rows, lanes] = jnp.where(real_rows(), value * gate, 0.0).astype(jnp.bfloat16)
        value = dact[rows, lanes] * (gate * (1.0 + value * (1.0 - gate)))
        value = jnp.where(real_rows(), value, 0.0)
        dact[rows, lanes] = value
        return value

    def store_one(rows, lanes, back):
        dlow[rows, lanes] = back(dact[rows, lanes])

    norm_back(
        count, BOT, slope_one, hid_one, sums, more, rstd, 0, gain_one,
        dgains.at[:, pl.ds(0, BOT)], dgains.at[:, pl.ds(BOT, BOT)], store_one,
    )
    for tap in range(TAPS):
        lanes = pl.ds(tap * BOT, BOT)
        dw_mid[0, lanes, :] = dot_rows(act[...], cols[:, lanes]).astype(jnp.bfloat16)


def back_in_body(count, grad, x, dres, w_in, dx, low, dw_in):
    def cast(frame, rows, lanes):
        low[rows, lanes] = x[rows, lanes].astype(jnp.bfloat16)

    each_chunk(count, D, cast)
    for part in range(D // BOT):
        lanes = pl.ds(part * BOT, BOT)
        dx[:, lanes] = dres[:, lanes] + dot_lanes(grad[...], w_in[lanes, :])
        dw_in[0, lanes, :] = dot_rows(low[:, lanes], grad[...]).astype(jnp.bfloat16)


def back_kernel(body, parts, tuned, counts, *refs):
    place, refs = (refs[0], list(refs[1:]))
    groups = []
    for number in (*counts[:2], len(dealt_shapes(parts, tuned)), len(parts), 1, counts[2]):
        groups.append(refs[:number])
        refs = refs[number:]
    ins, outs, dealt, made, sems, scratch = groups

    def done(index):
        start_deal(parts, tuned, place, index, made, dealt, sems[0])

    body(ins, outs, made, scratch, done)
    for index, array in enumerate(made):
        pltpu.make_async_copy(array, array, sems[0].at[index]).wait()


def back_call(name, body, ins, out_shape, scratch, parts, tuned, place):
    dealt = dealt_shapes(parts, tuned)
    counts = (len(ins), len(out_shape), len(scratch))
    outs = pl.pallas_call(
        functools.partial(back_kernel, body, parts, tuned, counts),
        out_shape=out_shape + [bf16(*shape) for shape in dealt],
        in_specs=in_smem() + in_vmem(len(ins)),
        out_specs=in_vmem(len(out_shape)) + hbm(len(dealt)),
        scratch_shapes=[pltpu.VMEM(whole_shape(part), jnp.bfloat16) for part in parts]
        + [pltpu.SemaphoreType.DMA((len(parts),))]
        + scratch,
        compiler_params=pltpu.CompilerParams(vmem_limit_bytes=VMEM_LIMIT),
        cost_estimate=LIGHT,
        name=name,
    )(place, *ins)
    return (list(outs[: len(out_shape)]), list(outs[len(out_shape) :]))


def back_out(grad, stream, hid_two, hid_three, rstd, w_out, gains, parts, tuned, place):
    rows = stream.shape[0]

    def body(ins, outs, made, scratch, done):
        back_out_body(rows // ROWS, *ins, *outs, scratch, made[0])
        done(0)

    ins = [grad, stream, hid_two, hid_three, rstd, w_out, gains]
    out_shape = [f32(rows, D), bf16(rows, BOT), f32(1, 2 * BOT + 2 * D)]
    return back_call("back_out", body, ins, out_shape, out_scratch(rows), parts, tuned, place)


def back_mid(grad, hid_one, rstd, w_mid, gains, shift, more, parts, tuned, place):
    rows = grad.shape[0]
    stats = stat_rows(rows // ROWS)

    def body(ins, outs, made, scratch, done):
        for index in range(1, len(made)):
            made[index][...] = ins[5 + index][...]
            done(index)
        back_mid_body(rows // ROWS, *ins[:6], *outs, scratch, made[0])
        done(0)

    scratch = [
        pltpu.VMEM((rows, BOT), jnp.bfloat16),
        pltpu.VMEM((rows, TAPS * BOT), jnp.bfloat16),
        pltpu.VMEM((rows, BOT), jnp.float32),
        pltpu.VMEM((stats, BOT), jnp.float32),
        pltpu.VMEM((stats, BOT), jnp.float32),
    ]
    ins = [grad, hid_one, rstd, w_mid, gains, shift, *more]
    out_shape = [bf16(rows, BOT), f32(1, 2 * BOT)]
    return back_call("back_mid", body, ins, out_shape, scratch, parts, tuned, place)


def back_between(grad, stream, dres, w_in, later, parts, tuned, place):
    rows = stream.shape[0]

    def body(ins, outs, made, scratch, done):
        dx, low, *rest = scratch
        back_in_body(rows // ROWS, *ins[:4], dx, low, made[0])
        done(0)
        back_out_body(rows // ROWS, dx, *ins[4:], *outs, rest, made[1])
        done(1)

    scratch = [pltpu.VMEM((rows, D), jnp.float32), pltpu.VMEM((rows, D), jnp.bfloat16)]
    scratch += out_scratch(rows)
    ins = [grad, stream, dres, w_in, *later]
    out_shape = [f32(rows, D), bf16(rows, BOT), f32(1, 2 * BOT + 2 * D)]
    return back_call("back_between", body, ins, out_shape, scratch, parts, tuned, place)


def back_first(grad, stream, dres, w_in, pixels, spread, dgains, parts, tuned, place):
    rows = stream.shape[0]

    def body(ins, outs, made, scratch, done):
        dx, low = scratch
        made[2][...] = ins[6][...]
        done(2)
        back_in_body(rows // ROWS, *ins[:4], dx, low, made[0])
        done(0)
        wide = [dot(ins[4][...], ins[5][half]).astype(jnp.bfloat16) for half in range(2)]
        for block in range(2):
            total = None
            for half in range(2):
                lanes = pl.ds((2 * half + block) * WIDTH, WIDTH)
                term = dot_rows(wide[half], dx[:, lanes].astype(jnp.bfloat16))
                total = term if total is None else total + term
            made[1][block] = total.astype(jnp.bfloat16)
        done(1)

    scratch = [pltpu.VMEM((rows, D), jnp.float32), pltpu.VMEM((rows, D), jnp.bfloat16)]
    ins = [grad, stream, dres, w_in, pixels, spread, dgains]
    return back_call("back_first", body, ins, [], scratch, parts, tuned, place)[1]


def spread_pixels(devices):
    rows = PATCH_IN // devices
    value = jnp.arange(PATCH_IN)
    at = value // rows * 2 * rows + value % rows
    return jnp.stack(
        [jnp.arange(2 * PATCH_IN)[None, :] == (at + half * rows)[:, None] for half in range(2)]
    ).astype(jnp.bfloat16)


def merge(value):
    return value.reshape(-1, value.shape[-1])


def fetch_ends(parts, tuned, place, sources, weights, sems):
    first = len(parts) - 2
    fetch(parts, tuned, place, sources, dict(enumerate(weights, first)), sems)

    def arrived(index):
        weight = weights[index]
        pltpu.make_async_copy(weight, weight, sems.at[first + index]).wait()
        return weight

    return arrived


def head_forward(count, stream, pool, arrived, games, pool_t, pooled):
    for part in range(D // ROWS):
        lanes = pl.ds(part * ROWS, ROWS)
        pool_t[:, lanes] = pool[lanes, :].astype(jnp.float32).T
    pooled[...] = jnp.zeros_like(pooled)

    def weigh(frame, rows, lanes):
        value = stream[rows, lanes].astype(jnp.bfloat16).astype(jnp.float32)
        pooled[frame, lanes] = jnp.sum(value * pool_t[:, lanes], axis=0, keepdims=True)

    each_chunk(count, D, weigh)
    before = dot(pooled[...].astype(jnp.bfloat16), merge(arrived(0)[...]))
    hidden = silu(before).astype(jnp.bfloat16)
    heads = arrived(1)
    scores = None
    for game in range(GAMES):
        pair = [dot(hidden, merge(heads[2 * game + half])) for half in range(2)]
        term = jnp.where(games == game, jnp.concatenate(pair, axis=1), 0.0)
        scores = term if scores is None else scores + term
    return ([pick_atoms(scores, action) for action in range(ACTIONS)], before, hidden)


def atom_lanes():
    return lax.broadcasted_iota(jnp.int32, (8, ROWS), 1)


def pick_atoms(scores, action):
    offset = action * ATOMS
    moved = pltpu.roll(scores, 2 * WIDTH - offset, 1) if offset else scores
    return jnp.where(atom_lanes() < ATOMS, moved[:, :ROWS], -1e30)


def support_lanes():
    return -10.0 + 20.0 / (ATOMS - 1) * atom_lanes().astype(jnp.float32)


def lane_sum(value):
    return jnp.sum(value, axis=1, keepdims=True)


def target_kernel(count, parts, tuned, place, stream, pool, whole, real, *refs):
    sources, (out, *weights, sems, pool_t, pooled) = (refs[:-6], refs[-6:])
    arrived = fetch_ends(parts, tuned, place, sources, weights, sems)
    logits, _, _ = head_forward(count, stream, pool, arrived, whole[:, 0:1], pool_t, pooled)
    chosen = None
    for action in range(ACTIONS):
        term = jnp.where(whole[:, 2:3] == action, logits[action], 0.0)
        chosen = term if chosen is None else chosen + term
    power = jnp.exp(chosen - jnp.max(chosen, axis=1, keepdims=True))
    probs = power / lane_sum(power)
    atoms = support_lanes()
    spacing = 20.0 / (ATOMS - 1)
    moved = jnp.clip(real[:, 0:1] + real[:, 1:2] * atoms, -10.0, 10.0)
    total = jnp.zeros_like(probs)
    for atom in range(ATOMS):
        near = 1.0 - jnp.abs(moved[:, atom : atom + 1] - atoms) / spacing
        total = total + probs[:, atom : atom + 1] * jnp.clip(near, 0.0, 1.0)
    inside = (atom_lanes() < ATOMS) & (lax.broadcasted_iota(jnp.int32, total.shape, 0) < count)
    out[...] = jnp.where(inside, total, 0.0)


def ends_scratch(parts, buffers, tuned):
    scratch = [pltpu.VMEM(shape, jnp.bfloat16) for shape in weight_shapes(parts, buffers, tuned)[-2:]]
    scratch += [pltpu.SemaphoreType.DMA((len(parts),))]
    return scratch + [pltpu.VMEM((ROWS, D), jnp.float32), pltpu.VMEM((8, D), jnp.float32)]


def head_target(stream, pool, whole, real, parts, buffers, tuned, place):
    count = stream.shape[0] // ROWS
    return pl.pallas_call(
        functools.partial(target_kernel, count, parts, tuned),
        out_shape=f32(8, ROWS),
        in_specs=in_smem() + in_vmem(4) + hbm(len(buffers)),
        out_specs=in_vmem(1)[0],
        scratch_shapes=ends_scratch(parts, buffers, tuned),
        compiler_params=pltpu.CompilerParams(vmem_limit_bytes=VMEM_LIMIT),
        cost_estimate=LIGHT,
        name="head_target",
    )(place, stream, pool, whole, real, *buffers)


def loss_kernel(count, frames_all, parts, tuned, place, stream, pool, target, whole, legal, *refs):
    sources, refs = (refs[:-10], refs[-10:])
    loss, dstream, dpool, acts, *weights, sems, pool_t, pooled, dpooled = refs
    arrived = fetch_ends(parts, tuned, place, sources, weights, sems)
    proj, heads = weights
    games, taken = (whole[:, 0:1], whole[:, 1:2])
    logits, before, hidden = head_forward(count, stream, pool, arrived, games, pool_t, pooled)
    atoms = support_lanes()
    inside = atom_lanes() < ATOMS
    logps, probs, values = ([], [], [])
    for value in logits:
        value = value - jnp.max(value, axis=1, keepdims=True)
        power = jnp.where(inside, jnp.exp(value), 0.0)
        mass = lane_sum(power)
        logps.append(value - jnp.log(mass))
        probs.append(power / mass)
        values.append(lane_sum(probs[-1] * atoms))
    masked = [
        jnp.where(legal[:, action : action + 1] > 0, values[action], -1e30)
        for action in range(ACTIONS)
    ]
    largest = functools.reduce(jnp.maximum, masked)
    powers = [jnp.exp(value - largest) for value in masked]
    mass = sum(powers[1:], powers[0])
    goal = target[...]
    goal_mass = lane_sum(goal)
    cross = taken_value = 0.0
    real = lax.broadcasted_iota(jnp.int32, (8, 1), 0) < count
    scale = jnp.where(real, 1.0 / frames_all, 0.0)
    spread = jnp.zeros((8, 2 * WIDTH), jnp.float32)
    for action in range(ACTIONS):
        here = jnp.where(taken == action, 1.0, 0.0)
        cross = cross - here * lane_sum(jnp.where(inside, goal * logps[action], 0.0))
        taken_value = taken_value + here * values[action]
        grad = here * (probs[action] * goal_mass - goal)
        pull = CQL_WEIGHT * (powers[action] / mass - here)
        grad = grad + pull * probs[action] * (atoms - values[action])
        grad = jnp.where(inside, grad * scale, 0.0)
        grad = jnp.concatenate([grad, jnp.zeros((8, 2 * WIDTH - ROWS), jnp.float32)], axis=1)
        offset = action * ATOMS
        spread = spread + (pltpu.roll(grad, offset, 1) if offset else grad)
    losses = cross + CQL_WEIGHT * (jnp.log(mass) + largest - taken_value)
    loss[...] = jnp.sum(jnp.where(real, losses, 0.0), axis=0, keepdims=True)
    dhidden = None
    spread = spread.astype(jnp.bfloat16)
    for game in range(GAMES):
        mine = jnp.where(games == game, spread, 0.0).astype(jnp.bfloat16)
        for half in range(2):
            part = mine[:, half * WIDTH : (half + 1) * WIDTH]
            term = dot_lanes(part, merge(heads[2 * game + half]))
            dhidden = term if dhidden is None else dhidden + term
    dbefore = (silu_slope(before) * dhidden).astype(jnp.bfloat16)
    pieces = [hidden, dbefore]
    pieces += [pooled[:, part * WIDTH : (part + 1) * WIDTH] for part in range(D // WIDTH)]
    lanes = lax.broadcasted_iota(jnp.int32, (8, WIDTH), 1)
    marked = jnp.where(lanes == WIDTH - 1, games.astype(jnp.float32), spread[:, WIDTH:].astype(jnp.float32))
    pieces += [spread[:, :WIDTH], marked]
    acts[...] = jnp.concatenate([piece.astype(jnp.float32) for piece in pieces]).astype(jnp.bfloat16)
    dpooled[...] = dot_lanes(dbefore, merge(proj[...])).astype(jnp.bfloat16).astype(jnp.float32)

    def push(frame, rows, lanes):
        dstream[rows, lanes] = dpooled[frame, lanes] * pool_t[:, lanes]

    each_chunk(count, D, push)

    def gather_pool(part, carry):
        lanes = pl.ds(pl.multiple_of(part * ROWS, ROWS), ROWS)
        total = None
        for frame in range(count):
            value = stream[pl.ds(frame * ROWS, ROWS), lanes].astype(jnp.bfloat16)
            term = value.astype(jnp.float32) * dpooled[pl.ds(frame, 1), lanes]
            total = term if total is None else total + term
        dpool[0, lanes, :] = total.T.astype(jnp.bfloat16)
        return carry

    lax.fori_loop(0, D // ROWS, gather_pool, 0)


def head_loss(stream, pool, target, whole, legal, frames_all, parts, buffers, tuned, place):
    rows = stream.shape[0]
    return pl.pallas_call(
        functools.partial(loss_kernel, rows // ROWS, frames_all, parts, tuned),
        out_shape=[f32(1, 1), f32(rows, D), bf16(1, D, ROWS), bf16(ACTS, WIDTH)],
        in_specs=in_smem() + in_vmem(5) + hbm(len(buffers)),
        out_specs=in_vmem(4),
        scratch_shapes=ends_scratch(parts, buffers, tuned) + [pltpu.VMEM((8, D), jnp.float32)],
        compiler_params=pltpu.CompilerParams(vmem_limit_bytes=VMEM_LIMIT),
        cost_estimate=LIGHT,
        name="head_loss",
    )(place, stream, pool, target, whole, legal, *buffers)


ACTS = 64


def own_heads_kernel(parts, tuned, place, *refs):
    sources, (heads, proj, acts, sems) = (refs[:-4], refs[-4:])
    fetch(parts, tuned, place, sources, {0: acts}, sems)
    pltpu.make_async_copy(acts, acts, sems.at[0]).wait()
    value = acts[...].reshape(-1, ACTS, WIDTH).astype(jnp.float32)
    pieces = [value[:, first : first + 8].reshape(-1, WIDTH) for first in range(0, ACTS, 8)]
    pieces = [piece.astype(jnp.bfloat16) for piece in pieces]
    hidden, dbefore, scores = (pieces[0], pieces[1], pieces[-2:])
    games = scores[1][:, WIDTH - 1 :].astype(jnp.float32)
    lanes = lax.broadcasted_iota(jnp.int32, scores[1].shape, 1)
    scores[1] = jnp.where(lanes < WIDTH - 1, scores[1].astype(jnp.float32), 0.0).astype(jnp.bfloat16)
    row = lax.broadcasted_iota(jnp.int32, (WIDTH, ROWS), 0)
    lane = lax.broadcasted_iota(jnp.int32, (WIDTH, ROWS), 1)

    def own(items, count):
        total = None
        for block, item in enumerate(items):
            wanted = (row + block * WIDTH == place[4] * count + lane) & (lane < count)
            term = dot(item, jnp.where(wanted, 1.0, 0.0).astype(jnp.bfloat16))
            total = term if total is None else total + term
        return total.astype(jnp.bfloat16)

    count = heads.shape[1]
    mine = own([hidden], count)
    for game in range(GAMES):
        for half in range(2):
            chosen = jnp.where(games == game, scores[half].astype(jnp.float32), 0.0)
            heads[2 * game + half] = dot_rows(mine, chosen.astype(jnp.bfloat16))[:count]
    count = proj.shape[1]
    proj[0] = dot_rows(own(pieces[2:-2], count), dbefore)[:count]


def own_heads(buffers, heads, proj, tuned, place):
    parts = [Part(1, ACTS, WIDTH)]
    return pl.pallas_call(
        functools.partial(own_heads_kernel, parts, tuned),
        out_shape=[f32(part.blocks, part.rows, part.lanes) for part in (heads, proj)],
        in_specs=in_smem() + hbm(len(buffers)),
        out_specs=in_vmem(2),
        scratch_shapes=[
            pltpu.VMEM(weight_shapes(parts, buffers, tuned)[0], jnp.bfloat16),
            pltpu.SemaphoreType.DMA((1,)),
        ],
        compiler_params=pltpu.CompilerParams(vmem_limit_bytes=VMEM_LIMIT),
        cost_estimate=LIGHT,
        name="own_heads",
    )(place, *buffers)


WIDTH = 512
TILE = 16
AXES = ("wide", "narrow")


def grid_sizes():
    return (lax.axis_size("wide") // 2, 2, lax.axis_size("narrow") // 2, 2)


def spot():
    sizes = grid_sizes()
    wide, narrow = (lax.axis_index("wide"), lax.axis_index("narrow"))
    place = [wide // sizes[1], wide % sizes[1], narrow // sizes[3], narrow % sizes[3]]
    return jnp.stack(place + [wide * lax.axis_size("narrow") + narrow]).astype(jnp.int32)


def hop(array, axis_of_core, step=1, swap=0):
    sizes = grid_sizes()

    def target(place):
        axis = axis_of_core[place[3]]
        other = list(place)
        other[axis] = place[axis] ^ swap if swap else (place[axis] + step) % sizes[axis]
        return other

    return send(array, target)


def flip(array, *bits):
    return send(array, lambda place: [value ^ bit for value, bit in zip(place, bits)])


def send(array, target):
    sizes = grid_sizes()
    pairs = []
    for place in itertools.product(*[range(size) for size in sizes]):
        pairs.append(
            tuple(
                ((z * sizes[1] + y) * sizes[2] + x) * sizes[3] + core
                for z, y, x, core in (place, target(place))
            )
        )
    return lax.ppermute(array, AXES, pairs)


ALONG_Z = (0, 0)
ACROSS = (3, 3)
NEAR = (2, 1)
FAR = (1, 2)


def hbm(number):
    return [pl.BlockSpec(memory_space=pl.ANY)] * number


def in_vmem(number):
    return [pl.BlockSpec(memory_space=pltpu.VMEM)] * number


def in_smem():
    return [pl.BlockSpec(memory_space=pltpu.SMEM)]


def copies(pairs, sems):
    started = [
        pltpu.make_async_copy(source, target, sems.at[index])
        for index, (source, target) in enumerate(pairs)
    ]
    for copy in started:
        copy.start()
    for copy in started:
        copy.wait()


class Part:
    def __init__(self, blocks, rows, lanes):
        self.blocks, self.rows, self.lanes = (blocks, rows, lanes)
        self.across = WIDTH // lanes
        self.travel = blocks * rows // self.across

    def moves(self):
        if self.across > 1:
            deep = self.rows // self.across
            return [(0, part * self.lanes, deep, 0, part * deep) for part in range(self.across)]
        return [(block * self.rows, 0, self.rows, block, 0) for block in range(self.blocks)]

    def pack(self, piece):
        if self.across > 1:
            piece = piece.reshape(self.across, self.rows // self.across, self.lanes)
            return piece.transpose(1, 0, 2).reshape(self.travel, WIDTH)
        return piece.reshape(self.travel, WIDTH)

    def unpack(self, rows):
        if self.across > 1:
            rows = rows.reshape(self.rows // self.across, self.across, self.lanes)
            return rows.transpose(1, 0, 2).reshape(1, self.rows, self.lanes)
        return rows.reshape(self.blocks, self.rows, self.lanes)

    def full(self, depth):
        return (self.blocks, depth, 2, 2, 2, self.rows, self.lanes)


def half_rows(parts):
    total = sum(part.travel for part in parts)
    return -(-total // (2 * TILE)) * TILE


def half_moves(parts):
    cut = half_rows(parts)
    halves = ([], [])
    offset = 0
    for index, part in enumerate(parts):
        for row, lane, rows, block, inner in part.moves():
            row = row + offset
            before = max(0, min(rows, cut - row))
            if before:
                halves[0].append((index, row, lane, before, block, inner))
            if rows - before:
                halves[1].append((index, row + before - cut, lane, rows - before, block, inner + before))
        offset += part.travel
    return halves


def unit(parts, depth):
    return (depth, 2, half_rows(parts), WIDTH)


def pack(parts, pieces):
    rows = jnp.concatenate([part.pack(piece) for part, piece in zip(parts, pieces)])
    return jnp.pad(rows, ((0, 2 * half_rows(parts) - rows.shape[0]), (0, 0)))


def assemble_pairs(parts, core, y, x, ins, outs):
    pairs = []
    for other, far, near in itertools.product((0, 1), repeat=3):
        half = core ^ other
        step = [0, 0, 0, 0]
        step[NEAR[half]], step[FAR[half]] = (near, far)
        at_y, at_x = (lax.rem(y + step[1], 2), lax.rem(x + step[2], 2))
        for index, row, lane, rows, block, inner in half_moves(parts)[half]:
            if index not in outs:
                continue
            pairs.append(
                (
                    index,
                    ins[2 * other + far].at[near, :, :, pl.ds(row, rows), pl.ds(lane, parts[index].lanes)],
                    outs[index].at[block, :, at_y, at_x, :, pl.ds(inner, rows)],
                )
            )
    return pairs


def fetch(parts, tuned, place, sources, weights, sems):
    if not tuned:
        for index, weight in weights.items():
            pltpu.make_async_copy(sources[index], weight, sems.at[index]).start()
        return
    for core in (0, 1):

        @pl.when(place[3] == core)
        def _():
            pairs = assemble_pairs(parts, core, place[1], place[2], sources, weights)
            for index, source, target in sorted(pairs, key=lambda pair: pair[0]):
                pltpu.make_async_copy(source, target, sems.at[index]).start()


def weight_shapes(parts, buffers, tuned):
    if tuned:
        return [part.full(buffers[0].shape[1]) for part in parts]
    return [item.shape for item in buffers]


def assemble_kernel(parts, some, place, *refs):
    outs, sems = (dict(zip(some, refs[4:-1])), refs[-1])
    fetch(parts, True, place, refs[:4], outs, sems)
    for index, out in outs.items():
        pltpu.make_async_copy(out, out, sems.at[index]).wait()


def assemble(parts, buffers, place, some=None):
    some = range(len(parts)) if some is None else some
    shapes = weight_shapes(parts, buffers, True)
    full = pl.pallas_call(
        functools.partial(assemble_kernel, parts, some),
        out_shape=[bf16(*shapes[index]) for index in some],
        in_specs=in_smem() + hbm(4),
        out_specs=in_vmem(len(some)),
        scratch_shapes=[pltpu.SemaphoreType.DMA((len(parts),))],
        compiler_params=pltpu.CompilerParams(vmem_limit_bytes=VMEM_LIMIT),
        cost_estimate=LIGHT,
        name="assemble",
    )(place, *buffers)
    return [merged(item) for item in full]


def merged(array):
    return array.reshape(array.shape[0], -1, array.shape[-1])


def in_order(own, other, bit):
    first = jnp.where(bit == 0, own, other)
    second = jnp.where(bit == 0, other, own)
    return jnp.stack([first, second])


def together(*trees):
    flat, tree = jax.tree.flatten(trees)
    return jax.tree.unflatten(tree, lax.optimization_barrier(flat))


def start_gather(groups, pieces, place):
    core = place[3]
    packed = [pack(parts, items) for parts, items in zip(groups, pieces)]
    halves = [half_rows(parts) for parts in groups]
    kept = [lax.dynamic_slice_in_dim(rows, core * half, half) for rows, half in zip(packed, halves)]
    sent = [
        lax.dynamic_slice_in_dim(rows, (1 - core) * half, half) for rows, half in zip(packed, halves)
    ]
    got = hop(jnp.concatenate(sent), ACROSS)
    held = []
    offset = 0
    for keep, half in zip(kept, halves):
        held.append(in_order(keep, got[offset : offset + half], core))
        offset += half
    return held


def pipelined_gather(groups, pieces, place, state, arrived):
    count = len(groups)
    low, high = (place[0] % 2, place[0] // 2)
    held = start_gather(groups[:1], pieces(None)[:1], place)
    for tick in range(count + 3):
        near, far, last = [index if 0 <= index < count else None for index in range(tick - 1, tick - 4, -1)]
        live = [index for index in (tick, near, far, last) if index is not None and index < count]
        if tick in (1, 2):
            live += range(tick + 1, count)
        items, state = together([held[index] for index in live], state)
        for index, item in zip(live, items):
            held[index] = item
        if tick == 0:
            held += start_gather(groups[1:2], pieces(held[0])[1:2], place)
            held += start_gather(groups[2:], pieces(held[1])[2:], place)
        if last is not None:
            own, arrived_far, other = held[last]
            held[last] = [own, arrived_far, other, hop(arrived_far, ACROSS)]
        if far is not None:
            held[far] = [held[far], hop(held[far], FAR), hop(held[far], ACROSS)]
        if near is not None:
            held[near] = [held[near], hop(held[near], NEAR)]
        if tick == 0:
            held[0] = [held[0]] + [hop(held[0], ALONG_Z, swap=bits) for bits in (1, 2, 3)]
        elif tick < count:
            held[tick] = [held[tick], hop(held[tick], ALONG_Z, swap=2)]
        if tick < 3:
            early = slice(tick + 1, tick + 2 if tick < 2 else count)
            got = hop(jnp.concatenate(held[early], axis=1), ALONG_Z, swap=1)
            ends = list(itertools.accumulate(half_rows(parts) for parts in groups[early]))
            got = jnp.split(got, ends[:-1], axis=1)
            held[early] = [in_order(item, other, low) for item, other in zip(held[early], got)]
        if last is not None:
            state = arrived(last, held[last], state)
        if tick < count:
            items, state = together(held[tick], state)
            if tick == 0:
                items = [in_order(*items[:2], low), in_order(*items[2:], low)]
            both = in_order(*items, high)
            held[tick] = both.reshape(-1, *both.shape[2:])
        if near is not None:
            items, state = together(held[near], state)
            held[near] = jnp.stack(items)
    return state


def whole_shape(part):
    return (part.blocks, part.rows * lax.axis_size(AXES), part.lanes)


def dealt_shapes(parts, tuned):
    if not tuned:
        return [whole_shape(part) for part in parts]
    size = (grid_sizes()[0], 2, half_rows(parts), WIDTH)
    return [lead + size for lead in ((2, 2), (2,), (), ())]


def start_deal(parts, tuned, place, wanted, arrays, dealt, sems):
    if not tuned:
        pltpu.make_async_copy(arrays[wanted], dealt[wanted], sems.at[wanted]).start()
        return
    array = arrays[wanted].reshape(*parts[wanted].full(grid_sizes()[0]))
    to_core, to_far, to_near, own = dealt
    for core in (0, 1):

        @pl.when(place[3] == core)
        def _():
            for other, far, near in itertools.product((0, 1), repeat=3):
                half = core ^ other
                step = [0, 0, 0, 0]
                step[NEAR[half]], step[FAR[half]] = (near, far)
                at_y, at_x = (lax.rem(place[1] + step[1], 2), lax.rem(place[2] + step[2], 2))
                if other:
                    target = to_core.at[far, near]
                elif far:
                    target = to_far.at[near]
                else:
                    target = to_near if near else own
                for index, row, lane, rows, block, inner in half_moves(parts)[half]:
                    if index == wanted:
                        pltpu.make_async_copy(
                            array.at[block, :, at_y, at_x, :, pl.ds(inner, rows)],
                            target.at[:, :, pl.ds(row, rows), pl.ds(lane, parts[index].lanes)],
                            sems.at[index],
                        ).start()


def add_up(*terms):
    total = terms[0].astype(jnp.float32)
    for term in terms[1:]:
        total = total + term.astype(jnp.float32)
    return total


def low_add(*terms):
    return add_up(*terms).astype(jnp.bfloat16)


def scatter_stages(place, direct):
    depth = grid_sizes()[0]
    z, core = (place[0], place[3])
    low, high = (z % 2, z // 2)

    def across(items):
        to_core, *rest = items
        return rest + [hop(to_core, ACROSS)]

    def far(items):
        to_far, to_near, own, from_core = items
        return [to_near, own, from_core, hop(low_add(to_far, from_core[1]), FAR)]

    def near(items):
        to_near, own, from_core, from_far = items
        from_near = hop(low_add(to_near, from_core[0, 1], from_far[1]), NEAR)
        return [own, from_core, from_far, from_near]

    def pick(array, at):
        return lax.dynamic_index_in_dim(array, at, 0, False)

    def gathered(items):
        own, from_core, from_far, from_near = items
        return lax.optimization_barrier(add_up(own, from_core[0, 0], from_far[0], from_near))

    def along(items):
        summed = gathered(items)
        sent = [pick(summed, lax.rem(z + step, depth)) for step in range(1, depth)]
        got = [hop(item.astype(jnp.bfloat16), ALONG_Z, step + 1) for step, item in enumerate(sent)]
        return [pick(summed, z)] + got

    def pairs(items):
        summed = gathered(items)
        summed = summed.reshape(2, 2, *summed.shape[1:])
        return [pick(summed, high), hop(pick(summed, 1 - high).astype(jnp.bfloat16), ALONG_Z, swap=2)]

    def neighbours(items):
        summed = add_up(*items)
        return [pick(summed, low), hop(pick(summed, 1 - low).astype(jnp.bfloat16), ALONG_Z, swap=1)]

    def finish(items):
        total = add_up(*items)
        other = hop(pick(total, 1 - core), ACROSS)
        return in_order(pick(total, core), other, core).reshape(-1, WIDTH)

    return [across, far, near] + ([along] if direct else [pairs, neighbours]) + [finish]


def share_stages(part, place):
    low, high = (place[0] % 2, place[0] // 2)

    def pairs(item):
        both = in_order(item, hop(item, ALONG_Z, swap=2), high)
        return both.reshape(-1, *both.shape[2:])

    return [
        lambda item: start_gather([[part]], [[item]], place)[0],
        lambda item: in_order(item, hop(item, ALONG_Z, swap=1), low),
        pairs,
        lambda item: jnp.stack([item, hop(item, NEAR)]),
        lambda item: [item, hop(item, FAR), hop(item, ACROSS)],
        lambda items: items + [hop(items[1], ACROSS)],
    ]


def pipelined_scatter(count, place, state, steps, shared):
    held, todo = ([], [])
    part, piece, more = shared
    share = share_stages(part, place)
    for tick in range(count + 5):
        live = [index for index in range(len(held)) if todo[index]]
        items, state, piece = together([held[index] for index in live], state, piece)
        for index, item in zip(live, items):
            held[index] = item
            for _ in range(2 if index == tick - 1 else 1):
                held[index] = todo[index].pop(0)(held[index])
        if share:
            piece = share.pop(0)(piece)
        elif more:
            piece = more.pop(0)(piece, held)
        if tick < count:
            dealt, state = steps[tick](state)
            held.append(dealt)
            todo.append(scatter_stages(place, tick >= count - 3))
    return (held, piece, state)


CQL_WEIGHT = 0.05
BETA_ONE = 0.5
BETA_TWO = 0.5
LEARNING_RATE = 0.25
WEIGHT_DECAY = 0.01
PATCH_IN = 256
DPROJ = 512
ACTIONS = 18
ATOMS = 51
GAMES = 4
BLOCKS = 2
STEP = 5
PLAYS = ACTIONS * ATOMS


def average_decay():
    return min(0.99, (1.0 + STEP) / (10.0 + STEP))


SWEEP = 8192


def lamb_parts(grads, params, first, second):
    momentum = BETA_ONE * first + (1.0 - BETA_ONE) * grads
    variance = BETA_TWO * second + (1.0 - BETA_TWO) * grads * grads
    direction = (
        momentum / (1.0 - BETA_ONE**STEP) / (jnp.sqrt(variance / (1.0 - BETA_TWO**STEP)) + 1e-06)
        + WEIGHT_DECAY * params
    )
    return (momentum, variance, direction)


def stretches(cuts):
    found = []
    at = 0
    for index, (start, size) in enumerate(cuts):
        end = start + size
        last = index == len(cuts) - 1
        whole = end if last else end // ROWS * ROWS
        found.append((at, whole - at, [index]))
        at = whole
        if end != whole:
            found.append((whole, ROWS, [index, index + 1]))
            at = whole + ROWS
    return found


def sweep(start, size, body, carry):
    steps = size // SWEEP

    def step(index, carry):
        return body(pl.ds(pl.multiple_of(start + index * SWEEP, ROWS), SWEEP), carry)

    if steps:
        carry = lax.fori_loop(0, steps, step, carry)
    return (carry, start + steps * SWEEP, size - steps * SWEEP)


def row_sum(value):
    return jnp.sum(value, axis=1, keepdims=True)


def put_rows(target, row, source, steps):
    for first, rows, lane, stride in steps:

        def step(index, carry):
            lanes = pl.ds(pl.multiple_of(lane + index * stride, ROWS), WIDTH)
            target[row : row + 1, lanes] = source[pl.ds(first + index, 1), :]
            return carry

        lax.fori_loop(0, rows, step, 0, unroll=4)


def block_rows(name, start, rows, first):
    if name == "w_out":
        count = rows // (D // BOT)
        return [(first + part * count, count, start + part * BOT, D) for part in range(D // BOT)]
    return [(first, rows, start, WIDTH)]


def patch_rows(rows, first):
    count = rows // 4
    return [
        (first + (2 * block + half) * count, count, half * (D // 2) + block * WIDTH, D)
        for block in range(2)
        for half in range(2)
    ]


def direction_kernel(cuts, moves, gain_at, *refs):
    top_cuts, block_cuts = cuts
    number = len(moves)
    sources, refs = (refs[:number], refs[number:])
    late, loss, *refs = refs
    top_ins, block_ins, refs = (refs[:3], refs[3:6], refs[6:])
    sums, *refs = refs
    top_outs, block_outs, (top_grad, block_grad) = (refs[:3], refs[3:6], refs[6:])
    for source, steps in zip(sources, moves):
        for row, placed in steps:
            put_rows(top_grad if row is None else block_grad, row or 0, source, placed)
    patch = top_cuts[0][1]
    top_grad[:, pl.ds(patch, late.shape[1])] = late[...]
    gain_start, gain_width = block_cuts[3]
    source, first = (sources[gain_at[0]], gain_at[1])
    block_grad[:, pl.ds(gain_start, gain_width)] = source[pl.ds(first, 8), :][:BLOCKS, :gain_width]

    def work(lanes, grad, ins, outs):
        param, *moments = [ref[:, lanes] for ref in ins]
        made = lamb_parts(grad[:, lanes], param, *moments)
        for ref, value in zip(outs, made):
            ref[:, lanes] = value
        return (param * param, made[2] * made[2])

    found = []

    def run(cuts, grad, ins, outs, first_lane, height):
        for start, size, segments in stretches(cuts):

            def step(lanes, carry):
                terms = work(lanes, grad, ins, outs)
                return [held + term for held, term in zip(carry, terms)]

            zeros = [jnp.zeros((height, SWEEP), jnp.float32)] * 2
            carry, begin, rest = sweep(start, size, step, zeros)
            sizes = [row_sum(value) for value in carry] if rest != size else None
            if rest:
                terms = work(pl.ds(begin, rest), grad, ins, outs)
                at = begin + lax.broadcasted_iota(jnp.int32, terms[0].shape, 1)
                if len(segments) > 1:
                    edge = cuts[segments[1]][0]
                    after = [row_sum(jnp.where(at >= edge, term, 0.0)) for term in terms]
                    found.extend((first_lane, segments[1], *item) for item in enumerate(after))
                    terms = [jnp.where(at < edge, term, 0.0) for term in terms]
                more = [row_sum(term) for term in terms]
                sizes = more if sizes is None else [held + term for held, term in zip(sizes, more)]
            found.extend((first_lane, segments[0], *item) for item in enumerate(sizes))

    run(top_cuts, top_grad, top_ins, top_outs, 0, 1)
    run(block_cuts, block_grad, block_ins, block_outs, len(top_cuts), BLOCKS)
    rows = lax.broadcasted_iota(jnp.int32, sums.shape, 0)
    lanes = lax.broadcasted_iota(jnp.int32, sums.shape, 1)
    result = jnp.where((rows == 2) & (lanes == 0), loss[...], 0.0)
    for first, segment, row, value in found:
        for part in range(value.shape[0]):
            lane = first + part * len(block_cuts) + segment
            here = (rows == row) & (lanes == lane)
            result = result + jnp.where(here, value[part : part + 1], 0.0)
    sums[...] = result


def directions(cuts, rows, moves, gain_at, late, loss, top_ins, block_ins):
    shapes = [f32(*top_ins[0].shape)] * 3 + [f32(*block_ins[0].shape)] * 3
    ins = [*rows, late, loss, *top_ins, *block_ins]
    return pl.pallas_call(
        functools.partial(direction_kernel, cuts, moves, gain_at),
        out_shape=[f32(8, ROWS)] + shapes,
        in_specs=in_vmem(len(ins)),
        out_specs=in_vmem(7),
        scratch_shapes=[
            pltpu.VMEM(top_ins[0].shape, jnp.float32),
            pltpu.VMEM(block_ins[0].shape, jnp.float32),
        ],
        compiler_params=pltpu.CompilerParams(vmem_limit_bytes=VMEM_LIMIT),
        cost_estimate=LIGHT,
        name="directions",
    )(*ins)


def update_kernel(cuts, sums, *refs):
    top_cuts, block_cuts = cuts
    top_ins, block_ins, refs = (refs[:3], refs[3:6], refs[6:])
    norms, *refs = refs
    top_outs, block_outs = (refs[:2], refs[2:])
    norm = jnp.sqrt(sums[...])
    norms[...] = norm
    ratio = LEARNING_RATE * (norm[0:1] / (norm[1:2] + 1e-06))
    decay = average_decay()

    def work(lanes, ins, outs, scale):
        param, direction, average = [ref[:, lanes] for ref in ins]
        updated, averaged, *half = outs
        value = param - scale * direction
        updated[:, lanes] = value
        averaged[:, lanes] = decay * average + (1.0 - decay) * value
        for ref in half:
            ref[:, lanes] = value.astype(jnp.bfloat16)

    def run(cuts, ins, outs, scales):
        for start, size, segments in stretches(cuts):
            scale = scales[segments[0]]

            def step(lanes, carry):
                work(lanes, ins, outs, scale)
                return carry

            _, begin, rest = sweep(start, size, step, 0)
            if rest:
                if len(segments) > 1:
                    at = begin + lax.broadcasted_iota(jnp.int32, (1, rest), 1)
                    scale = jnp.where(at < cuts[segments[1]][0], scale, scales[segments[1]])
                work(pl.ds(begin, rest), ins, outs, scale)

    lanes = [ratio[:, lane : lane + 1] for lane in range(len(top_cuts) + BLOCKS * len(block_cuts))]
    run(top_cuts, top_ins, top_outs, lanes[: len(top_cuts)])
    rest = lanes[len(top_cuts) :]
    scales = [jnp.concatenate(rest[index :: len(block_cuts)]) for index in range(len(block_cuts))]
    run(block_cuts, block_ins, block_outs, scales)


def update(cuts, sums, top_ins, block_ins):
    shapes = [f32(*array.shape) for array in [top_ins[0]] * 2 + [block_ins[0]] * 2]
    shapes.append(bf16(*block_ins[0].shape))
    return pl.pallas_call(
        functools.partial(update_kernel, cuts),
        out_shape=[f32(8, ROWS)] + shapes,
        in_specs=in_vmem(7),
        out_specs=in_vmem(6),
        compiler_params=pltpu.CompilerParams(vmem_limit_bytes=VMEM_LIMIT),
        cost_estimate=LIGHT,
        name="update",
    )(sums, *top_ins, *block_ins)


def segment_lengths():
    top = [PATCH_IN * D, D * PIX, D * DPROJ, DPROJ * GAMES * PLAYS]
    block = [D * BOT, 9 * BOT * BOT, BOT * D, 2 * (2 * BOT + D)]
    return (top, block)


def cut_points(lengths, devices):
    cuts = []
    offset = 0
    for length in lengths:
        width = length // devices
        cuts.append((offset, width))
        offset += width
    return cuts


def pack_top(flat, cuts):
    patch, pool, proj, heads = [flat[start : start + size] for start, size in cuts]
    patch = patch.reshape(-1, 2, 2, WIDTH).transpose(2, 1, 0, 3).reshape(2, -1, WIDTH)
    pool = jnp.pad(pool.reshape(1, -1, PIX), ((0, 0), (0, 0), (0, ROWS - PIX)))
    heads = jnp.pad(heads.reshape(-1, GAMES, PLAYS), ((0, 0), (0, 0), (0, 2 * WIDTH - PLAYS)))
    heads = heads.reshape(-1, 2 * GAMES, WIDTH).transpose(1, 0, 2)
    return [patch, pool, proj.reshape(1, -1, WIDTH), heads]


def flat_late(pool, proj, heads):
    heads = heads.transpose(1, 0, 2).reshape(-1, GAMES, 2 * WIDTH)[:, :, :PLAYS]
    return jnp.concatenate([item.reshape(-1) for item in (pool[:, :, :PIX], proj, heads)])


def pack_block(flat, cuts):
    w_in, w_mid, w_out = [flat[start : start + size] for start, size in cuts[:3]]
    w_out = w_out.reshape(-1, D // BOT, BOT).transpose(1, 0, 2)
    return [w_in.reshape(1, -1, BOT), w_mid.reshape(1, -1, BOT), w_out]


def parts_for(devices):
    rows = {"patch": 2 * PATCH_IN, "pool": D, "proj": D, "heads": DPROJ}
    rows |= {"w_in": D, "w_mid": TAPS * BOT, "w_out": BOT, "gains": TILE * devices}
    blocks = {"patch": 2, "heads": 2 * GAMES, "w_out": D // BOT}
    return {
        name: Part(blocks.get(name, 1), count // devices, ROWS if name == "pool" else WIDTH)
        for name, count in rows.items()
    }


def is_tuned(devices):
    parts = parts_for(devices).values()
    whole = all(part.rows // part.across % TILE == 0 for part in parts)
    return whole and lax.axis_size("wide") == 8 and lax.axis_size("narrow") == 4


def plain_gather(piece):
    return lax.all_gather(piece, AXES, axis=1, tiled=True)


def plain_scatter(array):
    return lax.psum_scatter(array, AXES, scatter_dimension=1, tiled=True).astype(jnp.float32)


def total(array):
    if lax.axis_size("wide") != 8 or lax.axis_size("narrow") != 4:
        return lax.psum(array, AXES)
    array = array + flip(array, 0, 0, 0, 1)
    array = (array + flip(array, 0, 0, 1, 0)) + (flip(array, 0, 1, 0, 0) + flip(array, 0, 1, 1, 0))
    one, two, three = [flip(array, bits, 0, 0, 0) for bits in (1, 2, 3)]
    return (array + two) + (one + three)


def frame_rows(frames):
    count = frames.shape[0]
    return jnp.pad(frames, ((0, 0), (0, ROWS - PIX), (0, 0))).reshape(count * ROWS, PATCH_IN)


def on_device(
    observed,
    following,
    game_ids,
    actions,
    legal_mask,
    rewards,
    discounts,
    done_flags,
    params_top,
    params_blocks,
    first_top,
    first_blocks,
    second_top,
    second_blocks,
    average_top,
    average_blocks,
    target_top,
    target_blocks,
):
    devices = lax.axis_size(AXES)
    frames_all = observed.shape[0] * devices
    top_lengths, block_lengths = segment_lengths()
    top_cuts = cut_points(top_lengths, devices)
    block_cuts = cut_points(block_lengths, devices)
    gain_start, gain_width = block_cuts[3]
    parts = parts_for(devices)
    tuned = is_tuned(devices)
    place = spot()
    shift = shifts()
    spread = spread_pixels(devices)
    count = observed.shape[0]
    whole = jnp.concatenate([game_ids[:, None], actions], axis=1)
    whole = jnp.pad(whole, ((0, 8 - count), (0, ROWS - 3)), constant_values=-1)
    legal = jnp.pad(legal_mask, ((0, 8 - count), (0, ROWS - ACTIONS)), constant_values=1)
    keep = discounts * (1.0 - done_flags.astype(jnp.float32))
    real = jnp.pad(jnp.stack([rewards, keep], axis=1), ((0, 8 - count), (0, ROWS - 2)))

    def read_pieces(early):
        sources = (target_top, target_blocks, params_top, params_blocks)
        if early is not None:
            early, sources = together(early, sources)
        tops = (sources[0], sources[2].astype(jnp.bfloat16))
        blocks = (sources[1], sources[3].astype(jnp.bfloat16))
        own = {}
        for net, top, flat in zip(("target", "online"), tops, blocks):
            for name, piece in zip(("patch", "pool", "proj", "heads"), pack_top(top, top_cuts)):
                own[net, name] = piece
            for index in range(BLOCKS):
                for name, piece in zip(block_names, pack_block(flat[index], block_cuts)):
                    own[net, name, index] = piece
        gain_rows = jnp.concatenate(blocks)[:, gain_start:]
        own["gains",] = jnp.pad(
            gain_rows, ((0, TILE - 2 * BLOCKS), (0, WIDTH - gain_width))
        ).reshape(1, TILE, WIDTH)
        return [[own[key] for key in group] for group in keys]

    block_names = ("w_in", "w_mid", "w_out")

    def part_of(key):
        return parts[key[0] if key[0] in parts else key[1]]

    full = {}

    def block_weight(index, name):
        return merged(full["online", name, index]).reshape(-1, BOT)

    def lead(group, buffers):
        return assemble(group_parts(group), buffers, place, [0])[0] if tuned else buffers[0]

    def hold(index, group, buffers, state):
        full["held", index] = (group, buffers)
        if index > 1:
            return state
        return state | {"target_pool": lead(group, buffers)[0]}

    def read_gains(group, buffers, state):
        gains = lead(group, buffers).reshape(devices, TILE, WIDTH)[:, : 2 * BLOCKS, :gain_width]
        gains = gains.transpose(1, 0, 2).reshape(2 * BLOCKS, -1).astype(jnp.float32)
        return run_block("target", 0, group, buffers, state | {"gains": gains})

    def target_ends(group, buffers, state):
        for index in range(1, BLOCKS):
            state = run_block("target", index, *full["held", index], state)
        target = head_target(
            state.pop("stream"), state.pop("target_pool"), whole, real,
            group_parts(group), buffers, tuned, place,
        )
        return state | {"target": target}

    def online_ends(group, buffers, state):
        loss, dstream, dpool, acts = head_loss(
            state.pop("stream"), state.pop("online_pool"), state.pop("target"), whole, legal, frames_all,
            group_parts(group), buffers, tuned, place,
        )
        return state | {"loss": loss, "grad": dstream, "pool": dpool, "acts": acts}

    def run_block(net, index, group, buffers, state):
        keep = net == "online"
        row = index + (BLOCKS if keep else 0)
        gain = state["gains"][row : row + 1]
        stream = [state["pixels" if keep else "following"], spread]
        if index:
            stream = [state["stream"]]
        skip = 1 if keys[group][0][-1] in ("gains", "pool") else 0
        out, *kept = block_forward(
            stream, gain, shift, group_parts(group), skip, buffers, place, keep, tuned
        )
        state = state | {"stream": out}
        if keep:
            start = kept.pop(0) if index == 0 else stream[0]
            full.update(zip([(net, name, index) for name in block_names], kept[-3:]))
            state |= {"kept%d" % index: [start, *kept[:-3]]}
            if index == 0:
                state |= {"online_pool": lead(group, buffers)[0]}
        return state

    keys, then = ([], [])
    ends = ("proj", "heads")

    def add_group(group, run, *names):
        keys.append(group)
        then.append(functools.partial(run, *names))

    def block_keys(net, index):
        return [(net, name, index) for name in block_names]

    for index in range(1, BLOCKS):
        start = [("target", "pool")] if index == 1 else []
        add_group(start + block_keys("target", index), hold, index)
    add_group([("gains",), ("target", "patch")] + block_keys("target", 0), read_gains)
    add_group([("target", name) for name in ends], target_ends)
    for index in range(BLOCKS):
        start = [] if index else [("online", "pool"), ("online", "patch")]
        add_group(start + block_keys("online", index), run_block, "online", index)
    add_group([("online", name) for name in ends], online_ends)

    def group_parts(group):
        return [part_of(key) for key in keys[group]]

    def arrived(group, buffers, state):
        return then[group](group, buffers, dict(state))

    state = {"following": frame_rows(following), "pixels": frame_rows(observed)}
    if tuned:
        groups = [group_parts(group) for group in range(len(keys))]
        state = pipelined_gather(groups, read_pieces, place, state, arrived)
    else:
        for group, items in enumerate(read_pieces(None)):
            state = arrived(group, [plain_gather(item) for item in items], state)

    keys = []
    steps = []

    def out_inputs(index, state):
        stream, hid_one, hid_two, hid_three, rstd = state["kept%d" % index]
        gain = state["gains"][BLOCKS + index : BLOCKS + index + 1]
        return [stream, hid_two, hid_three, rstd, block_weight(index, "w_out"), gain]

    def out_step(index, group, state):
        (dres, low, late), dealt = back_out(
            state.pop("grad"), *out_inputs(index, state), group, tuned, place
        )
        return (dealt, state | {"grad": dres, "low": low, "late%d" % index: late})

    def mid_step(index, group, state):
        stream, hid_one, hid_two, hid_three, rstd = state["kept%d" % index]
        gain = state["gains"][BLOCKS + index : BLOCKS + index + 1]
        more = [state.pop("pool")] if len(group) > 1 else []
        (low, early), dealt = back_mid(
            state["low"], hid_one, rstd, block_weight(index, "w_mid"), gain, shift, more,
            group, tuned, place,
        )
        return (dealt, state | {"low": low, "early%d" % index: early})

    def between_step(index, group, state):
        stream = state.pop("kept%d" % index)[0]
        (dres, low, late), dealt = back_between(
            state["low"], stream, state["grad"], block_weight(index, "w_in"),
            out_inputs(index - 1, state), group, tuned, place,
        )
        return (dealt, state | {"grad": dres, "low": low, "late%d" % (index - 1): late})

    def first_step(group, state):
        stream = state.pop("kept0")[0]
        dgains = [
            jnp.concatenate([state.pop("early%d" % index), state.pop("late%d" % index)], axis=1)
            for index in range(BLOCKS)
        ]
        dgains = jnp.concatenate(dgains).reshape(BLOCKS, devices, gain_width).transpose(1, 0, 2)
        dgains = jnp.pad(dgains, ((0, 0), (0, TILE - BLOCKS), (0, WIDTH - gain_width)))
        dgains = dgains.reshape(1, -1, WIDTH).astype(jnp.bfloat16)
        dealt = back_first(
            state.pop("low"), stream, state.pop("grad"), block_weight(0, "w_in"),
            state.pop("pixels"), spread, dgains, group, tuned, place,
        )
        return (dealt, state)

    def add_step(group, run, *names):
        keys.append(group)
        steps.append(
            lambda state: run(*names, [parts[key[0]] for key in group], dict(state))
        )

    loss_part, acts = (state.pop("loss"), state.pop("acts"))
    add_step([("w_out", BLOCKS - 1)], out_step, BLOCKS - 1)
    for index in reversed(range(BLOCKS)):
        more = [("pool",)] if index == BLOCKS - 1 else []
        add_step([("w_mid", index)] + more, mid_step, index)
        if index:
            add_step([("w_in", index), ("w_out", index - 1)], between_step, index)
    add_step([("w_in", 0), ("patch",), ("gains",)], first_step)
    def read_heads(buffers, rows):
        return own_heads(buffers, parts["heads"], parts["proj"], tuned, place)

    def read_late(pair, rows):
        pool = parts["pool"]
        first = parts["w_mid"].travel
        return flat_late(pool.unpack(rows[1][first : first + pool.travel]), pair[1], pair[0])[None]

    groups = [[parts[key[0]] for key in group] for group in keys]
    if tuned:
        shared = (Part(1, ACTS, WIDTH), acts[None], [read_heads, read_late])
        mine, late, state = pipelined_scatter(len(groups), place, state, steps, shared)
    else:
        mine = []
        for group, step in zip(groups, steps):
            arrays, state = step(state)
            mine.append(pack(group, [plain_scatter(array) for array in arrays]))
        late = read_late(read_heads([plain_gather(acts[None])], mine), mine)
    at = {}
    moves = []
    for number, group in enumerate(keys):
        first = 0
        steps = []
        for key in group:
            count = parts[key[0]].travel
            at[key] = (number, first)
            if len(key) > 1:
                start = block_cuts[block_names.index(key[0])][0]
                steps.append((key[1], block_rows(key[0], start, count, first)))
            elif key[0] == "patch":
                steps.append((None, patch_rows(count, first)))
            first += count
        moves.append(steps)
    cuts = (top_cuts, block_cuts)
    tops = [array[None] for array in (params_top, first_top, second_top, average_top)]
    sums, *made = directions(
        cuts, mine, moves, at["gains",], late, loss_part,
        tops[:3], [params_blocks, first_blocks, second_blocks],
    )
    momentum_top, variance_top, direction_top, momentum_blocks, variance_blocks, direction_blocks = made
    sums = total(sums)
    norms, *made = update(
        cuts, sums, [tops[0], direction_top, tops[3]],
        [params_blocks, direction_blocks, average_blocks],
    )
    updated_top, averaged_top, updated_blocks, averaged_blocks, half_blocks = made
    loss_total = sums[2, 0]
    matrix_norms = norms[:2, : len(top_cuts) + BLOCKS * len(block_cuts)]
    number, first = at["gains",]
    gain_grads = mine[number][first : first + BLOCKS, :gain_width]
    return (
        loss_total,
        matrix_norms,
        updated_top[0],
        updated_top[0].astype(jnp.bfloat16),
        momentum_top[0],
        variance_top[0],
        averaged_top[0],
        updated_blocks,
        half_blocks,
        momentum_blocks,
        variance_blocks,
        averaged_blocks,
        gain_grads,
    )


def solution(mesh):
    one = P(AXES)
    flat = P(None, AXES)
    return jax.shard_map(
        on_device,
        mesh=mesh,
        in_specs=(P(AXES, None, None),) * 2
        + (one, P(AXES, None), P(AXES, None))
        + (one,) * 3
        + (one, flat) * 5,
        out_specs=(P(), P()) + (one,) * 5 + (flat,) * 6,
        check_vma=False,
    )
```

```python
import functools
import itertools

import jax
import jax.numpy as jnp
from jax import lax
from jax.experimental import pallas as pl
from jax.experimental.pallas import tpu as pltpu
from jax.sharding import PartitionSpec as P

D = 2048
BOT = 512
GROUPS = 32
SIDE = 11
PIX = 121
TAPS = 9

ROWS = 128
LANES = 512
VMEM_LIMIT = 44 * 1024 * 1024
LIGHT = pl.CostEstimate(flops=1024, bytes_accessed=1024, transcendentals=0)


def shifts():
    pixel = jnp.arange(ROWS)
    row, col = (pixel // SIDE, pixel % SIDE)
    mats = []
    for tap in range(TAPS):
        at_row, at_col = (row + tap // 3 - 1, col + tap % 3 - 1)
        inside = (at_row >= 0) & (at_row < SIDE) & (at_col >= 0) & (at_col < SIDE) & (pixel < PIX)
        mats.append((inside[:, None] & (pixel[None, :] == (at_row * SIDE + at_col)[:, None])))
    return jnp.concatenate(mats, axis=0).astype(jnp.bfloat16)


def dot(left, right):
    return jnp.dot(left, right, preferred_element_type=jnp.float32)


def dot_rows(left, right):
    return lax.dot_general(
        left, right, (((0,), (0,)), ((), ())), preferred_element_type=jnp.float32
    )


def dot_lanes(left, right):
    return lax.dot_general(
        left, right, (((1,), (1,)), ((), ())), preferred_element_type=jnp.float32
    )


def each_chunk(count, chans, body, unroll=1):
    per = chans // LANES

    def step(index, carry):
        frame = index // per
        rows = pl.ds(pl.multiple_of(frame * ROWS, ROWS), ROWS)
        lanes = pl.ds(pl.multiple_of((index % per) * LANES, LANES), LANES)
        body(pl.ds(frame, 1), rows, lanes)
        return carry

    lax.fori_loop(0, count * per, step, 0, unroll=unroll)


def real_rows():
    return lax.broadcasted_iota(jnp.int32, (ROWS, LANES), 0) < PIX


def group_mean(sums):
    chans = sums.shape[1]
    width = chans // GROUPS
    lane = lax.broadcasted_iota(jnp.int32, sums.shape, 1)
    step = 1
    while step < width:
        ahead = pltpu.roll(sums, chans - step, 1)
        behind = pltpu.roll(sums, step, 1)
        sums = sums + jnp.where((lane & step) == 0, ahead, behind)
        step *= 2
    return sums * (1.0 / (PIX * width))


def silu(value):
    return value / (1.0 + jnp.exp(-value))


def silu_slope(value):
    gate = 1.0 / (1.0 + jnp.exp(-value))
    return gate * (1.0 + value * (1.0 - gate))


def normalise(count, chans, hid, sums, rstd, rstd_at):
    whole = pl.ds(0, chans)
    sums[:, whole] = jnp.zeros((sums.shape[0], chans), jnp.float32)

    def add(frame, rows, lanes):
        sums[frame, lanes] = jnp.sum(hid[rows, lanes], axis=0, keepdims=True)

    each_chunk(count, chans, add, unroll=2)
    sums[:, whole] = group_mean(sums[:, whole])

    def center(frame, rows, lanes):
        value = jnp.where(real_rows(), hid[rows, lanes] - sums[frame, lanes], 0.0)
        hid[rows, lanes] = value
        sums[frame, lanes] = jnp.sum(value * value, axis=0, keepdims=True)

    each_chunk(count, chans, center, unroll=2)
    at = pl.ds(rstd_at, chans)
    rstd[:, at] = lax.rsqrt(group_mean(sums[:, whole]) + 1e-05)


def forward_kernel(count, keep, parts, skip, tuned, row, *refs):
    refs = list(refs)
    number = len(parts) - skip
    first = number > 3

    def take(number):
        taken = refs[:number]
        del refs[:number]
        return taken

    (place,) = take(1)
    x = take(2 if first else 1)
    gains, shift = take(2)
    gains = gains.at[pl.ds(row, 1)]
    sources = take(4 if tuned else len(parts))
    (out,) = take(1)
    if keep:
        if first:
            (start,) = take(1)
        hid_one, hid_two, hid_three, rstd = take(4)
        kept_weights = take(3)
    weights = take(number)
    sems, back_sems, low, act, cols, sums = take(6)
    if not keep:
        hid_one, hid_two, hid_three, rstd = take(4)
        if first:
            (start,) = take(1)
    fetch(parts, tuned, place, sources, dict(enumerate(weights, skip)), sems)

    def arrived(index):
        weight = weights[index]
        pltpu.make_async_copy(weight, weight, sems.at[len(parts) + index]).wait()
        if keep and index >= -3:
            pltpu.make_async_copy(weight, kept_weights[index], back_sems.at[3 + index]).start()
        return weight

    def whole(value):
        return value.reshape(-1, value.shape[-1])

    if first:
        pixels, spread = x
        x = start
        patch = arrived(-4)
        for half in range(2):
            wide = dot(pixels[...], spread[half]).astype(jnp.bfloat16)
            for block in range(2):
                lanes = pl.ds((2 * half + block) * WIDTH, WIDTH)
                x[:, lanes] = dot(wide, whole(patch[block]))
    else:
        (x,) = x

    def cast(frame, rows, lanes):
        low[rows, lanes] = x[rows, lanes].astype(jnp.bfloat16)

    def activate(hid, at, offset):
        def body(frame, rows, lanes):
            gain = gains[:, pl.ds(offset + lanes.start, LANES)]
            bias = gains[:, pl.ds(offset + BOT + lanes.start, LANES)]
            value = hid[rows, lanes] * rstd[frame, pl.ds(at + lanes.start, LANES)]
            hid[rows, lanes] = value
            value = jnp.where(real_rows(), silu(value * gain + bias), 0.0)
            act[rows, lanes] = value.astype(jnp.bfloat16)

        return body

    each_chunk(count, D, cast)
    hid_one[...] = dot(low[...], whole(arrived(-3)[...]))
    normalise(count, BOT, hid_one, sums, rstd, 0)
    each_chunk(count, BOT, activate(hid_one, 0, 0))
    for frame in range(count):
        rows = pl.ds(frame * ROWS, ROWS)
        for tap in range(TAPS):
            picked = dot(shift[pl.ds(tap * ROWS, ROWS), :], act[rows, :])
            cols[rows, pl.ds(tap * BOT, BOT)] = picked.astype(jnp.bfloat16)
    hid_two[...] = dot(cols[...], whole(arrived(-2)[...]))
    normalise(count, BOT, hid_two, sums, rstd, BOT)
    each_chunk(count, BOT, activate(hid_two, BOT, 2 * BOT))
    w_out = arrived(-1)
    for part in range(D // BOT):
        hid_three[:, pl.ds(part * BOT, BOT)] = dot(act[...], whole(w_out[part]))
    normalise(count, D, hid_three, sums, rstd, 2 * BOT)

    def finish(frame, rows, lanes):
        gain = gains[:, pl.ds(4 * BOT + lanes.start, LANES)]
        bias = gains[:, pl.ds(4 * BOT + D + lanes.start, LANES)]
        value = hid_three[rows, lanes] * rstd[frame, pl.ds(2 * BOT + lanes.start, LANES)]
        if keep:
            hid_three[rows, lanes] = value
        value = silu(x[rows, lanes] + value * gain + bias)
        out[rows, lanes] = jnp.where(real_rows(), value, 0.0)

    each_chunk(count, D, finish)
    if keep:
        for index in (-3, -2, -1):
            pltpu.make_async_copy(weights[index], kept_weights[index], back_sems.at[3 + index]).wait()


def f32(*shape):
    return jax.ShapeDtypeStruct(shape, jnp.float32)


def bf16(*shape):
    return jax.ShapeDtypeStruct(shape, jnp.bfloat16)


def stat_rows(count):
    return -(-count // 8) * 8


def block_forward(stream, gains, shift, parts, skip, buffers, place, keep, tuned):
    first = len(parts) - skip > 3
    rows = stream[0].shape[0]
    count = rows // ROWS
    stats = stat_rows(count)
    kept = [
        ((rows, BOT), jnp.float32),
        ((rows, BOT), jnp.float32),
        ((rows, D), jnp.float32),
        ((stats, 2 * BOT + D), jnp.float32),
    ]
    start = [((rows, D), jnp.float32)] if first else []
    weights = weight_shapes(parts, buffers, tuned)[skip:]
    out_shape = [f32(rows, D)]
    out_specs = in_vmem(1)
    scratch = [pltpu.VMEM(shape, jnp.bfloat16) for shape in weights]
    scratch += [
        pltpu.SemaphoreType.DMA((len(parts),)),
        pltpu.SemaphoreType.DMA((3,)),
        pltpu.VMEM((rows, D), jnp.bfloat16),
        pltpu.VMEM((rows, BOT), jnp.bfloat16),
        pltpu.VMEM((rows, TAPS * BOT), jnp.bfloat16),
        pltpu.VMEM((stats, D), jnp.float32),
    ]
    if keep:
        out_shape += [jax.ShapeDtypeStruct(*item) for item in start + kept]
        out_shape += [jax.ShapeDtypeStruct(shape, jnp.bfloat16) for shape in weights[-3:]]
        out_specs += in_vmem(len(start + kept)) + hbm(3)
    else:
        scratch += [pltpu.VMEM(*item) for item in kept + start]
    return pl.pallas_call(
        functools.partial(forward_kernel, count, keep, parts, skip, tuned, gains[1]),
        out_shape=out_shape,
        in_specs=in_smem() + in_vmem(len(stream) + 2) + hbm(len(buffers)),
        out_specs=out_specs,
        scratch_shapes=scratch,
        compiler_params=pltpu.CompilerParams(vmem_limit_bytes=VMEM_LIMIT),
        cost_estimate=LIGHT,
        name="block_forward",
    )(place, *stream, gains[0], shift, *buffers)


def norm_back(count, chans, slope, hid, sums, more, rstd, rstd_at, gain, grad_gain, grad_bias, store):
    whole = pl.ds(0, chans)
    sums[:, whole] = jnp.zeros((sums.shape[0], chans), jnp.float32)
    more[:, whole] = jnp.zeros((sums.shape[0], chans), jnp.float32)

    def add(frame, rows, lanes):
        value = slope(frame, rows, lanes)
        sums[frame, lanes] = jnp.sum(value, axis=0, keepdims=True)
        more[frame, lanes] = jnp.sum(value * hid[rows, lanes], axis=0, keepdims=True)

    each_chunk(count, chans, add)
    grad_bias[...] = jnp.sum(sums[:, whole], axis=0, keepdims=True)
    grad_gain[...] = jnp.sum(more[:, whole], axis=0, keepdims=True)
    sums[:, whole] = group_mean(sums[:, whole] * gain[...])
    more[:, whole] = group_mean(more[:, whole] * gain[...])

    def spread(frame, rows, lanes):
        store(
            rows,
            lanes,
            lambda value: jnp.where(
                real_rows(),
                rstd[frame, pl.ds(rstd_at + lanes.start, LANES)]
                * (value * gain[:, lanes] - sums[frame, lanes] - hid[rows, lanes] * more[frame, lanes]),
                0.0,
            ).astype(jnp.bfloat16),
        )

    each_chunk(count, chans, spread)


def back_out_body(count, grad, x, hid_two, hid_three, rstd, w_out, gains, dres, dlow, dgains, scratch, dw_out):
    third, act, dact, sums, more = scratch
    gain_three, bias_three = (gains.at[:, pl.ds(4 * BOT, D)], gains.at[:, pl.ds(4 * BOT + D, D)])

    def slope_three(frame, rows, lanes):
        value = x[rows, lanes] + hid_three[rows, lanes] * gain_three[:, lanes] + bias_three[:, lanes]
        value = jnp.where(real_rows(), grad[rows, lanes] * silu_slope(value), 0.0)
        dres[rows, lanes] = value
        return value

    def store_three(rows, lanes, back):
        third[rows, lanes] = back(dres[rows, lanes])

    norm_back(
        count, D, slope_three, hid_three, sums, more, rstd, 2 * BOT, gain_three,
        dgains.at[:, pl.ds(2 * BOT, D)], dgains.at[:, pl.ds(2 * BOT + D, D)], store_three,
    )
    total = None
    for part in range(D // BOT):
        lanes = pl.ds(part * BOT, BOT)
        term = dot_lanes(third[:, lanes], w_out[lanes, :])
        total = term if total is None else total + term
    dact[...] = total
    gain_two, bias_two = (gains.at[:, pl.ds(2 * BOT, BOT)], gains.at[:, pl.ds(3 * BOT, BOT)])

    def slope_two(frame, rows, lanes):
        value = hid_two[rows, lanes] * gain_two[:, lanes] + bias_two[:, lanes]
        gate = 1.0 / (1.0 + jnp.exp(-value))
        act[rows, lanes] = jnp.where(real_rows(), value * gate, 0.0).astype(jnp.bfloat16)
        value = dact[rows, lanes] * (gate * (1.0 + value * (1.0 - gate)))
        value = jnp.where(real_rows(), value, 0.0)
        dact[rows, lanes] = value
        return value

    def store_two(rows, lanes, back):
        dlow[rows, lanes] = back(dact[rows, lanes])

    norm_back(
        count, BOT, slope_two, hid_two, sums, more, rstd, BOT, gain_two,
        dgains.at[:, pl.ds(0, BOT)], dgains.at[:, pl.ds(BOT, BOT)], store_two,
    )
    for part in range(D // BOT):
        lanes = pl.ds(part * BOT, BOT)
        dw_out[part] = dot_rows(act[...], third[:, lanes]).astype(jnp.bfloat16)


def out_scratch(rows):
    stats = stat_rows(rows // ROWS)
    return [
        pltpu.VMEM((rows, D), jnp.bfloat16),
        pltpu.VMEM((rows, BOT), jnp.bfloat16),
        pltpu.VMEM((rows, BOT), jnp.float32),
        pltpu.VMEM((stats, D), jnp.float32),
        pltpu.VMEM((stats, D), jnp.float32),
    ]


def back_mid_body(count, grad, hid_one, rstd, w_mid, gains, shift, dlow, dgains, scratch, dw_mid):
    act, cols, dact, sums, more = scratch
    gain_one, bias_one = (gains.at[:, pl.ds(0, BOT)], gains.at[:, pl.ds(BOT, BOT)])
    for frame in range(count):
        rows = pl.ds(frame * ROWS, ROWS)
        for tap in range(TAPS):
            picked = dot(shift[pl.ds((TAPS - 1 - tap) * ROWS, ROWS), :], grad[rows, :])
            cols[rows, pl.ds(tap * BOT, BOT)] = picked.astype(jnp.bfloat16)
    total = None
    for tap in range(TAPS):
        lanes = pl.ds(tap * BOT, BOT)
        term = dot_lanes(cols[:, lanes], w_mid[lanes, :])
        total = term if total is None else total + term
    dact[...] = total

    def slope_one(frame, rows, lanes):
        value = hid_one[rows, lanes] * gain_one[:, lanes] + bias_one[:, lanes]
        gate = 1.0 / (1.0 + jnp.exp(-value))
        act[rows, lanes] = jnp.where(real_rows(), value * gate, 0.0).astype(jnp.bfloat16)
        value = dact[rows, lanes] * (gate * (1.0 + value * (1.0 - gate)))
        value = jnp.where(real_rows(), value, 0.0)
        dact[rows, lanes] = value
        return value

    def store_one(rows, lanes, back):
        dlow[rows, lanes] = back(dact[rows, lanes])

    norm_back(
        count, BOT, slope_one, hid_one, sums, more, rstd, 0, gain_one,
        dgains.at[:, pl.ds(0, BOT)], dgains.at[:, pl.ds(BOT, BOT)], store_one,
    )
    for tap in range(TAPS):
        lanes = pl.ds(tap * BOT, BOT)
        dw_mid[0, lanes, :] = dot_rows(act[...], cols[:, lanes]).astype(jnp.bfloat16)


def back_in_body(count, grad, x, dres, w_in, dx, low, dw_in):
    def cast(frame, rows, lanes):
        low[rows, lanes] = x[rows, lanes].astype(jnp.bfloat16)

    each_chunk(count, D, cast)
    for part in range(D // BOT):
        lanes = pl.ds(part * BOT, BOT)
        dx[:, lanes] = dres[:, lanes] + dot_lanes(grad[...], w_in[lanes, :])
        dw_in[0, lanes, :] = dot_rows(low[:, lanes], grad[...]).astype(jnp.bfloat16)


def back_kernel(body, parts, tuned, counts, *refs):
    place, refs = (refs[0], list(refs[1:]))
    groups = []
    for number in (*counts[:2], len(dealt_shapes(parts, tuned)), len(parts), 1, counts[2]):
        groups.append(refs[:number])
        refs = refs[number:]
    ins, outs, dealt, made, sems, scratch = groups

    def done(index):
        start_deal(parts, tuned, place, index, made, dealt, sems[0])

    body(ins, outs, made, scratch, done)
    for index, array in enumerate(made):
        pltpu.make_async_copy(array, array, sems[0].at[index]).wait()


def back_call(name, body, ins, out_shape, scratch, parts, tuned, place):
    dealt = dealt_shapes(parts, tuned)
    counts = (len(ins), len(out_shape), len(scratch))
    outs = pl.pallas_call(
        functools.partial(back_kernel, body, parts, tuned, counts),
        out_shape=out_shape + [bf16(*shape) for shape in dealt],
        in_specs=in_smem() + in_vmem(len(ins)),
        out_specs=in_vmem(len(out_shape)) + hbm(len(dealt)),
        scratch_shapes=[pltpu.VMEM(whole_shape(part), jnp.bfloat16) for part in parts]
        + [pltpu.SemaphoreType.DMA((len(parts),))]
        + scratch,
        compiler_params=pltpu.CompilerParams(vmem_limit_bytes=VMEM_LIMIT),
        cost_estimate=LIGHT,
        name=name,
    )(place, *ins)
    return (list(outs[: len(out_shape)]), list(outs[len(out_shape) :]))


def back_out(grad, stream, hid_two, hid_three, rstd, w_out, gains, parts, tuned, place):
    rows = stream.shape[0]

    def body(ins, outs, made, scratch, done):
        gain = ins[6].at[pl.ds(gains[1], 1)]
        back_out_body(rows // ROWS, *ins[:6], gain, *outs, scratch, made[0])
        done(0)

    ins = [grad, stream, hid_two, hid_three, rstd, w_out, gains[0]]
    out_shape = [f32(rows, D), bf16(rows, BOT), f32(1, 2 * BOT + 2 * D)]
    return back_call("back_out", body, ins, out_shape, out_scratch(rows), parts, tuned, place)


def back_mid(grad, hid_one, rstd, w_mid, gains, shift, more, parts, tuned, place):
    rows = grad.shape[0]
    stats = stat_rows(rows // ROWS)

    def body(ins, outs, made, scratch, done):
        for index in range(1, len(made)):
            made[index][...] = ins[5 + index][...]
            done(index)
        gain = ins[4].at[pl.ds(gains[1], 1)]
        back_mid_body(rows // ROWS, *ins[:4], gain, ins[5], *outs, scratch, made[0])
        done(0)

    scratch = [
        pltpu.VMEM((rows, BOT), jnp.bfloat16),
        pltpu.VMEM((rows, TAPS * BOT), jnp.bfloat16),
        pltpu.VMEM((rows, BOT), jnp.float32),
        pltpu.VMEM((stats, BOT), jnp.float32),
        pltpu.VMEM((stats, BOT), jnp.float32),
    ]
    ins = [grad, hid_one, rstd, w_mid, gains[0], shift, *more]
    out_shape = [bf16(rows, BOT), f32(1, 2 * BOT)]
    return back_call("back_mid", body, ins, out_shape, scratch, parts, tuned, place)


def back_between(grad, stream, dres, w_in, later, parts, tuned, place):
    rows = stream.shape[0]
    *later, gains = later

    def body(ins, outs, made, scratch, done):
        dx, low, *rest = scratch
        back_in_body(rows // ROWS, *ins[:4], dx, low, made[0])
        done(0)
        gain = ins[-1].at[pl.ds(gains[1], 1)]
        back_out_body(rows // ROWS, dx, *ins[4:-1], gain, *outs, rest, made[1])
        done(1)

    scratch = [pltpu.VMEM((rows, D), jnp.float32), pltpu.VMEM((rows, D), jnp.bfloat16)]
    scratch += out_scratch(rows)
    ins = [grad, stream, dres, w_in, *later, gains[0]]
    out_shape = [f32(rows, D), bf16(rows, BOT), f32(1, 2 * BOT + 2 * D)]
    return back_call("back_between", body, ins, out_shape, scratch, parts, tuned, place)


def back_first(grad, stream, dres, w_in, pixels, spread, dgains, parts, tuned, place):
    rows = stream.shape[0]

    def body(ins, outs, made, scratch, done):
        dx, low = scratch
        made[2][...] = ins[6][...]
        done(2)
        back_in_body(rows // ROWS, *ins[:4], dx, low, made[0])
        done(0)
        wide = [dot(ins[4][...], ins[5][half]).astype(jnp.bfloat16) for half in range(2)]
        for block in range(2):
            total = None
            for half in range(2):
                lanes = pl.ds((2 * half + block) * WIDTH, WIDTH)
                term = dot_rows(wide[half], dx[:, lanes].astype(jnp.bfloat16))
                total = term if total is None else total + term
            made[1][block] = total.astype(jnp.bfloat16)
        done(1)

    scratch = [pltpu.VMEM((rows, D), jnp.float32), pltpu.VMEM((rows, D), jnp.bfloat16)]
    ins = [grad, stream, dres, w_in, pixels, spread, dgains]
    return back_call("back_first", body, ins, [], scratch, parts, tuned, place)[1]


def spread_pixels(devices):
    rows = PATCH_IN // devices
    value = jnp.arange(PATCH_IN)
    at = value // rows * 2 * rows + value % rows
    return jnp.stack(
        [jnp.arange(2 * PATCH_IN)[None, :] == (at + half * rows)[:, None] for half in range(2)]
    ).astype(jnp.bfloat16)


def merge(value):
    return value.reshape(-1, value.shape[-1])


def fetch_ends(parts, tuned, place, sources, weights, sems):
    first = len(parts) - 2
    fetch(parts, tuned, place, sources, dict(enumerate(weights, first)), sems)

    def arrived(index):
        weight = weights[index]
        pltpu.make_async_copy(weight, weight, sems.at[first + index]).wait()
        return weight

    return arrived


def head_forward(count, stream, pool, arrived, games, pool_t, pooled):
    for part in range(D // ROWS):
        lanes = pl.ds(part * ROWS, ROWS)
        pool_t[:, lanes] = pool[lanes, :].astype(jnp.float32).T
    pooled[...] = jnp.zeros_like(pooled)

    def weigh(frame, rows, lanes):
        value = stream[rows, lanes].astype(jnp.bfloat16).astype(jnp.float32)
        pooled[frame, lanes] = jnp.sum(value * pool_t[:, lanes], axis=0, keepdims=True)

    each_chunk(count, D, weigh)
    before = dot(pooled[...].astype(jnp.bfloat16), merge(arrived(0)[...]))
    hidden = silu(before).astype(jnp.bfloat16)
    heads = arrived(1)
    scores = None
    for game in range(GAMES):
        pair = [dot(hidden, merge(heads[2 * game + half])) for half in range(2)]
        term = jnp.where(games == game, jnp.concatenate(pair, axis=1), 0.0)
        scores = term if scores is None else scores + term
    return ([pick_atoms(scores, action) for action in range(ACTIONS)], before, hidden)


def atom_lanes():
    return lax.broadcasted_iota(jnp.int32, (8, ROWS), 1)


def pick_atoms(scores, action):
    offset = action * ATOMS
    moved = pltpu.roll(scores, 2 * WIDTH - offset, 1) if offset else scores
    return jnp.where(atom_lanes() < ATOMS, moved[:, :ROWS], -1e30)


def support_lanes():
    return -10.0 + 20.0 / (ATOMS - 1) * atom_lanes().astype(jnp.float32)


def lane_sum(value):
    return jnp.sum(value, axis=1, keepdims=True)


def target_kernel(count, parts, tuned, place, stream, pool, whole, real, *refs):
    sources, (out, *weights, sems, pool_t, pooled) = (refs[:-6], refs[-6:])
    arrived = fetch_ends(parts, tuned, place, sources, weights, sems)
    logits, _, _ = head_forward(count, stream, pool, arrived, whole[:, 0:1], pool_t, pooled)
    chosen = None
    for action in range(ACTIONS):
        term = jnp.where(whole[:, 2:3] == action, logits[action], 0.0)
        chosen = term if chosen is None else chosen + term
    power = jnp.exp(chosen - jnp.max(chosen, axis=1, keepdims=True))
    probs = power / lane_sum(power)
    atoms = support_lanes()
    spacing = 20.0 / (ATOMS - 1)
    moved = jnp.clip(real[:, 0:1] + real[:, 1:2] * atoms, -10.0, 10.0)
    total = jnp.zeros_like(probs)
    for atom in range(ATOMS):
        near = 1.0 - jnp.abs(moved[:, atom : atom + 1] - atoms) / spacing
        total = total + probs[:, atom : atom + 1] * jnp.clip(near, 0.0, 1.0)
    inside = (atom_lanes() < ATOMS) & (lax.broadcasted_iota(jnp.int32, total.shape, 0) < count)
    out[...] = jnp.where(inside, total, 0.0)


def ends_scratch(parts, buffers, tuned):
    scratch = [pltpu.VMEM(shape, jnp.bfloat16) for shape in weight_shapes(parts, buffers, tuned)[-2:]]
    scratch += [pltpu.SemaphoreType.DMA((len(parts),))]
    return scratch + [pltpu.VMEM((ROWS, D), jnp.float32), pltpu.VMEM((8, D), jnp.float32)]


def head_target(stream, pool, whole, real, parts, buffers, tuned, place):
    count = stream.shape[0] // ROWS
    return pl.pallas_call(
        functools.partial(target_kernel, count, parts, tuned),
        out_shape=f32(8, ROWS),
        in_specs=in_smem() + in_vmem(4) + hbm(len(buffers)),
        out_specs=in_vmem(1)[0],
        scratch_shapes=ends_scratch(parts, buffers, tuned),
        compiler_params=pltpu.CompilerParams(vmem_limit_bytes=VMEM_LIMIT),
        cost_estimate=LIGHT,
        name="head_target",
    )(place, stream, pool, whole, real, *buffers)


def loss_kernel(count, frames_all, parts, tuned, place, stream, pool, target, whole, legal, *refs):
    sources, refs = (refs[:-10], refs[-10:])
    loss, dstream, dpool, acts, *weights, sems, pool_t, pooled, dpooled = refs
    arrived = fetch_ends(parts, tuned, place, sources, weights, sems)
    proj, heads = weights
    games, taken = (whole[:, 0:1], whole[:, 1:2])
    logits, before, hidden = head_forward(count, stream, pool, arrived, games, pool_t, pooled)
    atoms = support_lanes()
    inside = atom_lanes() < ATOMS
    logps, probs, values = ([], [], [])
    for value in logits:
        value = value - jnp.max(value, axis=1, keepdims=True)
        power = jnp.where(inside, jnp.exp(value), 0.0)
        mass = lane_sum(power)
        logps.append(value - jnp.log(mass))
        probs.append(power / mass)
        values.append(lane_sum(probs[-1] * atoms))
    masked = [
        jnp.where(legal[:, action : action + 1] > 0, values[action], -1e30)
        for action in range(ACTIONS)
    ]
    largest = functools.reduce(jnp.maximum, masked)
    powers = [jnp.exp(value - largest) for value in masked]
    mass = sum(powers[1:], powers[0])
    goal = target[...]
    goal_mass = lane_sum(goal)
    cross = taken_value = 0.0
    real = lax.broadcasted_iota(jnp.int32, (8, 1), 0) < count
    scale = jnp.where(real, 1.0 / frames_all, 0.0)
    spread = jnp.zeros((8, 2 * WIDTH), jnp.float32)
    for action in range(ACTIONS):
        here = jnp.where(taken == action, 1.0, 0.0)
        cross = cross - here * lane_sum(jnp.where(inside, goal * logps[action], 0.0))
        taken_value = taken_value + here * values[action]
        grad = here * (probs[action] * goal_mass - goal)
        pull = CQL_WEIGHT * (powers[action] / mass - here)
        grad = grad + pull * probs[action] * (atoms - values[action])
        grad = jnp.where(inside, grad * scale, 0.0)
        grad = jnp.concatenate([grad, jnp.zeros((8, 2 * WIDTH - ROWS), jnp.float32)], axis=1)
        offset = action * ATOMS
        spread = spread + (pltpu.roll(grad, offset, 1) if offset else grad)
    losses = cross + CQL_WEIGHT * (jnp.log(mass) + largest - taken_value)
    loss[...] = jnp.sum(jnp.where(real, losses, 0.0), axis=0, keepdims=True)
    dhidden = None
    spread = spread.astype(jnp.bfloat16)
    for game in range(GAMES):
        mine = jnp.where(games == game, spread, 0.0).astype(jnp.bfloat16)
        for half in range(2):
            part = mine[:, half * WIDTH : (half + 1) * WIDTH]
            term = dot_lanes(part, merge(heads[2 * game + half]))
            dhidden = term if dhidden is None else dhidden + term
    dbefore = (silu_slope(before) * dhidden).astype(jnp.bfloat16)
    pieces = [hidden, dbefore]
    pieces += [pooled[:, part * WIDTH : (part + 1) * WIDTH] for part in range(D // WIDTH)]
    lanes = lax.broadcasted_iota(jnp.int32, (8, WIDTH), 1)
    marked = jnp.where(lanes == WIDTH - 1, games.astype(jnp.float32), spread[:, WIDTH:].astype(jnp.float32))
    pieces += [spread[:, :WIDTH], marked]
    acts[...] = jnp.concatenate([piece.astype(jnp.float32) for piece in pieces]).astype(jnp.bfloat16)
    dpooled[...] = dot_lanes(dbefore, merge(proj[...])).astype(jnp.bfloat16).astype(jnp.float32)

    def push(frame, rows, lanes):
        dstream[rows, lanes] = dpooled[frame, lanes] * pool_t[:, lanes]

    each_chunk(count, D, push)

    def gather_pool(part, carry):
        lanes = pl.ds(pl.multiple_of(part * ROWS, ROWS), ROWS)
        total = None
        for frame in range(count):
            value = stream[pl.ds(frame * ROWS, ROWS), lanes].astype(jnp.bfloat16)
            term = value.astype(jnp.float32) * dpooled[pl.ds(frame, 1), lanes]
            total = term if total is None else total + term
        dpool[0, lanes, :] = total.T.astype(jnp.bfloat16)
        return carry

    lax.fori_loop(0, D // ROWS, gather_pool, 0)


def head_loss(stream, pool, target, whole, legal, frames_all, parts, buffers, tuned, place):
    rows = stream.shape[0]
    return pl.pallas_call(
        functools.partial(loss_kernel, rows // ROWS, frames_all, parts, tuned),
        out_shape=[f32(1, 1), f32(rows, D), bf16(1, D, ROWS), bf16(ACTS, WIDTH)],
        in_specs=in_smem() + in_vmem(5) + hbm(len(buffers)),
        out_specs=in_vmem(4),
        scratch_shapes=ends_scratch(parts, buffers, tuned) + [pltpu.VMEM((8, D), jnp.float32)],
        compiler_params=pltpu.CompilerParams(vmem_limit_bytes=VMEM_LIMIT),
        cost_estimate=LIGHT,
        name="head_loss",
    )(place, stream, pool, target, whole, legal, *buffers)


ACTS = 64


def own_heads_kernel(parts, tuned, place, *refs):
    sources, (heads, proj, acts, sems) = (refs[:-4], refs[-4:])
    fetch(parts, tuned, place, sources, {0: acts}, sems)
    pltpu.make_async_copy(acts, acts, sems.at[0]).wait()
    value = acts[...].reshape(-1, ACTS, WIDTH).astype(jnp.float32)
    pieces = [value[:, first : first + 8].reshape(-1, WIDTH) for first in range(0, ACTS, 8)]
    pieces = [piece.astype(jnp.bfloat16) for piece in pieces]
    hidden, dbefore, scores = (pieces[0], pieces[1], pieces[-2:])
    games = scores[1][:, WIDTH - 1 :].astype(jnp.float32)
    lanes = lax.broadcasted_iota(jnp.int32, scores[1].shape, 1)
    scores[1] = jnp.where(lanes < WIDTH - 1, scores[1].astype(jnp.float32), 0.0).astype(jnp.bfloat16)
    row = lax.broadcasted_iota(jnp.int32, (WIDTH, ROWS), 0)
    lane = lax.broadcasted_iota(jnp.int32, (WIDTH, ROWS), 1)

    def own(items, count):
        total = None
        for block, item in enumerate(items):
            wanted = (row + block * WIDTH == place[4] * count + lane) & (lane < count)
            term = dot(item, jnp.where(wanted, 1.0, 0.0).astype(jnp.bfloat16))
            total = term if total is None else total + term
        return total.astype(jnp.bfloat16)

    count = heads.shape[1]
    mine = own([hidden], count)
    for game in range(GAMES):
        for half in range(2):
            chosen = jnp.where(games == game, scores[half].astype(jnp.float32), 0.0)
            heads[2 * game + half] = dot_rows(mine, chosen.astype(jnp.bfloat16))[:count]
    count = proj.shape[1]
    proj[0] = dot_rows(own(pieces[2:-2], count), dbefore)[:count]


def own_heads(buffers, heads, proj, tuned, place):
    parts = [Part(1, ACTS, WIDTH)]
    return pl.pallas_call(
        functools.partial(own_heads_kernel, parts, tuned),
        out_shape=[f32(part.blocks, part.rows, part.lanes) for part in (heads, proj)],
        in_specs=in_smem() + hbm(len(buffers)),
        out_specs=in_vmem(2),
        scratch_shapes=[
            pltpu.VMEM(weight_shapes(parts, buffers, tuned)[0], jnp.bfloat16),
            pltpu.SemaphoreType.DMA((1,)),
        ],
        compiler_params=pltpu.CompilerParams(vmem_limit_bytes=VMEM_LIMIT),
        cost_estimate=LIGHT,
        name="own_heads",
    )(place, *buffers)


WIDTH = 512
TILE = 16
AXES = ("wide", "narrow")


def grid_sizes():
    return (lax.axis_size("wide") // 2, 2, lax.axis_size("narrow") // 2, 2)


def spot():
    sizes = grid_sizes()
    wide, narrow = (lax.axis_index("wide"), lax.axis_index("narrow"))
    place = [wide // sizes[1], wide % sizes[1], narrow // sizes[3], narrow % sizes[3]]
    return jnp.stack(place + [wide * lax.axis_size("narrow") + narrow]).astype(jnp.int32)


def hop(array, axis_of_core, step=1, swap=0):
    sizes = grid_sizes()

    def target(place):
        axis = axis_of_core[place[3]]
        other = list(place)
        other[axis] = place[axis] ^ swap if swap else (place[axis] + step) % sizes[axis]
        return other

    return send(array, target)


def flip(array, *bits):
    return send(array, lambda place: [value ^ bit for value, bit in zip(place, bits)])


def send(array, target):
    sizes = grid_sizes()
    pairs = []
    for place in itertools.product(*[range(size) for size in sizes]):
        pairs.append(
            tuple(
                ((z * sizes[1] + y) * sizes[2] + x) * sizes[3] + core
                for z, y, x, core in (place, target(place))
            )
        )
    return lax.ppermute(array, AXES, pairs)


ALONG_Z = (0, 0)
ACROSS = (3, 3)
NEAR = (2, 1)
FAR = (1, 2)


def hbm(number):
    return [pl.BlockSpec(memory_space=pl.ANY)] * number


def in_vmem(number):
    return [pl.BlockSpec(memory_space=pltpu.VMEM)] * number


def in_smem():
    return [pl.BlockSpec(memory_space=pltpu.SMEM)]


def copies(pairs, sems):
    started = [
        pltpu.make_async_copy(source, target, sems.at[index])
        for index, (source, target) in enumerate(pairs)
    ]
    for copy in started:
        copy.start()
    for copy in started:
        copy.wait()


class Part:
    def __init__(self, blocks, rows, lanes):
        self.blocks, self.rows, self.lanes = (blocks, rows, lanes)
        self.across = WIDTH // lanes
        self.travel = blocks * rows // self.across

    def moves(self):
        if self.across > 1:
            deep = self.rows // self.across
            return [(0, part * self.lanes, deep, 0, part * deep) for part in range(self.across)]
        return [(block * self.rows, 0, self.rows, block, 0) for block in range(self.blocks)]

    def pack(self, piece):
        if self.across > 1:
            piece = piece.reshape(self.across, self.rows // self.across, self.lanes)
            return piece.transpose(1, 0, 2).reshape(self.travel, WIDTH)
        return piece.reshape(self.travel, WIDTH)

    def unpack(self, rows):
        if self.across > 1:
            rows = rows.reshape(self.rows // self.across, self.across, self.lanes)
            return rows.transpose(1, 0, 2).reshape(1, self.rows, self.lanes)
        return rows.reshape(self.blocks, self.rows, self.lanes)

    def full(self, depth):
        return (self.blocks, depth, 2, 2, 2, self.rows, self.lanes)


def half_rows(parts):
    total = sum(part.travel for part in parts)
    return -(-total // (2 * TILE)) * TILE


def half_moves(parts):
    cut = half_rows(parts)
    halves = ([], [])
    offset = 0
    for index, part in enumerate(parts):
        for row, lane, rows, block, inner in part.moves():
            row = row + offset
            before = max(0, min(rows, cut - row))
            if before:
                halves[0].append((index, row, lane, before, block, inner))
            if rows - before:
                halves[1].append((index, row + before - cut, lane, rows - before, block, inner + before))
        offset += part.travel
    return halves


def unit(parts, depth):
    return (depth, 2, half_rows(parts), WIDTH)


def pack(parts, pieces):
    rows = jnp.concatenate([part.pack(piece) for part, piece in zip(parts, pieces)])
    return jnp.pad(rows, ((0, 2 * half_rows(parts) - rows.shape[0]), (0, 0)))


def assemble_pairs(parts, core, y, x, ins, outs):
    pairs = []
    for other, far, near in itertools.product((0, 1), repeat=3):
        half = core ^ other
        step = [0, 0, 0, 0]
        step[NEAR[half]], step[FAR[half]] = (near, far)
        at_y, at_x = (lax.rem(y + step[1], 2), lax.rem(x + step[2], 2))
        for index, row, lane, rows, block, inner in half_moves(parts)[half]:
            if index not in outs:
                continue
            pairs.append(
                (
                    index,
                    ins[2 * other + far].at[near, :, :, pl.ds(row, rows), pl.ds(lane, parts[index].lanes)],
                    outs[index].at[block, :, at_y, at_x, :, pl.ds(inner, rows)],
                )
            )
    return pairs


def fetch(parts, tuned, place, sources, weights, sems):
    if not tuned:
        for index, weight in weights.items():
            pltpu.make_async_copy(sources[index], weight, sems.at[index]).start()
        return
    for core in (0, 1):

        @pl.when(place[3] == core)
        def _():
            pairs = assemble_pairs(parts, core, place[1], place[2], sources, weights)
            for index, source, target in sorted(pairs, key=lambda pair: pair[0]):
                pltpu.make_async_copy(source, target, sems.at[index]).start()


def weight_shapes(parts, buffers, tuned):
    if tuned:
        return [part.full(buffers[0].shape[1]) for part in parts]
    return [item.shape for item in buffers]


def assemble_kernel(parts, some, place, *refs):
    outs, sems = (dict(zip(some, refs[4:-1])), refs[-1])
    fetch(parts, True, place, refs[:4], outs, sems)
    for index, out in outs.items():
        pltpu.make_async_copy(out, out, sems.at[index]).wait()


def assemble(parts, buffers, place, some=None):
    some = range(len(parts)) if some is None else some
    shapes = weight_shapes(parts, buffers, True)
    full = pl.pallas_call(
        functools.partial(assemble_kernel, parts, some),
        out_shape=[bf16(*shapes[index]) for index in some],
        in_specs=in_smem() + hbm(4),
        out_specs=in_vmem(len(some)),
        scratch_shapes=[pltpu.SemaphoreType.DMA((len(parts),))],
        compiler_params=pltpu.CompilerParams(vmem_limit_bytes=VMEM_LIMIT),
        cost_estimate=LIGHT,
        name="assemble",
    )(place, *buffers)
    return [merged(item) for item in full]


def merged(array):
    return array.reshape(array.shape[0], -1, array.shape[-1])


def in_order(own, other, bit):
    first = jnp.where(bit == 0, own, other)
    second = jnp.where(bit == 0, other, own)
    return jnp.stack([first, second])


def together(*trees):
    flat, tree = jax.tree.flatten(trees)
    return jax.tree.unflatten(tree, lax.optimization_barrier(flat))


def start_gather(groups, pieces, place):
    core = place[3]
    packed = [pack(parts, items) for parts, items in zip(groups, pieces)]
    halves = [half_rows(parts) for parts in groups]
    kept = [lax.dynamic_slice_in_dim(rows, core * half, half) for rows, half in zip(packed, halves)]
    sent = [
        lax.dynamic_slice_in_dim(rows, (1 - core) * half, half) for rows, half in zip(packed, halves)
    ]
    got = hop(jnp.concatenate(sent), ACROSS)
    held = []
    offset = 0
    for keep, half in zip(kept, halves):
        held.append(in_order(keep, got[offset : offset + half], core))
        offset += half
    return held


def pipelined_gather(groups, pieces, place, state, arrived):
    count = len(groups)
    low, high = (place[0] % 2, place[0] // 2)
    held = start_gather(groups[:1], pieces(None)[:1], place)
    for tick in range(count + 3):
        near, far, last = [index if 0 <= index < count else None for index in range(tick - 1, tick - 4, -1)]
        live = [index for index in (tick, near, far, last) if index is not None and index < count]
        if tick in (1, 2):
            live += range(tick + 1, count)
        items, state = together([held[index] for index in live], state)
        for index, item in zip(live, items):
            held[index] = item
        if tick == 0:
            held += start_gather(groups[1:2], pieces(held[0])[1:2], place)
            held += start_gather(groups[2:], pieces(held[1])[2:], place)
        if last is not None:
            own, arrived_far, other = held[last]
            held[last] = [own, arrived_far, other, hop(arrived_far, ACROSS)]
        if far is not None:
            held[far] = [held[far], hop(held[far], FAR), hop(held[far], ACROSS)]
        if near is not None:
            held[near] = [held[near], hop(held[near], NEAR)]
        if tick == 0:
            held[0] = [held[0]] + [hop(held[0], ALONG_Z, swap=bits) for bits in (1, 2, 3)]
        elif tick < count:
            held[tick] = [held[tick], hop(held[tick], ALONG_Z, swap=2)]
        if tick < 3:
            early = slice(tick + 1, tick + 2 if tick < 2 else count)
            got = hop(jnp.concatenate(held[early], axis=1), ALONG_Z, swap=1)
            ends = list(itertools.accumulate(half_rows(parts) for parts in groups[early]))
            got = jnp.split(got, ends[:-1], axis=1)
            held[early] = [in_order(item, other, low) for item, other in zip(held[early], got)]
        if last is not None:
            state = arrived(last, held[last], state)
        if tick < count:
            items, state = together(held[tick], state)
            if tick == 0:
                items = [in_order(*items[:2], low), in_order(*items[2:], low)]
            both = in_order(*items, high)
            held[tick] = both.reshape(-1, *both.shape[2:])
        if near is not None:
            items, state = together(held[near], state)
            held[near] = jnp.stack(items)
    return state


def whole_shape(part):
    return (part.blocks, part.rows * lax.axis_size(AXES), part.lanes)


def dealt_shapes(parts, tuned):
    if not tuned:
        return [whole_shape(part) for part in parts]
    size = (grid_sizes()[0], 2, half_rows(parts), WIDTH)
    return [lead + size for lead in ((2, 2), (2,), (), ())]


def start_deal(parts, tuned, place, wanted, arrays, dealt, sems):
    if not tuned:
        pltpu.make_async_copy(arrays[wanted], dealt[wanted], sems.at[wanted]).start()
        return
    array = arrays[wanted].reshape(*parts[wanted].full(grid_sizes()[0]))
    to_core, to_far, to_near, own = dealt
    for core in (0, 1):

        @pl.when(place[3] == core)
        def _():
            for other, far, near in itertools.product((0, 1), repeat=3):
                half = core ^ other
                step = [0, 0, 0, 0]
                step[NEAR[half]], step[FAR[half]] = (near, far)
                at_y, at_x = (lax.rem(place[1] + step[1], 2), lax.rem(place[2] + step[2], 2))
                if other:
                    target = to_core.at[far, near]
                elif far:
                    target = to_far.at[near]
                else:
                    target = to_near if near else own
                for index, row, lane, rows, block, inner in half_moves(parts)[half]:
                    if index == wanted:
                        pltpu.make_async_copy(
                            array.at[block, :, at_y, at_x, :, pl.ds(inner, rows)],
                            target.at[:, :, pl.ds(row, rows), pl.ds(lane, parts[index].lanes)],
                            sems.at[index],
                        ).start()


def add_up(*terms):
    total = terms[0].astype(jnp.float32)
    for term in terms[1:]:
        total = total + term.astype(jnp.float32)
    return total


def low_add(*terms):
    return add_up(*terms).astype(jnp.bfloat16)


def scatter_stages(place, direct):
    depth = grid_sizes()[0]
    z, core = (place[0], place[3])
    low, high = (z % 2, z // 2)

    def across(items):
        to_core, *rest = items
        return rest + [hop(to_core, ACROSS)]

    def far(items):
        to_far, to_near, own, from_core = items
        return [to_near, own, from_core, hop(low_add(to_far, from_core[1]), FAR)]

    def near(items):
        to_near, own, from_core, from_far = items
        from_near = hop(low_add(to_near, from_core[0, 1], from_far[1]), NEAR)
        return [own, from_core, from_far, from_near]

    def pick(array, at):
        return lax.dynamic_index_in_dim(array, at, 0, False)

    def gathered(items):
        own, from_core, from_far, from_near = items
        return lax.optimization_barrier(add_up(own, from_core[0, 0], from_far[0], from_near))

    def along(items):
        summed = gathered(items)
        sent = [pick(summed, lax.rem(z + step, depth)) for step in range(1, depth)]
        got = [hop(item.astype(jnp.bfloat16), ALONG_Z, step + 1) for step, item in enumerate(sent)]
        return [pick(summed, z)] + got

    def pairs(items):
        summed = gathered(items)
        summed = summed.reshape(2, 2, *summed.shape[1:])
        return [pick(summed, high), hop(pick(summed, 1 - high).astype(jnp.bfloat16), ALONG_Z, swap=2)]

    def neighbours(items):
        summed = add_up(*items)
        return [pick(summed, low), hop(pick(summed, 1 - low).astype(jnp.bfloat16), ALONG_Z, swap=1)]

    def finish(items):
        total = add_up(*items)
        other = hop(pick(total, 1 - core), ACROSS)
        return in_order(pick(total, core), other, core).reshape(-1, WIDTH)

    return [across, far, near] + ([along] if direct else [pairs, neighbours]) + [finish]


def share_stages(part, place):
    low, high = (place[0] % 2, place[0] // 2)

    def pairs(item):
        both = in_order(item, hop(item, ALONG_Z, swap=2), high)
        return both.reshape(-1, *both.shape[2:])

    return [
        lambda item: start_gather([[part]], [[item]], place)[0],
        lambda item: in_order(item, hop(item, ALONG_Z, swap=1), low),
        pairs,
        lambda item: jnp.stack([item, hop(item, NEAR)]),
        lambda item: [item, hop(item, FAR), hop(item, ACROSS)],
        lambda items: items + [hop(items[1], ACROSS)],
    ]


def pipelined_scatter(count, place, state, steps, shared):
    held, todo = ([], [])
    part, piece, more = shared
    share = share_stages(part, place)
    for tick in range(count + 5):
        live = [index for index in range(len(held)) if todo[index]]
        items, state, piece = together([held[index] for index in live], state, piece)
        for index, item in zip(live, items):
            held[index] = item
            for _ in range(2 if index == tick - 1 else 1):
                held[index] = todo[index].pop(0)(held[index])
        if share:
            piece = share.pop(0)(piece)
        elif more:
            piece = more.pop(0)(piece, held)
        if tick < count:
            dealt, state = steps[tick](state)
            held.append(dealt)
            todo.append(scatter_stages(place, tick >= count - 3))
    return (held, piece, state)


CQL_WEIGHT = 0.05
BETA_ONE = 0.5
BETA_TWO = 0.5
LEARNING_RATE = 0.25
WEIGHT_DECAY = 0.01
PATCH_IN = 256
DPROJ = 512
ACTIONS = 18
ATOMS = 51
GAMES = 4
BLOCKS = 2
STEP = 5
PLAYS = ACTIONS * ATOMS


def average_decay():
    return min(0.99, (1.0 + STEP) / (10.0 + STEP))


SWEEP = 8192


def lamb_parts(grads, params, first, second):
    momentum = BETA_ONE * first + (1.0 - BETA_ONE) * grads
    variance = BETA_TWO * second + (1.0 - BETA_TWO) * grads * grads
    direction = (
        momentum / (1.0 - BETA_ONE**STEP) / (jnp.sqrt(variance / (1.0 - BETA_TWO**STEP)) + 1e-06)
        + WEIGHT_DECAY * params
    )
    return (momentum, variance, direction)


def stretches(cuts):
    found = []
    at = 0
    for index, (start, size) in enumerate(cuts):
        end = start + size
        last = index == len(cuts) - 1
        whole = end if last else end // ROWS * ROWS
        found.append((at, whole - at, [index]))
        at = whole
        if end != whole:
            found.append((whole, ROWS, [index, index + 1]))
            at = whole + ROWS
    return found


def sweep(start, size, body, carry):
    steps = size // SWEEP

    def step(index, carry):
        return body(pl.ds(pl.multiple_of(start + index * SWEEP, ROWS), SWEEP), carry)

    if steps:
        carry = lax.fori_loop(0, steps, step, carry)
    return (carry, start + steps * SWEEP, size - steps * SWEEP)


def row_sum(value):
    return jnp.sum(value, axis=1, keepdims=True)


def put_rows(target, row, source, steps):
    for first, rows, lane, stride in steps:

        def step(index, carry):
            lanes = pl.ds(pl.multiple_of(lane + index * stride, ROWS), WIDTH)
            target[row : row + 1, lanes] = source[pl.ds(first + index, 1), :]
            return carry

        lax.fori_loop(0, rows, step, 0, unroll=4)


def block_rows(name, start, rows, first):
    if name == "w_out":
        count = rows // (D // BOT)
        return [(first + part * count, count, start + part * BOT, D) for part in range(D // BOT)]
    return [(first, rows, start, WIDTH)]


def patch_rows(rows, first):
    count = rows // 4
    return [
        (first + (2 * block + half) * count, count, half * (D // 2) + block * WIDTH, D)
        for block in range(2)
        for half in range(2)
    ]


def direction_kernel(cuts, moves, gain_at, *refs):
    top_cuts, block_cuts = cuts
    number = len(moves)
    sources, refs = (refs[:number], refs[number:])
    late, loss, *refs = refs
    top_ins, block_ins, refs = (refs[:3], refs[3:6], refs[6:])
    sums, *refs = refs
    top_outs, block_outs, (top_grad, block_grad) = (refs[:3], refs[3:6], refs[6:])
    for source, steps in zip(sources, moves):
        for row, placed in steps:
            put_rows(top_grad if row is None else block_grad, row or 0, source, placed)
    patch = top_cuts[0][1]
    top_grad[:, pl.ds(patch, late.shape[1])] = late[...]
    gain_start, gain_width = block_cuts[3]
    source, first = (sources[gain_at[0]], gain_at[1])
    block_grad[:, pl.ds(gain_start, gain_width)] = source[pl.ds(first, 8), :][:BLOCKS, :gain_width]

    def work(lanes, grad, ins, outs):
        param, *moments = [ref[:, lanes] for ref in ins]
        made = lamb_parts(grad[:, lanes], param, *moments)
        for ref, value in zip(outs, made):
            ref[:, lanes] = value
        return (param * param, made[2] * made[2])

    found = []

    def run(cuts, grad, ins, outs, first_lane, height):
        for start, size, segments in stretches(cuts):

            def step(lanes, carry):
                terms = work(lanes, grad, ins, outs)
                return [held + term for held, term in zip(carry, terms)]

            zeros = [jnp.zeros((height, SWEEP), jnp.float32)] * 2
            carry, begin, rest = sweep(start, size, step, zeros)
            sizes = [row_sum(value) for value in carry] if rest != size else None
            if rest:
                terms = work(pl.ds(begin, rest), grad, ins, outs)
                at = begin + lax.broadcasted_iota(jnp.int32, terms[0].shape, 1)
                if len(segments) > 1:
                    edge = cuts[segments[1]][0]
                    after = [row_sum(jnp.where(at >= edge, term, 0.0)) for term in terms]
                    found.extend((first_lane, segments[1], *item) for item in enumerate(after))
                    terms = [jnp.where(at < edge, term, 0.0) for term in terms]
                more = [row_sum(term) for term in terms]
                sizes = more if sizes is None else [held + term for held, term in zip(sizes, more)]
            found.extend((first_lane, segments[0], *item) for item in enumerate(sizes))

    run(top_cuts, top_grad, top_ins, top_outs, 0, 1)
    run(block_cuts, block_grad, block_ins, block_outs, len(top_cuts), BLOCKS)
    rows = lax.broadcasted_iota(jnp.int32, sums.shape, 0)
    lanes = lax.broadcasted_iota(jnp.int32, sums.shape, 1)
    result = jnp.where((rows == 2) & (lanes == 0), loss[...], 0.0)
    for first, segment, row, value in found:
        for part in range(value.shape[0]):
            lane = first + part * len(block_cuts) + segment
            here = (rows == row) & (lanes == lane)
            result = result + jnp.where(here, value[part : part + 1], 0.0)
    sums[...] = result


def directions(cuts, rows, moves, gain_at, late, loss, top_ins, block_ins):
    shapes = [f32(*top_ins[0].shape)] * 3 + [f32(*block_ins[0].shape)] * 3
    ins = [*rows, late, loss, *top_ins, *block_ins]
    return pl.pallas_call(
        functools.partial(direction_kernel, cuts, moves, gain_at),
        out_shape=[f32(8, ROWS)] + shapes,
        in_specs=in_vmem(len(ins)),
        out_specs=in_vmem(7),
        scratch_shapes=[
            pltpu.VMEM(top_ins[0].shape, jnp.float32),
            pltpu.VMEM(block_ins[0].shape, jnp.float32),
        ],
        compiler_params=pltpu.CompilerParams(vmem_limit_bytes=VMEM_LIMIT),
        cost_estimate=LIGHT,
        name="directions",
    )(*ins)


def update_kernel(cuts, sums, *refs):
    top_cuts, block_cuts = cuts
    top_ins, block_ins, refs = (refs[:3], refs[3:6], refs[6:])
    norms, *refs = refs
    top_outs, block_outs = (refs[:2], refs[2:])
    norm = jnp.sqrt(sums[...])
    norms[...] = norm
    ratio = LEARNING_RATE * (norm[0:1] / (norm[1:2] + 1e-06))
    decay = average_decay()

    def work(lanes, ins, outs, scale):
        param, direction, average = [ref[:, lanes] for ref in ins]
        updated, averaged, *half = outs
        value = param - scale * direction
        updated[:, lanes] = value
        averaged[:, lanes] = decay * average + (1.0 - decay) * value
        for ref in half:
            ref[:, lanes] = value.astype(jnp.bfloat16)

    def run(cuts, ins, outs, scales):
        for start, size, segments in stretches(cuts):
            scale = scales[segments[0]]

            def step(lanes, carry):
                work(lanes, ins, outs, scale)
                return carry

            _, begin, rest = sweep(start, size, step, 0)
            if rest:
                if len(segments) > 1:
                    at = begin + lax.broadcasted_iota(jnp.int32, (1, rest), 1)
                    scale = jnp.where(at < cuts[segments[1]][0], scale, scales[segments[1]])
                work(pl.ds(begin, rest), ins, outs, scale)

    lanes = [ratio[:, lane : lane + 1] for lane in range(len(top_cuts) + BLOCKS * len(block_cuts))]
    run(top_cuts, top_ins, top_outs, lanes[: len(top_cuts)])
    rest = lanes[len(top_cuts) :]
    scales = [jnp.concatenate(rest[index :: len(block_cuts)]) for index in range(len(block_cuts))]
    run(block_cuts, block_ins, block_outs, scales)


def update(cuts, sums, top_ins, block_ins):
    shapes = [f32(*array.shape) for array in [top_ins[0]] * 2 + [block_ins[0]] * 2]
    shapes.append(bf16(*block_ins[0].shape))
    return pl.pallas_call(
        functools.partial(update_kernel, cuts),
        out_shape=[f32(8, ROWS)] + shapes,
        in_specs=in_vmem(7),
        out_specs=in_vmem(6),
        compiler_params=pltpu.CompilerParams(vmem_limit_bytes=VMEM_LIMIT),
        cost_estimate=LIGHT,
        name="update",
    )(sums, *top_ins, *block_ins)


def segment_lengths():
    top = [PATCH_IN * D, D * PIX, D * DPROJ, DPROJ * GAMES * PLAYS]
    block = [D * BOT, 9 * BOT * BOT, BOT * D, 2 * (2 * BOT + D)]
    return (top, block)


def cut_points(lengths, devices):
    cuts = []
    offset = 0
    for length in lengths:
        width = length // devices
        cuts.append((offset, width))
        offset += width
    return cuts


def pack_top(flat, cuts):
    patch, pool, proj, heads = [flat[start : start + size] for start, size in cuts]
    patch = patch.reshape(-1, 2, 2, WIDTH).transpose(2, 1, 0, 3).reshape(2, -1, WIDTH)
    pool = jnp.pad(pool.reshape(1, -1, PIX), ((0, 0), (0, 0), (0, ROWS - PIX)))
    heads = jnp.pad(heads.reshape(-1, GAMES, PLAYS), ((0, 0), (0, 0), (0, 2 * WIDTH - PLAYS)))
    heads = heads.reshape(-1, 2 * GAMES, WIDTH).transpose(1, 0, 2)
    return [patch, pool, proj.reshape(1, -1, WIDTH), heads]


def flat_late(pool, proj, heads):
    heads = heads.transpose(1, 0, 2).reshape(-1, GAMES, 2 * WIDTH)[:, :, :PLAYS]
    return jnp.concatenate([item.reshape(-1) for item in (pool[:, :, :PIX], proj, heads)])


def pack_block(flat, cuts):
    w_in, w_mid, w_out = [flat[start : start + size] for start, size in cuts[:3]]
    w_out = w_out.reshape(-1, D // BOT, BOT).transpose(1, 0, 2)
    return [w_in.reshape(1, -1, BOT), w_mid.reshape(1, -1, BOT), w_out]


def parts_for(devices):
    rows = {"patch": 2 * PATCH_IN, "pool": D, "proj": D, "heads": DPROJ}
    rows |= {"w_in": D, "w_mid": TAPS * BOT, "w_out": BOT, "gains": TILE * devices}
    blocks = {"patch": 2, "heads": 2 * GAMES, "w_out": D // BOT}
    return {
        name: Part(blocks.get(name, 1), count // devices, ROWS if name == "pool" else WIDTH)
        for name, count in rows.items()
    }


def is_tuned(devices):
    parts = parts_for(devices).values()
    whole = all(part.rows // part.across % TILE == 0 for part in parts)
    return whole and lax.axis_size("wide") == 8 and lax.axis_size("narrow") == 4


def plain_gather(piece):
    return lax.all_gather(piece, AXES, axis=1, tiled=True)


def plain_scatter(array):
    return lax.psum_scatter(array, AXES, scatter_dimension=1, tiled=True).astype(jnp.float32)


def total(array):
    if lax.axis_size("wide") != 8 or lax.axis_size("narrow") != 4:
        return lax.psum(array, AXES)
    array = array + flip(array, 0, 0, 0, 1)
    array = (array + flip(array, 0, 0, 1, 0)) + (flip(array, 0, 1, 0, 0) + flip(array, 0, 1, 1, 0))
    one, two, three = [flip(array, bits, 0, 0, 0) for bits in (1, 2, 3)]
    return (array + two) + (one + three)


def frame_rows(frames):
    count = frames.shape[0]
    return jnp.pad(frames, ((0, 0), (0, ROWS - PIX), (0, 0))).reshape(count * ROWS, PATCH_IN)


def on_device(
    observed,
    following,
    game_ids,
    actions,
    legal_mask,
    rewards,
    discounts,
    done_flags,
    params_top,
    params_blocks,
    first_top,
    first_blocks,
    second_top,
    second_blocks,
    average_top,
    average_blocks,
    target_top,
    target_blocks,
):
    devices = lax.axis_size(AXES)
    frames_all = observed.shape[0] * devices
    top_lengths, block_lengths = segment_lengths()
    top_cuts = cut_points(top_lengths, devices)
    block_cuts = cut_points(block_lengths, devices)
    gain_start, gain_width = block_cuts[3]
    parts = parts_for(devices)
    tuned = is_tuned(devices)
    place = spot()
    shift = shifts()
    spread = spread_pixels(devices)
    count = observed.shape[0]
    whole = jnp.concatenate([game_ids[:, None], actions], axis=1)
    whole = jnp.pad(whole, ((0, 8 - count), (0, ROWS - 3)), constant_values=-1)
    legal = jnp.pad(legal_mask, ((0, 8 - count), (0, ROWS - ACTIONS)), constant_values=1)
    keep = discounts * (1.0 - done_flags.astype(jnp.float32))
    real = jnp.pad(jnp.stack([rewards, keep], axis=1), ((0, 8 - count), (0, ROWS - 2)))

    def read_pieces(early):
        sources = (target_top, target_blocks, params_top, params_blocks)
        if early is not None:
            early, sources = together(early, sources)
        tops = (sources[0], sources[2].astype(jnp.bfloat16))
        blocks = (sources[1], sources[3].astype(jnp.bfloat16))
        own = {}
        for net, top, flat in zip(("target", "online"), tops, blocks):
            for name, piece in zip(("patch", "pool", "proj", "heads"), pack_top(top, top_cuts)):
                own[net, name] = piece
            for index in range(BLOCKS):
                for name, piece in zip(block_names, pack_block(flat[index], block_cuts)):
                    own[net, name, index] = piece
        gain_rows = jnp.concatenate(blocks)[:, gain_start:]
        own["gains",] = jnp.pad(
            gain_rows, ((0, TILE - 2 * BLOCKS), (0, WIDTH - gain_width))
        ).reshape(1, TILE, WIDTH)
        return [[own[key] for key in group] for group in keys]

    block_names = ("w_in", "w_mid", "w_out")

    def part_of(key):
        return parts[key[0] if key[0] in parts else key[1]]

    full = {}

    def block_weight(index, name):
        return merged(full["online", name, index]).reshape(-1, BOT)

    def lead(group, buffers):
        return assemble(group_parts(group), buffers, place, [0])[0] if tuned else buffers[0]

    def hold(index, group, buffers, state):
        full["held", index] = (group, buffers)
        if index > 1:
            return state
        return state | {"target_pool": lead(group, buffers)[0]}

    def read_gains(group, buffers, state):
        gains = lead(group, buffers).reshape(devices, TILE, WIDTH)[:, : 2 * BLOCKS, :gain_width]
        gains = gains.transpose(1, 0, 2).reshape(2 * BLOCKS, -1).astype(jnp.float32)
        return run_block("target", 0, group, buffers, state | {"gains": gains})

    def target_ends(group, buffers, state):
        for index in range(1, BLOCKS):
            state = run_block("target", index, *full["held", index], state)
        target = head_target(
            state.pop("stream"), state.pop("target_pool"), whole, real,
            group_parts(group), buffers, tuned, place,
        )
        return state | {"target": target}

    def online_ends(group, buffers, state):
        loss, dstream, dpool, acts = head_loss(
            state.pop("stream"), state.pop("online_pool"), state.pop("target"), whole, legal, frames_all,
            group_parts(group), buffers, tuned, place,
        )
        return state | {"loss": loss, "grad": dstream, "pool": dpool, "acts": acts}

    def run_block(net, index, group, buffers, state):
        keep = net == "online"
        row = index + (BLOCKS if keep else 0)
        gain = (state["gains"], row)
        stream = [state["pixels" if keep else "following"], spread]
        if index:
            stream = [state["stream"]]
        skip = 1 if keys[group][0][-1] in ("gains", "pool") else 0
        out, *kept = block_forward(
            stream, gain, shift, group_parts(group), skip, buffers, place, keep, tuned
        )
        state = state | {"stream": out}
        if keep:
            start = kept.pop(0) if index == 0 else stream[0]
            full.update(zip([(net, name, index) for name in block_names], kept[-3:]))
            state |= {"kept%d" % index: [start, *kept[:-3]]}
            if index == 0:
                state |= {"online_pool": lead(group, buffers)[0]}
        return state

    keys, then = ([], [])
    ends = ("proj", "heads")

    def add_group(group, run, *names):
        keys.append(group)
        then.append(functools.partial(run, *names))

    def block_keys(net, index):
        return [(net, name, index) for name in block_names]

    for index in range(1, BLOCKS):
        start = [("target", "pool")] if index == 1 else []
        add_group(start + block_keys("target", index), hold, index)
    add_group([("gains",), ("target", "patch")] + block_keys("target", 0), read_gains)
    add_group([("target", name) for name in ends], target_ends)
    for index in range(BLOCKS):
        start = [] if index else [("online", "pool"), ("online", "patch")]
        add_group(start + block_keys("online", index), run_block, "online", index)
    add_group([("online", name) for name in ends], online_ends)

    def group_parts(group):
        return [part_of(key) for key in keys[group]]

    def arrived(group, buffers, state):
        return then[group](group, buffers, dict(state))

    state = {"following": frame_rows(following), "pixels": frame_rows(observed)}
    if tuned:
        groups = [group_parts(group) for group in range(len(keys))]
        state = pipelined_gather(groups, read_pieces, place, state, arrived)
    else:
        for group, items in enumerate(read_pieces(None)):
            state = arrived(group, [plain_gather(item) for item in items], state)

    keys = []
    steps = []

    def out_inputs(index, state):
        stream, hid_one, hid_two, hid_three, rstd = state["kept%d" % index]
        gain = (state["gains"], BLOCKS + index)
        return [stream, hid_two, hid_three, rstd, block_weight(index, "w_out"), gain]

    def out_step(index, group, state):
        (dres, low, late), dealt = back_out(
            state.pop("grad"), *out_inputs(index, state), group, tuned, place
        )
        return (dealt, state | {"grad": dres, "low": low, "late%d" % index: late})

    def mid_step(index, group, state):
        stream, hid_one, hid_two, hid_three, rstd = state["kept%d" % index]
        gain = (state["gains"], BLOCKS + index)
        more = [state.pop("pool")] if len(group) > 1 else []
        (low, early), dealt = back_mid(
            state["low"], hid_one, rstd, block_weight(index, "w_mid"), gain, shift, more,
            group, tuned, place,
        )
        return (dealt, state | {"low": low, "early%d" % index: early})

    def between_step(index, group, state):
        stream = state.pop("kept%d" % index)[0]
        (dres, low, late), dealt = back_between(
            state["low"], stream, state["grad"], block_weight(index, "w_in"),
            out_inputs(index - 1, state), group, tuned, place,
        )
        return (dealt, state | {"grad": dres, "low": low, "late%d" % (index - 1): late})

    def first_step(group, state):
        stream = state.pop("kept0")[0]
        dgains = [
            jnp.concatenate([state.pop("early%d" % index), state.pop("late%d" % index)], axis=1)
            for index in range(BLOCKS)
        ]
        dgains = jnp.concatenate(dgains).reshape(BLOCKS, devices, gain_width).transpose(1, 0, 2)
        dgains = jnp.pad(dgains, ((0, 0), (0, TILE - BLOCKS), (0, WIDTH - gain_width)))
        dgains = dgains.reshape(1, -1, WIDTH).astype(jnp.bfloat16)
        dealt = back_first(
            state.pop("low"), stream, state.pop("grad"), block_weight(0, "w_in"),
            state.pop("pixels"), spread, dgains, group, tuned, place,
        )
        return (dealt, state)

    def add_step(group, run, *names):
        keys.append(group)
        steps.append(
            lambda state: run(*names, [parts[key[0]] for key in group], dict(state))
        )

    loss_part, acts = (state.pop("loss"), state.pop("acts"))
    add_step([("w_out", BLOCKS - 1)], out_step, BLOCKS - 1)
    for index in reversed(range(BLOCKS)):
        more = [("pool",)] if index == BLOCKS - 1 else []
        add_step([("w_mid", index)] + more, mid_step, index)
        if index:
            add_step([("w_in", index), ("w_out", index - 1)], between_step, index)
    add_step([("w_in", 0), ("patch",), ("gains",)], first_step)
    def read_heads(buffers, rows):
        return own_heads(buffers, parts["heads"], parts["proj"], tuned, place)

    def read_late(pair, rows):
        pool = parts["pool"]
        first = parts["w_mid"].travel
        return flat_late(pool.unpack(rows[1][first : first + pool.travel]), pair[1], pair[0])[None]

    groups = [[parts[key[0]] for key in group] for group in keys]
    if tuned:
        shared = (Part(1, ACTS, WIDTH), acts[None], [read_heads, read_late])
        mine, late, state = pipelined_scatter(len(groups), place, state, steps, shared)
    else:
        mine = []
        for group, step in zip(groups, steps):
            arrays, state = step(state)
            mine.append(pack(group, [plain_scatter(array) for array in arrays]))
        late = read_late(read_heads([plain_gather(acts[None])], mine), mine)
    at = {}
    moves = []
    for number, group in enumerate(keys):
        first = 0
        steps = []
        for key in group:
            count = parts[key[0]].travel
            at[key] = (number, first)
            if len(key) > 1:
                start = block_cuts[block_names.index(key[0])][0]
                steps.append((key[1], block_rows(key[0], start, count, first)))
            elif key[0] == "patch":
                steps.append((None, patch_rows(count, first)))
            first += count
        moves.append(steps)
    cuts = (top_cuts, block_cuts)
    tops = [array[None] for array in (params_top, first_top, second_top, average_top)]
    sums, *made = directions(
        cuts, mine, moves, at["gains",], late, loss_part,
        tops[:3], [params_blocks, first_blocks, second_blocks],
    )
    momentum_top, variance_top, direction_top, momentum_blocks, variance_blocks, direction_blocks = made
    sums = total(sums)
    norms, *made = update(
        cuts, sums, [tops[0], direction_top, tops[3]],
        [params_blocks, direction_blocks, average_blocks],
    )
    updated_top, averaged_top, updated_blocks, averaged_blocks, half_blocks = made
    loss_total = sums[2, 0]
    matrix_norms = norms[:2, : len(top_cuts) + BLOCKS * len(block_cuts)]
    number, first = at["gains",]
    gain_grads = mine[number][first : first + BLOCKS, :gain_width]
    return (
        loss_total,
        matrix_norms,
        updated_top[0],
        updated_top[0].astype(jnp.bfloat16),
        momentum_top[0],
        variance_top[0],
        averaged_top[0],
        updated_blocks,
        half_blocks,
        momentum_blocks,
        variance_blocks,
        averaged_blocks,
        gain_grads,
    )


def solution(mesh):
    one = P(AXES)
    flat = P(None, AXES)
    return jax.shard_map(
        on_device,
        mesh=mesh,
        in_specs=(P(AXES, None, None),) * 2
        + (one, P(AXES, None), P(AXES, None))
        + (one,) * 3
        + (one, flat) * 5,
        out_specs=(P(), P()) + (one,) * 5 + (flat,) * 6,
        check_vma=False,
    )
```
